32 devices in a mesh: scen: 4 (over y, x), gx: 2 (over core), gy: 4 (over z).
Axes of the slice: x: 2, y: 2, z: 4, core: 2. Of those that a mesh axis runs over, the one named last changes fastest.
Arguments:
- perm_log: float32 [2, 128, 512], P(None, 'gx', 'gy'), may hold values from -2.5 to 2.5
- facies: int32 [2, 128, 512], P(None, 'gx', 'gy'), may hold values from 0 to 3
- facies_scale: float32 [4], replicated, may hold values from 0.5 to 2
- accumulation: float32 [2, 128, 512], P(None, 'gx', 'gy'), may hold values from 0.05 to 0.5
- previous_pressure: float32 [4, 2, 128, 512], P('scen', None, 'gx', 'gy'), may hold values from -6 to 6
- observed: float32 [4, 2, 128, 512], P('scen', None, 'gx', 'gy'), may hold values from -6 to 6
- well_cells: int32 [4, 5], P('scen'), may hold values from 0 to 131071
- well_rates: float32 [4, 5], P('scen'), may hold values from 5 to 20
Outputs:
- pressure: float32 [4, 2, 128, 512], P('scen', None, 'gx', 'gy')
- adjoint: float32 [4, 2, 128, 512], P('scen', None, 'gx', 'gy')
- gradient: float32 [2, 128, 512], P(None, 'gx', 'gy')
The draws below stay inside these ranges and needn't reach their ends.
Inputs may be any that keep to these rules, and one draw needn't show every extreme that they name: `well_cells`: a flat index layer * 128 * 512 + row * 512 + column of a grid cell; several wells may share a cell.
All inputs are finite; a program needn't handle non-finite values.
Results may differ from the reference program's by a relative error of at most 0.0001.
Values sent between devices are 32-bit elements; how exact they have to be, the bound alone decides.
No kernel may reach another device: no remote copies, remote signals or barrier semaphores. Data moves between devices by JAX's collectives and lax.ppermute only.
A program may use at most 128 MiB of HBM per device.

```python
import math
import jax
import jax.numpy as jnp

LZ = 2
WELLS = 5
FACIES = 4
SMOOTH = 2
COARSE = 4
SCEN = 4
NX = 128
NY = 512


def touch_ends(values, own_key, least, high):
    index_at = [jax.random.randint(jax.random.fold_in(own_key, axis), (), 0, length) for axis, length in enumerate(values.shape)]
    main_axis = values.shape.index(max(values.shape))
    beside = index_at[:main_axis] + [(index_at[main_axis] + 1) % values.shape[main_axis]] + index_at[main_axis + 1:]
    return values.at[tuple(index_at)].set(least).at[tuple(beside)].set(high)


def levels(stream_key, shape, shards, smallest, high):
    def one(axis_at, parts):
        heights = jax.random.uniform(jax.random.fold_in(jax.random.fold_in(stream_key, 6), axis_at), (parts,), jnp.float32, smallest / len(shards), high / len(shards))
        return jnp.repeat(jnp.exp(heights), shape[axis_at] // parts).reshape((-1,) + (1,) * (len(shape) - axis_at - 1))

    factor_of = one(*shards[0])
    for cut in shards[1:]:
        factor_of = factor_of * one(*cut)
    return factor_of


def scatter_about(rng, extent, width, most, cuts=(), kind=jnp.bfloat16):
    drawn = jax.random.normal(rng, extent, jnp.float32) * width
    if len(cuts) > 0:
        drawn = levels(rng, extent, cuts, -0.22, 0.18) * drawn
    return jnp.clip(drawn, min=-most, max=most).astype(kind)


def setup_inputs(seed: int = 0) -> dict:
    arg_keys = jax.random.split(jax.random.key(seed), 9)
    return {
        "perm_log": scatter_about(arg_keys[0], (LZ, NX, NY), 0.7, 2.5, ((1, 2), (2, 4)), jnp.float32),
        "facies": touch_ends(jax.random.randint(arg_keys[1], (LZ, NX, NY), 0, FACIES), jax.random.fold_in(arg_keys[1], 1), 0, FACIES - 1).astype(jnp.int32),
        "facies_scale": jnp.clip(jnp.exp(jax.random.uniform(arg_keys[2], (FACIES,), jnp.float32, math.log(0.5), math.log(2.0))), 0.5, 2.0),
        "accumulation": jnp.clip(jnp.exp(math.log(0.5) - 2.3025851 * jax.random.uniform(arg_keys[3], (LZ, NX, NY), jnp.float32) ** levels(arg_keys[3], (LZ, NX, NY), ((1, 2), (2, 4)), -0.2, 0.2)), 0.05, 0.5),
        "previous_pressure": scatter_about(arg_keys[4], (SCEN, LZ, NX, NY), 1.0, 6.0, ((0, 4), (2, 2), (3, 4)), jnp.float32),
        "observed": scatter_about(arg_keys[5], (SCEN, LZ, NX, NY), 1.0, 6.0, ((0, 4), (2, 2), (3, 4)), jnp.float32),
        "well_cells": touch_ends(jax.random.randint(arg_keys[6], (SCEN, WELLS), 0, LZ * NX * NY), jax.random.fold_in(arg_keys[6], 1), 0, (LZ * NX * NY) - 1).astype(jnp.int32),
        "well_rates": jnp.clip(5.0 + 15.0 * jax.random.uniform(arg_keys[7], (SCEN, WELLS), jnp.float32) ** levels(arg_keys[7], (SCEN, WELLS), ((0, 4),), -0.2, 0.2), 5.0, 20.0),
    }


vertical = 0.3
damping = 0.8


def harmonic(left, right):
    return 2.0 * left * right / (left + right)


def planar(padded):
    return (padded[..., :-2, 1:-1], padded[..., 2:, 1:-1], padded[..., 1:-1, :-2], padded[..., 1:-1, 2:])


def layer_pair(values):
    padded = jnp.pad(values, ((1, 1), (0, 0), (0, 0)))
    return padded[:-2], padded[2:]


def padded_neighbours(values):
    return planar(jnp.pad(values, ((0, 0), (1, 1), (1, 1))))


def build_coeffs(permeability, beside, accumulation):
    below, above = layer_pair(permeability)
    return jnp.stack([harmonic(permeability, beside[0]), harmonic(permeability, beside[1]),
                      harmonic(permeability, beside[2]), harmonic(permeability, beside[3]),
                      vertical * harmonic(permeability, below), vertical * harmonic(permeability, above),
                      accumulation])


def coarsen(coeffs):
    member_count, layer_count, row_count, col_count = coeffs.shape
    quads = coeffs.reshape(member_count, layer_count, row_count // 2, 2, col_count // 2, 2)
    return jnp.stack([quads[0, :, :, 0, :, 0] + quads[0, :, :, 0, :, 1],
                      quads[1, :, :, 1, :, 0] + quads[1, :, :, 1, :, 1],
                      quads[2, :, :, 0, :, 0] + quads[2, :, :, 1, :, 0],
                      quads[3, :, :, 0, :, 1] + quads[3, :, :, 1, :, 1],
                      jnp.sum(quads[4], (2, 4)), jnp.sum(quads[5], (2, 4)), jnp.sum(quads[6], (2, 4))])


def restrict(values):
    layer_count, row_count, col_count = values.shape
    return values.reshape(layer_count, row_count // 2, 2, col_count // 2, 2).sum((2, 4))


def upsample(values):
    return jnp.repeat(jnp.repeat(values, 2, 1), 2, 2)


def apply_op(values, grid_level):
    coeffs, diagonal = grid_level
    row_lo, row_hi, col_lo, col_hi = padded_neighbours(values)
    layer_lo, layer_hi = layer_pair(values)
    return diagonal * values - (coeffs[0] * row_lo + coeffs[1] * row_hi + coeffs[2] * col_lo
                                + coeffs[3] * col_hi + coeffs[4] * layer_lo + coeffs[5] * layer_hi)


def smooth(values, target, grid_level, sweeps):
    for _ in range(sweeps):
        values = values + damping * (target - apply_op(values, grid_level)) / grid_level[1]
    return values


def vcycle(target, initial, grids):
    finest, middle, bottom = grids
    fine_field = smooth(initial, target, finest, SMOOTH)
    middle_target = restrict(target - apply_op(fine_field, finest))
    middle_field = smooth(jnp.zeros_like(middle_target), middle_target, middle, SMOOTH)
    bottom_target = restrict(middle_target - apply_op(middle_field, middle))
    bottom_field = smooth(jnp.zeros_like(bottom_target), bottom_target, bottom, COARSE)
    middle_field = smooth(middle_field + upsample(bottom_field), middle_target, middle, SMOOTH)
    fine_field = fine_field + upsample(middle_field)
    return smooth(fine_field, target, finest, SMOOTH)


def face_term(permeability, perm_side, pressure, pressure_side, adjoint, adjoint_side, weight):
    total_perm = permeability + perm_side
    return weight * permeability * 2.0 * perm_side * perm_side / (total_perm * total_perm) * (adjoint - adjoint_side) * (pressure - pressure_side)


def gradient_terms(permeability, perm_six, pressure, pressure_six, adjoint, adjoint_six):
    weights = (1.0, 1.0, 1.0, 1.0, vertical, vertical)
    total = jnp.zeros_like(permeability)
    for number in range(6):
        total = total + face_term(permeability, perm_six[number], pressure, pressure_six[number],
                                  adjoint, adjoint_six[number], weights[number])
    return total


def with_diagonal(coeffs):
    return (coeffs, jnp.sum(coeffs, 0))


def reference(perm_log, facies, facies_scale, accumulation, previous_pressure, observed, well_cells, well_rates):
    facies_factor = jnp.zeros_like(perm_log)
    for label in range(FACIES):
        facies_factor = facies_factor + jnp.where(facies == label, facies_scale[label], jnp.float32(0.0))
    permeability = jnp.exp(perm_log) * facies_factor
    coeffs = build_coeffs(permeability, padded_neighbours(permeability), accumulation)
    middle = coarsen(coeffs)
    bottom = coarsen(middle)
    grids = (with_diagonal(coeffs), with_diagonal(middle), with_diagonal(bottom))
    perm_six = padded_neighbours(permeability) + layer_pair(permeability)
    total = jnp.zeros_like(permeability)
    pressures = []
    adjoints = []
    for scenario in range(SCEN):
        source = jnp.zeros((LZ * NX * NY,), perm_log.dtype).at[well_cells[scenario]].add(well_rates[scenario]).reshape(LZ, NX, NY)
        pressure = vcycle(accumulation * previous_pressure[scenario] + source, previous_pressure[scenario], grids)
        adjoint = vcycle(pressure - observed[scenario], jnp.zeros_like(pressure), grids)
        total = total + gradient_terms(permeability, perm_six, pressure,
                                       padded_neighbours(pressure) + layer_pair(pressure),
                                       adjoint, padded_neighbours(adjoint) + layer_pair(adjoint))
        pressures.append(pressure)
        adjoints.append(adjoint)
    return jnp.stack(pressures), jnp.stack(adjoints), -total
```

```python
from functools import partial

import jax
import jax.numpy as jnp
from jax import lax
from jax.experimental import pallas as pl
from jax.experimental.pallas import tpu as pltpu
from jax.sharding import PartitionSpec as P

WELLS = 5
FACIES = 4
LAYERS = 2
SMOOTH = 2
COARSE = 4

vertical = 0.3
damping = 0.8

LANES = 128
HALF = 64
SUB = 8
PERM, ACC, PREV, OBS = range(4)


def lane_index():
    return lax.broadcasted_iota(jnp.int32, (SUB, LANES), 1)


def row_index():
    return lax.broadcasted_iota(jnp.int32, (SUB, LANES), 0)


def lane_roll(value, shift):
    return pltpu.roll(value, shift % LANES, value.ndim - 1)


def row_roll(value, shift):
    return pltpu.roll(value, shift % SUB, 0)


def pack_kernel(scale, perm_log, facies, acc, prev, obs, own, to_left, to_right):
    label = facies[...]
    factor = jnp.zeros(label.shape, jnp.float32)
    for number in range(FACIES):
        factor = factor + jnp.where(label == number, scale[number], jnp.float32(0.0))
    fields = (jnp.exp(perm_log[...]) * factor, acc[...], prev[0], obs[0])
    low = lax.broadcasted_iota(jnp.int32, label.shape, 2) < HALF
    for number in range(4):
        own[number] = fields[number]
    for pair in range(2):
        first, second = fields[2 * pair], lane_roll(fields[2 * pair + 1], HALF)
        to_left[pair] = jnp.where(low, first, second)
        to_right[pair] = jnp.where(low, second, first)


class Level:
    def __init__(self, count, span, refs):
        self.count = count
        self.span = span
        (self.c_north, self.c_south, self.c_west, self.c_east, self.c_layer, self.weight, self.diag, self.target,
         self.now, self.later) = refs

    def keys(self, blocks):
        for b in range(blocks):
            for t in range(self.count):
                for u in range(2):
                    for layer in range(LAYERS):
                        yield layer, u, b, t


def east_of(pair, span):
    edge = lane_index() >= LANES - span
    rolled = [lane_roll(value, -span) for value in pair]
    return [jnp.where(edge, rolled[1 - u], rolled[u]) for u in range(2)]


def west_of(pair, span):
    edge = lane_index() < span
    rolled = [lane_roll(value, span) for value in pair]
    return [jnp.where(edge, rolled[1 - u], rolled[u]) for u in range(2)]


def row_before(values, blocks):
    edge = row_index() < 1
    rolled = [row_roll(value, 1) for value in values]
    return [jnp.where(edge, rolled[(b - 1) % blocks], rolled[b]) for b in range(blocks)]


def row_after(values, blocks):
    edge = row_index() >= SUB - 1
    rolled = [row_roll(value, -1) for value in values]
    return [jnp.where(edge, rolled[(b + 1) % blocks], rolled[b]) for b in range(blocks)]


def neighbour_sums(level, source, blocks):
    last = level.count - 1
    before, after = {}, {}
    for layer in range(LAYERS):
        for u in range(2):
            lows = row_before([source[layer, u, b, last] for b in range(blocks)], blocks)
            highs = row_after([source[layer, u, b, 0] for b in range(blocks)], blocks)
            for b in range(blocks):
                before[layer, u, b] = lows[b]
                after[layer, u, b] = highs[b]
    for b in range(blocks):
        for t in range(level.count):
            here = [[source[layer, u, b, t] for u in range(2)] for layer in range(LAYERS)]
            for layer in range(LAYERS):
                east = east_of(here[layer], level.span)
                west = west_of(here[layer], level.span)
                for u in range(2):
                    north = source[layer, u, b, t - 1] if t > 0 else before[layer, u, b]
                    south = source[layer, u, b, t + 1] if t < last else after[layer, u, b]
                    key = layer, u, b, t
                    total = (level.c_north[key] * north + level.c_south[key] * south
                             + (level.c_west[key] * west[u] + level.c_east[key] * east[u])
                             + level.c_layer[u, b, t] * here[1 - layer][u])
                    yield key, here[layer][u], total


def sweep(level, source, result, blocks):
    for key, value, total in neighbour_sums(level, source, blocks):
        result[key] = (1.0 - damping) * value + level.weight[key] * (level.target[key] + total)


def sweeps(level, count, blocks):
    for _ in range(count):
        sweep(level, level.now, level.later, blocks)
        level.now, level.later = level.later, level.now


def first_sweep(level, blocks):
    for key in level.keys(blocks):
        level.now[key] = level.weight[key] * level.target[key]


def pair_sum(value, span):
    lower = lane_index() % (2 * span) < span
    return value + jnp.where(lower, lane_roll(value, -span), lane_roll(value, span))


def low_group(value, span):
    return jnp.where(lane_index() % (2 * span) < span, value, lane_roll(value, span))


def high_group(value, span):
    return jnp.where(lane_index() % (2 * span) < span, lane_roll(value, -span), value)


def restrict_residual(fine, coarse, blocks):
    partial_sum = {}
    for key, value, total in neighbour_sums(fine, fine.now, blocks):
        layer, u, b, t = key
        residual = fine.target[key] + total - fine.diag[key] * value
        if t % 2 == 0:
            partial_sum[layer, u, b] = residual
        else:
            coarse.target[layer, u, b, t // 2] = pair_sum(partial_sum[layer, u, b] + residual, fine.span)


def prolong(coarse, fine, blocks):
    for key in fine.keys(blocks):
        layer, u, b, t = key
        fine.now[key] = fine.now[key] + coarse.now[layer, u, b, t // 2]


def vcycle(levels, from_zero, blocks):
    finest, middle, bottom = levels
    if from_zero:
        first_sweep(finest, blocks)
    sweeps(finest, SMOOTH - int(from_zero), blocks)
    restrict_residual(finest, middle, blocks)
    first_sweep(middle, blocks)
    sweeps(middle, SMOOTH - 1, blocks)
    restrict_residual(middle, bottom, blocks)
    first_sweep(bottom, blocks)
    sweeps(bottom, COARSE - 1, blocks)
    prolong(bottom, middle, blocks)
    sweeps(middle, SMOOTH, blocks)
    prolong(middle, finest, blocks)
    sweeps(finest, SMOOTH, blocks)


def harmonic(left, right):
    return 2.0 * left * right / jnp.maximum(left + right, 1e-20)


def with_weight(level, key, accumulated):
    layer, u, b, t = key
    diag = (level.c_north[key] + level.c_south[key] + level.c_west[key] + level.c_east[key]
            + level.c_layer[u, b, t] + accumulated)
    level.diag[key] = diag
    level.weight[key] = damping / jnp.maximum(diag, 1e-20)


def coarse_coeffs(fine, coarse, fine_acc, coarse_acc, blocks):
    span = fine.span
    for key in coarse.keys(blocks):
        layer, u, b, t = key
        one, two = (layer, u, b, 2 * t), (layer, u, b, 2 * t + 1)
        coarse.c_north[key] = pair_sum(fine.c_north[one], span)
        coarse.c_south[key] = pair_sum(fine.c_south[two], span)
        coarse.c_west[key] = low_group(fine.c_west[one] + fine.c_west[two], span)
        coarse.c_east[key] = high_group(fine.c_east[one] + fine.c_east[two], span)
        if layer == 0:
            coarse.c_layer[u, b, t] = pair_sum(fine.c_layer[one[1:]] + fine.c_layer[two[1:]], span)
        accumulated = pair_sum(fine_acc[one] + fine_acc[two], span)
        if coarse_acc is not None:
            coarse_acc[key] = accumulated
        with_weight(coarse, key, accumulated)


def cycle_kernel(grid_shape, gx_count, blocks, *refs):
    cells, rates = refs[:2]
    inputs = [refs[2 + 3 * b:5 + 3 * b] for b in range(blocks)]
    refs = refs[2 + 3 * blocks:]
    pressure_out, adjoint_out, terms_out = refs[:3]
    refs = refs[3:]
    perm, acc, middle_acc, pressure = refs[:4]
    refs = refs[4:]
    count = inputs[0][0].shape[2] // SUB
    levels = [Level(count >> depth, 1 << depth, refs[10 * depth:10 * depth + 10]) for depth in range(3)]
    finest, middle, bottom = levels
    low_lanes = lane_index() < HALF

    def rows(t):
        return pl.ds(t, SUB, stride=count)

    def field(number, key):
        layer, u, b, t = key
        own, right, left = inputs[b]
        if u == 0:
            return own[number, layer, rows(t), :]
        pair = number // 2
        from_right, from_left = right[pair, layer, rows(t), :], left[pair, layer, rows(t), :]
        if number % 2 == 0:
            return jnp.where(low_lanes, from_right, from_left)
        return lane_roll(jnp.where(low_lanes, from_left, from_right), HALF)

    gx = lax.axis_index("gx")
    if blocks == 3:
        joined = [1.0, 0.0, 1.0]
    elif blocks == 2:
        joined = [1.0 - gx.astype(jnp.float32), gx.astype(jnp.float32)]
    else:
        joined = [0.0]

    for key in finest.keys(blocks):
        perm[key] = field(PERM, key)
        acc[key] = field(ACC, key)
        start = field(PREV, key)
        finest.now[key] = start
        finest.target[key] = acc[key] * start

    layer_count, total_rows, total_cols = grid_shape
    block_rows, block_cols = SUB * count, LANES
    for well in range(WELLS):
        cell = cells[0, well]
        layer = cell // (total_rows * total_cols)
        row = cell // total_cols % total_rows - gx * block_rows
        col = cell % total_cols - lax.axis_index("gy") * block_cols
        if blocks == 3:
            row_inside = (row >= -block_rows) & (row < 2 * block_rows)
        elif blocks == 2:
            row_inside = row >= -block_rows
        else:
            row_inside = row >= 0
        inside = row_inside & (col >= -HALF) & (col < block_cols + HALF)
        row = jnp.where(row < 0, row + blocks * block_rows, row)
        col = jnp.where(col < 0, col + 2 * block_cols, col)
        row = jnp.where(inside, row, 0)
        col = jnp.where(inside, col, 0)
        rate = jnp.where(inside, rates[0, well], 0.0)
        in_block = row % block_rows
        place = layer, col // LANES, row // block_rows, in_block % count
        hit = (row_index() == in_block // count) & (lane_index() == col % LANES)
        finest.target[place] = finest.target[place] + jnp.where(hit, rate, 0.0)

    for layer in range(LAYERS):
        for u in range(2):
            heads = [perm[layer, u, b, 0] for b in range(blocks)]
            edge = row_index() >= SUB - 1
            rolled = [row_roll(value, -1) for value in heads]
            after = [jnp.where(edge, joined[b] * rolled[(b + 1) % blocks], rolled[b]) for b in range(blocks)]
            for b in range(blocks):
                for t in range(count):
                    beyond = perm[layer, u, b, t + 1] if t < count - 1 else after[b]
                    finest.c_south[layer, u, b, t] = harmonic(perm[layer, u, b, t], beyond)
            before = row_before([finest.c_south[layer, u, b, count - 1] for b in range(blocks)], blocks)
            for b in range(blocks):
                for t in range(count):
                    finest.c_north[layer, u, b, t] = finest.c_south[layer, u, b, t - 1] if t > 0 else before[b]
    for b in range(blocks):
        for t in range(count):
            for u in range(2):
                finest.c_layer[u, b, t] = vertical * harmonic(perm[0, u, b, t], perm[1, u, b, t])
            for layer in range(LAYERS):
                here = [perm[layer, u, b, t] for u in range(2)]
                beyond = east_of(here, 1)
                east = [harmonic(here[u], beyond[u]) for u in range(2)]
                west = west_of(east, 1)
                for u in range(2):
                    finest.c_east[layer, u, b, t] = east[u]
                    finest.c_west[layer, u, b, t] = west[u]
    for key in finest.keys(blocks):
        with_weight(finest, key, acc[key])
    coarse_coeffs(finest, middle, acc, middle_acc, blocks)
    coarse_coeffs(middle, bottom, middle_acc, None, blocks)

    vcycle(levels, False, blocks)
    for key in finest.keys(blocks):
        value = finest.now[key]
        pressure[key] = value
        finest.target[key] = value - field(OBS, key)
    vcycle(levels, True, blocks)

    fields = (pressure, finest.now)
    last = count - 1
    ends = {}
    for number, values in enumerate(fields):
        for layer in range(LAYERS):
            ends[number, layer] = (
                row_before([values[layer, 0, b, last] for b in range(blocks)], blocks)[0],
                row_after([values[layer, 0, b, 0] for b in range(blocks)], blocks)[0],
            )
    for t in range(count):
        for layer in range(LAYERS):
            key = layer, 0, 0, t
            differences = []
            for number, values in enumerate(fields):
                pair = [values[layer, u, 0, t] for u in range(2)]
                here = pair[0]
                beside = (
                    values[layer, 0, 0, t - 1] if t > 0 else ends[number, layer][0],
                    values[layer, 0, 0, t + 1] if t < last else ends[number, layer][1],
                    west_of(pair, 1)[0],
                    east_of(pair, 1)[0],
                    values[1 - layer, 0, 0, t],
                )
                differences.append([here - other for other in beside])
                (pressure_out, adjoint_out)[number][0, layer, rows(t), :] = here
            total = jnp.zeros((SUB, LANES), jnp.float32)
            coeffs = (finest.c_north[key], finest.c_south[key], finest.c_west[key], finest.c_east[key])
            for number, coeff in enumerate(coeffs):
                total = total + coeff * coeff * (differences[0][number] * differences[1][number])
            coeff = finest.c_layer[0, 0, t]
            total = total + (1.0 / vertical) * (coeff * coeff) * (differences[0][4] * differences[1][4])
            terms_out[layer, rows(t), :] = -0.5 * total / perm[key]


def moved(value, gx_step, gy_step):
    gx_count, gy_count = lax.axis_size("gx"), lax.axis_size("gy")
    pairs = []
    for x in range(gx_count):
        for y in range(gy_count):
            from_x, from_y = x + gx_step, y + gy_step
            if gx_count == 2:
                from_x %= 2
            if 0 <= from_x < gx_count and 0 <= from_y < gy_count:
                pairs.append((from_x * gy_count + from_y, x * gy_count + y))
    return lax.ppermute(value, ("gx", "gy"), pairs)


def summed(value, axis):
    count = lax.axis_size(axis)
    distance = 1
    while distance < count:
        value = value + lax.ppermute(value, axis, [(i, i ^ distance) for i in range(count)])
        distance *= 2
    return value


def shards(
    perm_log,
    facies,
    facies_scale,
    accumulation,
    previous_pressure,
    observed,
    well_cells,
    well_rates,
):
    layer_count, row_count, col_count = perm_log.shape
    gx_count, gy_count = lax.axis_size("gx"), lax.axis_size("gy")
    vmem = pl.BlockSpec(memory_space=pltpu.VMEM)
    smem = pl.BlockSpec(memory_space=pltpu.SMEM)
    f32 = jnp.float32
    own, to_left, to_right = pl.pallas_call(
        pack_kernel,
        out_shape=[
            jax.ShapeDtypeStruct((4, layer_count, row_count, col_count), f32),
            jax.ShapeDtypeStruct((2, layer_count, row_count, col_count), f32),
            jax.ShapeDtypeStruct((2, layer_count, row_count, col_count), f32),
        ],
        in_specs=[smem] + [vmem] * 5,
        out_specs=[vmem] * 3,
        name="pack",
    )(facies_scale, perm_log, facies, accumulation, previous_pressure, observed)

    steps = (0, 1) if gx_count == 2 else (0, 1, -1) if gx_count > 2 else (0,)
    blocks = len(steps)
    operands = []
    for step in steps:
        operands += [own if step == 0 else moved(own, step, 0), moved(to_left, step, 1), moved(to_right, step, -1)]

    count = row_count // SUB
    scratch = [pltpu.VMEM((LAYERS, 2, blocks, count, SUB, LANES), f32)] * 2
    scratch += [pltpu.VMEM((LAYERS, 2, blocks, count // 2, SUB, LANES), f32)]
    scratch += [pltpu.VMEM((LAYERS, 2, blocks, count, SUB, LANES), f32)]
    for depth in range(3):
        whole = pltpu.VMEM((LAYERS, 2, blocks, count >> depth, SUB, LANES), f32)
        scratch += [whole] * 4 + [pltpu.VMEM((2, blocks, count >> depth, SUB, LANES), f32)] + [whole] * 5
    state = jax.ShapeDtypeStruct((1, layer_count, row_count, col_count), f32)
    grid_shape = (layer_count, row_count * gx_count, col_count * gy_count)
    pressure, adjoint, terms = pl.pallas_call(
        partial(cycle_kernel, grid_shape, gx_count, blocks),
        out_shape=[state, state, jax.ShapeDtypeStruct((layer_count, row_count, col_count), f32)],
        in_specs=[smem] * 2 + [vmem] * (3 * blocks),
        out_specs=[vmem] * 3,
        scratch_shapes=scratch,
        compiler_params=pltpu.CompilerParams(vmem_limit_bytes=24 * 1024 * 1024),
        name="cycles",
    )(well_cells, well_rates, *operands)
    return pressure, adjoint, summed(terms, "scen")


def solution(mesh):
    return jax.shard_map(
        shards,
        mesh=mesh,
        in_specs=(
            P(None, "gx", "gy"),
            P(None, "gx", "gy"),
            P(),
            P(None, "gx", "gy"),
            P("scen", None, "gx", "gy"),
            P("scen", None, "gx", "gy"),
            P("scen", None),
            P("scen", None),
        ),
        out_specs=(P("scen", None, "gx", "gy"), P("scen", None, "gx", "gy"), P(None, "gx", "gy")),
        check_vma=False,
    )
```

```python
from functools import partial

import jax
import jax.numpy as jnp
from jax import lax
from jax.experimental import pallas as pl
from jax.experimental.pallas import tpu as pltpu
from jax.sharding import PartitionSpec as P

WELLS = 5
FACIES = 4
LAYERS = 2
SMOOTH = 2
COARSE = 4

vertical = 0.3
damping = 0.8

LANES = 128
HALF = 64
SUB = 8
PERM, ACC, PREV, OBS = range(4)


def lane_index():
    return lax.broadcasted_iota(jnp.int32, (SUB, LANES), 1)


def row_index():
    return lax.broadcasted_iota(jnp.int32, (SUB, LANES), 0)


def lane_roll(value, shift):
    return pltpu.roll(value, shift % LANES, value.ndim - 1)


def row_roll(value, shift):
    return pltpu.roll(value, shift % SUB, 0)


def pack_kernel(scale, perm_log_hbm, facies_hbm, acc_hbm, prev_hbm, obs_hbm, own, to_left, to_right,
                perm_log, facies, acc, prev, obs, sems):
    pairs = ((perm_log_hbm, perm_log), (facies_hbm, facies), (acc_hbm, acc), (prev_hbm, prev), (obs_hbm, obs))
    copies = [pltpu.make_async_copy(source, target, sems.at[i]) for i, (source, target) in enumerate(pairs)]
    for copy in copies:
        copy.start()
    for copy in copies:
        copy.wait()
    label = facies[...]
    factor = jnp.zeros(label.shape, jnp.float32)
    for number in range(FACIES):
        factor = factor + jnp.where(label == number, scale[number], jnp.float32(0.0))
    fields = (jnp.exp(perm_log[...]) * factor, acc[...], prev[0], obs[0])
    low = lax.broadcasted_iota(jnp.int32, label.shape, 2) < HALF
    for number in range(4):
        own[number] = fields[number]
    for pair in range(2):
        first, second = fields[2 * pair], lane_roll(fields[2 * pair + 1], HALF)
        to_left[pair] = jnp.where(low, first, second)
        to_right[pair] = jnp.where(low, second, first)


def merge_kernel(from_right, from_left, beside):
    low = lax.broadcasted_iota(jnp.int32, beside.shape[1:], 2) < HALF
    for pair in range(2):
        right, left = from_right[pair], from_left[pair]
        beside[2 * pair] = jnp.where(low, right, left)
        beside[2 * pair + 1] = lane_roll(jnp.where(low, left, right), HALF)


class Level:
    def __init__(self, count, span, refs):
        self.count = count
        self.span = span
        (self.c_north, self.c_south, self.c_west, self.c_east, self.c_layer, self.weight, self.diag, self.target,
         self.now, self.later) = refs

    def keys(self, blocks):
        for b in range(blocks):
            for t in range(self.count):
                for u in range(2):
                    for layer in range(LAYERS):
                        yield layer, u, b, t


def east_of(pair, span):
    edge = lane_index() >= LANES - span
    rolled = [lane_roll(value, -span) for value in pair]
    return [jnp.where(edge, rolled[1 - u], rolled[u]) for u in range(2)]


def west_of(pair, span):
    edge = lane_index() < span
    rolled = [lane_roll(value, span) for value in pair]
    return [jnp.where(edge, rolled[1 - u], rolled[u]) for u in range(2)]


def row_before(values, blocks):
    edge = row_index() < 1
    rolled = [row_roll(value, 1) for value in values]
    return [jnp.where(edge, rolled[(b - 1) % blocks], rolled[b]) for b in range(blocks)]


def row_after(values, blocks):
    edge = row_index() >= SUB - 1
    rolled = [row_roll(value, -1) for value in values]
    return [jnp.where(edge, rolled[(b + 1) % blocks], rolled[b]) for b in range(blocks)]


def neighbour_sums(level, source, blocks):
    last = level.count - 1
    before, after = {}, {}
    for layer in range(LAYERS):
        for u in range(2):
            lows = row_before([source[layer, u, b, last] for b in range(blocks)], blocks)
            highs = row_after([source[layer, u, b, 0] for b in range(blocks)], blocks)
            for b in range(blocks):
                before[layer, u, b] = lows[b]
                after[layer, u, b] = highs[b]
    for b in range(blocks):
        for t in range(level.count):
            here = [[source[layer, u, b, t] for u in range(2)] for layer in range(LAYERS)]
            for layer in range(LAYERS):
                east = east_of(here[layer], level.span)
                west = west_of(here[layer], level.span)
                for u in range(2):
                    north = source[layer, u, b, t - 1] if t > 0 else before[layer, u, b]
                    south = source[layer, u, b, t + 1] if t < last else after[layer, u, b]
                    key = layer, u, b, t
                    total = (level.c_north[key] * north + level.c_south[key] * south
                             + (level.c_west[key] * west[u] + level.c_east[key] * east[u])
                             + level.c_layer[u, b, t] * here[1 - layer][u])
                    yield key, here[layer][u], total


def sweep(level, source, result, blocks):
    for key, value, total in neighbour_sums(level, source, blocks):
        result[key] = (1.0 - damping) * value + level.weight[key] * (level.target[key] + total)


def sweeps(level, count, blocks):
    for _ in range(count):
        sweep(level, level.now, level.later, blocks)
        level.now, level.later = level.later, level.now


def first_sweep(level, blocks):
    for key in level.keys(blocks):
        level.now[key] = level.weight[key] * level.target[key]


def pair_sum(value, span):
    lower = lane_index() % (2 * span) < span
    return value + jnp.where(lower, lane_roll(value, -span), lane_roll(value, span))


def low_group(value, span):
    return jnp.where(lane_index() % (2 * span) < span, value, lane_roll(value, span))


def high_group(value, span):
    return jnp.where(lane_index() % (2 * span) < span, lane_roll(value, -span), value)


def restrict_residual(fine, coarse, blocks):
    partial_sum = {}
    for key, value, total in neighbour_sums(fine, fine.now, blocks):
        layer, u, b, t = key
        residual = fine.target[key] + total - fine.diag[key] * value
        if t % 2 == 0:
            partial_sum[layer, u, b] = residual
        else:
            coarse.target[layer, u, b, t // 2] = pair_sum(partial_sum[layer, u, b] + residual, fine.span)


def prolong(coarse, fine, blocks):
    for key in fine.keys(blocks):
        layer, u, b, t = key
        fine.now[key] = fine.now[key] + coarse.now[layer, u, b, t // 2]


def vcycle(levels, from_zero, blocks):
    finest, middle, bottom = levels
    if from_zero:
        first_sweep(finest, blocks)
    sweeps(finest, SMOOTH - int(from_zero), blocks)
    restrict_residual(finest, middle, blocks)
    first_sweep(middle, blocks)
    sweeps(middle, SMOOTH - 1, blocks)
    restrict_residual(middle, bottom, blocks)
    first_sweep(bottom, blocks)
    sweeps(bottom, COARSE - 1, blocks)
    prolong(bottom, middle, blocks)
    sweeps(middle, SMOOTH, blocks)
    prolong(middle, finest, blocks)
    sweeps(finest, SMOOTH, blocks)


def harmonic(left, right):
    return 2.0 * left * right / jnp.maximum(left + right, 1e-20)


def with_weight(level, key, accumulated):
    layer, u, b, t = key
    diag = (level.c_north[key] + level.c_south[key] + level.c_west[key] + level.c_east[key]
            + level.c_layer[u, b, t] + accumulated)
    level.diag[key] = diag
    level.weight[key] = damping / jnp.maximum(diag, 1e-20)


def coarse_coeffs(fine, coarse, fine_acc, coarse_acc, blocks):
    span = fine.span
    for key in coarse.keys(blocks):
        layer, u, b, t = key
        one, two = (layer, u, b, 2 * t), (layer, u, b, 2 * t + 1)
        coarse.c_north[key] = pair_sum(fine.c_north[one], span)
        coarse.c_south[key] = pair_sum(fine.c_south[two], span)
        coarse.c_west[key] = low_group(fine.c_west[one] + fine.c_west[two], span)
        coarse.c_east[key] = high_group(fine.c_east[one] + fine.c_east[two], span)
        if layer == 0:
            coarse.c_layer[u, b, t] = pair_sum(fine.c_layer[one[1:]] + fine.c_layer[two[1:]], span)
        accumulated = pair_sum(fine_acc[one] + fine_acc[two], span)
        if coarse_acc is not None:
            coarse_acc[key] = accumulated
        with_weight(coarse, key, accumulated)


def cycle_kernel(grid_shape, gx_count, blocks, *refs):
    cells, rates = refs[:2]
    inputs = [refs[2 + 2 * b:4 + 2 * b] for b in range(blocks)]
    refs = refs[2 + 2 * blocks:]
    pressure_out, adjoint_out, terms_out = refs[:3]
    refs = refs[3:]
    perm, acc, middle_acc, pressure = refs[:4]
    refs = refs[4:]
    count = inputs[0][0].shape[2] // SUB
    levels = [Level(count >> depth, 1 << depth, refs[10 * depth:10 * depth + 10]) for depth in range(3)]
    finest, middle, bottom = levels

    def rows(t):
        return pl.ds(t, SUB, stride=count)

    def field(number, key):
        layer, u, b, t = key
        return inputs[b][u][number, layer, rows(t), :]

    gx = lax.axis_index("gx")
    if blocks == 3:
        joined = [1.0, 0.0, 1.0]
    elif blocks == 2:
        joined = [1.0 - gx.astype(jnp.float32), gx.astype(jnp.float32)]
    else:
        joined = [0.0]

    for key in finest.keys(blocks):
        perm[key] = field(PERM, key)
        acc[key] = field(ACC, key)
        start = field(PREV, key)
        finest.now[key] = start
        finest.target[key] = acc[key] * start

    layer_count, total_rows, total_cols = grid_shape
    block_rows, block_cols = SUB * count, LANES
    for well in range(WELLS):
        cell = cells[0, well]
        layer = cell // (total_rows * total_cols)
        row = cell // total_cols % total_rows - gx * block_rows
        col = cell % total_cols - lax.axis_index("gy") * block_cols
        if blocks == 3:
            row_inside = (row >= -block_rows) & (row < 2 * block_rows)
        elif blocks == 2:
            row_inside = row >= -block_rows
        else:
            row_inside = row >= 0
        inside = row_inside & (col >= -HALF) & (col < block_cols + HALF)
        row = jnp.where(row < 0, row + blocks * block_rows, row)
        col = jnp.where(col < 0, col + 2 * block_cols, col)
        row = jnp.where(inside, row, 0)
        col = jnp.where(inside, col, 0)
        rate = jnp.where(inside, rates[0, well], 0.0)
        in_block = row % block_rows
        place = layer, col // LANES, row // block_rows, in_block % count
        hit = (row_index() == in_block // count) & (lane_index() == col % LANES)
        finest.target[place] = finest.target[place] + jnp.where(hit, rate, 0.0)

    for layer in range(LAYERS):
        for u in range(2):
            heads = [perm[layer, u, b, 0] for b in range(blocks)]
            edge = row_index() >= SUB - 1
            rolled = [row_roll(value, -1) for value in heads]
            after = [jnp.where(edge, joined[b] * rolled[(b + 1) % blocks], rolled[b]) for b in range(blocks)]
            for b in range(blocks):
                for t in range(count):
                    beyond = perm[layer, u, b, t + 1] if t < count - 1 else after[b]
                    finest.c_south[layer, u, b, t] = harmonic(perm[layer, u, b, t], beyond)
            before = row_before([finest.c_south[layer, u, b, count - 1] for b in range(blocks)], blocks)
            for b in range(blocks):
                for t in range(count):
                    finest.c_north[layer, u, b, t] = finest.c_south[layer, u, b, t - 1] if t > 0 else before[b]
    for b in range(blocks):
        for t in range(count):
            for u in range(2):
                finest.c_layer[u, b, t] = vertical * harmonic(perm[0, u, b, t], perm[1, u, b, t])
            for layer in range(LAYERS):
                here = [perm[layer, u, b, t] for u in range(2)]
                beyond = east_of(here, 1)
                east = [harmonic(here[u], beyond[u]) for u in range(2)]
                west = west_of(east, 1)
                for u in range(2):
                    finest.c_east[layer, u, b, t] = east[u]
                    finest.c_west[layer, u, b, t] = west[u]
    for key in finest.keys(blocks):
        with_weight(finest, key, acc[key])
    coarse_coeffs(finest, middle, acc, middle_acc, blocks)
    coarse_coeffs(middle, bottom, middle_acc, None, blocks)

    vcycle(levels, False, blocks)
    for key in finest.keys(blocks):
        value = finest.now[key]
        pressure[key] = value
        finest.target[key] = value - field(OBS, key)
    vcycle(levels, True, blocks)

    fields = (pressure, finest.now)
    last = count - 1
    ends = {}
    for number, values in enumerate(fields):
        for layer in range(LAYERS):
            ends[number, layer] = (
                row_before([values[layer, 0, b, last] for b in range(blocks)], blocks)[0],
                row_after([values[layer, 0, b, 0] for b in range(blocks)], blocks)[0],
            )
    for t in range(count):
        for layer in range(LAYERS):
            key = layer, 0, 0, t
            differences = []
            for number, values in enumerate(fields):
                pair = [values[layer, u, 0, t] for u in range(2)]
                here = pair[0]
                beside = (
                    values[layer, 0, 0, t - 1] if t > 0 else ends[number, layer][0],
                    values[layer, 0, 0, t + 1] if t < last else ends[number, layer][1],
                    west_of(pair, 1)[0],
                    east_of(pair, 1)[0],
                    values[1 - layer, 0, 0, t],
                )
                differences.append([here - other for other in beside])
                (pressure_out, adjoint_out)[number][0, layer, rows(t), :] = here
            total = jnp.zeros((SUB, LANES), jnp.float32)
            coeffs = (finest.c_north[key], finest.c_south[key], finest.c_west[key], finest.c_east[key])
            for number, coeff in enumerate(coeffs):
                total = total + coeff * coeff * (differences[0][number] * differences[1][number])
            coeff = finest.c_layer[0, 0, t]
            total = total + (1.0 / vertical) * (coeff * coeff) * (differences[0][4] * differences[1][4])
            terms_out[layer, rows(t), :] = -0.5 * total / perm[key]


def moved(value, axis, step):
    count = lax.axis_size(axis)
    ring = axis == "gx" and count == 2
    pairs = [((i + step) % count, i) for i in range(count) if ring or 0 <= i + step < count]
    return lax.ppermute(value, axis, pairs)


def summed(value, axis):
    count = lax.axis_size(axis)
    others = [lax.ppermute(value, axis, [(i, i ^ step) for i in range(count)]) for step in range(1, count)]
    terms = [value] + others
    while len(terms) > 1:
        terms = [terms[i] + terms[i + 1] for i in range(0, len(terms), 2)]
    return terms[0]


def in_hbm(value):
    return pltpu.with_memory_space_constraint(value, pltpu.HBM)


def shards(
    perm_log,
    facies,
    facies_scale,
    accumulation,
    previous_pressure,
    observed,
    well_cells,
    well_rates,
):
    layer_count, row_count, col_count = perm_log.shape
    gx_count, gy_count = lax.axis_size("gx"), lax.axis_size("gy")
    vmem = pl.BlockSpec(memory_space=pltpu.VMEM)
    smem = pl.BlockSpec(memory_space=pltpu.SMEM)
    hbm = pl.BlockSpec(memory_space=pltpu.HBM)
    f32 = jnp.float32
    fields = (perm_log, facies, accumulation, previous_pressure, observed)
    own, to_left, to_right = pl.pallas_call(
        pack_kernel,
        out_shape=[
            pltpu.VMEM((4, layer_count, row_count, col_count), f32),
            pltpu.VMEM((2, layer_count, row_count, col_count), f32),
            pltpu.VMEM((2, layer_count, row_count, col_count), f32),
        ],
        in_specs=[smem] + [hbm] * 5,
        out_specs=[vmem] * 3,
        scratch_shapes=[pltpu.VMEM(value.shape, value.dtype) for value in fields] + [pltpu.SemaphoreType.DMA((5,))],
        name="pack",
    )(in_hbm(facies_scale), *[in_hbm(value) for value in fields])

    steps = (0, 1) if gx_count == 2 else (0, 1, -1) if gx_count > 2 else (0,)
    blocks = len(steps)
    owns = [own] + [moved(own, "gx", step) for step in steps[1:]]
    beside = pl.pallas_call(
        merge_kernel,
        out_shape=pltpu.VMEM((4, layer_count, row_count, col_count), f32),
        in_specs=[vmem] * 2,
        out_specs=vmem,
        name="merge",
    )(moved(to_left, "gy", 1), moved(to_right, "gy", -1))
    besides = [beside] + [moved(beside, "gx", step) for step in steps[1:]]
    operands = [value for pair in zip(owns, besides) for value in pair]

    count = row_count // SUB
    scratch = [pltpu.VMEM((LAYERS, 2, blocks, count, SUB, LANES), f32)] * 2
    scratch += [pltpu.VMEM((LAYERS, 2, blocks, count // 2, SUB, LANES), f32)]
    scratch += [pltpu.VMEM((LAYERS, 2, blocks, count, SUB, LANES), f32)]
    for depth in range(3):
        whole = pltpu.VMEM((LAYERS, 2, blocks, count >> depth, SUB, LANES), f32)
        scratch += [whole] * 4 + [pltpu.VMEM((2, blocks, count >> depth, SUB, LANES), f32)] + [whole] * 5
    state = jax.ShapeDtypeStruct((1, layer_count, row_count, col_count), f32)
    grid_shape = (layer_count, row_count * gx_count, col_count * gy_count)
    pressure, adjoint, terms = pl.pallas_call(
        partial(cycle_kernel, grid_shape, gx_count, blocks),
        out_shape=[state, state, jax.ShapeDtypeStruct((layer_count, row_count, col_count), f32)],
        in_specs=[smem] * 2 + [vmem] * (2 * blocks),
        out_specs=[vmem] * 3,
        scratch_shapes=scratch,
        compiler_params=pltpu.CompilerParams(vmem_limit_bytes=24 * 1024 * 1024),
        name="cycles",
    )(in_hbm(well_cells), in_hbm(well_rates), *operands)
    return pressure, adjoint, summed(terms, "scen")


def solution(mesh):
    return jax.shard_map(
        shards,
        mesh=mesh,
        in_specs=(
            P(None, "gx", "gy"),
            P(None, "gx", "gy"),
            P(),
            P(None, "gx", "gy"),
            P("scen", None, "gx", "gy"),
            P("scen", None, "gx", "gy"),
            P("scen", None),
            P("scen", None),
        ),
        out_specs=(P("scen", None, "gx", "gy"), P("scen", None, "gx", "gy"), P(None, "gx", "gy")),
        check_vma=False,
    )
```

```python
from functools import partial

import jax
import jax.numpy as jnp
from jax import lax
from jax.experimental import pallas as pl
from jax.experimental.pallas import tpu as pltpu
from jax.sharding import PartitionSpec as P

WELLS = 5
FACIES = 4
LAYERS = 2
SMOOTH = 2
COARSE = 4

vertical = 0.3
damping = 0.8

LANES = 128
HALF = 64
SUB = 8
PERM, ACC, PREV, OBS = range(4)


def lane_index():
    return lax.broadcasted_iota(jnp.int32, (SUB, LANES), 1)


def row_index():
    return lax.broadcasted_iota(jnp.int32, (SUB, LANES), 0)


def lane_roll(value, shift):
    return pltpu.roll(value, shift % LANES, value.ndim - 1)


def row_roll(value, shift):
    return pltpu.roll(value, shift % SUB, 0)


def pack_kernel(scale_hbm, perm_log_hbm, facies_hbm, acc_hbm, prev_hbm, obs_hbm, own, to_left, to_right,
                scale, perm_log, facies, acc, prev, obs, sems):
    pairs = ((scale_hbm, scale), (perm_log_hbm, perm_log), (facies_hbm, facies), (acc_hbm, acc), (prev_hbm, prev),
             (obs_hbm, obs))
    copies = [pltpu.make_async_copy(source, target, sems.at[i]) for i, (source, target) in enumerate(pairs)]
    for copy in copies:
        copy.start()
    for copy in copies:
        copy.wait()
    label = facies[...]
    factor = jnp.zeros(label.shape, jnp.float32)
    for number in range(FACIES):
        factor = factor + jnp.where(label == number, scale[number], jnp.float32(0.0))
    fields = (jnp.exp(perm_log[...]) * factor, acc[...], prev[0], obs[0])
    low = lax.broadcasted_iota(jnp.int32, label.shape, 2) < HALF
    for number in range(4):
        own[number] = fields[number]
    for pair in range(2):
        first, second = fields[2 * pair], lane_roll(fields[2 * pair + 1], HALF)
        to_left[pair] = jnp.where(low, first, second)
        to_right[pair] = jnp.where(low, second, first)


def merge_kernel(from_right, from_left, beside):
    low = lax.broadcasted_iota(jnp.int32, beside.shape[1:], 2) < HALF
    for pair in range(2):
        right, left = from_right[pair], from_left[pair]
        beside[2 * pair] = jnp.where(low, right, left)
        beside[2 * pair + 1] = lane_roll(jnp.where(low, left, right), HALF)


class Level:
    def __init__(self, count, span, refs):
        self.count = count
        self.span = span
        (self.c_north, self.c_south, self.c_west, self.c_east, self.c_layer, self.weight, self.diag, self.target,
         self.now, self.later) = refs

    def keys(self, blocks):
        for b in range(blocks):
            for t in range(self.count):
                for u in range(2):
                    for layer in range(LAYERS):
                        yield layer, u, b, t


def east_of(pair, span):
    edge = lane_index() >= LANES - span
    rolled = [lane_roll(value, -span) for value in pair]
    return [jnp.where(edge, rolled[1 - u], rolled[u]) for u in range(2)]


def west_of(pair, span):
    edge = lane_index() < span
    rolled = [lane_roll(value, span) for value in pair]
    return [jnp.where(edge, rolled[1 - u], rolled[u]) for u in range(2)]


def row_before(values, blocks):
    edge = row_index() < 1
    rolled = [row_roll(value, 1) for value in values]
    return [jnp.where(edge, rolled[(b - 1) % blocks], rolled[b]) for b in range(blocks)]


def row_after(values, blocks):
    edge = row_index() >= SUB - 1
    rolled = [row_roll(value, -1) for value in values]
    return [jnp.where(edge, rolled[(b + 1) % blocks], rolled[b]) for b in range(blocks)]


def neighbour_sums(level, source, blocks):
    last = level.count - 1
    before, after = {}, {}
    for layer in range(LAYERS):
        for u in range(2):
            lows = row_before([source[layer, u, b, last] for b in range(blocks)], blocks)
            highs = row_after([source[layer, u, b, 0] for b in range(blocks)], blocks)
            for b in range(blocks):
                before[layer, u, b] = lows[b]
                after[layer, u, b] = highs[b]
    for b in range(blocks):
        for t in range(level.count):
            here = [[source[layer, u, b, t] for u in range(2)] for layer in range(LAYERS)]
            for layer in range(LAYERS):
                east = east_of(here[layer], level.span)
                west = west_of(here[layer], level.span)
                for u in range(2):
                    north = source[layer, u, b, t - 1] if t > 0 else before[layer, u, b]
                    south = source[layer, u, b, t + 1] if t < last else after[layer, u, b]
                    key = layer, u, b, t
                    total = (level.c_north[key] * north + level.c_south[key] * south
                             + (level.c_west[key] * west[u] + level.c_east[key] * east[u])
                             + level.c_layer[u, b, t] * here[1 - layer][u])
                    yield key, here[layer][u], total


def sweep(level, source, result, blocks):
    for key, value, total in neighbour_sums(level, source, blocks):
        result[key] = (1.0 - damping) * value + level.weight[key] * (level.target[key] + total)


def sweeps(level, count, blocks):
    for _ in range(count):
        sweep(level, level.now, level.later, blocks)
        level.now, level.later = level.later, level.now


def first_sweep(level, blocks):
    for key in level.keys(blocks):
        level.now[key] = level.weight[key] * level.target[key]


def pair_sum(value, span):
    lower = lane_index() % (2 * span) < span
    return value + jnp.where(lower, lane_roll(value, -span), lane_roll(value, span))


def low_group(value, span):
    return jnp.where(lane_index() % (2 * span) < span, value, lane_roll(value, span))


def high_group(value, span):
    return jnp.where(lane_index() % (2 * span) < span, lane_roll(value, -span), value)


def restrict_residual(fine, coarse, blocks):
    partial_sum = {}
    for key, value, total in neighbour_sums(fine, fine.now, blocks):
        layer, u, b, t = key
        residual = fine.target[key] + total - fine.diag[key] * value
        if t % 2 == 0:
            partial_sum[layer, u, b] = residual
        else:
            coarse.target[layer, u, b, t // 2] = pair_sum(partial_sum[layer, u, b] + residual, fine.span)


def prolong(coarse, fine, blocks):
    for key in fine.keys(blocks):
        layer, u, b, t = key
        fine.now[key] = fine.now[key] + coarse.now[layer, u, b, t // 2]


def vcycle(levels, from_zero, blocks):
    finest, middle, bottom = levels
    if from_zero:
        first_sweep(finest, blocks)
    sweeps(finest, SMOOTH - int(from_zero), blocks)
    restrict_residual(finest, middle, blocks)
    first_sweep(middle, blocks)
    sweeps(middle, SMOOTH - 1, blocks)
    restrict_residual(middle, bottom, blocks)
    first_sweep(bottom, blocks)
    sweeps(bottom, COARSE - 1, blocks)
    prolong(bottom, middle, blocks)
    sweeps(middle, SMOOTH, blocks)
    prolong(middle, finest, blocks)
    sweeps(finest, SMOOTH, blocks)


def harmonic(left, right):
    return 2.0 * left * right / jnp.maximum(left + right, 1e-20)


def with_weight(level, key, accumulated):
    layer, u, b, t = key
    diag = (level.c_north[key] + level.c_south[key] + level.c_west[key] + level.c_east[key]
            + level.c_layer[u, b, t] + accumulated)
    level.diag[key] = diag
    level.weight[key] = damping / jnp.maximum(diag, 1e-20)


def coarse_coeffs(fine, coarse, fine_acc, coarse_acc, blocks):
    span = fine.span
    for key in coarse.keys(blocks):
        layer, u, b, t = key
        one, two = (layer, u, b, 2 * t), (layer, u, b, 2 * t + 1)
        coarse.c_north[key] = pair_sum(fine.c_north[one], span)
        coarse.c_south[key] = pair_sum(fine.c_south[two], span)
        coarse.c_west[key] = low_group(fine.c_west[one] + fine.c_west[two], span)
        coarse.c_east[key] = high_group(fine.c_east[one] + fine.c_east[two], span)
        if layer == 0:
            coarse.c_layer[u, b, t] = pair_sum(fine.c_layer[one[1:]] + fine.c_layer[two[1:]], span)
        accumulated = pair_sum(fine_acc[one] + fine_acc[two], span)
        if coarse_acc is not None:
            coarse_acc[key] = accumulated
        with_weight(coarse, key, accumulated)


def cycle_kernel(grid_shape, gx_count, blocks, *refs):
    cells_hbm, rates_hbm = refs[:2]
    inputs = [refs[2 + 2 * b:4 + 2 * b] for b in range(blocks)]
    refs = refs[2 + 2 * blocks:]
    pressure_out, adjoint_out, terms_out = refs[:3]
    refs = refs[3:]
    cells, rates, sems, perm, acc, middle_acc, pressure, pressure_rows, adjoint_rows = refs[:9]
    refs = refs[9:]
    copies = [pltpu.make_async_copy(cells_hbm, cells, sems.at[0]), pltpu.make_async_copy(rates_hbm, rates, sems.at[1])]
    for copy in copies:
        copy.start()
    count = inputs[0][0].shape[2] // SUB
    levels = [Level(count >> depth, 1 << depth, refs[10 * depth:10 * depth + 10]) for depth in range(3)]
    finest, middle, bottom = levels

    def rows(t):
        return pl.ds(t, SUB, stride=count)

    def field(number, key):
        layer, u, b, t = key
        return inputs[b][u][number, layer, rows(t), :]

    gx = lax.axis_index("gx")
    if blocks == 3:
        joined = [1.0, 0.0, 1.0]
    elif blocks == 2:
        joined = [1.0 - gx.astype(jnp.float32), gx.astype(jnp.float32)]
    else:
        joined = [0.0]

    for key in finest.keys(blocks):
        perm[key] = field(PERM, key)
        acc[key] = field(ACC, key)
        start = field(PREV, key)
        finest.now[key] = start
        finest.target[key] = acc[key] * start

    for copy in copies:
        copy.wait()
    layer_count, total_rows, total_cols = grid_shape
    block_rows, block_cols = SUB * count, LANES
    for well in range(WELLS):
        cell = cells[0, well]
        layer = cell // (total_rows * total_cols)
        row = cell // total_cols % total_rows - gx * block_rows
        col = cell % total_cols - lax.axis_index("gy") * block_cols
        if blocks == 3:
            row_inside = (row >= -block_rows) & (row < 2 * block_rows)
        elif blocks == 2:
            row_inside = row >= -block_rows
        else:
            row_inside = row >= 0
        inside = row_inside & (col >= -HALF) & (col < block_cols + HALF)
        row = jnp.where(row < 0, row + blocks * block_rows, row)
        col = jnp.where(col < 0, col + 2 * block_cols, col)
        row = jnp.where(inside, row, 0)
        col = jnp.where(inside, col, 0)
        rate = jnp.where(inside, rates[0, well], 0.0)
        in_block = row % block_rows
        place = layer, col // LANES, row // block_rows, in_block % count
        hit = (row_index() == in_block // count) & (lane_index() == col % LANES)
        finest.target[place] = finest.target[place] + jnp.where(hit, rate, 0.0)

    for layer in range(LAYERS):
        for u in range(2):
            heads = [perm[layer, u, b, 0] for b in range(blocks)]
            edge = row_index() >= SUB - 1
            rolled = [row_roll(value, -1) for value in heads]
            after = [jnp.where(edge, joined[b] * rolled[(b + 1) % blocks], rolled[b]) for b in range(blocks)]
            for b in range(blocks):
                for t in range(count):
                    beyond = perm[layer, u, b, t + 1] if t < count - 1 else after[b]
                    finest.c_south[layer, u, b, t] = harmonic(perm[layer, u, b, t], beyond)
            before = row_before([finest.c_south[layer, u, b, count - 1] for b in range(blocks)], blocks)
            for b in range(blocks):
                for t in range(count):
                    finest.c_north[layer, u, b, t] = finest.c_south[layer, u, b, t - 1] if t > 0 else before[b]
    for b in range(blocks):
        for t in range(count):
            for u in range(2):
                finest.c_layer[u, b, t] = vertical * harmonic(perm[0, u, b, t], perm[1, u, b, t])
            for layer in range(LAYERS):
                here = [perm[layer, u, b, t] for u in range(2)]
                beyond = east_of(here, 1)
                east = [harmonic(here[u], beyond[u]) for u in range(2)]
                west = west_of(east, 1)
                for u in range(2):
                    finest.c_east[layer, u, b, t] = east[u]
                    finest.c_west[layer, u, b, t] = west[u]
    for key in finest.keys(blocks):
        with_weight(finest, key, acc[key])
    coarse_coeffs(finest, middle, acc, middle_acc, blocks)
    coarse_coeffs(middle, bottom, middle_acc, None, blocks)

    vcycle(levels, False, blocks)
    for key in finest.keys(blocks):
        value = finest.now[key]
        pressure[key] = value
        finest.target[key] = value - field(OBS, key)
        layer, u, b, t = key
        if u == 0 and b == 0:
            pressure_rows[0, layer, rows(t), :] = value
    pressure_copy = pltpu.make_async_copy(pressure_rows, pressure_out, sems.at[2])
    pressure_copy.start()
    vcycle(levels, True, blocks)
    for t in range(count):
        for layer in range(LAYERS):
            adjoint_rows[0, layer, rows(t), :] = finest.now[layer, 0, 0, t]
    adjoint_copy = pltpu.make_async_copy(adjoint_rows, adjoint_out, sems.at[3])
    adjoint_copy.start()

    fields = (pressure, finest.now)
    last = count - 1
    ends = {}
    for number, values in enumerate(fields):
        for layer in range(LAYERS):
            ends[number, layer] = (
                row_before([values[layer, 0, b, last] for b in range(blocks)], blocks)[0],
                row_after([values[layer, 0, b, 0] for b in range(blocks)], blocks)[0],
            )
    for t in range(count):
        for layer in range(LAYERS):
            key = layer, 0, 0, t
            differences = []
            for number, values in enumerate(fields):
                pair = [values[layer, u, 0, t] for u in range(2)]
                here = pair[0]
                beside = (
                    values[layer, 0, 0, t - 1] if t > 0 else ends[number, layer][0],
                    values[layer, 0, 0, t + 1] if t < last else ends[number, layer][1],
                    west_of(pair, 1)[0],
                    east_of(pair, 1)[0],
                    values[1 - layer, 0, 0, t],
                )
                differences.append([here - other for other in beside])
            total = jnp.zeros((SUB, LANES), jnp.float32)
            coeffs = (finest.c_north[key], finest.c_south[key], finest.c_west[key], finest.c_east[key])
            for number, coeff in enumerate(coeffs):
                total = total + coeff * coeff * (differences[0][number] * differences[1][number])
            coeff = finest.c_layer[0, 0, t]
            total = total + (1.0 / vertical) * (coeff * coeff) * (differences[0][4] * differences[1][4])
            total = -0.5 * total / perm[key]
            for copy in range(terms_out.shape[0]):
                terms_out[copy, layer, rows(t), :] = total
    pressure_copy.wait()
    adjoint_copy.wait()


def moved(value, axis, step):
    count = lax.axis_size(axis)
    ring = axis == "gx" and count == 2
    pairs = [((i + step) % count, i) for i in range(count) if ring or 0 <= i + step < count]
    return lax.ppermute(value, axis, pairs)


def summed(copies, axis):
    return jnp.sum(lax.all_to_all(copies, axis, 0, 0), 0)


def in_hbm(value):
    return pltpu.with_memory_space_constraint(value, pltpu.HBM)


def in_vmem(value):
    return pltpu.with_memory_space_constraint(value, pltpu.VMEM)


def shards(
    perm_log,
    facies,
    facies_scale,
    accumulation,
    previous_pressure,
    observed,
    well_cells,
    well_rates,
):
    layer_count, row_count, col_count = perm_log.shape
    gx_count, gy_count = lax.axis_size("gx"), lax.axis_size("gy")
    vmem = pl.BlockSpec(memory_space=pltpu.VMEM)
    hbm = pl.BlockSpec(memory_space=pltpu.HBM)
    f32 = jnp.float32
    fields = (perm_log, facies, accumulation, previous_pressure, observed)
    own, to_left, to_right = pl.pallas_call(
        pack_kernel,
        out_shape=[
            pltpu.VMEM((4, layer_count, row_count, col_count), f32),
            pltpu.VMEM((2, layer_count, row_count, col_count), f32),
            pltpu.VMEM((2, layer_count, row_count, col_count), f32),
        ],
        in_specs=[hbm] * 6,
        out_specs=[vmem] * 3,
        scratch_shapes=[pltpu.SMEM(facies_scale.shape, f32)]
        + [pltpu.VMEM(value.shape, value.dtype) for value in fields] + [pltpu.SemaphoreType.DMA((6,))],
        name="pack",
    )(in_hbm(facies_scale), *[in_hbm(value) for value in fields])

    steps = (0, 1) if gx_count == 2 else (0, 1, -1) if gx_count > 2 else (0,)
    blocks = len(steps)
    owns = [own] + [moved(own, "gx", step) for step in steps[1:]]
    beside = pl.pallas_call(
        merge_kernel,
        out_shape=pltpu.VMEM((4, layer_count, row_count, col_count), f32),
        in_specs=[vmem] * 2,
        out_specs=vmem,
        name="merge",
    )(in_vmem(moved(to_left, "gy", 1)), in_vmem(moved(to_right, "gy", -1)))
    besides = [beside] + [moved(beside, "gx", step) for step in steps[1:]]
    operands = [in_vmem(value) for pair in zip(owns, besides) for value in pair]

    count = row_count // SUB
    scratch = [pltpu.SMEM(well_cells.shape, jnp.int32), pltpu.SMEM(well_rates.shape, f32), pltpu.SemaphoreType.DMA((4,))]
    scratch += [pltpu.VMEM((LAYERS, 2, blocks, count, SUB, LANES), f32)] * 2
    scratch += [pltpu.VMEM((LAYERS, 2, blocks, count // 2, SUB, LANES), f32)]
    scratch += [pltpu.VMEM((LAYERS, 2, blocks, count, SUB, LANES), f32)]
    scratch += [pltpu.VMEM((1, layer_count, row_count, col_count), f32)] * 2
    for depth in range(3):
        whole = pltpu.VMEM((LAYERS, 2, blocks, count >> depth, SUB, LANES), f32)
        scratch += [whole] * 4 + [pltpu.VMEM((2, blocks, count >> depth, SUB, LANES), f32)] + [whole] * 5
    state = jax.ShapeDtypeStruct((1, layer_count, row_count, col_count), f32)
    grid_shape = (layer_count, row_count * gx_count, col_count * gy_count)
    pressure, adjoint, terms = pl.pallas_call(
        partial(cycle_kernel, grid_shape, gx_count, blocks),
        out_shape=[state, state, pltpu.VMEM((lax.axis_size("scen"), layer_count, row_count, col_count), f32)],
        in_specs=[hbm] * 2 + [vmem] * (2 * blocks),
        out_specs=[hbm, hbm, vmem],
        scratch_shapes=scratch,
        compiler_params=pltpu.CompilerParams(vmem_limit_bytes=24 * 1024 * 1024),
        name="cycles",
    )(in_hbm(well_cells), in_hbm(well_rates), *operands)
    return pressure, adjoint, summed(terms, "scen")


def solution(mesh):
    return jax.shard_map(
        shards,
        mesh=mesh,
        in_specs=(
            P(None, "gx", "gy"),
            P(None, "gx", "gy"),
            P(),
            P(None, "gx", "gy"),
            P("scen", None, "gx", "gy"),
            P("scen", None, "gx", "gy"),
            P("scen", None),
            P("scen", None),
        ),
        out_specs=(P("scen", None, "gx", "gy"), P("scen", None, "gx", "gy"), P(None, "gx", "gy")),
        check_vma=False,
    )
```

```python
from functools import partial

import jax
import jax.numpy as jnp
from jax import lax
from jax.experimental import pallas as pl
from jax.experimental.pallas import tpu as pltpu
from jax.sharding import PartitionSpec as P

WELLS = 5
FACIES = 4
LAYERS = 2
SMOOTH = 2
COARSE = 4

vertical = 0.3
damping = 0.8

LANES = 128
HALF = 64
SUB = 8
PERM, ACC, PREV, OBS = range(4)
LEVELS = ((2, 1), (1, 1), (1, 2))


def lane_index():
    return lax.broadcasted_iota(jnp.int32, (SUB, LANES), 1)


def row_index():
    return lax.broadcasted_iota(jnp.int32, (SUB, LANES), 0)


def lane_roll(value, shift):
    return pltpu.roll(value, shift % LANES, value.ndim - 1)


def row_roll(value, shift):
    return pltpu.roll(value, shift % SUB, 0)


def shuffle(value, inverse):
    rows = lax.broadcasted_iota(jnp.int32, (LANES, LANES), 0)
    cols = lax.broadcasted_iota(jnp.int32, (LANES, LANES), 1)
    natural, place = (cols, rows) if inverse else (rows, cols)
    matrix = (natural == 2 * (place % HALF) + place // HALF).astype(jnp.float32)
    flat = value.reshape(-1, LANES)
    moved_columns = lax.dot(flat, matrix, precision=lax.Precision.HIGHEST, preferred_element_type=jnp.float32)
    return moved_columns.reshape(value.shape)


def pack_kernel(scale_hbm, perm_log_hbm, facies_hbm, acc_hbm, prev_hbm, obs_hbm, own, to_left, to_right,
                scale, perm_log, facies, acc, prev, obs, sems):
    pairs = ((scale_hbm, scale), (perm_log_hbm, perm_log), (facies_hbm, facies), (acc_hbm, acc), (prev_hbm, prev),
             (obs_hbm, obs))
    copies = [pltpu.make_async_copy(source, target, sems.at[i]) for i, (source, target) in enumerate(pairs)]
    for copy in copies:
        copy.start()
    for copy in copies:
        copy.wait()
    label = facies[...]
    factor = jnp.zeros(label.shape, jnp.float32)
    for number in range(FACIES):
        factor = factor + jnp.where(label == number, scale[number], jnp.float32(0.0))
    fields = [shuffle(value, False) for value in (jnp.exp(perm_log[...]) * factor, acc[...], prev[0], obs[0])]
    low = lax.broadcasted_iota(jnp.int32, label.shape, 2) % HALF < HALF // 2
    for number in range(4):
        own[number] = fields[number]
    for pair in range(2):
        first = lane_roll(fields[2 * pair], HALF)
        second = lane_roll(fields[2 * pair + 1], HALF + HALF // 2)
        to_left[pair] = jnp.where(low, first, second)
        to_right[pair] = jnp.where(low, second, first)


def merge_kernel(from_right, from_left, beside):
    low = lax.broadcasted_iota(jnp.int32, beside.shape[1:], 2) % HALF < HALF // 2
    for pair in range(2):
        right, left = from_right[pair], from_left[pair]
        beside[2 * pair] = jnp.where(low, right, left)
        beside[2 * pair + 1] = lane_roll(jnp.where(low, left, right), -(HALF // 2))


class Level:
    def __init__(self, count, width, span, blocks, refs):
        self.count = count
        self.width = width
        self.span = span
        self.blocks = blocks
        (self.c_south, self.c_first, self.c_inner, self.c_east, self.c_west, self.c_layer, self.weight, self.diag,
         self.target, self.now, self.later) = refs

    @staticmethod
    def scratch(count, width, blocks):
        def vectors(*lead):
            return pltpu.VMEM(lead + (SUB, LANES), jnp.float32)

        whole = vectors(LAYERS, width, blocks, count)
        edge = vectors(LAYERS, blocks, count)
        return [whole, vectors(LAYERS, width, blocks), edge, edge, edge, vectors(width, blocks, count)] + [whole] * 5

    def steps(self, ring=None):
        for b in range(self.blocks):
            for t in range(self.count):
                if ring is None or b == 0 or t < ring or t >= self.count - ring:
                    yield b, t

    def members(self):
        for layer in range(LAYERS):
            for u in range(self.width):
                yield layer, u


def row_before(values):
    edge = row_index() < 1
    rolled = [row_roll(value, 1) for value in values]
    return [jnp.where(edge, rolled[b - 1], rolled[b]) for b in range(len(values))]


def row_after(values):
    edge = row_index() >= SUB - 1
    rolled = [row_roll(value, -1) for value in values]
    return [jnp.where(edge, rolled[(b + 1) % len(values)], rolled[b]) for b in range(len(values))]


class Field:
    def __init__(self, level, source):
        self.source = source
        self.count = level.count
        self.read = {}
        self.before, self.after = {}, {}
        for layer, u in level.members():
            lows = row_before([source[layer, u, b, level.count - 1] for b in range(level.blocks)])
            highs = row_after([source[layer, u, b, 0] for b in range(level.blocks)])
            for b in range(level.blocks):
                self.before[layer, u, b] = lows[b]
                self.after[layer, u, b] = highs[b]

    def at(self, layer, u, b, t):
        if t < 0:
            return self.before[layer, u, b]
        if t >= self.count:
            return self.after[layer, u, b]
        key = layer, u, b, t
        if key not in self.read:
            self.read[key] = self.source[key]
        return self.read[key]


def row_coeff(level, layer, u, b, t):
    return level.c_south[layer, u, b, t] if t >= 0 else level.c_first[layer, u, b]


def neighbour_sums(level, source, ring=None):
    field = Field(level, source)
    coeffs = {}
    for b, t in level.steps(ring):
        for member in level.members():
            for at in (t - 1, t):
                if (member, b, at) not in coeffs:
                    coeffs[member, b, at] = row_coeff(level, *member, b, at)
        layer_coeffs = [level.c_layer[u, b, t] for u in range(level.width)]
        for layer in range(LAYERS):
            here = [field.at(layer, u, b, t) for u in range(level.width)]
            east_coeff, west_coeff = level.c_east[layer, b, t], level.c_west[layer, b, t]
            if level.width == 2:
                inner = level.c_inner[layer, b, t]
                beside = [inner * here[1] + west_coeff * lane_roll(here[1], 1),
                          inner * here[0] + east_coeff * lane_roll(here[0], -1)]
            else:
                beside = [east_coeff * lane_roll(here[0], -level.span) + west_coeff * lane_roll(here[0], level.span)]
            for u in range(level.width):
                total = (coeffs[(layer, u), b, t - 1] * field.at(layer, u, b, t - 1)
                         + coeffs[(layer, u), b, t] * field.at(layer, u, b, t + 1)
                         + (beside[u] + layer_coeffs[u] * field.at(1 - layer, u, b, t)))
                yield (layer, u, b, t), here[u], total


def sweep(level, source, result, ring=None):
    for key, value, total in neighbour_sums(level, source, ring):
        result[key] = (1.0 - damping) * value + level.weight[key] * (level.target[key] + total)


def sweeps(level, count, ring=None):
    for number in range(count):
        sweep(level, level.now, level.later, None if ring is None else ring + count - 1 - number)
        level.now, level.later = level.later, level.now


def first_sweep(level):
    for b, t in level.steps():
        for layer, u in level.members():
            key = layer, u, b, t
            level.now[key] = level.weight[key] * level.target[key]


def pair_sum(value, span):
    lower = lane_index() % (2 * span) < span
    return value + jnp.where(lower, lane_roll(value, -span), lane_roll(value, span))


def low_group(value, span):
    return jnp.where(lane_index() % (2 * span) < span, value, lane_roll(value, span))


def high_group(value, span):
    return jnp.where(lane_index() % (2 * span) < span, lane_roll(value, -span), value)


def column_sum(values, level):
    return values[0] + values[1] if level.width == 2 else pair_sum(values[0], level.span)


def restrict_residual(fine, coarse):
    residuals = {}
    for key, value, total in neighbour_sums(fine, fine.now):
        layer, u, b, t = key
        residuals[key] = fine.target[key] + total - fine.diag[key] * value
        if t % 2 == 1 and u == fine.width - 1:
            rows = [residuals[layer, v, b, t - 1] + residuals[layer, v, b, t] for v in range(fine.width)]
            coarse.target[layer, 0, b, t // 2] = column_sum(rows, fine)


def prolong(coarse, fine, ring=None):
    for b, t in fine.steps(ring):
        for layer, u in fine.members():
            key = layer, u, b, t
            fine.now[key] = fine.now[key] + coarse.now[layer, 0, b, t // 2]


def vcycle(levels, from_zero, ring=None):
    finest, middle, bottom = levels
    if from_zero:
        first_sweep(finest)
    sweeps(finest, SMOOTH - int(from_zero))
    restrict_residual(finest, middle)
    first_sweep(middle)
    sweeps(middle, SMOOTH - 1)
    restrict_residual(middle, bottom)
    first_sweep(bottom)
    sweeps(bottom, COARSE - 1)
    prolong(bottom, middle)
    sweeps(middle, SMOOTH)
    prolong(middle, finest, None if ring is None else ring + SMOOTH)
    sweeps(finest, SMOOTH, ring)


def harmonic(left, right):
    return 2.0 * left * right / jnp.maximum(left + right, 1e-20)


def finest_coeffs(level, perm, joined):
    last = level.count - 1
    for layer, u in level.members():
        heads = [perm[layer, u, b, 0] for b in range(level.blocks)]
        rolled = [row_roll(value, -1) for value in heads]
        edge = row_index() >= SUB - 1
        for b in range(level.blocks):
            after = jnp.where(edge, joined[b] * rolled[(b + 1) % level.blocks], rolled[b])
            for t in range(level.count):
                beyond = perm[layer, u, b, t + 1] if t < last else after
                level.c_south[layer, u, b, t] = harmonic(perm[layer, u, b, t], beyond)
        firsts = row_before([level.c_south[layer, u, b, last] for b in range(level.blocks)])
        for b in range(level.blocks):
            level.c_first[layer, u, b] = firsts[b]
    for b, t in level.steps():
        for u in range(level.width):
            level.c_layer[u, b, t] = vertical * harmonic(perm[0, u, b, t], perm[1, u, b, t])
        for layer in range(LAYERS):
            even, odd = perm[layer, 0, b, t], perm[layer, 1, b, t]
            level.c_inner[layer, b, t] = harmonic(even, odd)
            east = harmonic(odd, lane_roll(even, -1))
            level.c_east[layer, b, t] = east
            level.c_west[layer, b, t] = lane_roll(east, 1)


def with_weight(level, acc):
    for b, t in level.steps():
        for layer, u in level.members():
            key = layer, u, b, t
            if level.width == 2:
                beside = level.c_inner[layer, b, t] + (level.c_west, level.c_east)[u][layer, b, t]
            else:
                beside = level.c_west[layer, b, t] + level.c_east[layer, b, t]
            diag = (row_coeff(level, layer, u, b, t - 1) + row_coeff(level, layer, u, b, t)
                    + (beside + level.c_layer[u, b, t]) + acc[key])
            level.diag[key] = diag
            level.weight[key] = damping / jnp.maximum(diag, 1e-20)


def coarse_coeffs(fine, coarse, fine_acc, coarse_acc):
    width = range(fine.width)
    for b in range(coarse.blocks):
        for layer in range(LAYERS):
            coarse.c_first[layer, 0, b] = column_sum([fine.c_first[layer, u, b] for u in width], fine)
    for b, t in coarse.steps():
        one, two = 2 * t, 2 * t + 1
        coarse.c_layer[0, b, t] = column_sum([fine.c_layer[u, b, one] + fine.c_layer[u, b, two] for u in width], fine)
        for layer in range(LAYERS):
            coarse.c_south[layer, 0, b, t] = column_sum([fine.c_south[layer, u, b, two] for u in width], fine)
            coarse_acc[layer, 0, b, t] = column_sum(
                [fine_acc[layer, u, b, one] + fine_acc[layer, u, b, two] for u in width], fine)
            west = fine.c_west[layer, b, one] + fine.c_west[layer, b, two]
            east = fine.c_east[layer, b, one] + fine.c_east[layer, b, two]
            if fine.width == 1:
                west, east = low_group(west, fine.span), high_group(east, fine.span)
            coarse.c_west[layer, b, t] = west
            coarse.c_east[layer, b, t] = east
    with_weight(coarse, coarse_acc)


def own_columns(even, odd):
    return jnp.where(lane_index() < HALF, even, lane_roll(odd, HALF))


def face_terms(level, pressure, adjoint, perm):
    def face(coeff, one, two):
        changes = [field.at(*one) - (field.at(*two) if isinstance(two, tuple) else two[number])
                   for number, field in enumerate((pressure, adjoint))]
        return (coeff * coeff) * (changes[0] * changes[1])

    rows = {(layer, u): face(level.c_first[layer, u, 0], (layer, u, 0, -1), (layer, u, 0, 0))
            for layer, u in level.members()}
    for t in range(level.count):
        between = [(1.0 / vertical) * face(level.c_layer[u, 0, t], (0, u, 0, t), (1, u, 0, t)) for u in range(2)]
        for layer in range(LAYERS):
            inner = face(level.c_inner[layer, 0, t], (layer, 0, 0, t), (layer, 1, 0, t))
            easts = [lane_roll(field.at(layer, 0, 0, t), -1) for field in (pressure, adjoint)]
            east = face(level.c_east[layer, 0, t], (layer, 1, 0, t), easts)
            terms = []
            for u in range(2):
                south = face(level.c_south[layer, u, 0, t], (layer, u, 0, t), (layer, u, 0, t + 1))
                beside = lane_roll(east, 1) if u == 0 else east
                total = rows[layer, u] + south + (inner + beside) + between[u]
                rows[layer, u] = south
                terms.append(-0.5 * total / perm[layer, u, 0, t])
            yield layer, t, own_columns(*terms)


def cycle_kernel(grid_shape, blocks, *refs):
    cells_hbm, rates_hbm = refs[:2]
    inputs = [refs[2 + 2 * b:4 + 2 * b] for b in range(blocks)]
    refs = refs[2 + 2 * blocks:]
    pressure_out, adjoint_out, terms_out = refs[:3]
    cells, rates, sems, perm, acc, middle_acc, bottom_acc, pressure, pressure_rows, adjoint_rows, terms_rows = refs[3:14]
    refs = refs[14:]
    copies = [pltpu.make_async_copy(cells_hbm, cells, sems.at[0]), pltpu.make_async_copy(rates_hbm, rates, sems.at[1])]
    for copy in copies:
        copy.start()
    count = inputs[0][0].shape[2] // SUB
    levels = [Level(count >> depth, width, span, blocks, refs[11 * depth:11 * depth + 11])
              for depth, (width, span) in enumerate(LEVELS)]
    finest, middle, bottom = levels

    def rows(t):
        return pl.ds(t, SUB, stride=count)

    def fields(number, layer, b, t):
        low = lane_index() < HALF
        own, beside = [value[number, layer, rows(t), :] for value in inputs[b]]
        return jnp.where(low, own, beside), lane_roll(jnp.where(low, beside, own), HALF)

    gx = lax.axis_index("gx")
    if blocks == 3:
        joined = [1.0, 0.0, 1.0]
    elif blocks == 2:
        joined = [1.0 - gx.astype(jnp.float32), gx.astype(jnp.float32)]
    else:
        joined = [0.0]

    for b, t in finest.steps():
        for layer in range(LAYERS):
            perms, accs, starts = [fields(number, layer, b, t) for number in (PERM, ACC, PREV)]
            for u in range(2):
                key = layer, u, b, t
                perm[key] = perms[u]
                acc[key] = accs[u]
                finest.now[key] = starts[u]
                finest.target[key] = accs[u] * starts[u]

    for copy in copies:
        copy.wait()
    layer_count, total_rows, total_cols = grid_shape
    block_rows, block_cols = SUB * count, LANES
    for well in range(WELLS):
        cell = cells[0, well]
        layer = cell // (total_rows * total_cols)
        row = cell // total_cols % total_rows - gx * block_rows
        col = cell % total_cols - lax.axis_index("gy") * block_cols
        if blocks == 3:
            row_inside = (row >= -block_rows) & (row < 2 * block_rows)
        elif blocks == 2:
            row_inside = row >= -block_rows
        else:
            row_inside = row >= 0
        inside = row_inside & (col >= -HALF) & (col < block_cols + HALF)
        row = jnp.where(row < 0, row + blocks * block_rows, row)
        col = jnp.where(col < 0, col + 2 * block_cols, col)
        row = jnp.where(inside, row, 0)
        col = jnp.where(inside, col, 0)
        rate = jnp.where(inside, rates[0, well], 0.0)
        in_block = row % block_rows
        place = layer, col % 2, row // block_rows, in_block % count
        hit = (row_index() == in_block // count) & (lane_index() == col // 2)
        finest.target[place] = finest.target[place] + jnp.where(hit, rate, 0.0)

    finest_coeffs(finest, perm, joined)
    with_weight(finest, acc)
    coarse_coeffs(finest, middle, acc, middle_acc)
    coarse_coeffs(middle, bottom, middle_acc, bottom_acc)

    vcycle(levels, False)
    for b, t in finest.steps():
        for layer in range(LAYERS):
            observed = fields(OBS, layer, b, t)
            values = []
            for u in range(2):
                key = layer, u, b, t
                values.append(finest.now[key])
                pressure[key] = values[u]
                finest.target[key] = values[u] - observed[u]
            if b == 0:
                pressure_rows[0, layer, rows(t), :] = own_columns(*values)
    pressure_rows[...] = shuffle(pressure_rows[...], True)
    pressure_copy = pltpu.make_async_copy(pressure_rows, pressure_out, sems.at[2])
    pressure_copy.start()
    vcycle(levels, True, 1)
    for t in range(count):
        for layer in range(LAYERS):
            adjoint_rows[0, layer, rows(t), :] = own_columns(*[finest.now[layer, u, 0, t] for u in range(2)])
    adjoint_rows[...] = shuffle(adjoint_rows[...], True)
    adjoint_copy = pltpu.make_async_copy(adjoint_rows, adjoint_out, sems.at[3])
    adjoint_copy.start()

    for layer, t, terms in face_terms(finest, Field(finest, pressure), Field(finest, finest.now), perm):
        terms_rows[layer, rows(t), :] = terms
    terms_out[...] = shuffle(terms_rows[...], True)
    pressure_copy.wait()
    adjoint_copy.wait()


def moved(value, axis, step):
    count = lax.axis_size(axis)
    ring = axis == "gx" and count == 2
    pairs = [((i + step) % count, i) for i in range(count) if ring or 0 <= i + step < count]
    return lax.ppermute(value, axis, pairs)


def summed(value, axis):
    count = lax.axis_size(axis)
    others = [lax.ppermute(value, axis, [(i, i ^ step) for i in range(count)]) for step in range(1, count)]
    terms = [value] + others
    while len(terms) > 1:
        terms = [terms[i] + terms[i + 1] for i in range(0, len(terms), 2)]
    return terms[0]


def in_hbm(value):
    return pltpu.with_memory_space_constraint(value, pltpu.HBM)


def in_vmem(value):
    return pltpu.with_memory_space_constraint(value, pltpu.VMEM)


def shards(
    perm_log,
    facies,
    facies_scale,
    accumulation,
    previous_pressure,
    observed,
    well_cells,
    well_rates,
):
    layer_count, row_count, col_count = perm_log.shape
    gx_count, gy_count = lax.axis_size("gx"), lax.axis_size("gy")
    vmem = pl.BlockSpec(memory_space=pltpu.VMEM)
    hbm = pl.BlockSpec(memory_space=pltpu.HBM)
    f32 = jnp.float32
    fields = (perm_log, facies, accumulation, previous_pressure, observed)
    own, to_left, to_right = pl.pallas_call(
        pack_kernel,
        out_shape=[
            pltpu.VMEM((4, layer_count, row_count, col_count), f32),
            pltpu.VMEM((2, layer_count, row_count, col_count), f32),
            pltpu.VMEM((2, layer_count, row_count, col_count), f32),
        ],
        in_specs=[hbm] * 6,
        out_specs=[vmem] * 3,
        scratch_shapes=[pltpu.SMEM(facies_scale.shape, f32)]
        + [pltpu.VMEM(value.shape, value.dtype) for value in fields] + [pltpu.SemaphoreType.DMA((6,))],
        name="pack",
    )(in_hbm(facies_scale), *[in_hbm(value) for value in fields])

    steps = (0, 1) if gx_count == 2 else (0, 1, -1) if gx_count > 2 else (0,)
    blocks = len(steps)
    owns = [own] + [moved(own, "gx", step) for step in steps[1:]]
    beside = pl.pallas_call(
        merge_kernel,
        out_shape=pltpu.VMEM((4, layer_count, row_count, col_count), f32),
        in_specs=[vmem] * 2,
        out_specs=vmem,
        name="merge",
    )(in_vmem(moved(to_left, "gy", 1)), in_vmem(moved(to_right, "gy", -1)))
    besides = [beside] + [moved(beside, "gx", step) for step in steps[1:]]
    operands = [in_vmem(value) for pair in zip(owns, besides) for value in pair]

    count = row_count // SUB
    block = (layer_count, row_count, col_count)
    scratch = [pltpu.SMEM(well_cells.shape, jnp.int32), pltpu.SMEM(well_rates.shape, f32), pltpu.SemaphoreType.DMA((4,))]
    whole = [pltpu.VMEM((LAYERS, width, blocks, count >> depth, SUB, LANES), f32) for depth, (width, _) in enumerate(LEVELS)]
    scratch += [whole[0], whole[0], whole[1], whole[2], whole[0]]
    scratch += [pltpu.VMEM((1,) + block, f32)] * 2 + [pltpu.VMEM(block, f32)]
    for depth, (width, _) in enumerate(LEVELS):
        scratch += Level.scratch(count >> depth, width, blocks)
    state = jax.ShapeDtypeStruct((1, layer_count, row_count, col_count), f32)
    grid_shape = (layer_count, row_count * gx_count, col_count * gy_count)
    pressure, adjoint, terms = pl.pallas_call(
        partial(cycle_kernel, grid_shape, blocks),
        out_shape=[state, state, pltpu.VMEM(block, f32)],
        in_specs=[hbm] * 2 + [vmem] * (2 * blocks),
        out_specs=[hbm, hbm, vmem],
        scratch_shapes=scratch,
        compiler_params=pltpu.CompilerParams(vmem_limit_bytes=24 * 1024 * 1024),
        name="cycles",
    )(in_hbm(well_cells), in_hbm(well_rates), *operands)
    return pressure, adjoint, summed(terms, "scen")


def solution(mesh):
    return jax.shard_map(
        shards,
        mesh=mesh,
        in_specs=(
            P(None, "gx", "gy"),
            P(None, "gx", "gy"),
            P(),
            P(None, "gx", "gy"),
            P("scen", None, "gx", "gy"),
            P("scen", None, "gx", "gy"),
            P("scen", None),
            P("scen", None),
        ),
        out_specs=(P("scen", None, "gx", "gy"), P("scen", None, "gx", "gy"), P(None, "gx", "gy")),
        check_vma=False,
    )
```

```python
from functools import partial

import jax
import jax.numpy as jnp
from jax import lax
from jax.experimental import pallas as pl
from jax.experimental.pallas import tpu as pltpu
from jax.sharding import PartitionSpec as P

WELLS = 5
FACIES = 4
LAYERS = 2
SMOOTH = 2
COARSE = 4

vertical = 0.3
damping = 0.8

LANES = 128
HALF = 64
SUB = 8
PERM, ACC, PREV, OBS = range(4)
LEVELS = ((2, 1), (1, 1), (1, 2))


def lane_index():
    return lax.broadcasted_iota(jnp.int32, (SUB, LANES), 1)


def row_index():
    return lax.broadcasted_iota(jnp.int32, (SUB, LANES), 0)


def lane_roll(value, shift):
    return pltpu.roll(value, shift % LANES, value.ndim - 1)


def row_roll(value, shift):
    return pltpu.roll(value, shift % SUB, 0)


def shuffle(value, inverse):
    rows = lax.broadcasted_iota(jnp.int32, (LANES, LANES), 0)
    cols = lax.broadcasted_iota(jnp.int32, (LANES, LANES), 1)
    natural, place = (cols, rows) if inverse else (rows, cols)
    matrix = (natural == 2 * (place % HALF) + place // HALF).astype(jnp.float32)
    flat = value.reshape(-1, LANES)
    moved_columns = lax.dot(flat, matrix, precision=lax.Precision.HIGHEST, preferred_element_type=jnp.float32)
    return moved_columns.reshape(value.shape)


def pack_kernel(scale_hbm, perm_log_hbm, facies_hbm, acc_hbm, prev_hbm, obs_hbm, own, *refs):
    sides = refs[:-7]
    scale, perm_log, facies, acc, prev, obs, sems = refs[-7:]
    pairs = ((scale_hbm, scale), (perm_log_hbm, perm_log), (facies_hbm, facies), (acc_hbm, acc), (prev_hbm, prev),
             (obs_hbm, obs))
    copies = [pltpu.make_async_copy(source, target, sems.at[i]) for i, (source, target) in enumerate(pairs)]
    for copy in copies:
        copy.start()
    for copy in copies:
        copy.wait()
    label = facies[...]
    factor = jnp.zeros(label.shape, jnp.float32)
    for number in range(FACIES):
        factor = factor + jnp.where(label == number, scale[number], jnp.float32(0.0))
    fields = [shuffle(value, False) for value in (jnp.exp(perm_log[...]) * factor, acc[...], prev[0], obs[0])]
    low = lax.broadcasted_iota(jnp.int32, label.shape, 2) % HALF < HALF // 2
    for number in range(4):
        own[number] = fields[number]
    if sides:
        to_left, to_right = sides
        for pair in range(2):
            first = lane_roll(fields[2 * pair], HALF)
            second = lane_roll(fields[2 * pair + 1], HALF + HALF // 2)
            to_left[pair] = jnp.where(low, first, second)
            to_right[pair] = jnp.where(low, second, first)


def side_kernel(own, other, message):
    low = lax.broadcasted_iota(jnp.int32, own.shape[1:], 2) % HALF < HALF // 2
    first_low = low == (lax.axis_index("gx") == 0)
    for b, block in enumerate((own, other)):
        for pair in range(2):
            first = lane_roll(block[2 * pair], HALF)
            second = lane_roll(block[2 * pair + 1], HALF + HALF // 2)
            message[b, pair] = jnp.where(first_low, first, second)


def join_kernel(mine, theirs, *besides):
    low = lax.broadcasted_iota(jnp.int32, besides[0].shape[1:], 2) % HALF < HALF // 2
    mine_low = low == (lax.axis_index("gx") == 0)
    for b, beside in enumerate(besides):
        for pair in range(2):
            one, two = mine[b, pair], theirs[1 - b, pair]
            beside[2 * pair] = jnp.where(mine_low, one, two)
            beside[2 * pair + 1] = lane_roll(jnp.where(mine_low, two, one), -(HALF // 2))


def merge_kernel(from_right, from_left, beside):
    low = lax.broadcasted_iota(jnp.int32, beside.shape[1:], 2) % HALF < HALF // 2
    for pair in range(2):
        right, left = from_right[pair], from_left[pair]
        beside[2 * pair] = jnp.where(low, right, left)
        beside[2 * pair + 1] = lane_roll(jnp.where(low, left, right), -(HALF // 2))


class Level:
    def __init__(self, count, width, span, blocks, refs):
        self.count = count
        self.width = width
        self.span = span
        self.blocks = blocks
        (self.c_south, self.c_first, self.c_inner, self.c_east, self.c_west, self.c_layer, self.weight, self.diag,
         self.target, self.now, self.later) = refs

    @staticmethod
    def scratch(count, width, blocks):
        def vectors(*lead):
            return pltpu.VMEM(lead + (SUB, LANES), jnp.float32)

        whole = vectors(LAYERS, width, blocks, count)
        edge = vectors(LAYERS, blocks, count)
        return [whole, vectors(LAYERS, width, blocks), edge, edge, edge, vectors(width, blocks, count)] + [whole] * 5

    def steps(self, ring=None):
        for b in range(self.blocks):
            for t in range(self.count):
                if ring is None or b == 0 or t < ring or t >= self.count - ring:
                    yield b, t

    def members(self):
        for layer in range(LAYERS):
            for u in range(self.width):
                yield layer, u


def row_before(values):
    edge = row_index() < 1
    rolled = [row_roll(value, 1) for value in values]
    return [jnp.where(edge, rolled[b - 1], rolled[b]) for b in range(len(values))]


def row_after(values):
    edge = row_index() >= SUB - 1
    rolled = [row_roll(value, -1) for value in values]
    return [jnp.where(edge, rolled[(b + 1) % len(values)], rolled[b]) for b in range(len(values))]


class Field:
    def __init__(self, level, source):
        self.source = source
        self.count = level.count
        self.read = {}
        self.before, self.after = {}, {}
        for layer, u in level.members():
            lows = row_before([source[layer, u, b, level.count - 1] for b in range(level.blocks)])
            highs = row_after([source[layer, u, b, 0] for b in range(level.blocks)])
            for b in range(level.blocks):
                self.before[layer, u, b] = lows[b]
                self.after[layer, u, b] = highs[b]

    def at(self, layer, u, b, t):
        if t < 0:
            return self.before[layer, u, b]
        if t >= self.count:
            return self.after[layer, u, b]
        key = layer, u, b, t
        if key not in self.read:
            self.read[key] = self.source[key]
        return self.read[key]


def row_coeff(level, layer, u, b, t):
    return level.c_south[layer, u, b, t] if t >= 0 else level.c_first[layer, u, b]


def neighbour_sums(level, source, ring=None):
    field = Field(level, source)
    coeffs = {}
    for b, t in level.steps(ring):
        for member in level.members():
            for at in (t - 1, t):
                if (member, b, at) not in coeffs:
                    coeffs[member, b, at] = row_coeff(level, *member, b, at)
        layer_coeffs = [level.c_layer[u, b, t] for u in range(level.width)]
        for layer in range(LAYERS):
            here = [field.at(layer, u, b, t) for u in range(level.width)]
            east_coeff, west_coeff = level.c_east[layer, b, t], level.c_west[layer, b, t]
            if level.width == 2:
                inner = level.c_inner[layer, b, t]
                beside = [inner * here[1] + west_coeff * lane_roll(here[1], 1),
                          inner * here[0] + east_coeff * lane_roll(here[0], -1)]
            else:
                beside = [east_coeff * lane_roll(here[0], -level.span) + west_coeff * lane_roll(here[0], level.span)]
            for u in range(level.width):
                total = (coeffs[(layer, u), b, t - 1] * field.at(layer, u, b, t - 1)
                         + coeffs[(layer, u), b, t] * field.at(layer, u, b, t + 1)
                         + (beside[u] + layer_coeffs[u] * field.at(1 - layer, u, b, t)))
                yield (layer, u, b, t), here[u], total


def sweep(level, source, result, ring=None):
    for key, value, total in neighbour_sums(level, source, ring):
        result[key] = (1.0 - damping) * value + level.weight[key] * (level.target[key] + total)


def sweeps(level, count, ring=None):
    for number in range(count):
        sweep(level, level.now, level.later, None if ring is None else ring + count - 1 - number)
        level.now, level.later = level.later, level.now


def first_sweep(level):
    for b, t in level.steps():
        for layer, u in level.members():
            key = layer, u, b, t
            level.now[key] = level.weight[key] * level.target[key]


def pair_sum(value, span):
    lower = lane_index() % (2 * span) < span
    return value + jnp.where(lower, lane_roll(value, -span), lane_roll(value, span))


def low_group(value, span):
    return jnp.where(lane_index() % (2 * span) < span, value, lane_roll(value, span))


def high_group(value, span):
    return jnp.where(lane_index() % (2 * span) < span, lane_roll(value, -span), value)


def column_sum(values, level):
    return values[0] + values[1] if level.width == 2 else pair_sum(values[0], level.span)


def restrict_residual(fine, coarse):
    residuals = {}
    for key, value, total in neighbour_sums(fine, fine.now):
        layer, u, b, t = key
        residuals[key] = fine.target[key] + total - fine.diag[key] * value
        if t % 2 == 1 and u == fine.width - 1:
            rows = [residuals[layer, v, b, t - 1] + residuals[layer, v, b, t] for v in range(fine.width)]
            coarse.target[layer, 0, b, t // 2] = column_sum(rows, fine)


def prolong(coarse, fine, ring=None):
    for b, t in fine.steps(ring):
        for layer, u in fine.members():
            key = layer, u, b, t
            fine.now[key] = fine.now[key] + coarse.now[layer, 0, b, t // 2]


def vcycle(levels, from_zero, ring=None):
    finest, middle, bottom = levels
    if from_zero:
        first_sweep(finest)
    sweeps(finest, SMOOTH - int(from_zero))
    restrict_residual(finest, middle)
    first_sweep(middle)
    sweeps(middle, SMOOTH - 1)
    restrict_residual(middle, bottom)
    first_sweep(bottom)
    sweeps(bottom, COARSE - 1)
    prolong(bottom, middle)
    sweeps(middle, SMOOTH)
    prolong(middle, finest, None if ring is None else ring + SMOOTH)
    sweeps(finest, SMOOTH, ring)


def harmonic(left, right):
    return 2.0 * left * right / jnp.maximum(left + right, 1e-20)


def finest_coeffs(level, perm, joined):
    last = level.count - 1
    for layer, u in level.members():
        heads = [perm[layer, u, b, 0] for b in range(level.blocks)]
        rolled = [row_roll(value, -1) for value in heads]
        edge = row_index() >= SUB - 1
        for b in range(level.blocks):
            after = jnp.where(edge, joined[b] * rolled[(b + 1) % level.blocks], rolled[b])
            for t in range(level.count):
                beyond = perm[layer, u, b, t + 1] if t < last else after
                level.c_south[layer, u, b, t] = harmonic(perm[layer, u, b, t], beyond)
        firsts = row_before([level.c_south[layer, u, b, last] for b in range(level.blocks)])
        for b in range(level.blocks):
            level.c_first[layer, u, b] = firsts[b]
    for b, t in level.steps():
        for u in range(level.width):
            level.c_layer[u, b, t] = vertical * harmonic(perm[0, u, b, t], perm[1, u, b, t])
        for layer in range(LAYERS):
            even, odd = perm[layer, 0, b, t], perm[layer, 1, b, t]
            level.c_inner[layer, b, t] = harmonic(even, odd)
            east = harmonic(odd, lane_roll(even, -1))
            level.c_east[layer, b, t] = east
            level.c_west[layer, b, t] = lane_roll(east, 1)


def with_weight(level, acc):
    for b, t in level.steps():
        for layer, u in level.members():
            key = layer, u, b, t
            if level.width == 2:
                beside = level.c_inner[layer, b, t] + (level.c_west, level.c_east)[u][layer, b, t]
            else:
                beside = level.c_west[layer, b, t] + level.c_east[layer, b, t]
            diag = (row_coeff(level, layer, u, b, t - 1) + row_coeff(level, layer, u, b, t)
                    + (beside + level.c_layer[u, b, t]) + acc[key])
            level.diag[key] = diag
            level.weight[key] = damping / jnp.maximum(diag, 1e-20)


def coarse_coeffs(fine, coarse, fine_acc, coarse_acc):
    width = range(fine.width)
    for b in range(coarse.blocks):
        for layer in range(LAYERS):
            coarse.c_first[layer, 0, b] = column_sum([fine.c_first[layer, u, b] for u in width], fine)
    for b, t in coarse.steps():
        one, two = 2 * t, 2 * t + 1
        coarse.c_layer[0, b, t] = column_sum([fine.c_layer[u, b, one] + fine.c_layer[u, b, two] for u in width], fine)
        for layer in range(LAYERS):
            coarse.c_south[layer, 0, b, t] = column_sum([fine.c_south[layer, u, b, two] for u in width], fine)
            coarse_acc[layer, 0, b, t] = column_sum(
                [fine_acc[layer, u, b, one] + fine_acc[layer, u, b, two] for u in width], fine)
            west = fine.c_west[layer, b, one] + fine.c_west[layer, b, two]
            east = fine.c_east[layer, b, one] + fine.c_east[layer, b, two]
            if fine.width == 1:
                west, east = low_group(west, fine.span), high_group(east, fine.span)
            coarse.c_west[layer, b, t] = west
            coarse.c_east[layer, b, t] = east
    with_weight(coarse, coarse_acc)


def own_columns(even, odd):
    return jnp.where(lane_index() < HALF, even, lane_roll(odd, HALF))


def face_terms(level, pressure, adjoint, perm):
    def face(coeff, one, two):
        changes = [field.at(*one) - (field.at(*two) if isinstance(two, tuple) else two[number])
                   for number, field in enumerate((pressure, adjoint))]
        return (coeff * coeff) * (changes[0] * changes[1])

    rows = {(layer, u): face(level.c_first[layer, u, 0], (layer, u, 0, -1), (layer, u, 0, 0))
            for layer, u in level.members()}
    for t in range(level.count):
        between = [(1.0 / vertical) * face(level.c_layer[u, 0, t], (0, u, 0, t), (1, u, 0, t)) for u in range(2)]
        for layer in range(LAYERS):
            inner = face(level.c_inner[layer, 0, t], (layer, 0, 0, t), (layer, 1, 0, t))
            easts = [lane_roll(field.at(layer, 0, 0, t), -1) for field in (pressure, adjoint)]
            east = face(level.c_east[layer, 0, t], (layer, 1, 0, t), easts)
            terms = []
            for u in range(2):
                south = face(level.c_south[layer, u, 0, t], (layer, u, 0, t), (layer, u, 0, t + 1))
                beside = lane_roll(east, 1) if u == 0 else east
                total = rows[layer, u] + south + (inner + beside) + between[u]
                rows[layer, u] = south
                terms.append(-0.5 * total / perm[layer, u, 0, t])
            yield layer, t, own_columns(*terms)


def cycle_kernel(grid_shape, blocks, *refs):
    cells_hbm, rates_hbm = refs[:2]
    inputs = [refs[2 + 2 * b:4 + 2 * b] for b in range(blocks)]
    refs = refs[2 + 2 * blocks:]
    pressure_out, adjoint_out, terms_out = refs[:3]
    cells, rates, sems, perm, acc, middle_acc, bottom_acc, pressure, pressure_rows, adjoint_rows, terms_rows = refs[3:14]
    refs = refs[14:]
    copies = [pltpu.make_async_copy(cells_hbm, cells, sems.at[0]), pltpu.make_async_copy(rates_hbm, rates, sems.at[1])]
    for copy in copies:
        copy.start()
    count = inputs[0][0].shape[2] // SUB
    levels = [Level(count >> depth, width, span, blocks, refs[11 * depth:11 * depth + 11])
              for depth, (width, span) in enumerate(LEVELS)]
    finest, middle, bottom = levels

    def rows(t):
        return pl.ds(t, SUB, stride=count)

    def fields(number, layer, b, t):
        low = lane_index() < HALF
        own, beside = [value[number, layer, rows(t), :] for value in inputs[b]]
        return jnp.where(low, own, beside), lane_roll(jnp.where(low, beside, own), HALF)

    gx = lax.axis_index("gx")
    if blocks == 3:
        joined = [1.0, 0.0, 1.0]
    elif blocks == 2:
        joined = [1.0 - gx.astype(jnp.float32), gx.astype(jnp.float32)]
    else:
        joined = [0.0]

    for b, t in finest.steps():
        for layer in range(LAYERS):
            perms, accs, starts = [fields(number, layer, b, t) for number in (PERM, ACC, PREV)]
            for u in range(2):
                key = layer, u, b, t
                perm[key] = perms[u]
                acc[key] = accs[u]
                finest.now[key] = starts[u]
                finest.target[key] = accs[u] * starts[u]

    for copy in copies:
        copy.wait()
    layer_count, total_rows, total_cols = grid_shape
    block_rows, block_cols = SUB * count, LANES
    for well in range(WELLS):
        cell = cells[0, well]
        layer = cell // (total_rows * total_cols)
        row = cell // total_cols % total_rows - gx * block_rows
        col = cell % total_cols - lax.axis_index("gy") * block_cols
        if blocks == 3:
            row_inside = (row >= -block_rows) & (row < 2 * block_rows)
        elif blocks == 2:
            row_inside = row >= -block_rows
        else:
            row_inside = row >= 0
        inside = row_inside & (col >= -HALF) & (col < block_cols + HALF)
        row = jnp.where(row < 0, row + blocks * block_rows, row)
        col = jnp.where(col < 0, col + 2 * block_cols, col)
        row = jnp.where(inside, row, 0)
        col = jnp.where(inside, col, 0)
        rate = jnp.where(inside, rates[0, well], 0.0)
        in_block = row % block_rows
        place = layer, col % 2, row // block_rows, in_block % count
        hit = (row_index() == in_block // count) & (lane_index() == col // 2)
        finest.target[place] = finest.target[place] + jnp.where(hit, rate, 0.0)

    finest_coeffs(finest, perm, joined)
    with_weight(finest, acc)
    coarse_coeffs(finest, middle, acc, middle_acc)
    coarse_coeffs(middle, bottom, middle_acc, bottom_acc)

    vcycle(levels, False)
    for b, t in finest.steps():
        for layer in range(LAYERS):
            observed = fields(OBS, layer, b, t)
            values = []
            for u in range(2):
                key = layer, u, b, t
                values.append(finest.now[key])
                pressure[key] = values[u]
                finest.target[key] = values[u] - observed[u]
            if b == 0:
                pressure_rows[0, layer, rows(t), :] = own_columns(*values)
    pressure_rows[...] = shuffle(pressure_rows[...], True)
    pressure_copy = pltpu.make_async_copy(pressure_rows, pressure_out, sems.at[2])
    pressure_copy.start()
    vcycle(levels, True, 1)
    for t in range(count):
        for layer in range(LAYERS):
            adjoint_rows[0, layer, rows(t), :] = own_columns(*[finest.now[layer, u, 0, t] for u in range(2)])
    adjoint_rows[...] = shuffle(adjoint_rows[...], True)
    adjoint_copy = pltpu.make_async_copy(adjoint_rows, adjoint_out, sems.at[3])
    adjoint_copy.start()

    for layer, t, terms in face_terms(finest, Field(finest, pressure), Field(finest, finest.now), perm):
        terms_rows[layer, rows(t), :] = terms
    terms_out[...] = shuffle(terms_rows[...], True)
    pressure_copy.wait()
    adjoint_copy.wait()


def moved(value, axis, step):
    count = lax.axis_size(axis)
    ring = axis == "gx" and count == 2
    pairs = [((i + step) % count, i) for i in range(count) if ring or 0 <= i + step < count]
    return lax.ppermute(value, axis, pairs)


def summed(value, axis):
    count = lax.axis_size(axis)
    others = [lax.ppermute(value, axis, [(i, i ^ step) for i in range(count)]) for step in range(1, count)]
    terms = [value] + others
    while len(terms) > 1:
        terms = [terms[i] + terms[i + 1] for i in range(0, len(terms), 2)]
    return terms[0]


def in_hbm(value):
    return pltpu.with_memory_space_constraint(value, pltpu.HBM)


def in_vmem(value):
    return pltpu.with_memory_space_constraint(value, pltpu.VMEM)


def shards(
    perm_log,
    facies,
    facies_scale,
    accumulation,
    previous_pressure,
    observed,
    well_cells,
    well_rates,
):
    layer_count, row_count, col_count = perm_log.shape
    gx_count, gy_count = lax.axis_size("gx"), lax.axis_size("gy")
    vmem = pl.BlockSpec(memory_space=pltpu.VMEM)
    hbm = pl.BlockSpec(memory_space=pltpu.HBM)
    f32 = jnp.float32
    fields = (perm_log, facies, accumulation, previous_pressure, observed)
    block = (layer_count, row_count, col_count)
    steps = (0, 1) if gx_count == 2 else (0, 1, -1) if gx_count > 2 else (0,)
    blocks = len(steps)
    packed_shapes = [pltpu.VMEM((4,) + block, f32)] + [pltpu.VMEM((2,) + block, f32)] * (0 if blocks == 2 else 2)
    own, *sides = pl.pallas_call(
        pack_kernel,
        out_shape=packed_shapes,
        in_specs=[hbm] * 6,
        out_specs=[vmem] * len(packed_shapes),
        scratch_shapes=[pltpu.SMEM(facies_scale.shape, f32)]
        + [pltpu.VMEM(value.shape, value.dtype) for value in fields] + [pltpu.SemaphoreType.DMA((6,))],
        name="pack",
    )(in_hbm(facies_scale), *[in_hbm(value) for value in fields])

    owns = [own] + [moved(own, "gx", step) for step in steps[1:]]
    if blocks == 2:
        message = pl.pallas_call(
            side_kernel,
            out_shape=pltpu.VMEM((2, 2) + block, f32),
            in_specs=[vmem] * 2,
            out_specs=vmem,
            name="side",
        )(*[in_vmem(value) for value in owns])
        pairs = [(y, y - 1) for y in range(1, gy_count)]
        pairs += [(gy_count + y, gy_count + y + 1) for y in range(gy_count - 1)]
        mine = lax.ppermute(message, ("gx", "gy"), pairs)
        besides = pl.pallas_call(
            join_kernel,
            out_shape=[pltpu.VMEM((4,) + block, f32)] * 2,
            in_specs=[vmem] * 2,
            out_specs=[vmem] * 2,
            name="join",
        )(in_vmem(mine), in_vmem(moved(mine, "gx", 1)))
    else:
        beside = pl.pallas_call(
            merge_kernel,
            out_shape=pltpu.VMEM((4,) + block, f32),
            in_specs=[vmem] * 2,
            out_specs=vmem,
            name="merge",
        )(in_vmem(moved(sides[0], "gy", 1)), in_vmem(moved(sides[1], "gy", -1)))
        besides = [beside] + [moved(beside, "gx", step) for step in steps[1:]]
    operands = [in_vmem(value) for pair in zip(owns, besides) for value in pair]

    count = row_count // SUB
    scratch = [pltpu.SMEM(well_cells.shape, jnp.int32), pltpu.SMEM(well_rates.shape, f32), pltpu.SemaphoreType.DMA((4,))]
    whole = [pltpu.VMEM((LAYERS, width, blocks, count >> depth, SUB, LANES), f32) for depth, (width, _) in enumerate(LEVELS)]
    scratch += [whole[0], whole[0], whole[1], whole[2], whole[0]]
    scratch += [pltpu.VMEM((1,) + block, f32)] * 2 + [pltpu.VMEM(block, f32)]
    for depth, (width, _) in enumerate(LEVELS):
        scratch += Level.scratch(count >> depth, width, blocks)
    state = jax.ShapeDtypeStruct((1, layer_count, row_count, col_count), f32)
    grid_shape = (layer_count, row_count * gx_count, col_count * gy_count)
    pressure, adjoint, terms = pl.pallas_call(
        partial(cycle_kernel, grid_shape, blocks),
        out_shape=[state, state, pltpu.VMEM(block, f32)],
        in_specs=[hbm] * 2 + [vmem] * (2 * blocks),
        out_specs=[hbm, hbm, vmem],
        scratch_shapes=scratch,
        compiler_params=pltpu.CompilerParams(vmem_limit_bytes=24 * 1024 * 1024),
        name="cycles",
    )(in_hbm(well_cells), in_hbm(well_rates), *operands)
    return pressure, adjoint, summed(terms, "scen")


def solution(mesh):
    return jax.shard_map(
        shards,
        mesh=mesh,
        in_specs=(
            P(None, "gx", "gy"),
            P(None, "gx", "gy"),
            P(),
            P(None, "gx", "gy"),
            P("scen", None, "gx", "gy"),
            P("scen", None, "gx", "gy"),
            P("scen", None),
            P("scen", None),
        ),
        out_specs=(P("scen", None, "gx", "gy"), P("scen", None, "gx", "gy"), P(None, "gx", "gy")),
        check_vma=False,
    )
```

```python
from functools import partial

import jax
import jax.numpy as jnp
from jax import lax
from jax.experimental import pallas as pl
from jax.experimental.pallas import tpu as pltpu
from jax.sharding import PartitionSpec as P

WELLS = 5
FACIES = 4
LAYERS = 2
SMOOTH = 2
COARSE = 4

vertical = 0.3
damping = 0.8

LANES = 128
HALF = 64
SUB = 8
PERM, ACC, PREV, OBS = range(4)
NEAR = 26
ROOM = HALF // 2 - NEAR
LEVELS = ((2, 1), (1, 1), (1, 2))


def lane_index():
    return lax.broadcasted_iota(jnp.int32, (SUB, LANES), 1)


def row_index():
    return lax.broadcasted_iota(jnp.int32, (SUB, LANES), 0)


def lane_roll(value, shift):
    return pltpu.roll(value, shift % LANES, value.ndim - 1)


def row_roll(value, shift):
    return pltpu.roll(value, shift % SUB, 0)


def shuffle(value, inverse):
    rows = lax.broadcasted_iota(jnp.int32, (LANES, LANES), 0)
    cols = lax.broadcasted_iota(jnp.int32, (LANES, LANES), 1)
    natural, place = (cols, rows) if inverse else (rows, cols)
    matrix = (natural == 2 * (place % HALF) + place // HALF).astype(jnp.bfloat16)
    rest = value.reshape(-1, LANES)
    total = None
    for _ in range(3):
        part = rest.astype(jnp.bfloat16)
        rest = rest - part.astype(jnp.float32)
        moved_part = jnp.dot(part, matrix, preferred_element_type=jnp.float32)
        total = moved_part if total is None else total + moved_part
    return total.reshape(value.shape)


def place_in_half(shape):
    return lax.broadcasted_iota(jnp.int32, shape, len(shape) - 1) % HALF


def spare_lanes(number, place):
    shift = NEAR - number * ROOM
    low, high = number * ROOM, HALF - (number + 1) * ROOM
    return (((place >= NEAR) & (place < HALF // 2), (place >= low) & (place < low + ROOM), shift),
            ((place >= HALF // 2) & (place < HALF - NEAR), (place >= high) & (place < high + ROOM), -shift))


def pack_kernel(scale_hbm, perm_log_hbm, facies_hbm, acc_hbm, prev_hbm, obs_hbm, own, message_a, message_b,
                scale, perm_log, facies, acc, prev, obs, sems):
    pairs = ((scale_hbm, scale), (perm_log_hbm, perm_log), (facies_hbm, facies), (acc_hbm, acc), (prev_hbm, prev),
             (obs_hbm, obs))
    copies = [pltpu.make_async_copy(source, target, sems.at[i]) for i, (source, target) in enumerate(pairs)]
    for copy in copies:
        copy.start()
    for copy in copies:
        copy.wait()
    label = facies[...]
    factor = jnp.zeros(label.shape, jnp.float32)
    for number in range(FACIES):
        factor = factor + jnp.where(label == number, scale[number], jnp.float32(0.0))
    fields = [shuffle(value, False) for value in (jnp.exp(perm_log[...]) * factor, acc[...], prev[0], obs[0])]
    for number in range(4):
        own[number] = fields[number]
    place = place_in_half(label.shape)
    full = []
    for number in range(3):
        value = fields[number]
        for lanes, _, shift in spare_lanes(number, place):
            value = jnp.where(lanes, lane_roll(fields[OBS], shift), value)
        full.append(value)
    low = place_in_half(label.shape[1:]) < HALF // 2
    left_first = low == (lax.axis_index("gy") % 2 == 1)
    couples = [(full[0][layer], full[1][layer]) for layer in range(LAYERS)] + [(full[2][0], full[2][1])]
    for plane, (one, two) in enumerate(couples):
        first, second = lane_roll(one, HALF), lane_roll(two, HALF + HALF // 2)
        message_a[plane] = jnp.where(left_first, first, second)
        message_b[plane] = jnp.where(left_first, second, first)


def merge_kernel(message_a, message_b, beside):
    place = place_in_half(beside.shape[2:])
    from_a = (place < HALF // 2) != (lax.axis_index("gy") % 2 == 1)
    full = [[], [], []]
    for plane in range(3):
        a, b = message_a[plane], message_b[plane]
        one = jnp.where(from_a, a, b)
        two = lane_roll(jnp.where(from_a, b, a), -(HALF // 2))
        for number, value in zip((0, 1) if plane < 2 else (2, 2), (one, two)):
            full[number].append(value)
    near = (place < NEAR) | (place >= HALF - NEAR)
    for layer in range(LAYERS):
        observed = jnp.zeros(place.shape, jnp.float32)
        for number in range(3):
            value = full[number][layer]
            beside[number, layer] = jnp.where(near, value, 0.0)
            for _, lanes, shift in spare_lanes(number, place):
                observed = jnp.where(lanes, lane_roll(value, -shift), observed)
        beside[OBS, layer] = observed


class Level:
    def __init__(self, count, width, span, blocks, refs):
        self.count = count
        self.width = width
        self.span = span
        self.blocks = blocks
        (self.c_south, self.c_first, self.c_inner, self.c_east, self.c_west, self.c_layer, self.weight, self.diag,
         self.target, self.now, self.later) = refs

    @staticmethod
    def scratch(count, width, blocks):
        def vectors(*lead):
            return pltpu.VMEM(lead + (SUB, LANES), jnp.float32)

        whole = vectors(LAYERS, width, blocks, count)
        edge = vectors(LAYERS, blocks, count)
        return [whole, vectors(LAYERS, width, blocks), edge, edge, edge, vectors(width, blocks, count)] + [whole] * 5

    def steps(self, ring=None):
        for b in range(self.blocks):
            for t in range(self.count):
                if ring is None or b == 0 or t < ring or t >= self.count - ring:
                    yield b, t

    def members(self):
        for layer in range(LAYERS):
            for u in range(self.width):
                yield layer, u


def row_before(values):
    edge = row_index() < 1
    rolled = [row_roll(value, 1) for value in values]
    return [jnp.where(edge, rolled[b - 1], rolled[b]) for b in range(len(values))]


def row_after(values):
    edge = row_index() >= SUB - 1
    rolled = [row_roll(value, -1) for value in values]
    return [jnp.where(edge, rolled[(b + 1) % len(values)], rolled[b]) for b in range(len(values))]


class Field:
    def __init__(self, level, source):
        self.source = source
        self.count = level.count
        self.read = {}
        self.before, self.after = {}, {}
        for layer, u in level.members():
            lows = row_before([source[layer, u, b, level.count - 1] for b in range(level.blocks)])
            highs = row_after([source[layer, u, b, 0] for b in range(level.blocks)])
            for b in range(level.blocks):
                self.before[layer, u, b] = lows[b]
                self.after[layer, u, b] = highs[b]

    def at(self, layer, u, b, t):
        if t < 0:
            return self.before[layer, u, b]
        if t >= self.count:
            return self.after[layer, u, b]
        key = layer, u, b, t
        if key not in self.read:
            self.read[key] = self.source[key]
        return self.read[key]


def row_coeff(level, layer, u, b, t):
    return level.c_south[layer, u, b, t] if t >= 0 else level.c_first[layer, u, b]


def neighbour_sums(level, source, ring=None):
    field = Field(level, source)
    coeffs = {}
    for b, t in level.steps(ring):
        for member in level.members():
            for at in (t - 1, t):
                if (member, b, at) not in coeffs:
                    coeffs[member, b, at] = row_coeff(level, *member, b, at)
        layer_coeffs = [level.c_layer[u, b, t] for u in range(level.width)]
        for layer in range(LAYERS):
            here = [field.at(layer, u, b, t) for u in range(level.width)]
            east_coeff, west_coeff = level.c_east[layer, b, t], level.c_west[layer, b, t]
            if level.width == 2:
                inner = level.c_inner[layer, b, t]
                beside = [inner * here[1] + west_coeff * lane_roll(here[1], 1),
                          inner * here[0] + east_coeff * lane_roll(here[0], -1)]
            else:
                beside = [east_coeff * lane_roll(here[0], -level.span) + west_coeff * lane_roll(here[0], level.span)]
            for u in range(level.width):
                total = (coeffs[(layer, u), b, t - 1] * field.at(layer, u, b, t - 1)
                         + coeffs[(layer, u), b, t] * field.at(layer, u, b, t + 1)
                         + (beside[u] + layer_coeffs[u] * field.at(1 - layer, u, b, t)))
                yield (layer, u, b, t), here[u], total


def sweep(level, source, result, ring=None):
    for key, value, total in neighbour_sums(level, source, ring):
        result[key] = (1.0 - damping) * value + level.weight[key] * (level.target[key] + total)


def sweeps(level, count, ring=None):
    for number in range(count):
        sweep(level, level.now, level.later, None if ring is None else ring + count - 1 - number)
        level.now, level.later = level.later, level.now


def first_sweep(level):
    for b, t in level.steps():
        for layer, u in level.members():
            key = layer, u, b, t
            level.now[key] = level.weight[key] * level.target[key]


def pair_sum(value, span):
    lower = lane_index() % (2 * span) < span
    return value + jnp.where(lower, lane_roll(value, -span), lane_roll(value, span))


def low_group(value, span):
    return jnp.where(lane_index() % (2 * span) < span, value, lane_roll(value, span))


def high_group(value, span):
    return jnp.where(lane_index() % (2 * span) < span, lane_roll(value, -span), value)


def column_sum(values, level):
    return values[0] + values[1] if level.width == 2 else pair_sum(values[0], level.span)


def restrict_residual(fine, coarse):
    residuals = {}
    for key, value, total in neighbour_sums(fine, fine.now):
        layer, u, b, t = key
        residuals[key] = fine.target[key] + total - fine.diag[key] * value
        if t % 2 == 1 and u == fine.width - 1:
            rows = [residuals[layer, v, b, t - 1] + residuals[layer, v, b, t] for v in range(fine.width)]
            coarse.target[layer, 0, b, t // 2] = column_sum(rows, fine)


def prolong(coarse, fine, ring=None):
    for b, t in fine.steps(ring):
        for layer, u in fine.members():
            key = layer, u, b, t
            fine.now[key] = fine.now[key] + coarse.now[layer, 0, b, t // 2]


def vcycle(levels, from_zero, ring=None):
    finest, middle, bottom = levels
    if from_zero:
        first_sweep(finest)
    sweeps(finest, SMOOTH - int(from_zero))
    restrict_residual(finest, middle)
    first_sweep(middle)
    sweeps(middle, SMOOTH - 1)
    restrict_residual(middle, bottom)
    first_sweep(bottom)
    sweeps(bottom, COARSE - 1)
    prolong(bottom, middle)
    sweeps(middle, SMOOTH)
    prolong(middle, finest, None if ring is None else ring + SMOOTH)
    sweeps(finest, SMOOTH, ring)


def harmonic(left, right):
    return 2.0 * left * right / jnp.maximum(left + right, 1e-20)


def finest_coeffs(level, perm, joined):
    last = level.count - 1
    for layer, u in level.members():
        heads = [perm[layer, u, b, 0] for b in range(level.blocks)]
        rolled = [row_roll(value, -1) for value in heads]
        edge = row_index() >= SUB - 1
        for b in range(level.blocks):
            after = jnp.where(edge, joined[b] * rolled[(b + 1) % level.blocks], rolled[b])
            for t in range(level.count):
                beyond = perm[layer, u, b, t + 1] if t < last else after
                level.c_south[layer, u, b, t] = harmonic(perm[layer, u, b, t], beyond)
        firsts = row_before([level.c_south[layer, u, b, last] for b in range(level.blocks)])
        for b in range(level.blocks):
            level.c_first[layer, u, b] = firsts[b]
    for b, t in level.steps():
        for u in range(level.width):
            level.c_layer[u, b, t] = vertical * harmonic(perm[0, u, b, t], perm[1, u, b, t])
        for layer in range(LAYERS):
            even, odd = perm[layer, 0, b, t], perm[layer, 1, b, t]
            level.c_inner[layer, b, t] = harmonic(even, odd)
            east = harmonic(odd, lane_roll(even, -1))
            level.c_east[layer, b, t] = east
            level.c_west[layer, b, t] = lane_roll(east, 1)


def with_weight(level, acc):
    for b, t in level.steps():
        for layer, u in level.members():
            key = layer, u, b, t
            if level.width == 2:
                beside = level.c_inner[layer, b, t] + (level.c_west, level.c_east)[u][layer, b, t]
            else:
                beside = level.c_west[layer, b, t] + level.c_east[layer, b, t]
            diag = (row_coeff(level, layer, u, b, t - 1) + row_coeff(level, layer, u, b, t)
                    + (beside + level.c_layer[u, b, t]) + acc[key])
            level.diag[key] = diag
            level.weight[key] = damping / jnp.maximum(diag, 1e-20)


def coarse_coeffs(fine, coarse, fine_acc, coarse_acc):
    width = range(fine.width)
    for b in range(coarse.blocks):
        for layer in range(LAYERS):
            coarse.c_first[layer, 0, b] = column_sum([fine.c_first[layer, u, b] for u in width], fine)
    for b, t in coarse.steps():
        one, two = 2 * t, 2 * t + 1
        coarse.c_layer[0, b, t] = column_sum([fine.c_layer[u, b, one] + fine.c_layer[u, b, two] for u in width], fine)
        for layer in range(LAYERS):
            coarse.c_south[layer, 0, b, t] = column_sum([fine.c_south[layer, u, b, two] for u in width], fine)
            coarse_acc[layer, 0, b, t] = column_sum(
                [fine_acc[layer, u, b, one] + fine_acc[layer, u, b, two] for u in width], fine)
            west = fine.c_west[layer, b, one] + fine.c_west[layer, b, two]
            east = fine.c_east[layer, b, one] + fine.c_east[layer, b, two]
            if fine.width == 1:
                west, east = low_group(west, fine.span), high_group(east, fine.span)
            coarse.c_west[layer, b, t] = west
            coarse.c_east[layer, b, t] = east
    with_weight(coarse, coarse_acc)


def own_columns(even, odd):
    return jnp.where(lane_index() < HALF, even, lane_roll(odd, HALF))


def face_terms(level, pressure, adjoint, perm):
    def face(coeff, one, two):
        changes = [field.at(*one) - (field.at(*two) if isinstance(two, tuple) else two[number])
                   for number, field in enumerate((pressure, adjoint))]
        return (coeff * coeff) * (changes[0] * changes[1])

    rows = {(layer, u): face(level.c_first[layer, u, 0], (layer, u, 0, -1), (layer, u, 0, 0))
            for layer, u in level.members()}
    for t in range(level.count):
        between = [(1.0 / vertical) * face(level.c_layer[u, 0, t], (0, u, 0, t), (1, u, 0, t)) for u in range(2)]
        for layer in range(LAYERS):
            inner = face(level.c_inner[layer, 0, t], (layer, 0, 0, t), (layer, 1, 0, t))
            easts = [lane_roll(field.at(layer, 0, 0, t), -1) for field in (pressure, adjoint)]
            east = face(level.c_east[layer, 0, t], (layer, 1, 0, t), easts)
            terms = []
            for u in range(2):
                south = face(level.c_south[layer, u, 0, t], (layer, u, 0, t), (layer, u, 0, t + 1))
                beside = lane_roll(east, 1) if u == 0 else east
                total = rows[layer, u] + south + (inner + beside) + between[u]
                rows[layer, u] = south
                terms.append(-0.5 * total / perm[layer, u, 0, t])
            yield layer, t, own_columns(*terms)


def cycle_kernel(grid_shape, blocks, *refs):
    cells_hbm, rates_hbm = refs[:2]
    inputs = [refs[2 + 2 * b:4 + 2 * b] for b in range(blocks)]
    refs = refs[2 + 2 * blocks:]
    pressure_out, adjoint_out, terms_out = refs[:3]
    cells, rates, sems, perm, acc, middle_acc, bottom_acc, pressure, pressure_rows, adjoint_rows, terms_rows = refs[3:14]
    refs = refs[14:]
    copies = [pltpu.make_async_copy(cells_hbm, cells, sems.at[0]), pltpu.make_async_copy(rates_hbm, rates, sems.at[1])]
    for copy in copies:
        copy.start()
    count = inputs[0][0].shape[2] // SUB
    levels = [Level(count >> depth, width, span, blocks, refs[11 * depth:11 * depth + 11])
              for depth, (width, span) in enumerate(LEVELS)]
    finest, middle, bottom = levels

    def rows(t):
        return pl.ds(t, SUB, stride=count)

    def fields(number, layer, b, t):
        low = lane_index() < HALF
        own, beside = [value[number, layer, rows(t), :] for value in inputs[b]]
        return jnp.where(low, own, beside), lane_roll(jnp.where(low, beside, own), HALF)

    gx = lax.axis_index("gx")
    if blocks == 3:
        joined = [1.0, 0.0, 1.0]
    elif blocks == 2:
        joined = [1.0 - gx.astype(jnp.float32), gx.astype(jnp.float32)]
    else:
        joined = [0.0]

    for b, t in finest.steps():
        for layer in range(LAYERS):
            perms, accs, starts = [fields(number, layer, b, t) for number in (PERM, ACC, PREV)]
            for u in range(2):
                key = layer, u, b, t
                perm[key] = perms[u]
                acc[key] = accs[u]
                finest.now[key] = starts[u]
                finest.target[key] = accs[u] * starts[u]

    for copy in copies:
        copy.wait()
    layer_count, total_rows, total_cols = grid_shape
    block_rows, block_cols = SUB * count, LANES
    for well in range(WELLS):
        cell = cells[0, well]
        layer = cell // (total_rows * total_cols)
        row = cell // total_cols % total_rows - gx * block_rows
        col = cell % total_cols - lax.axis_index("gy") * block_cols
        if blocks == 3:
            row_inside = (row >= -block_rows) & (row < 2 * block_rows)
        elif blocks == 2:
            row_inside = row >= -block_rows
        else:
            row_inside = row >= 0
        inside = row_inside & (col >= -HALF) & (col < block_cols + HALF)
        row = jnp.where(row < 0, row + blocks * block_rows, row)
        col = jnp.where(col < 0, col + 2 * block_cols, col)
        row = jnp.where(inside, row, 0)
        col = jnp.where(inside, col, 0)
        rate = jnp.where(inside, rates[0, well], 0.0)
        in_block = row % block_rows
        place = layer, col % 2, row // block_rows, in_block % count
        hit = (row_index() == in_block // count) & (lane_index() == col // 2)
        finest.target[place] = finest.target[place] + jnp.where(hit, rate, 0.0)

    finest_coeffs(finest, perm, joined)
    with_weight(finest, acc)
    coarse_coeffs(finest, middle, acc, middle_acc)
    coarse_coeffs(middle, bottom, middle_acc, bottom_acc)

    vcycle(levels, False)
    for b, t in finest.steps():
        for layer in range(LAYERS):
            observed = fields(OBS, layer, b, t)
            values = []
            for u in range(2):
                key = layer, u, b, t
                values.append(finest.now[key])
                pressure[key] = values[u]
                finest.target[key] = values[u] - observed[u]
            if b == 0:
                pressure_rows[0, layer, rows(t), :] = own_columns(*values)
    pressure_rows[...] = shuffle(pressure_rows[...], True)
    pressure_copy = pltpu.make_async_copy(pressure_rows, pressure_out, sems.at[2])
    pressure_copy.start()
    vcycle(levels, True, 1)
    for t in range(count):
        for layer in range(LAYERS):
            adjoint_rows[0, layer, rows(t), :] = own_columns(*[finest.now[layer, u, 0, t] for u in range(2)])
    adjoint_rows[...] = shuffle(adjoint_rows[...], True)
    adjoint_copy = pltpu.make_async_copy(adjoint_rows, adjoint_out, sems.at[3])
    adjoint_copy.start()

    for layer, t, terms in face_terms(finest, Field(finest, pressure), Field(finest, finest.now), perm):
        terms_rows[layer, rows(t), :] = terms
    terms_out[...] = shuffle(terms_rows[...], True)
    pressure_copy.wait()
    adjoint_copy.wait()


def moved(value, axis, step):
    count = lax.axis_size(axis)
    ring = axis == "gx" and count == 2
    pairs = [((i + step) % count, i) for i in range(count) if ring or 0 <= i + step < count]
    return lax.ppermute(value, axis, pairs)


def swapped(value, axis, first):
    pairs = []
    for i in range(first, lax.axis_size(axis) - 1, 2):
        pairs += [(i, i + 1), (i + 1, i)]
    return lax.ppermute(value, axis, pairs)


def summed(value, axis):
    count = lax.axis_size(axis)
    others = [lax.ppermute(value, axis, [(i, i ^ step) for i in range(count)]) for step in range(count - 1, 0, -1)]
    terms = [value] + others[::-1]
    while len(terms) > 1:
        terms = [terms[i] + terms[i + 1] for i in range(0, len(terms), 2)]
    return terms[0]


def in_hbm(value):
    return pltpu.with_memory_space_constraint(value, pltpu.HBM)


def in_vmem(value):
    return pltpu.with_memory_space_constraint(value, pltpu.VMEM)


def shards(
    perm_log,
    facies,
    facies_scale,
    accumulation,
    previous_pressure,
    observed,
    well_cells,
    well_rates,
):
    layer_count, row_count, col_count = perm_log.shape
    gx_count, gy_count = lax.axis_size("gx"), lax.axis_size("gy")
    vmem = pl.BlockSpec(memory_space=pltpu.VMEM)
    hbm = pl.BlockSpec(memory_space=pltpu.HBM)
    f32 = jnp.float32
    fields = (perm_log, facies, accumulation, previous_pressure, observed)
    block = (layer_count, row_count, col_count)
    own, message_a, message_b = pl.pallas_call(
        pack_kernel,
        out_shape=[
            pltpu.VMEM((4,) + block, f32),
            pltpu.VMEM((3,) + block[1:], f32),
            pltpu.VMEM((3,) + block[1:], f32),
        ],
        in_specs=[hbm] * 6,
        out_specs=[vmem] * 3,
        scratch_shapes=[pltpu.SMEM(facies_scale.shape, f32)]
        + [pltpu.VMEM(value.shape, value.dtype) for value in fields] + [pltpu.SemaphoreType.DMA((6,))],
        name="pack",
    )(in_hbm(facies_scale), *[in_hbm(value) for value in fields])

    steps = (0, 1) if gx_count == 2 else (0, 1, -1) if gx_count > 2 else (0,)
    blocks = len(steps)
    owns = [own] + [moved(own, "gx", step) for step in steps[1:]]
    beside = pl.pallas_call(
        merge_kernel,
        out_shape=pltpu.VMEM((4, layer_count, row_count, col_count), f32),
        in_specs=[vmem] * 2,
        out_specs=vmem,
        name="merge",
    )(in_vmem(swapped(message_a, "gy", 0)), in_vmem(swapped(message_b, "gy", 1)))
    besides = [beside] + [moved(beside, "gx", step) for step in steps[1:]]
    operands = [in_vmem(value) for pair in zip(owns, besides) for value in pair]

    count = row_count // SUB
    scratch = [pltpu.SMEM(well_cells.shape, jnp.int32), pltpu.SMEM(well_rates.shape, f32), pltpu.SemaphoreType.DMA((4,))]
    whole = [pltpu.VMEM((LAYERS, width, blocks, count >> depth, SUB, LANES), f32) for depth, (width, _) in enumerate(LEVELS)]
    scratch += [whole[0], whole[0], whole[1], whole[2], whole[0]]
    scratch += [pltpu.VMEM((1,) + block, f32)] * 2 + [pltpu.VMEM(block, f32)]
    for depth, (width, _) in enumerate(LEVELS):
        scratch += Level.scratch(count >> depth, width, blocks)
    state = jax.ShapeDtypeStruct((1, layer_count, row_count, col_count), f32)
    grid_shape = (layer_count, row_count * gx_count, col_count * gy_count)
    pressure, adjoint, terms = pl.pallas_call(
        partial(cycle_kernel, grid_shape, blocks),
        out_shape=[state, state, pltpu.VMEM(block, f32)],
        in_specs=[hbm] * 2 + [vmem] * (2 * blocks),
        out_specs=[hbm, hbm, vmem],
        scratch_shapes=scratch,
        compiler_params=pltpu.CompilerParams(vmem_limit_bytes=24 * 1024 * 1024),
        name="cycles",
    )(in_hbm(well_cells), in_hbm(well_rates), *operands)
    return pressure, adjoint, summed(terms, "scen")


def solution(mesh):
    return jax.shard_map(
        shards,
        mesh=mesh,
        in_specs=(
            P(None, "gx", "gy"),
            P(None, "gx", "gy"),
            P(),
            P(None, "gx", "gy"),
            P("scen", None, "gx", "gy"),
            P("scen", None, "gx", "gy"),
            P("scen", None),
            P("scen", None),
        ),
        out_specs=(P("scen", None, "gx", "gy"), P("scen", None, "gx", "gy"), P(None, "gx", "gy")),
        check_vma=False,
    )
```

```python
from functools import partial

import jax
import jax.numpy as jnp
from jax import lax
from jax.experimental import pallas as pl
from jax.experimental.pallas import tpu as pltpu
from jax.sharding import PartitionSpec as P

WELLS = 5
FACIES = 4
LAYERS = 2
SMOOTH = 2
COARSE = 4

vertical = 0.3
damping = 0.8

LANES = 128
HALF = 64
SUB = 8
PERM, ACC, PREV, OBS = range(4)
NEAR = 26
ROOM = HALF // 2 - NEAR
LEVELS = ((2, 1), (1, 1), (1, 2))


def lane_index():
    return lax.broadcasted_iota(jnp.int32, (SUB, LANES), 1)


def row_index():
    return lax.broadcasted_iota(jnp.int32, (SUB, LANES), 0)


def lane_roll(value, shift):
    return pltpu.roll(value, shift % LANES, value.ndim - 1)


def row_roll(value, shift):
    return pltpu.roll(value, shift % SUB, 0)


def shuffle(value, inverse):
    rows = lax.broadcasted_iota(jnp.int32, (LANES, LANES), 0)
    cols = lax.broadcasted_iota(jnp.int32, (LANES, LANES), 1)
    natural, place = (cols, rows) if inverse else (rows, cols)
    matrix = (natural == 2 * (place % HALF) + place // HALF).astype(jnp.bfloat16)
    rest = value.reshape(-1, LANES)
    total = None
    for _ in range(3):
        part = rest.astype(jnp.bfloat16)
        rest = rest - part.astype(jnp.float32)
        moved_part = jnp.dot(part, matrix, preferred_element_type=jnp.float32)
        total = moved_part if total is None else total + moved_part
    return total.reshape(value.shape)


def place_in_half(shape):
    return lax.broadcasted_iota(jnp.int32, shape, len(shape) - 1) % HALF


def spare_lanes(number, place):
    shift = NEAR - number * ROOM
    low, high = number * ROOM, HALF - (number + 1) * ROOM
    return (((place >= NEAR) & (place < HALF // 2), (place >= low) & (place < low + ROOM), shift),
            ((place >= HALF // 2) & (place < HALF - NEAR), (place >= high) & (place < high + ROOM), -shift))


def left_in_first_round():
    return (lax.axis_index("gy") + lax.axis_index("gx")) % 2 == 1


def pack_kernel(scale_hbm, perm_log_hbm, facies_hbm, acc_hbm, prev_hbm, obs_hbm, own, message_a, message_b,
                scale, perm_log, facies, acc, prev, obs, sems):
    pairs = ((scale_hbm, scale), (perm_log_hbm, perm_log), (facies_hbm, facies), (acc_hbm, acc), (prev_hbm, prev),
             (obs_hbm, obs))
    copies = [pltpu.make_async_copy(source, target, sems.at[i]) for i, (source, target) in enumerate(pairs)]
    for copy in copies:
        copy.start()
    for copy in copies:
        copy.wait()
    label = facies[...]
    factor = jnp.zeros(label.shape, jnp.float32)
    for number in range(FACIES):
        factor = factor + jnp.where(label == number, scale[number], jnp.float32(0.0))
    fields = [shuffle(value, False) for value in (jnp.exp(perm_log[...]) * factor, acc[...], prev[0], obs[0])]
    for number in range(4):
        own[number] = fields[number]
    place = place_in_half(label.shape)
    full = []
    for number in range(3):
        value = fields[number]
        for lanes, _, shift in spare_lanes(number, place):
            value = jnp.where(lanes, lane_roll(fields[OBS], shift), value)
        full.append(value)
    low = place_in_half(label.shape[1:]) < HALF // 2
    left_first = low == left_in_first_round()
    couples = [(full[0][layer], full[1][layer]) for layer in range(LAYERS)] + [(full[2][0], full[2][1])]
    for plane, (one, two) in enumerate(couples):
        first, second = lane_roll(one, HALF), lane_roll(two, HALF + HALF // 2)
        message_a[plane] = jnp.where(left_first, first, second)
        message_b[plane] = jnp.where(left_first, second, first)


def merge_kernel(message_a, message_b, beside):
    place = place_in_half(beside.shape[2:])
    from_a = (place < HALF // 2) != left_in_first_round()
    full = [[], [], []]
    for plane in range(3):
        a, b = message_a[plane], message_b[plane]
        one = jnp.where(from_a, a, b)
        two = lane_roll(jnp.where(from_a, b, a), -(HALF // 2))
        for number, value in zip((0, 1) if plane < 2 else (2, 2), (one, two)):
            full[number].append(value)
    near = (place < NEAR) | (place >= HALF - NEAR)
    for layer in range(LAYERS):
        observed = jnp.zeros(place.shape, jnp.float32)
        for number in range(3):
            value = full[number][layer]
            beside[number, layer] = jnp.where(near, value, 0.0)
            for _, lanes, shift in spare_lanes(number, place):
                observed = jnp.where(lanes, lane_roll(value, -shift), observed)
        beside[OBS, layer] = observed


class Level:
    def __init__(self, count, width, span, blocks, refs):
        self.count = count
        self.width = width
        self.span = span
        self.blocks = blocks
        (self.c_south, self.c_first, self.c_inner, self.c_east, self.c_west, self.c_layer, self.weight,
         self.diag) = refs[:8]
        self.target, self.now, self.later = refs[8:] or ({}, {}, {})

    @staticmethod
    def scratch(count, width, blocks):
        def vectors(*lead):
            return pltpu.VMEM(lead + (SUB, LANES), jnp.float32)

        whole = vectors(LAYERS, width, blocks, count)
        edge = vectors(LAYERS, blocks, count)
        return [whole, vectors(LAYERS, width, blocks), edge, edge, edge, vectors(width, blocks, count)] + [whole] * (5 if width == 2 else 2)

    def steps(self, ring=None):
        for b in range(self.blocks):
            for t in range(self.count):
                if ring is None or b == 0 or t < ring or t >= self.count - ring:
                    yield b, t

    def members(self):
        for layer in range(LAYERS):
            for u in range(self.width):
                yield layer, u


def row_before(values):
    edge = row_index() < 1
    rolled = [row_roll(value, 1) for value in values]
    return [jnp.where(edge, rolled[b - 1], rolled[b]) for b in range(len(values))]


def row_after(values):
    edge = row_index() >= SUB - 1
    rolled = [row_roll(value, -1) for value in values]
    return [jnp.where(edge, rolled[(b + 1) % len(values)], rolled[b]) for b in range(len(values))]


class Field:
    def __init__(self, level, source):
        self.source = source
        self.count = level.count
        self.read = {}
        self.before, self.after = {}, {}
        for layer, u in level.members():
            lows = row_before([source[layer, u, b, level.count - 1] for b in range(level.blocks)])
            highs = row_after([source[layer, u, b, 0] for b in range(level.blocks)])
            for b in range(level.blocks):
                self.before[layer, u, b] = lows[b]
                self.after[layer, u, b] = highs[b]

    def at(self, layer, u, b, t):
        if t < 0:
            return self.before[layer, u, b]
        if t >= self.count:
            return self.after[layer, u, b]
        key = layer, u, b, t
        if key not in self.read:
            self.read[key] = self.source[key]
        return self.read[key]


def row_coeff(level, layer, u, b, t):
    return level.c_south[layer, u, b, t] if t >= 0 else level.c_first[layer, u, b]


def neighbour_sums(level, source, ring=None):
    field = Field(level, source)
    coeffs = {}
    for b, t in level.steps(ring):
        for member in level.members():
            for at in (t - 1, t):
                if (member, b, at) not in coeffs:
                    coeffs[member, b, at] = row_coeff(level, *member, b, at)
        layer_coeffs = [level.c_layer[u, b, t] for u in range(level.width)]
        for layer in range(LAYERS):
            here = [field.at(layer, u, b, t) for u in range(level.width)]
            east_coeff, west_coeff = level.c_east[layer, b, t], level.c_west[layer, b, t]
            if level.width == 2:
                inner = level.c_inner[layer, b, t]
                beside = [inner * here[1] + west_coeff * lane_roll(here[1], 1),
                          inner * here[0] + east_coeff * lane_roll(here[0], -1)]
            else:
                beside = [east_coeff * lane_roll(here[0], -level.span) + west_coeff * lane_roll(here[0], level.span)]
            for u in range(level.width):
                total = (coeffs[(layer, u), b, t - 1] * field.at(layer, u, b, t - 1)
                         + coeffs[(layer, u), b, t] * field.at(layer, u, b, t + 1)
                         + (beside[u] + layer_coeffs[u] * field.at(1 - layer, u, b, t)))
                yield (layer, u, b, t), here[u], total


def sweep(level, source, result, ring=None):
    for key, value, total in neighbour_sums(level, source, ring):
        result[key] = (1.0 - damping) * value + level.weight[key] * (level.target[key] + total)


def sweeps(level, count, ring=None):
    for number in range(count):
        sweep(level, level.now, level.later, None if ring is None else ring + count - 1 - number)
        level.now, level.later = level.later, level.now


def first_sweep(level):
    for b, t in level.steps():
        for layer, u in level.members():
            key = layer, u, b, t
            level.now[key] = level.weight[key] * level.target[key]


def pair_sum(value, span):
    lower = lane_index() % (2 * span) < span
    return value + jnp.where(lower, lane_roll(value, -span), lane_roll(value, span))


def low_group(value, span):
    return jnp.where(lane_index() % (2 * span) < span, value, lane_roll(value, span))


def high_group(value, span):
    return jnp.where(lane_index() % (2 * span) < span, lane_roll(value, -span), value)


def column_sum(values, level):
    return values[0] + values[1] if level.width == 2 else pair_sum(values[0], level.span)


def restrict_residual(fine, coarse):
    residuals = {}
    for key, value, total in neighbour_sums(fine, fine.now):
        layer, u, b, t = key
        residuals[key] = fine.target[key] + total - fine.diag[key] * value
        if t % 2 == 1 and u == fine.width - 1:
            rows = [residuals[layer, v, b, t - 1] + residuals[layer, v, b, t] for v in range(fine.width)]
            coarse.target[layer, 0, b, t // 2] = column_sum(rows, fine)


def prolong(coarse, fine, ring=None):
    for b, t in fine.steps(ring):
        for layer, u in fine.members():
            key = layer, u, b, t
            fine.now[key] = fine.now[key] + coarse.now[layer, 0, b, t // 2]


def vcycle(levels, from_zero, ring=None):
    finest, middle, bottom = levels
    if from_zero:
        first_sweep(finest)
    sweeps(finest, SMOOTH - int(from_zero))
    restrict_residual(finest, middle)
    first_sweep(middle)
    sweeps(middle, SMOOTH - 1)
    restrict_residual(middle, bottom)
    first_sweep(bottom)
    sweeps(bottom, COARSE - 1)
    prolong(bottom, middle)
    sweeps(middle, SMOOTH)
    prolong(middle, finest, None if ring is None else ring + SMOOTH)
    sweeps(finest, SMOOTH, ring)


def divide(value, by):
    estimate = pl.reciprocal(by, approx=True)
    return value * (estimate * (2.0 - by * estimate))


def harmonic(left, right):
    return divide(2.0 * left * right, jnp.maximum(left + right, 1e-20))


def finest_coeffs(level, perm, joined):
    last = level.count - 1
    for layer, u in level.members():
        heads = [perm[layer, u, b, 0] for b in range(level.blocks)]
        rolled = [row_roll(value, -1) for value in heads]
        edge = row_index() >= SUB - 1
        for b in range(level.blocks):
            after = jnp.where(edge, joined[b] * rolled[(b + 1) % level.blocks], rolled[b])
            for t in range(level.count):
                beyond = perm[layer, u, b, t + 1] if t < last else after
                level.c_south[layer, u, b, t] = harmonic(perm[layer, u, b, t], beyond)
        firsts = row_before([level.c_south[layer, u, b, last] for b in range(level.blocks)])
        for b in range(level.blocks):
            level.c_first[layer, u, b] = firsts[b]
    for b, t in level.steps():
        for u in range(level.width):
            level.c_layer[u, b, t] = vertical * harmonic(perm[0, u, b, t], perm[1, u, b, t])
        for layer in range(LAYERS):
            even, odd = perm[layer, 0, b, t], perm[layer, 1, b, t]
            level.c_inner[layer, b, t] = harmonic(even, odd)
            east = harmonic(odd, lane_roll(even, -1))
            level.c_east[layer, b, t] = east
            level.c_west[layer, b, t] = lane_roll(east, 1)


def with_weight(level, acc):
    for b, t in level.steps():
        for layer, u in level.members():
            key = layer, u, b, t
            if level.width == 2:
                beside = level.c_inner[layer, b, t] + (level.c_west, level.c_east)[u][layer, b, t]
            else:
                beside = level.c_west[layer, b, t] + level.c_east[layer, b, t]
            diag = (row_coeff(level, layer, u, b, t - 1) + row_coeff(level, layer, u, b, t)
                    + (beside + level.c_layer[u, b, t]) + acc[key])
            level.diag[key] = diag
            level.weight[key] = divide(damping, jnp.maximum(diag, 1e-20))


def coarse_coeffs(fine, coarse, fine_acc, coarse_acc):
    width = range(fine.width)
    for b in range(coarse.blocks):
        for layer in range(LAYERS):
            coarse.c_first[layer, 0, b] = column_sum([fine.c_first[layer, u, b] for u in width], fine)
    for b, t in coarse.steps():
        one, two = 2 * t, 2 * t + 1
        coarse.c_layer[0, b, t] = column_sum([fine.c_layer[u, b, one] + fine.c_layer[u, b, two] for u in width], fine)
        for layer in range(LAYERS):
            coarse.c_south[layer, 0, b, t] = column_sum([fine.c_south[layer, u, b, two] for u in width], fine)
            coarse_acc[layer, 0, b, t] = column_sum(
                [fine_acc[layer, u, b, one] + fine_acc[layer, u, b, two] for u in width], fine)
            west = fine.c_west[layer, b, one] + fine.c_west[layer, b, two]
            east = fine.c_east[layer, b, one] + fine.c_east[layer, b, two]
            if fine.width == 1:
                west, east = low_group(west, fine.span), high_group(east, fine.span)
            coarse.c_west[layer, b, t] = west
            coarse.c_east[layer, b, t] = east
    with_weight(coarse, coarse_acc)


def own_columns(even, odd):
    return jnp.where(lane_index() < HALF, even, lane_roll(odd, HALF))


def face_terms(level, pressure, adjoint, perm):
    def face(coeff, one, two):
        changes = [field.at(*one) - (field.at(*two) if isinstance(two, tuple) else two[number])
                   for number, field in enumerate((pressure, adjoint))]
        return (coeff * coeff) * (changes[0] * changes[1])

    rows = {(layer, u): face(level.c_first[layer, u, 0], (layer, u, 0, -1), (layer, u, 0, 0))
            for layer, u in level.members()}
    for t in range(level.count):
        between = [(1.0 / vertical) * face(level.c_layer[u, 0, t], (0, u, 0, t), (1, u, 0, t)) for u in range(2)]
        for layer in range(LAYERS):
            inner = face(level.c_inner[layer, 0, t], (layer, 0, 0, t), (layer, 1, 0, t))
            easts = [lane_roll(field.at(layer, 0, 0, t), -1) for field in (pressure, adjoint)]
            east = face(level.c_east[layer, 0, t], (layer, 1, 0, t), easts)
            terms = []
            for u in range(2):
                south = face(level.c_south[layer, u, 0, t], (layer, u, 0, t), (layer, u, 0, t + 1))
                beside = lane_roll(east, 1) if u == 0 else east
                total = rows[layer, u] + south + (inner + beside) + between[u]
                rows[layer, u] = south
                terms.append(divide(-0.5 * total, perm[layer, u, 0, t]))
            yield layer, t, own_columns(*terms)


def cycle_kernel(grid_shape, blocks, *refs):
    cells_hbm, rates_hbm = refs[:2]
    inputs = [refs[2 + 2 * b:4 + 2 * b] for b in range(blocks)]
    refs = refs[2 + 2 * blocks:]
    pressure_out, adjoint_out, terms_out = refs[:3]
    cells, rates, sems, perm, acc, middle_acc, bottom_acc, pressure, pressure_rows, adjoint_rows, terms_rows = refs[3:14]
    refs = refs[14:]
    copies = [pltpu.make_async_copy(cells_hbm, cells, sems.at[0]), pltpu.make_async_copy(rates_hbm, rates, sems.at[1])]
    for copy in copies:
        copy.start()
    count = inputs[0][0].shape[2] // SUB
    bounds = (0, 11, 19, 27)
    levels = [Level(count >> depth, width, span, blocks, refs[bounds[depth]:bounds[depth + 1]])
              for depth, (width, span) in enumerate(LEVELS)]
    finest, middle, bottom = levels

    def rows(t):
        return pl.ds(t, SUB, stride=count)

    def fields(number, layer, b, t):
        low = lane_index() < HALF
        own, beside = [value[number, layer, rows(t), :] for value in inputs[b]]
        return jnp.where(low, own, beside), lane_roll(jnp.where(low, beside, own), HALF)

    gx = lax.axis_index("gx")
    if blocks == 3:
        joined = [1.0, 0.0, 1.0]
    elif blocks == 2:
        joined = [1.0 - gx.astype(jnp.float32), gx.astype(jnp.float32)]
    else:
        joined = [0.0]

    for b, t in finest.steps():
        for layer in range(LAYERS):
            perms, accs, starts = [fields(number, layer, b, t) for number in (PERM, ACC, PREV)]
            for u in range(2):
                key = layer, u, b, t
                perm[key] = perms[u]
                acc[key] = accs[u]
                finest.now[key] = starts[u]
                finest.target[key] = accs[u] * starts[u]

    for copy in copies:
        copy.wait()
    layer_count, total_rows, total_cols = grid_shape
    block_rows, block_cols = SUB * count, LANES
    for well in range(WELLS):
        cell = cells[0, well]
        layer = cell // (total_rows * total_cols)
        row = cell // total_cols % total_rows - gx * block_rows
        col = cell % total_cols - lax.axis_index("gy") * block_cols
        if blocks == 3:
            row_inside = (row >= -block_rows) & (row < 2 * block_rows)
        elif blocks == 2:
            row_inside = row >= -block_rows
        else:
            row_inside = row >= 0
        inside = row_inside & (col >= -HALF) & (col < block_cols + HALF)
        row = jnp.where(row < 0, row + blocks * block_rows, row)
        col = jnp.where(col < 0, col + 2 * block_cols, col)
        row = jnp.where(inside, row, 0)
        col = jnp.where(inside, col, 0)
        rate = jnp.where(inside, rates[0, well], 0.0)
        in_block = row % block_rows
        place = layer, col % 2, row // block_rows, in_block % count
        hit = (row_index() == in_block // count) & (lane_index() == col // 2)
        finest.target[place] = finest.target[place] + jnp.where(hit, rate, 0.0)

    finest_coeffs(finest, perm, joined)
    with_weight(finest, acc)
    coarse_coeffs(finest, middle, acc, middle_acc)
    coarse_coeffs(middle, bottom, middle_acc, bottom_acc)

    vcycle(levels, False)
    for b, t in finest.steps():
        for layer in range(LAYERS):
            observed = fields(OBS, layer, b, t)
            values = []
            for u in range(2):
                key = layer, u, b, t
                values.append(finest.now[key])
                pressure[key] = values[u]
                finest.target[key] = values[u] - observed[u]
            if b == 0:
                pressure_rows[0, layer, rows(t), :] = own_columns(*values)
    pressure_rows[...] = shuffle(pressure_rows[...], True)
    pressure_copy = pltpu.make_async_copy(pressure_rows, pressure_out, sems.at[2])
    pressure_copy.start()
    vcycle(levels, True, 1)
    for t in range(count):
        for layer in range(LAYERS):
            adjoint_rows[0, layer, rows(t), :] = own_columns(*[finest.now[layer, u, 0, t] for u in range(2)])
    adjoint_rows[...] = shuffle(adjoint_rows[...], True)
    adjoint_copy = pltpu.make_async_copy(adjoint_rows, adjoint_out, sems.at[3])
    adjoint_copy.start()

    for layer, t, terms in face_terms(finest, Field(finest, pressure), Field(finest, finest.now), perm):
        terms_rows[layer, rows(t), :] = terms
    terms_out[...] = shuffle(terms_rows[...], True)
    pressure_copy.wait()
    adjoint_copy.wait()


def moved(value, axis, step):
    count = lax.axis_size(axis)
    ring = axis == "gx" and count == 2
    pairs = [((i + step) % count, i) for i in range(count) if ring or 0 <= i + step < count]
    return lax.ppermute(value, axis, pairs)


def swapped(value, number):
    gx_count, gy_count = lax.axis_size("gx"), lax.axis_size("gy")
    pairs = []
    for x in range(gx_count):
        for y in range((x + number) % 2, gy_count - 1, 2):
            one, two = x * gy_count + y, x * gy_count + y + 1
            pairs += [(one, two), (two, one)]
    return lax.ppermute(value, ("gx", "gy"), pairs)


def summed(value):
    scen_count, gx_count = lax.axis_size("scen"), lax.axis_size("gx")
    orders = [list(range(1, scen_count))] * 2
    if scen_count == 4:
        orders = [[1, 2, 3], [2, 1, 3]]
    others = []
    for turn in range(scen_count - 1):
        pairs = [(i * gx_count + x, (i ^ orders[x % 2][turn]) * gx_count + x)
                 for i in range(scen_count) for x in range(gx_count)]
        others.append(lax.ppermute(value, ("scen", "gx"), pairs))
    terms = [value] + others
    while len(terms) > 1:
        terms = [terms[i] + terms[i + 1] for i in range(0, len(terms), 2)]
    return terms[0]


def in_hbm(value):
    return pltpu.with_memory_space_constraint(value, pltpu.HBM)


def in_vmem(value):
    return pltpu.with_memory_space_constraint(value, pltpu.VMEM)


def shards(
    perm_log,
    facies,
    facies_scale,
    accumulation,
    previous_pressure,
    observed,
    well_cells,
    well_rates,
):
    layer_count, row_count, col_count = perm_log.shape
    gx_count, gy_count = lax.axis_size("gx"), lax.axis_size("gy")
    vmem = pl.BlockSpec(memory_space=pltpu.VMEM)
    hbm = pl.BlockSpec(memory_space=pltpu.HBM)
    f32 = jnp.float32
    fields = (perm_log, facies, accumulation, previous_pressure, observed)
    block = (layer_count, row_count, col_count)
    own, message_a, message_b = pl.pallas_call(
        pack_kernel,
        out_shape=[
            pltpu.VMEM((4,) + block, f32),
            pltpu.VMEM((3,) + block[1:], f32),
            pltpu.VMEM((3,) + block[1:], f32),
        ],
        in_specs=[hbm] * 6,
        out_specs=[vmem] * 3,
        scratch_shapes=[pltpu.SMEM(facies_scale.shape, f32)]
        + [pltpu.VMEM(value.shape, value.dtype) for value in fields] + [pltpu.SemaphoreType.DMA((6,))],
        name="pack",
    )(in_hbm(facies_scale), *[in_hbm(value) for value in fields])

    steps = (0, 1) if gx_count == 2 else (0, 1, -1) if gx_count > 2 else (0,)
    blocks = len(steps)
    owns = [own] + [moved(own, "gx", step) for step in steps[1:]]
    beside = pl.pallas_call(
        merge_kernel,
        out_shape=pltpu.VMEM((4, layer_count, row_count, col_count), f32),
        in_specs=[vmem] * 2,
        out_specs=vmem,
        name="merge",
    )(in_vmem(swapped(message_a, 0)), in_vmem(swapped(message_b, 1)))
    besides = [beside] + [moved(beside, "gx", step) for step in steps[1:]]
    operands = [in_vmem(value) for pair in zip(owns, besides) for value in pair]

    count = row_count // SUB
    scratch = [pltpu.SMEM(well_cells.shape, jnp.int32), pltpu.SMEM(well_rates.shape, f32), pltpu.SemaphoreType.DMA((4,))]
    whole = [pltpu.VMEM((LAYERS, width, blocks, count >> depth, SUB, LANES), f32) for depth, (width, _) in enumerate(LEVELS)]
    scratch += [whole[0], whole[0], whole[1], whole[2], whole[0]]
    scratch += [pltpu.VMEM((1,) + block, f32)] * 2 + [pltpu.VMEM(block, f32)]
    for depth, (width, _) in enumerate(LEVELS):
        scratch += Level.scratch(count >> depth, width, blocks)
    state = jax.ShapeDtypeStruct((1, layer_count, row_count, col_count), f32)
    grid_shape = (layer_count, row_count * gx_count, col_count * gy_count)
    pressure, adjoint, terms = pl.pallas_call(
        partial(cycle_kernel, grid_shape, blocks),
        out_shape=[state, state, pltpu.VMEM(block, f32)],
        in_specs=[hbm] * 2 + [vmem] * (2 * blocks),
        out_specs=[hbm, hbm, vmem],
        scratch_shapes=scratch,
        compiler_params=pltpu.CompilerParams(vmem_limit_bytes=24 * 1024 * 1024),
        name="cycles",
    )(in_hbm(well_cells), in_hbm(well_rates), *operands)
    return pressure, adjoint, summed(terms)


def solution(mesh):
    return jax.shard_map(
        shards,
        mesh=mesh,
        in_specs=(
            P(None, "gx", "gy"),
            P(None, "gx", "gy"),
            P(),
            P(None, "gx", "gy"),
            P("scen", None, "gx", "gy"),
            P("scen", None, "gx", "gy"),
            P("scen", None),
            P("scen", None),
        ),
        out_specs=(P("scen", None, "gx", "gy"), P("scen", None, "gx", "gy"), P(None, "gx", "gy")),
        check_vma=False,
    )
```

```python
from functools import partial

import jax
import jax.numpy as jnp
from jax import lax
from jax.experimental import pallas as pl
from jax.experimental.pallas import tpu as pltpu
from jax.sharding import PartitionSpec as P

WELLS = 5
FACIES = 4
LAYERS = 2
SMOOTH = 2
COARSE = 4

vertical = 0.3
damping = 0.8

LANES = 128
HALF = 64
SUB = 8
PERM, ACC, PREV, OBS = range(4)
NEAR = 26
ROOM = HALF // 2 - NEAR
LEVELS = ((2, 1), (1, 1), (1, 2))


def lane_index():
    return lax.broadcasted_iota(jnp.int32, (SUB, LANES), 1)


def row_index():
    return lax.broadcasted_iota(jnp.int32, (SUB, LANES), 0)


def lane_roll(value, shift):
    return pltpu.roll(value, shift % LANES, value.ndim - 1)


def row_roll(value, shift):
    return pltpu.roll(value, shift % SUB, 0)


def shuffle(value, inverse):
    rows = lax.broadcasted_iota(jnp.int32, (LANES, LANES), 0)
    cols = lax.broadcasted_iota(jnp.int32, (LANES, LANES), 1)
    natural, place = (cols, rows) if inverse else (rows, cols)
    matrix = (natural == 2 * (place % HALF) + place // HALF).astype(jnp.bfloat16)
    rest = value.reshape(-1, LANES)
    total = None
    for _ in range(3):
        part = rest.astype(jnp.bfloat16)
        rest = rest - part.astype(jnp.float32)
        moved_part = jnp.dot(part, matrix, preferred_element_type=jnp.float32)
        total = moved_part if total is None else total + moved_part
    return total.reshape(value.shape)


def place_in_half(shape):
    return lax.broadcasted_iota(jnp.int32, shape, len(shape) - 1) % HALF


def spare_lanes(number, place):
    shift = NEAR - number * ROOM
    low, high = number * ROOM, HALF - (number + 1) * ROOM
    return (((place >= NEAR) & (place < HALF // 2), (place >= low) & (place < low + ROOM), shift),
            ((place >= HALF // 2) & (place < HALF - NEAR), (place >= high) & (place < high + ROOM), -shift))


def pack_kernel(scale_hbm, perm_log_hbm, facies_hbm, acc_hbm, prev_hbm, obs_hbm, own, message_a, message_b,
                scale, perm_log, facies, acc, prev, obs, sems):
    pairs = ((scale_hbm, scale), (perm_log_hbm, perm_log), (facies_hbm, facies), (acc_hbm, acc), (prev_hbm, prev),
             (obs_hbm, obs))
    copies = [pltpu.make_async_copy(source, target, sems.at[i]) for i, (source, target) in enumerate(pairs)]
    for copy in copies:
        copy.start()
    for copy in copies:
        copy.wait()
    label = facies[...]
    factor = jnp.zeros(label.shape, jnp.float32)
    for number in range(FACIES):
        factor = factor + jnp.where(label == number, scale[number], jnp.float32(0.0))
    fields = [shuffle(value, False) for value in (jnp.exp(perm_log[...]) * factor, acc[...], prev[0], obs[0])]
    for number in range(4):
        own[number] = fields[number]
    place = place_in_half(label.shape)
    full = []
    for number in range(3):
        value = fields[number]
        for lanes, _, shift in spare_lanes(number, place):
            value = jnp.where(lanes, lane_roll(fields[OBS], shift), value)
        full.append(value)
    low = place_in_half(label.shape[1:]) < HALF // 2
    left_first = low == (lax.axis_index("gy") % 2 == 1)
    couples = [(full[0][layer], full[1][layer]) for layer in range(LAYERS)] + [(full[2][0], full[2][1])]
    for plane, (one, two) in enumerate(couples):
        first, second = lane_roll(one, HALF), lane_roll(two, HALF + HALF // 2)
        message_a[plane] = jnp.where(left_first, first, second)
        message_b[plane] = jnp.where(left_first, second, first)


def merge_kernel(message_a, message_b, beside):
    place = place_in_half(beside.shape[2:])
    gy, gy_count = lax.axis_index("gy"), lax.axis_size("gy")
    inside = ((place < HALF // 2) & (gy < gy_count - 1)) | ((place >= HALF // 2) & (gy > 0))
    from_a = (place < HALF // 2) != (lax.axis_index("gy") % 2 == 1)
    full = [[], [], []]
    for plane in range(3):
        a, b = message_a[plane], message_b[plane]
        one = jnp.where(from_a, a, b)
        two = lane_roll(jnp.where(from_a, b, a), -(HALF // 2))
        for number, value in zip((0, 1) if plane < 2 else (2, 2), (one, two)):
            full[number].append(value)
    near = ((place < NEAR) | (place >= HALF - NEAR)) & inside
    for layer in range(LAYERS):
        observed = jnp.zeros(place.shape, jnp.float32)
        for number in range(3):
            value = full[number][layer]
            beside[number, layer] = jnp.where(near, value, 0.0)
            for _, lanes, shift in spare_lanes(number, place):
                observed = jnp.where(lanes, lane_roll(value, -shift), observed)
        beside[OBS, layer] = jnp.where(inside, observed, 0.0)


class Level:
    def __init__(self, count, width, span, blocks, refs):
        self.count = count
        self.width = width
        self.span = span
        self.blocks = blocks
        (self.c_south, self.c_first, self.c_inner, self.c_east, self.c_west, self.c_layer, self.weight, self.diag,
         self.target, self.now, self.later) = refs

    @staticmethod
    def scratch(count, width, blocks):
        def vectors(*lead):
            return pltpu.VMEM(lead + (SUB, LANES), jnp.float32)

        whole = vectors(LAYERS, width, blocks, count)
        edge = vectors(LAYERS, blocks, count)
        return [whole, vectors(LAYERS, width, blocks), edge, edge, edge, vectors(width, blocks, count)] + [whole] * 5

    def steps(self, ring=None):
        for b in range(self.blocks):
            for t in range(self.count):
                if ring is None or b == 0 or t < ring or t >= self.count - ring:
                    yield b, t

    def members(self):
        for layer in range(LAYERS):
            for u in range(self.width):
                yield layer, u


def row_before(values):
    edge = row_index() < 1
    rolled = [row_roll(value, 1) for value in values]
    return [jnp.where(edge, rolled[b - 1], rolled[b]) for b in range(len(values))]


def row_after(values):
    edge = row_index() >= SUB - 1
    rolled = [row_roll(value, -1) for value in values]
    return [jnp.where(edge, rolled[(b + 1) % len(values)], rolled[b]) for b in range(len(values))]


class Field:
    def __init__(self, level, source, coarse=None):
        self.source = source
        self.coarse = coarse
        self.count = level.count
        self.read = {}
        self.before, self.after = {}, {}
        for layer, u in level.members():
            lows = row_before([self.value(layer, u, b, level.count - 1) for b in range(level.blocks)])
            highs = row_after([self.value(layer, u, b, 0) for b in range(level.blocks)])
            for b in range(level.blocks):
                self.before[layer, u, b] = lows[b]
                self.after[layer, u, b] = highs[b]

    def value(self, layer, u, b, t):
        value = self.source[layer, u, b, t]
        return value if self.coarse is None else value + self.coarse[layer, 0, b, t // 2]

    def at(self, layer, u, b, t):
        if t < 0:
            return self.before[layer, u, b]
        if t >= self.count:
            return self.after[layer, u, b]
        key = layer, u, b, t
        if key not in self.read:
            self.read[key] = self.value(*key)
        return self.read[key]


def row_coeff(level, layer, u, b, t):
    return level.c_south[layer, u, b, t] if t >= 0 else level.c_first[layer, u, b]


def neighbour_sums(level, source, ring=None, coarse=None):
    field = Field(level, source, coarse)
    coeffs = {}
    for b, t in level.steps(ring):
        for member in level.members():
            for at in (t - 1, t):
                if (member, b, at) not in coeffs:
                    coeffs[member, b, at] = row_coeff(level, *member, b, at)
        layer_coeffs = [level.c_layer[u, b, t] for u in range(level.width)]
        for layer in range(LAYERS):
            here = [field.at(layer, u, b, t) for u in range(level.width)]
            east_coeff, west_coeff = level.c_east[layer, b, t], level.c_west[layer, b, t]
            if level.width == 2:
                inner = level.c_inner[layer, b, t]
                beside = [inner * here[1] + west_coeff * lane_roll(here[1], 1),
                          inner * here[0] + east_coeff * lane_roll(here[0], -1)]
            else:
                beside = [east_coeff * lane_roll(here[0], -level.span) + west_coeff * lane_roll(here[0], level.span)]
            for u in range(level.width):
                total = (coeffs[(layer, u), b, t - 1] * field.at(layer, u, b, t - 1)
                         + coeffs[(layer, u), b, t] * field.at(layer, u, b, t + 1)
                         + (beside[u] + layer_coeffs[u] * field.at(1 - layer, u, b, t)))
                yield (layer, u, b, t), here[u], total


def sweep(level, source, result, ring=None, coarse=None):
    for key, value, total in neighbour_sums(level, source, ring, coarse):
        result[key] = (1.0 - damping) * value + level.weight[key] * (level.target[key] + total)


def sweeps(level, count, ring=None, coarse=None):
    for number in range(count):
        sweep(level, level.now, level.later, None if ring is None else ring + count - 1 - number,
              coarse if number == 0 else None)
        level.now, level.later = level.later, level.now


def first_sweep(level):
    for b, t in level.steps():
        for layer, u in level.members():
            key = layer, u, b, t
            level.now[key] = level.weight[key] * level.target[key]


def pair_sum(value, span):
    lower = lane_index() % (2 * span) < span
    return value + jnp.where(lower, lane_roll(value, -span), lane_roll(value, span))


def low_group(value, span):
    return jnp.where(lane_index() % (2 * span) < span, value, lane_roll(value, span))


def high_group(value, span):
    return jnp.where(lane_index() % (2 * span) < span, lane_roll(value, -span), value)


def column_sum(values, level):
    return values[0] + values[1] if level.width == 2 else pair_sum(values[0], level.span)


def restrict_residual(fine, coarse):
    residuals = {}
    for key, value, total in neighbour_sums(fine, fine.now):
        layer, u, b, t = key
        residuals[key] = fine.target[key] + total - fine.diag[key] * value
        if t % 2 == 1 and u == fine.width - 1:
            rows = [residuals[layer, v, b, t - 1] + residuals[layer, v, b, t] for v in range(fine.width)]
            coarse.target[layer, 0, b, t // 2] = column_sum(rows, fine)


def vcycle(levels, from_zero, ring=None):
    finest, middle, bottom = levels
    if from_zero:
        first_sweep(finest)
    sweeps(finest, SMOOTH - int(from_zero))
    restrict_residual(finest, middle)
    first_sweep(middle)
    sweeps(middle, SMOOTH - 1)
    restrict_residual(middle, bottom)
    first_sweep(bottom)
    sweeps(bottom, COARSE - 1)
    sweeps(middle, SMOOTH, None, bottom.now)
    sweeps(finest, SMOOTH, ring, middle.now)


def harmonic(left, right):
    return 2.0 * left * right / jnp.maximum(left + right, 1e-20)


def finest_coeffs(level, perm, joined):
    last = level.count - 1
    for layer, u in level.members():
        heads = [perm[layer, u, b, 0] for b in range(level.blocks)]
        rolled = [row_roll(value, -1) for value in heads]
        edge = row_index() >= SUB - 1
        for b in range(level.blocks):
            after = jnp.where(edge, joined[b] * rolled[(b + 1) % level.blocks], rolled[b])
            for t in range(level.count):
                beyond = perm[layer, u, b, t + 1] if t < last else after
                level.c_south[layer, u, b, t] = harmonic(perm[layer, u, b, t], beyond)
        firsts = row_before([level.c_south[layer, u, b, last] for b in range(level.blocks)])
        for b in range(level.blocks):
            level.c_first[layer, u, b] = firsts[b]
    for b, t in level.steps():
        for u in range(level.width):
            level.c_layer[u, b, t] = vertical * harmonic(perm[0, u, b, t], perm[1, u, b, t])
        for layer in range(LAYERS):
            even, odd = perm[layer, 0, b, t], perm[layer, 1, b, t]
            level.c_inner[layer, b, t] = harmonic(even, odd)
            east = harmonic(odd, lane_roll(even, -1))
            level.c_east[layer, b, t] = east
            level.c_west[layer, b, t] = lane_roll(east, 1)


def with_weight(level, acc):
    for b, t in level.steps():
        for layer, u in level.members():
            key = layer, u, b, t
            if level.width == 2:
                beside = level.c_inner[layer, b, t] + (level.c_west, level.c_east)[u][layer, b, t]
            else:
                beside = level.c_west[layer, b, t] + level.c_east[layer, b, t]
            diag = (row_coeff(level, layer, u, b, t - 1) + row_coeff(level, layer, u, b, t)
                    + (beside + level.c_layer[u, b, t]) + acc[key])
            level.diag[key] = diag
            level.weight[key] = damping / jnp.maximum(diag, 1e-20)


def coarse_coeffs(fine, coarse, fine_acc, coarse_acc):
    width = range(fine.width)
    for b in range(coarse.blocks):
        for layer in range(LAYERS):
            coarse.c_first[layer, 0, b] = column_sum([fine.c_first[layer, u, b] for u in width], fine)
    for b, t in coarse.steps():
        one, two = 2 * t, 2 * t + 1
        coarse.c_layer[0, b, t] = column_sum([fine.c_layer[u, b, one] + fine.c_layer[u, b, two] for u in width], fine)
        for layer in range(LAYERS):
            coarse.c_south[layer, 0, b, t] = column_sum([fine.c_south[layer, u, b, two] for u in width], fine)
            coarse_acc[layer, 0, b, t] = column_sum(
                [fine_acc[layer, u, b, one] + fine_acc[layer, u, b, two] for u in width], fine)
            west = fine.c_west[layer, b, one] + fine.c_west[layer, b, two]
            east = fine.c_east[layer, b, one] + fine.c_east[layer, b, two]
            if fine.width == 1:
                west, east = low_group(west, fine.span), high_group(east, fine.span)
            coarse.c_west[layer, b, t] = west
            coarse.c_east[layer, b, t] = east
    with_weight(coarse, coarse_acc)


def own_columns(even, odd):
    return jnp.where(lane_index() < HALF, even, lane_roll(odd, HALF))


def face_terms(level, pressure, adjoint, perm):
    def face(coeff, one, two):
        changes = [field.at(*one) - (field.at(*two) if isinstance(two, tuple) else two[number])
                   for number, field in enumerate((pressure, adjoint))]
        return (coeff * coeff) * (changes[0] * changes[1])

    rows = {(layer, u): face(level.c_first[layer, u, 0], (layer, u, 0, -1), (layer, u, 0, 0))
            for layer, u in level.members()}
    for t in range(level.count):
        between = [(1.0 / vertical) * face(level.c_layer[u, 0, t], (0, u, 0, t), (1, u, 0, t)) for u in range(2)]
        for layer in range(LAYERS):
            inner = face(level.c_inner[layer, 0, t], (layer, 0, 0, t), (layer, 1, 0, t))
            easts = [lane_roll(field.at(layer, 0, 0, t), -1) for field in (pressure, adjoint)]
            east = face(level.c_east[layer, 0, t], (layer, 1, 0, t), easts)
            terms = []
            for u in range(2):
                south = face(level.c_south[layer, u, 0, t], (layer, u, 0, t), (layer, u, 0, t + 1))
                beside = lane_roll(east, 1) if u == 0 else east
                total = rows[layer, u] + south + (inner + beside) + between[u]
                rows[layer, u] = south
                terms.append(-0.5 * total / perm[layer, u, 0, t])
            yield layer, t, own_columns(*terms)


def order_kernel(shuffled, ordered):
    ordered[...] = shuffle(shuffled[...], True)


def cycle_kernel(grid_shape, blocks, *refs):
    cells_hbm, rates_hbm = refs[:2]
    inputs = [refs[2 + 2 * b:4 + 2 * b] for b in range(blocks)]
    refs = refs[2 + 2 * blocks:]
    pressure_out, adjoint_out, terms_out = refs[:3]
    cells, rates, sems, perm, acc, middle_acc, bottom_acc, pressure, pressure_rows, terms_rows = refs[3:13]
    refs = refs[13:]
    copies = [pltpu.make_async_copy(cells_hbm, cells, sems.at[0]), pltpu.make_async_copy(rates_hbm, rates, sems.at[1])]
    for copy in copies:
        copy.start()
    count = inputs[0][0].shape[2] // SUB
    levels = [Level(count >> depth, width, span, blocks, refs[11 * depth:11 * depth + 11])
              for depth, (width, span) in enumerate(LEVELS)]
    finest, middle, bottom = levels

    def rows(t):
        return pl.ds(t, SUB, stride=count)

    def fields(number, layer, b, t):
        low = lane_index() < HALF
        own, beside = [value[number, layer, rows(t), :] for value in inputs[b]]
        return jnp.where(low, own, beside), lane_roll(jnp.where(low, beside, own), HALF)

    gx = lax.axis_index("gx")
    if blocks == 3:
        joined = [1.0, 0.0, 1.0]
    elif blocks == 2:
        joined = [1.0 - gx.astype(jnp.float32), gx.astype(jnp.float32)]
    else:
        joined = [0.0]

    for b, t in finest.steps():
        for layer in range(LAYERS):
            perms, accs, starts = [fields(number, layer, b, t) for number in (PERM, ACC, PREV)]
            for u in range(2):
                key = layer, u, b, t
                perm[key] = perms[u]
                acc[key] = accs[u]
                finest.now[key] = starts[u]
                finest.target[key] = accs[u] * starts[u]

    for copy in copies:
        copy.wait()
    layer_count, total_rows, total_cols = grid_shape
    block_rows, block_cols = SUB * count, LANES
    for well in range(WELLS):
        cell = cells[0, well]
        layer = cell // (total_rows * total_cols)
        row = cell // total_cols % total_rows - gx * block_rows
        col = cell % total_cols - lax.axis_index("gy") * block_cols
        if blocks == 3:
            row_inside = (row >= -block_rows) & (row < 2 * block_rows)
        elif blocks == 2:
            row_inside = row >= -block_rows
        else:
            row_inside = row >= 0
        inside = row_inside & (col >= -HALF) & (col < block_cols + HALF)
        row = jnp.where(row < 0, row + blocks * block_rows, row)
        col = jnp.where(col < 0, col + 2 * block_cols, col)
        row = jnp.where(inside, row, 0)
        col = jnp.where(inside, col, 0)
        rate = jnp.where(inside, rates[0, well], 0.0)
        in_block = row % block_rows
        place = layer, col % 2, row // block_rows, in_block % count
        hit = (row_index() == in_block // count) & (lane_index() == col // 2)
        finest.target[place] = finest.target[place] + jnp.where(hit, rate, 0.0)

    finest_coeffs(finest, perm, joined)
    with_weight(finest, acc)
    coarse_coeffs(finest, middle, acc, middle_acc)
    coarse_coeffs(middle, bottom, middle_acc, bottom_acc)

    vcycle(levels, False)
    for b, t in finest.steps():
        for layer in range(LAYERS):
            observed = fields(OBS, layer, b, t)
            values = []
            for u in range(2):
                key = layer, u, b, t
                values.append(finest.now[key])
                pressure[key] = values[u]
                finest.target[key] = values[u] - observed[u]
            if b == 0:
                pressure_rows[0, layer, rows(t), :] = own_columns(*values)
    pressure_rows[...] = shuffle(pressure_rows[...], True)
    pressure_copy = pltpu.make_async_copy(pressure_rows, pressure_out, sems.at[2])
    pressure_copy.start()
    vcycle(levels, True, 1)
    for t in range(count):
        for layer in range(LAYERS):
            adjoint_out[0, layer, rows(t), :] = own_columns(*[finest.now[layer, u, 0, t] for u in range(2)])

    for layer, t, terms in face_terms(finest, Field(finest, pressure), Field(finest, finest.now), perm):
        terms_rows[layer, rows(t), :] = terms
    terms_out[...] = shuffle(terms_rows[...], True)
    pressure_copy.wait()


def moved(value, axis, step):
    count = lax.axis_size(axis)
    ring = axis == "gx" and count == 2
    pairs = [((i + step) % count, i) for i in range(count) if ring or 0 <= i + step < count]
    return lax.ppermute(value, axis, pairs)


def swapped(value, axis, first):
    count = lax.axis_size(axis)
    pairs = {i: i for i in range(count)}
    for i in range(first, count - 1, 2):
        pairs[i], pairs[i + 1] = i + 1, i
    return lax.ppermute(value, axis, list(pairs.items()))


def summed(value, axis):
    count = lax.axis_size(axis)
    others = [lax.ppermute(value, axis, [(i, i ^ step) for i in range(count)]) for step in range(count - 1, 0, -1)]
    terms = [value] + others[::-1]
    while len(terms) > 1:
        terms = [terms[i] + terms[i + 1] for i in range(0, len(terms), 2)]
    return terms[0]


def in_hbm(value):
    return pltpu.with_memory_space_constraint(value, pltpu.HBM)


def in_vmem(value):
    return pltpu.with_memory_space_constraint(value, pltpu.VMEM)


def shards(
    perm_log,
    facies,
    facies_scale,
    accumulation,
    previous_pressure,
    observed,
    well_cells,
    well_rates,
):
    layer_count, row_count, col_count = perm_log.shape
    gx_count, gy_count = lax.axis_size("gx"), lax.axis_size("gy")
    vmem = pl.BlockSpec(memory_space=pltpu.VMEM)
    hbm = pl.BlockSpec(memory_space=pltpu.HBM)
    f32 = jnp.float32
    fields = (perm_log, facies, accumulation, previous_pressure, observed)
    block = (layer_count, row_count, col_count)
    own, message_a, message_b = pl.pallas_call(
        pack_kernel,
        out_shape=[
            pltpu.VMEM((4,) + block, f32),
            pltpu.VMEM((3,) + block[1:], f32),
            pltpu.VMEM((3,) + block[1:], f32),
        ],
        in_specs=[hbm] * 6,
        out_specs=[vmem] * 3,
        scratch_shapes=[pltpu.SMEM(facies_scale.shape, f32)]
        + [pltpu.VMEM(value.shape, value.dtype) for value in fields] + [pltpu.SemaphoreType.DMA((6,))],
        name="pack",
    )(in_hbm(facies_scale), *[in_hbm(value) for value in fields])

    steps = (0, 1) if gx_count == 2 else (0, 1, -1) if gx_count > 2 else (0,)
    blocks = len(steps)
    owns = [own] + [moved(own, "gx", step) for step in steps[1:]]
    beside = pl.pallas_call(
        merge_kernel,
        out_shape=pltpu.VMEM((4, layer_count, row_count, col_count), f32),
        in_specs=[vmem] * 2,
        out_specs=vmem,
        name="merge",
    )(in_vmem(swapped(message_a, "gy", 0)), in_vmem(swapped(message_b, "gy", 1)))
    besides = [beside] + [moved(beside, "gx", step) for step in steps[1:]]
    operands = [in_vmem(value) for pair in zip(owns, besides) for value in pair]

    count = row_count // SUB
    scratch = [pltpu.SMEM(well_cells.shape, jnp.int32), pltpu.SMEM(well_rates.shape, f32), pltpu.SemaphoreType.DMA((3,))]
    whole = [pltpu.VMEM((LAYERS, width, blocks, count >> depth, SUB, LANES), f32) for depth, (width, _) in enumerate(LEVELS)]
    scratch += [whole[0], whole[0], whole[1], whole[2], whole[0]]
    scratch += [pltpu.VMEM((1,) + block, f32), pltpu.VMEM(block, f32)]
    for depth, (width, _) in enumerate(LEVELS):
        scratch += Level.scratch(count >> depth, width, blocks)
    state = jax.ShapeDtypeStruct((1, layer_count, row_count, col_count), f32)
    grid_shape = (layer_count, row_count * gx_count, col_count * gy_count)
    pressure, shuffled, terms = pl.pallas_call(
        partial(cycle_kernel, grid_shape, blocks),
        out_shape=[state, pltpu.VMEM((1,) + block, f32), pltpu.VMEM(block, f32)],
        in_specs=[hbm] * 2 + [vmem] * (2 * blocks),
        out_specs=[hbm, vmem, vmem],
        scratch_shapes=scratch,
        compiler_params=pltpu.CompilerParams(vmem_limit_bytes=24 * 1024 * 1024),
        name="cycles",
    )(in_hbm(well_cells), in_hbm(well_rates), *operands)
    gradient = summed(terms, "scen")
    adjoint = pl.pallas_call(
        order_kernel,
        out_shape=state,
        in_specs=[vmem],
        out_specs=vmem,
        cost_estimate=pl.CostEstimate(flops=2 * row_count * LANES**2 * 8, bytes_accessed=2**18, transcendentals=0),
        name="order",
    )(in_vmem(shuffled))
    return pressure, adjoint, gradient


def solution(mesh):
    return jax.shard_map(
        shards,
        mesh=mesh,
        in_specs=(
            P(None, "gx", "gy"),
            P(None, "gx", "gy"),
            P(),
            P(None, "gx", "gy"),
            P("scen", None, "gx", "gy"),
            P("scen", None, "gx", "gy"),
            P("scen", None),
            P("scen", None),
        ),
        out_specs=(P("scen", None, "gx", "gy"), P("scen", None, "gx", "gy"), P(None, "gx", "gy")),
        check_vma=False,
    )
```

```python
from functools import partial

import jax
import jax.numpy as jnp
from jax import lax
from jax.experimental import pallas as pl
from jax.experimental.pallas import tpu as pltpu
from jax.sharding import PartitionSpec as P

WELLS = 5
FACIES = 4
LAYERS = 2
SMOOTH = 2
COARSE = 4

vertical = 0.3
damping = 0.8

LANES = 128
HALF = 64
SUB = 8
PERM, ACC, PREV, OBS = range(4)
NEAR = 26
ROOM = HALF // 2 - NEAR
LEVELS = ((2, 1), (1, 1), (1, 2))


def lane_index():
    return lax.broadcasted_iota(jnp.int32, (SUB, LANES), 1)


def row_index():
    return lax.broadcasted_iota(jnp.int32, (SUB, LANES), 0)


def lane_roll(value, shift):
    return pltpu.roll(value, shift % LANES, value.ndim - 1)


def row_roll(value, shift):
    return pltpu.roll(value, shift % SUB, 0)


def shuffle(value, inverse):
    rows = lax.broadcasted_iota(jnp.int32, (LANES, LANES), 0)
    cols = lax.broadcasted_iota(jnp.int32, (LANES, LANES), 1)
    natural, place = (cols, rows) if inverse else (rows, cols)
    matrix = (natural == 2 * (place % HALF) + place // HALF).astype(jnp.bfloat16)
    rest = value.reshape(-1, LANES)
    total = None
    for _ in range(3):
        part = rest.astype(jnp.bfloat16)
        rest = rest - part.astype(jnp.float32)
        moved_part = jnp.dot(part, matrix, preferred_element_type=jnp.float32)
        total = moved_part if total is None else total + moved_part
    return total.reshape(value.shape)


def place_in_half(shape):
    return lax.broadcasted_iota(jnp.int32, shape, len(shape) - 1) % HALF


def spare_lanes(number, place):
    shift = NEAR - number * ROOM
    low, high = number * ROOM, HALF - (number + 1) * ROOM
    return (((place >= NEAR) & (place < HALF // 2), (place >= low) & (place < low + ROOM), shift),
            ((place >= HALF // 2) & (place < HALF - NEAR), (place >= high) & (place < high + ROOM), -shift))


def interleaved(rows):
    count = rows.shape[0] // SUB
    return jnp.concatenate([rows[pl.ds(t, SUB, stride=count), :] for t in range(count)], axis=0)


def put_in_order(shuffled, ordered):
    count = ordered.shape[-2] // SUB
    natural = shuffle(shuffled, True)
    for layer in range(LAYERS):
        for t in range(count):
            ordered[layer, pl.ds(t, SUB, stride=count), :] = natural[layer, t * SUB:(t + 1) * SUB]


def pack_kernel(scale_hbm, perm_log_hbm, facies_hbm, acc_hbm, prev_hbm, obs_hbm, own, message_a, message_b,
                scale, perm_log, facies, acc, prev, obs, sems):
    pairs = ((scale_hbm, scale), (perm_log_hbm, perm_log), (facies_hbm, facies), (acc_hbm, acc), (prev_hbm, prev),
             (obs_hbm, obs))
    copies = [pltpu.make_async_copy(source, target, sems.at[i]) for i, (source, target) in enumerate(pairs)]
    for copy in copies:
        copy.start()
    for copy in copies:
        copy.wait()

    def layers(ref):
        return jnp.stack([interleaved(ref.at[layer]) for layer in range(LAYERS)])

    label = layers(facies)
    factor = jnp.zeros(label.shape, jnp.float32)
    for number in range(FACIES):
        factor = factor + jnp.where(label == number, scale[number], jnp.float32(0.0))
    fields = [shuffle(value, False) for value in (jnp.exp(layers(perm_log)) * factor, layers(acc), layers(prev.at[0]), layers(obs.at[0]))]
    for number in range(4):
        own[number] = fields[number]
    place = place_in_half(label.shape)
    full = []
    for number in range(3):
        value = fields[number]
        for lanes, _, shift in spare_lanes(number, place):
            value = jnp.where(lanes, lane_roll(fields[OBS], shift), value)
        full.append(value)
    low = place_in_half(label.shape[1:]) < HALF // 2
    left_first = low == (lax.axis_index("gy") % 2 == 1)
    couples = [(full[0][layer], full[1][layer]) for layer in range(LAYERS)] + [(full[2][0], full[2][1])]
    for plane, (one, two) in enumerate(couples):
        first, second = lane_roll(one, HALF), lane_roll(two, HALF + HALF // 2)
        message_a[plane] = jnp.where(left_first, first, second)
        message_b[plane] = jnp.where(left_first, second, first)


def merge_kernel(message_a, message_b, beside):
    place = place_in_half(beside.shape[2:])
    from_a = (place < HALF // 2) != (lax.axis_index("gy") % 2 == 1)
    full = [[], [], []]
    for plane in range(3):
        a, b = message_a[plane], message_b[plane]
        one = jnp.where(from_a, a, b)
        two = lane_roll(jnp.where(from_a, b, a), -(HALF // 2))
        for number, value in zip((0, 1) if plane < 2 else (2, 2), (one, two)):
            full[number].append(value)
    near = (place < NEAR) | (place >= HALF - NEAR)
    for layer in range(LAYERS):
        observed = jnp.zeros(place.shape, jnp.float32)
        for number in range(3):
            value = full[number][layer]
            beside[number, layer] = jnp.where(near, value, 0.0)
            for _, lanes, shift in spare_lanes(number, place):
                observed = jnp.where(lanes, lane_roll(value, -shift), observed)
        beside[OBS, layer] = observed


class Level:
    def __init__(self, count, width, span, blocks, refs):
        self.count = count
        self.width = width
        self.span = span
        self.blocks = blocks
        (self.c_south, self.c_first, self.c_inner, self.c_east, self.c_west, self.c_layer, self.weight, self.diag,
         self.target, self.now, self.later) = refs

    @staticmethod
    def scratch(count, width, blocks):
        def vectors(*lead):
            return pltpu.VMEM(lead + (SUB, LANES), jnp.float32)

        whole = vectors(LAYERS, width, blocks, count)
        edge = vectors(LAYERS, blocks, count)
        return [whole, vectors(LAYERS, width, blocks), edge, edge, edge, vectors(width, blocks, count)] + [whole] * 5

    def steps(self, ring=None):
        for b in range(self.blocks):
            for t in range(self.count):
                if ring is None or b == 0 or t < ring or t >= self.count - ring:
                    yield b, t

    def members(self):
        for layer in range(LAYERS):
            for u in range(self.width):
                yield layer, u


def row_before(values):
    edge = row_index() < 1
    rolled = [row_roll(value, 1) for value in values]
    return [jnp.where(edge, rolled[b - 1], rolled[b]) for b in range(len(values))]


def row_after(values):
    edge = row_index() >= SUB - 1
    rolled = [row_roll(value, -1) for value in values]
    return [jnp.where(edge, rolled[(b + 1) % len(values)], rolled[b]) for b in range(len(values))]


class Field:
    def __init__(self, level, source, coarse=None):
        self.source = source
        self.coarse = coarse
        self.count = level.count
        self.read = {}
        self.before, self.after = {}, {}
        for layer, u in level.members():
            lows = row_before([self.value(layer, u, b, level.count - 1) for b in range(level.blocks)])
            highs = row_after([self.value(layer, u, b, 0) for b in range(level.blocks)])
            for b in range(level.blocks):
                self.before[layer, u, b] = lows[b]
                self.after[layer, u, b] = highs[b]

    def value(self, layer, u, b, t):
        value = self.source[layer, u, b, t]
        return value if self.coarse is None else value + self.coarse[layer, 0, b, t // 2]

    def at(self, layer, u, b, t):
        if t < 0:
            return self.before[layer, u, b]
        if t >= self.count:
            return self.after[layer, u, b]
        key = layer, u, b, t
        if key not in self.read:
            self.read[key] = self.value(*key)
        return self.read[key]


def row_coeff(level, layer, u, b, t):
    return level.c_south[layer, u, b, t] if t >= 0 else level.c_first[layer, u, b]


def neighbour_sums(level, source, ring=None, coarse=None):
    field = Field(level, source, coarse)
    coeffs = {}
    for b, t in level.steps(ring):
        for member in level.members():
            for at in (t - 1, t):
                if (member, b, at) not in coeffs:
                    coeffs[member, b, at] = row_coeff(level, *member, b, at)
        layer_coeffs = [level.c_layer[u, b, t] for u in range(level.width)]
        for layer in range(LAYERS):
            here = [field.at(layer, u, b, t) for u in range(level.width)]
            east_coeff, west_coeff = level.c_east[layer, b, t], level.c_west[layer, b, t]
            if level.width == 2:
                inner = level.c_inner[layer, b, t]
                beside = [inner * here[1] + west_coeff * lane_roll(here[1], 1),
                          inner * here[0] + east_coeff * lane_roll(here[0], -1)]
            else:
                beside = [east_coeff * lane_roll(here[0], -level.span) + west_coeff * lane_roll(here[0], level.span)]
            for u in range(level.width):
                total = (coeffs[(layer, u), b, t - 1] * field.at(layer, u, b, t - 1)
                         + coeffs[(layer, u), b, t] * field.at(layer, u, b, t + 1)
                         + (beside[u] + layer_coeffs[u] * field.at(1 - layer, u, b, t)))
                yield (layer, u, b, t), here[u], total


def sweep(level, source, result, ring=None, coarse=None):
    for key, value, total in neighbour_sums(level, source, ring, coarse):
        result[key] = (1.0 - damping) * value + level.weight[key] * (level.target[key] + total)


def sweeps(level, count, ring=None, coarse=None):
    for number in range(count):
        sweep(level, level.now, level.later, None if ring is None else ring + count - 1 - number,
              coarse if number == 0 else None)
        level.now, level.later = level.later, level.now


def first_sweep(level):
    for b, t in level.steps():
        for layer, u in level.members():
            key = layer, u, b, t
            level.now[key] = level.weight[key] * level.target[key]


def pair_sum(value, span):
    lower = lane_index() % (2 * span) < span
    return value + jnp.where(lower, lane_roll(value, -span), lane_roll(value, span))


def low_group(value, span):
    return jnp.where(lane_index() % (2 * span) < span, value, lane_roll(value, span))


def high_group(value, span):
    return jnp.where(lane_index() % (2 * span) < span, lane_roll(value, -span), value)


def column_sum(values, level):
    return values[0] + values[1] if level.width == 2 else pair_sum(values[0], level.span)


def restrict_residual(fine, coarse):
    residuals = {}
    for key, value, total in neighbour_sums(fine, fine.now):
        layer, u, b, t = key
        residuals[key] = fine.target[key] + total - fine.diag[key] * value
        if t % 2 == 1 and u == fine.width - 1:
            rows = [residuals[layer, v, b, t - 1] + residuals[layer, v, b, t] for v in range(fine.width)]
            coarse.target[layer, 0, b, t // 2] = column_sum(rows, fine)


def vcycle(levels, from_zero, ring=None):
    finest, middle, bottom = levels
    if from_zero:
        first_sweep(finest)
    sweeps(finest, SMOOTH - int(from_zero))
    restrict_residual(finest, middle)
    first_sweep(middle)
    sweeps(middle, SMOOTH - 1)
    restrict_residual(middle, bottom)
    first_sweep(bottom)
    sweeps(bottom, COARSE - 1)
    sweeps(middle, SMOOTH, None, bottom.now)
    sweeps(finest, SMOOTH, ring, middle.now)


def harmonic(left, right):
    return 2.0 * left * right / jnp.maximum(left + right, 1e-20)


def finest_coeffs(level, perm, joined):
    last = level.count - 1
    for layer, u in level.members():
        heads = [perm[layer, u, b, 0] for b in range(level.blocks)]
        rolled = [row_roll(value, -1) for value in heads]
        edge = row_index() >= SUB - 1
        for b in range(level.blocks):
            after = jnp.where(edge, joined[b] * rolled[(b + 1) % level.blocks], rolled[b])
            for t in range(level.count):
                beyond = perm[layer, u, b, t + 1] if t < last else after
                level.c_south[layer, u, b, t] = harmonic(perm[layer, u, b, t], beyond)
        firsts = row_before([level.c_south[layer, u, b, last] for b in range(level.blocks)])
        for b in range(level.blocks):
            level.c_first[layer, u, b] = firsts[b]
    for b, t in level.steps():
        for u in range(level.width):
            level.c_layer[u, b, t] = vertical * harmonic(perm[0, u, b, t], perm[1, u, b, t])
        for layer in range(LAYERS):
            even, odd = perm[layer, 0, b, t], perm[layer, 1, b, t]
            level.c_inner[layer, b, t] = harmonic(even, odd)
            east = harmonic(odd, lane_roll(even, -1))
            level.c_east[layer, b, t] = east
            level.c_west[layer, b, t] = lane_roll(east, 1)


def with_weight(level, acc):
    for b, t in level.steps():
        for layer, u in level.members():
            key = layer, u, b, t
            if level.width == 2:
                beside = level.c_inner[layer, b, t] + (level.c_west, level.c_east)[u][layer, b, t]
            else:
                beside = level.c_west[layer, b, t] + level.c_east[layer, b, t]
            diag = (row_coeff(level, layer, u, b, t - 1) + row_coeff(level, layer, u, b, t)
                    + (beside + level.c_layer[u, b, t]) + acc[key])
            level.diag[key] = diag
            level.weight[key] = damping / jnp.maximum(diag, 1e-20)


def coarse_coeffs(fine, coarse, fine_acc, coarse_acc):
    width = range(fine.width)
    for b in range(coarse.blocks):
        for layer in range(LAYERS):
            coarse.c_first[layer, 0, b] = column_sum([fine.c_first[layer, u, b] for u in width], fine)
    for b, t in coarse.steps():
        one, two = 2 * t, 2 * t + 1
        coarse.c_layer[0, b, t] = column_sum([fine.c_layer[u, b, one] + fine.c_layer[u, b, two] for u in width], fine)
        for layer in range(LAYERS):
            coarse.c_south[layer, 0, b, t] = column_sum([fine.c_south[layer, u, b, two] for u in width], fine)
            coarse_acc[layer, 0, b, t] = column_sum(
                [fine_acc[layer, u, b, one] + fine_acc[layer, u, b, two] for u in width], fine)
            west = fine.c_west[layer, b, one] + fine.c_west[layer, b, two]
            east = fine.c_east[layer, b, one] + fine.c_east[layer, b, two]
            if fine.width == 1:
                west, east = low_group(west, fine.span), high_group(east, fine.span)
            coarse.c_west[layer, b, t] = west
            coarse.c_east[layer, b, t] = east
    with_weight(coarse, coarse_acc)


def own_columns(even, odd):
    return jnp.where(lane_index() < HALF, even, lane_roll(odd, HALF))


def face_terms(level, pressure, adjoint, perm):
    def face(coeff, one, two):
        changes = [field.at(*one) - (field.at(*two) if isinstance(two, tuple) else two[number])
                   for number, field in enumerate((pressure, adjoint))]
        return (coeff * coeff) * (changes[0] * changes[1])

    rows = {(layer, u): face(level.c_first[layer, u, 0], (layer, u, 0, -1), (layer, u, 0, 0))
            for layer, u in level.members()}
    for t in range(level.count):
        between = [(1.0 / vertical) * face(level.c_layer[u, 0, t], (0, u, 0, t), (1, u, 0, t)) for u in range(2)]
        for layer in range(LAYERS):
            inner = face(level.c_inner[layer, 0, t], (layer, 0, 0, t), (layer, 1, 0, t))
            easts = [lane_roll(field.at(layer, 0, 0, t), -1) for field in (pressure, adjoint)]
            east = face(level.c_east[layer, 0, t], (layer, 1, 0, t), easts)
            terms = []
            for u in range(2):
                south = face(level.c_south[layer, u, 0, t], (layer, u, 0, t), (layer, u, 0, t + 1))
                beside = lane_roll(east, 1) if u == 0 else east
                total = rows[layer, u] + south + (inner + beside) + between[u]
                rows[layer, u] = south
                terms.append(-0.5 * total / perm[layer, u, 0, t])
            yield layer, t, own_columns(*terms)


def order_kernel(shuffled, ordered):
    put_in_order(shuffled[...], ordered.at[0])


def cycle_kernel(grid_shape, blocks, *refs):
    cells_hbm, rates_hbm = refs[:2]
    inputs = [refs[2 + 2 * b:4 + 2 * b] for b in range(blocks)]
    refs = refs[2 + 2 * blocks:]
    pressure_out, adjoint_out, terms_out = refs[:3]
    cells, rates, sems, perm, acc, middle_acc, bottom_acc, pressure, pressure_rows, terms_rows = refs[3:13]
    refs = refs[13:]
    copies = [pltpu.make_async_copy(cells_hbm, cells, sems.at[0]), pltpu.make_async_copy(rates_hbm, rates, sems.at[1])]
    for copy in copies:
        copy.start()
    count = inputs[0][0].shape[2] // SUB
    levels = [Level(count >> depth, width, span, blocks, refs[11 * depth:11 * depth + 11])
              for depth, (width, span) in enumerate(LEVELS)]
    finest, middle, bottom = levels

    def rows(t):
        return pl.ds(t * SUB, SUB)

    def fields(number, layer, b, t):
        low = lane_index() < HALF
        own, beside = [value[number, layer, rows(t), :] for value in inputs[b]]
        return jnp.where(low, own, beside), lane_roll(jnp.where(low, beside, own), HALF)

    gx = lax.axis_index("gx")
    if blocks == 3:
        joined = [1.0, 0.0, 1.0]
    elif blocks == 2:
        joined = [1.0 - gx.astype(jnp.float32), gx.astype(jnp.float32)]
    else:
        joined = [0.0]

    for b, t in finest.steps():
        for layer in range(LAYERS):
            perms, accs, starts = [fields(number, layer, b, t) for number in (PERM, ACC, PREV)]
            for u in range(2):
                key = layer, u, b, t
                perm[key] = perms[u]
                acc[key] = accs[u]
                finest.now[key] = starts[u]
                finest.target[key] = accs[u] * starts[u]

    for copy in copies:
        copy.wait()
    layer_count, total_rows, total_cols = grid_shape
    block_rows, block_cols = SUB * count, LANES
    for well in range(WELLS):
        cell = cells[0, well]
        layer = cell // (total_rows * total_cols)
        row = cell // total_cols % total_rows - gx * block_rows
        col = cell % total_cols - lax.axis_index("gy") * block_cols
        if blocks == 3:
            row_inside = (row >= -block_rows) & (row < 2 * block_rows)
        elif blocks == 2:
            row_inside = row >= -block_rows
        else:
            row_inside = row >= 0
        inside = row_inside & (col >= -HALF) & (col < block_cols + HALF)
        row = jnp.where(row < 0, row + blocks * block_rows, row)
        col = jnp.where(col < 0, col + 2 * block_cols, col)
        row = jnp.where(inside, row, 0)
        col = jnp.where(inside, col, 0)
        rate = jnp.where(inside, rates[0, well], 0.0)
        in_block = row % block_rows
        place = layer, col % 2, row // block_rows, in_block % count
        hit = (row_index() == in_block // count) & (lane_index() == col // 2)
        finest.target[place] = finest.target[place] + jnp.where(hit, rate, 0.0)

    finest_coeffs(finest, perm, joined)
    with_weight(finest, acc)
    coarse_coeffs(finest, middle, acc, middle_acc)
    coarse_coeffs(middle, bottom, middle_acc, bottom_acc)

    vcycle(levels, False)
    for b, t in finest.steps():
        for layer in range(LAYERS):
            observed = fields(OBS, layer, b, t)
            values = []
            for u in range(2):
                key = layer, u, b, t
                values.append(finest.now[key])
                pressure[key] = values[u]
                finest.target[key] = values[u] - observed[u]
            if b == 0:
                terms_rows[layer, rows(t), :] = own_columns(*values)
    put_in_order(terms_rows[...], pressure_rows.at[0])
    pressure_copy = pltpu.make_async_copy(pressure_rows, pressure_out, sems.at[2])
    pressure_copy.start()
    vcycle(levels, True, 1)
    for t in range(count):
        for layer in range(LAYERS):
            adjoint_out[layer, rows(t), :] = own_columns(*[finest.now[layer, u, 0, t] for u in range(2)])

    for layer, t, terms in face_terms(finest, Field(finest, pressure), Field(finest, finest.now), perm):
        terms_rows[layer, rows(t), :] = terms
    put_in_order(terms_rows[...], terms_out)
    pressure_copy.wait()


def moved(value, axis, step):
    count = lax.axis_size(axis)
    ring = axis == "gx" and count == 2
    pairs = [((i + step) % count, i) for i in range(count) if ring or 0 <= i + step < count]
    return lax.ppermute(value, axis, pairs)


def swapped(value, axis, first):
    pairs = []
    for i in range(first, lax.axis_size(axis) - 1, 2):
        pairs += [(i, i + 1), (i + 1, i)]
    return lax.ppermute(value, axis, pairs)


def summed(value, axis):
    count = lax.axis_size(axis)
    others = [lax.ppermute(value, axis, [(i, i ^ step) for i in range(count)]) for step in range(count - 1, 0, -1)]
    terms = [value] + others[::-1]
    while len(terms) > 1:
        terms = [terms[i] + terms[i + 1] for i in range(0, len(terms), 2)]
    return terms[0]


def in_hbm(value):
    return pltpu.with_memory_space_constraint(value, pltpu.HBM)


def in_vmem(value):
    return pltpu.with_memory_space_constraint(value, pltpu.VMEM)


def shards(
    perm_log,
    facies,
    facies_scale,
    accumulation,
    previous_pressure,
    observed,
    well_cells,
    well_rates,
):
    layer_count, row_count, col_count = perm_log.shape
    gx_count, gy_count = lax.axis_size("gx"), lax.axis_size("gy")
    vmem = pl.BlockSpec(memory_space=pltpu.VMEM)
    hbm = pl.BlockSpec(memory_space=pltpu.HBM)
    f32 = jnp.float32
    fields = (perm_log, facies, accumulation, previous_pressure, observed)
    block = (layer_count, row_count, col_count)
    own, message_a, message_b = pl.pallas_call(
        pack_kernel,
        out_shape=[
            pltpu.VMEM((4,) + block, f32),
            pltpu.VMEM((3,) + block[1:], f32),
            pltpu.VMEM((3,) + block[1:], f32),
        ],
        in_specs=[hbm] * 6,
        out_specs=[vmem] * 3,
        scratch_shapes=[pltpu.SMEM(facies_scale.shape, f32)]
        + [pltpu.VMEM(value.shape, value.dtype) for value in fields] + [pltpu.SemaphoreType.DMA((6,))],
        name="pack",
    )(in_hbm(facies_scale), *[in_hbm(value) for value in fields])

    steps = (0, 1) if gx_count == 2 else (0, 1, -1) if gx_count > 2 else (0,)
    blocks = len(steps)
    owns = [own] + [moved(own, "gx", step) for step in steps[1:]]
    beside = pl.pallas_call(
        merge_kernel,
        out_shape=pltpu.VMEM((4, layer_count, row_count, col_count), f32),
        in_specs=[vmem] * 2,
        out_specs=vmem,
        name="merge",
    )(in_vmem(swapped(message_a, "gy", 0)), in_vmem(swapped(message_b, "gy", 1)))
    besides = [beside] + [moved(beside, "gx", step) for step in steps[1:]]
    operands = [in_vmem(value) for pair in zip(owns, besides) for value in pair]

    count = row_count // SUB
    scratch = [pltpu.SMEM(well_cells.shape, jnp.int32), pltpu.SMEM(well_rates.shape, f32), pltpu.SemaphoreType.DMA((3,))]
    whole = [pltpu.VMEM((LAYERS, width, blocks, count >> depth, SUB, LANES), f32) for depth, (width, _) in enumerate(LEVELS)]
    scratch += [whole[0], whole[0], whole[1], whole[2], whole[0]]
    scratch += [pltpu.VMEM((1,) + block, f32), pltpu.VMEM(block, f32)]
    for depth, (width, _) in enumerate(LEVELS):
        scratch += Level.scratch(count >> depth, width, blocks)
    state = jax.ShapeDtypeStruct((1, layer_count, row_count, col_count), f32)
    grid_shape = (layer_count, row_count * gx_count, col_count * gy_count)
    pressure, shuffled, terms = pl.pallas_call(
        partial(cycle_kernel, grid_shape, blocks),
        out_shape=[state, pltpu.VMEM(block, f32), pltpu.VMEM(block, f32)],
        in_specs=[hbm] * 2 + [vmem] * (2 * blocks),
        out_specs=[hbm, vmem, vmem],
        scratch_shapes=scratch,
        compiler_params=pltpu.CompilerParams(vmem_limit_bytes=24 * 1024 * 1024),
        name="cycles",
    )(in_hbm(well_cells), in_hbm(well_rates), *operands)
    gradient = summed(terms, "scen")
    adjoint = pl.pallas_call(
        order_kernel,
        out_shape=state,
        in_specs=[vmem],
        out_specs=vmem,
        cost_estimate=pl.CostEstimate(flops=2 * row_count * LANES**2 * 8, bytes_accessed=2**18, transcendentals=0),
        name="order",
    )(in_vmem(shuffled))
    return pressure, adjoint, gradient


def solution(mesh):
    return jax.shard_map(
        shards,
        mesh=mesh,
        in_specs=(
            P(None, "gx", "gy"),
            P(None, "gx", "gy"),
            P(),
            P(None, "gx", "gy"),
            P("scen", None, "gx", "gy"),
            P("scen", None, "gx", "gy"),
            P("scen", None),
            P("scen", None),
        ),
        out_specs=(P("scen", None, "gx", "gy"), P("scen", None, "gx", "gy"), P(None, "gx", "gy")),
        check_vma=False,
    )
```

```python
from functools import partial

import jax
import jax.numpy as jnp
from jax import lax
from jax.experimental import pallas as pl
from jax.experimental.pallas import tpu as pltpu
from jax.sharding import PartitionSpec as P

WELLS = 5
FACIES = 4
LAYERS = 2
SMOOTH = 2
COARSE = 4

vertical = 0.3
damping = 0.8

LANES = 128
HALF = 64
SUB = 8
PERM, ACC, PREV, OBS = range(4)
NEAR = 26
ROOM = HALF // 2 - NEAR
LEVELS = ((2, 1), (1, 1), (1, 2))


def lane_index():
    return lax.broadcasted_iota(jnp.int32, (SUB, LANES), 1)


def row_index():
    return lax.broadcasted_iota(jnp.int32, (SUB, LANES), 0)


def lane_roll(value, shift):
    return pltpu.roll(value, shift % LANES, value.ndim - 1)


def row_roll(value, shift):
    return pltpu.roll(value, shift % SUB, 0)


def shuffle(value, inverse):
    rows = lax.broadcasted_iota(jnp.int32, (LANES, LANES), 0)
    cols = lax.broadcasted_iota(jnp.int32, (LANES, LANES), 1)
    natural, place = (cols, rows) if inverse else (rows, cols)
    matrix = (natural == 2 * (place % HALF) + place // HALF).astype(jnp.bfloat16)
    rest = value.reshape(-1, LANES)
    total = None
    for _ in range(3):
        part = rest.astype(jnp.bfloat16)
        rest = rest - part.astype(jnp.float32)
        moved_part = jnp.dot(part, matrix, preferred_element_type=jnp.float32)
        total = moved_part if total is None else total + moved_part
    return total.reshape(value.shape)


def place_in_half(shape):
    return lax.broadcasted_iota(jnp.int32, shape, len(shape) - 1) % HALF


def spare_lanes(number, place):
    shift = NEAR - number * ROOM
    low, high = number * ROOM, HALF - (number + 1) * ROOM
    return (((place >= NEAR) & (place < HALF // 2), (place >= low) & (place < low + ROOM), shift),
            ((place >= HALF // 2) & (place < HALF - NEAR), (place >= high) & (place < high + ROOM), -shift))


def interleaved(rows):
    count = rows.shape[0] // SUB
    return jnp.concatenate([rows[pl.ds(t, SUB, stride=count), :] for t in range(count)], axis=0)


def put_in_order(shuffled, ordered):
    count = ordered.shape[-2] // SUB
    natural = shuffle(shuffled, True)
    for layer in range(LAYERS):
        for t in range(count):
            ordered[layer, pl.ds(t, SUB, stride=count), :] = natural[layer, t * SUB:(t + 1) * SUB]


def pack_kernel(scale_hbm, perm_log_hbm, facies_hbm, acc_hbm, prev_hbm, obs_hbm, own, message_a, message_b,
                scale, perm_log, facies, acc, prev, obs, sems):
    pairs = ((scale_hbm, scale), (perm_log_hbm, perm_log), (facies_hbm, facies), (acc_hbm, acc), (prev_hbm, prev),
             (obs_hbm, obs))
    copies = [pltpu.make_async_copy(source, target, sems.at[i]) for i, (source, target) in enumerate(pairs)]
    for copy in copies:
        copy.start()
    for copy in copies:
        copy.wait()

    def layers(ref):
        return jnp.stack([interleaved(ref.at[layer]) for layer in range(LAYERS)])

    label = layers(facies)
    factor = jnp.zeros(label.shape, jnp.float32)
    for number in range(FACIES):
        factor = factor + jnp.where(label == number, scale[number], jnp.float32(0.0))
    fields = [shuffle(value, False) for value in (jnp.exp(layers(perm_log)) * factor, layers(acc), layers(prev.at[0]), layers(obs.at[0]))]
    for number in range(4):
        own[number] = fields[number]
    place = place_in_half(label.shape)
    full = []
    for number in range(3):
        value = fields[number]
        for lanes, _, shift in spare_lanes(number, place):
            value = jnp.where(lanes, lane_roll(fields[OBS], shift), value)
        full.append(value)
    low = place_in_half(label.shape[1:]) < HALF // 2
    left_first = low == (lax.axis_index("gy") % 2 == 1)
    couples = [(full[0][layer], full[1][layer]) for layer in range(LAYERS)] + [(full[2][0], full[2][1])]
    for plane, (one, two) in enumerate(couples):
        first, second = lane_roll(one, HALF), lane_roll(two, HALF + HALF // 2)
        message_a[plane] = jnp.where(left_first, first, second)
        message_b[plane] = jnp.where(left_first, second, first)


def merge_kernel(message_a, message_b, beside):
    place = place_in_half(beside.shape[2:])
    from_a = (place < HALF // 2) != (lax.axis_index("gy") % 2 == 1)
    full = [[], [], []]
    for plane in range(3):
        a, b = message_a[plane], message_b[plane]
        one = jnp.where(from_a, a, b)
        two = lane_roll(jnp.where(from_a, b, a), -(HALF // 2))
        for number, value in zip((0, 1) if plane < 2 else (2, 2), (one, two)):
            full[number].append(value)
    near = (place < NEAR) | (place >= HALF - NEAR)
    for layer in range(LAYERS):
        observed = jnp.zeros(place.shape, jnp.float32)
        for number in range(3):
            value = full[number][layer]
            beside[number, layer] = jnp.where(near, value, 0.0)
            for _, lanes, shift in spare_lanes(number, place):
                observed = jnp.where(lanes, lane_roll(value, -shift), observed)
        beside[OBS, layer] = observed


class State:
    def __init__(self, ref, level):
        self.ref = ref
        self.level = level

    def place(self, key):
        layer, u, b, t = key
        count = self.level.count
        return layer, u, pl.ds(SUB + b * SUB * count + t, SUB, stride=count)

    def __getitem__(self, key):
        layer, u, rows = self.place(key)
        return self.ref[layer, u, rows, :]

    def __setitem__(self, key, value):
        layer, u, rows = self.place(key)
        self.ref[layer, u, rows, :] = value

    def wrap(self):
        rows = SUB * self.level.count * self.level.blocks
        for layer, u in self.level.members():
            self.ref[layer, u, SUB - 1:SUB, :] = self.ref[layer, u, SUB + rows - 1:SUB + rows, :]
            self.ref[layer, u, SUB + rows:SUB + rows + 1, :] = self.ref[layer, u, SUB:SUB + 1, :]

    @staticmethod
    def scratch(count, width, blocks):
        return pltpu.VMEM((LAYERS, width, SUB * (count * blocks + 2), LANES), jnp.float32)


class Level:
    def __init__(self, count, width, span, blocks, refs):
        self.count = count
        self.width = width
        self.span = span
        self.blocks = blocks
        (self.c_south, self.c_first, self.c_inner, self.c_east, self.c_west, self.c_layer, self.weight, self.diag,
         self.target, now, later) = refs
        self.now, self.later = State(now, self), State(later, self)

    @staticmethod
    def scratch(count, width, blocks):
        def vectors(*lead):
            return pltpu.VMEM(lead + (SUB, LANES), jnp.float32)

        whole = vectors(LAYERS, width, blocks, count)
        edge = vectors(LAYERS, blocks, count)
        return [whole, vectors(LAYERS, width, blocks), edge, edge, edge, vectors(width, blocks, count)] + [whole] * 3 + [
            State.scratch(count, width, blocks)] * 2

    def steps(self, ring=None):
        for b in range(self.blocks):
            for t in range(self.count):
                if ring is None or b == 0 or t < ring or t >= self.count - ring:
                    yield b, t

    def members(self):
        for layer in range(LAYERS):
            for u in range(self.width):
                yield layer, u


def row_before(values):
    edge = row_index() < 1
    rolled = [row_roll(value, 1) for value in values]
    return [jnp.where(edge, rolled[b - 1], rolled[b]) for b in range(len(values))]


class Field:
    def __init__(self, source, coarse=None):
        self.source = source
        self.coarse = coarse
        self.read = {}

    def at(self, layer, u, b, t):
        key = layer, u, b, t
        if key not in self.read:
            value = self.source[key]
            self.read[key] = value if self.coarse is None else value + self.coarse[layer, 0, b, t // 2]
        return self.read[key]


def row_coeff(level, layer, u, b, t):
    return level.c_south[layer, u, b, t] if t >= 0 else level.c_first[layer, u, b]


def neighbour_sums(level, source, ring=None, coarse=None):
    field = Field(source, coarse)
    coeffs = {}
    for b, t in level.steps(ring):
        for member in level.members():
            for at in (t - 1, t):
                if (member, b, at) not in coeffs:
                    coeffs[member, b, at] = row_coeff(level, *member, b, at)
        layer_coeffs = [level.c_layer[u, b, t] for u in range(level.width)]
        for layer in range(LAYERS):
            here = [field.at(layer, u, b, t) for u in range(level.width)]
            east_coeff, west_coeff = level.c_east[layer, b, t], level.c_west[layer, b, t]
            if level.width == 2:
                inner = level.c_inner[layer, b, t]
                beside = [inner * here[1] + west_coeff * lane_roll(here[1], 1),
                          inner * here[0] + east_coeff * lane_roll(here[0], -1)]
            else:
                beside = [east_coeff * lane_roll(here[0], -level.span) + west_coeff * lane_roll(here[0], level.span)]
            for u in range(level.width):
                total = (coeffs[(layer, u), b, t - 1] * field.at(layer, u, b, t - 1)
                         + coeffs[(layer, u), b, t] * field.at(layer, u, b, t + 1)
                         + (beside[u] + layer_coeffs[u] * field.at(1 - layer, u, b, t)))
                yield (layer, u, b, t), here[u], total


def sweep(level, source, result, ring=None, coarse=None):
    for key, value, total in neighbour_sums(level, source, ring, coarse):
        result[key] = (1.0 - damping) * value + level.weight[key] * (level.target[key] + total)
    result.wrap()


def sweeps(level, count, ring=None, coarse=None):
    for number in range(count):
        sweep(level, level.now, level.later, None if ring is None else ring + count - 1 - number,
              coarse if number == 0 else None)
        level.now, level.later = level.later, level.now


def first_sweep(level):
    for b, t in level.steps():
        for layer, u in level.members():
            key = layer, u, b, t
            level.now[key] = level.weight[key] * level.target[key]
    level.now.wrap()


def pair_sum(value, span):
    lower = lane_index() % (2 * span) < span
    return value + jnp.where(lower, lane_roll(value, -span), lane_roll(value, span))


def low_group(value, span):
    return jnp.where(lane_index() % (2 * span) < span, value, lane_roll(value, span))


def high_group(value, span):
    return jnp.where(lane_index() % (2 * span) < span, lane_roll(value, -span), value)


def column_sum(values, level):
    return values[0] + values[1] if level.width == 2 else pair_sum(values[0], level.span)


def restrict_residual(fine, coarse):
    residuals = {}
    for key, value, total in neighbour_sums(fine, fine.now):
        layer, u, b, t = key
        residuals[key] = fine.target[key] + total - fine.diag[key] * value
        if t % 2 == 1 and u == fine.width - 1:
            rows = [residuals[layer, v, b, t - 1] + residuals[layer, v, b, t] for v in range(fine.width)]
            coarse.target[layer, 0, b, t // 2] = column_sum(rows, fine)


def vcycle(levels, from_zero, ring=None):
    finest, middle, bottom = levels
    if from_zero:
        first_sweep(finest)
    sweeps(finest, SMOOTH - int(from_zero))
    restrict_residual(finest, middle)
    first_sweep(middle)
    sweeps(middle, SMOOTH - 1)
    restrict_residual(middle, bottom)
    first_sweep(bottom)
    sweeps(bottom, COARSE - 1)
    sweeps(middle, SMOOTH, None, bottom.now)
    sweeps(finest, SMOOTH, ring, middle.now)


def harmonic(left, right):
    return 2.0 * left * right / jnp.maximum(left + right, 1e-20)


def finest_coeffs(level, perm, joined):
    last = level.count - 1
    for layer, u in level.members():
        heads = [perm[layer, u, b, 0] for b in range(level.blocks)]
        rolled = [row_roll(value, -1) for value in heads]
        edge = row_index() >= SUB - 1
        for b in range(level.blocks):
            after = jnp.where(edge, joined[b] * rolled[(b + 1) % level.blocks], rolled[b])
            for t in range(level.count):
                beyond = perm[layer, u, b, t + 1] if t < last else after
                level.c_south[layer, u, b, t] = harmonic(perm[layer, u, b, t], beyond)
        firsts = row_before([level.c_south[layer, u, b, last] for b in range(level.blocks)])
        for b in range(level.blocks):
            level.c_first[layer, u, b] = firsts[b]
    for b, t in level.steps():
        for u in range(level.width):
            level.c_layer[u, b, t] = vertical * harmonic(perm[0, u, b, t], perm[1, u, b, t])
        for layer in range(LAYERS):
            even, odd = perm[layer, 0, b, t], perm[layer, 1, b, t]
            level.c_inner[layer, b, t] = harmonic(even, odd)
            east = harmonic(odd, lane_roll(even, -1))
            level.c_east[layer, b, t] = east
            level.c_west[layer, b, t] = lane_roll(east, 1)


def with_weight(level, acc):
    for b, t in level.steps():
        for layer, u in level.members():
            key = layer, u, b, t
            if level.width == 2:
                beside = level.c_inner[layer, b, t] + (level.c_west, level.c_east)[u][layer, b, t]
            else:
                beside = level.c_west[layer, b, t] + level.c_east[layer, b, t]
            diag = (row_coeff(level, layer, u, b, t - 1) + row_coeff(level, layer, u, b, t)
                    + (beside + level.c_layer[u, b, t]) + acc[key])
            level.diag[key] = diag
            level.weight[key] = damping / jnp.maximum(diag, 1e-20)


def coarse_coeffs(fine, coarse, fine_acc, coarse_acc):
    width = range(fine.width)
    for b in range(coarse.blocks):
        for layer in range(LAYERS):
            coarse.c_first[layer, 0, b] = column_sum([fine.c_first[layer, u, b] for u in width], fine)
    for b, t in coarse.steps():
        one, two = 2 * t, 2 * t + 1
        coarse.c_layer[0, b, t] = column_sum([fine.c_layer[u, b, one] + fine.c_layer[u, b, two] for u in width], fine)
        for layer in range(LAYERS):
            coarse.c_south[layer, 0, b, t] = column_sum([fine.c_south[layer, u, b, two] for u in width], fine)
            coarse_acc[layer, 0, b, t] = column_sum(
                [fine_acc[layer, u, b, one] + fine_acc[layer, u, b, two] for u in width], fine)
            west = fine.c_west[layer, b, one] + fine.c_west[layer, b, two]
            east = fine.c_east[layer, b, one] + fine.c_east[layer, b, two]
            if fine.width == 1:
                west, east = low_group(west, fine.span), high_group(east, fine.span)
            coarse.c_west[layer, b, t] = west
            coarse.c_east[layer, b, t] = east
    with_weight(coarse, coarse_acc)


def own_columns(even, odd):
    return jnp.where(lane_index() < HALF, even, lane_roll(odd, HALF))


def face_terms(level, pressure, adjoint, perm):
    def face(coeff, one, two):
        changes = [field.at(*one) - (field.at(*two) if isinstance(two, tuple) else two[number])
                   for number, field in enumerate((pressure, adjoint))]
        return (coeff * coeff) * (changes[0] * changes[1])

    rows = {(layer, u): face(level.c_first[layer, u, 0], (layer, u, 0, -1), (layer, u, 0, 0))
            for layer, u in level.members()}
    for t in range(level.count):
        between = [(1.0 / vertical) * face(level.c_layer[u, 0, t], (0, u, 0, t), (1, u, 0, t)) for u in range(2)]
        for layer in range(LAYERS):
            inner = face(level.c_inner[layer, 0, t], (layer, 0, 0, t), (layer, 1, 0, t))
            easts = [lane_roll(field.at(layer, 0, 0, t), -1) for field in (pressure, adjoint)]
            east = face(level.c_east[layer, 0, t], (layer, 1, 0, t), easts)
            terms = []
            for u in range(2):
                south = face(level.c_south[layer, u, 0, t], (layer, u, 0, t), (layer, u, 0, t + 1))
                beside = lane_roll(east, 1) if u == 0 else east
                total = rows[layer, u] + south + (inner + beside) + between[u]
                rows[layer, u] = south
                terms.append(-0.5 * total / perm[layer, u, 0, t])
            yield layer, t, own_columns(*terms)


def order_kernel(shuffled, ordered):
    put_in_order(shuffled[...], ordered.at[0])


def cycle_kernel(grid_shape, blocks, *refs):
    cells_hbm, rates_hbm = refs[:2]
    inputs = [refs[2 + 2 * b:4 + 2 * b] for b in range(blocks)]
    refs = refs[2 + 2 * blocks:]
    pressure_out, adjoint_out, terms_out = refs[:3]
    cells, rates, sems, perm, acc, middle_acc, bottom_acc, pressure, pressure_rows, terms_rows = refs[3:13]
    refs = refs[13:]
    copies = [pltpu.make_async_copy(cells_hbm, cells, sems.at[0]), pltpu.make_async_copy(rates_hbm, rates, sems.at[1])]
    for copy in copies:
        copy.start()
    count = inputs[0][0].shape[2] // SUB
    levels = [Level(count >> depth, width, span, blocks, refs[11 * depth:11 * depth + 11])
              for depth, (width, span) in enumerate(LEVELS)]
    finest, middle, bottom = levels
    pressure = State(pressure, finest)

    def rows(t):
        return pl.ds(t * SUB, SUB)

    def fields(number, layer, b, t):
        low = lane_index() < HALF
        own, beside = [value[number, layer, rows(t), :] for value in inputs[b]]
        return jnp.where(low, own, beside), lane_roll(jnp.where(low, beside, own), HALF)

    gx = lax.axis_index("gx")
    if blocks == 3:
        joined = [1.0, 0.0, 1.0]
    elif blocks == 2:
        joined = [1.0 - gx.astype(jnp.float32), gx.astype(jnp.float32)]
    else:
        joined = [0.0]

    for b, t in finest.steps():
        for layer in range(LAYERS):
            perms, accs, starts = [fields(number, layer, b, t) for number in (PERM, ACC, PREV)]
            for u in range(2):
                key = layer, u, b, t
                perm[key] = perms[u]
                acc[key] = accs[u]
                finest.now[key] = starts[u]
                finest.target[key] = accs[u] * starts[u]
    finest.now.wrap()

    for copy in copies:
        copy.wait()
    layer_count, total_rows, total_cols = grid_shape
    block_rows, block_cols = SUB * count, LANES
    for well in range(WELLS):
        cell = cells[0, well]
        layer = cell // (total_rows * total_cols)
        row = cell // total_cols % total_rows - gx * block_rows
        col = cell % total_cols - lax.axis_index("gy") * block_cols
        if blocks == 3:
            row_inside = (row >= -block_rows) & (row < 2 * block_rows)
        elif blocks == 2:
            row_inside = row >= -block_rows
        else:
            row_inside = row >= 0
        inside = row_inside & (col >= -HALF) & (col < block_cols + HALF)
        row = jnp.where(row < 0, row + blocks * block_rows, row)
        col = jnp.where(col < 0, col + 2 * block_cols, col)
        row = jnp.where(inside, row, 0)
        col = jnp.where(inside, col, 0)
        rate = jnp.where(inside, rates[0, well], 0.0)
        in_block = row % block_rows
        place = layer, col % 2, row // block_rows, in_block % count
        hit = (row_index() == in_block // count) & (lane_index() == col // 2)
        finest.target[place] = finest.target[place] + jnp.where(hit, rate, 0.0)

    finest_coeffs(finest, perm, joined)
    with_weight(finest, acc)
    coarse_coeffs(finest, middle, acc, middle_acc)
    coarse_coeffs(middle, bottom, middle_acc, bottom_acc)

    vcycle(levels, False)
    for b, t in finest.steps():
        for layer in range(LAYERS):
            observed = fields(OBS, layer, b, t)
            values = []
            for u in range(2):
                key = layer, u, b, t
                values.append(finest.now[key])
                pressure[key] = values[u]
                finest.target[key] = values[u] - observed[u]
            if b == 0:
                terms_rows[layer, rows(t), :] = own_columns(*values)
    pressure.wrap()
    put_in_order(terms_rows[...], pressure_rows.at[0])
    pressure_copy = pltpu.make_async_copy(pressure_rows, pressure_out, sems.at[2])
    pressure_copy.start()
    vcycle(levels, True, 1)
    for t in range(count):
        for layer in range(LAYERS):
            adjoint_out[layer, rows(t), :] = own_columns(*[finest.now[layer, u, 0, t] for u in range(2)])

    for layer, t, terms in face_terms(finest, Field(pressure), Field(finest.now), perm):
        terms_rows[layer, rows(t), :] = terms
    put_in_order(terms_rows[...], terms_out)
    pressure_copy.wait()


def moved(value, axis, step):
    count = lax.axis_size(axis)
    ring = axis == "gx" and count == 2
    pairs = [((i + step) % count, i) for i in range(count) if ring or 0 <= i + step < count]
    return lax.ppermute(value, axis, pairs)


def swapped(value, axis, first):
    pairs = []
    for i in range(first, lax.axis_size(axis) - 1, 2):
        pairs += [(i, i + 1), (i + 1, i)]
    return lax.ppermute(value, axis, pairs)


def summed(value, axis):
    count = lax.axis_size(axis)
    others = [lax.ppermute(value, axis, [(i, i ^ step) for i in range(count)]) for step in range(count - 1, 0, -1)]
    terms = [value] + others[::-1]
    while len(terms) > 1:
        terms = [terms[i] + terms[i + 1] for i in range(0, len(terms), 2)]
    return terms[0]


def in_hbm(value):
    return pltpu.with_memory_space_constraint(value, pltpu.HBM)


def in_vmem(value):
    return pltpu.with_memory_space_constraint(value, pltpu.VMEM)


def shards(
    perm_log,
    facies,
    facies_scale,
    accumulation,
    previous_pressure,
    observed,
    well_cells,
    well_rates,
):
    layer_count, row_count, col_count = perm_log.shape
    gx_count, gy_count = lax.axis_size("gx"), lax.axis_size("gy")
    vmem = pl.BlockSpec(memory_space=pltpu.VMEM)
    hbm = pl.BlockSpec(memory_space=pltpu.HBM)
    f32 = jnp.float32
    fields = (perm_log, facies, accumulation, previous_pressure, observed)
    block = (layer_count, row_count, col_count)
    own, message_a, message_b = pl.pallas_call(
        pack_kernel,
        out_shape=[
            pltpu.VMEM((4,) + block, f32),
            pltpu.VMEM((3,) + block[1:], f32),
            pltpu.VMEM((3,) + block[1:], f32),
        ],
        in_specs=[hbm] * 6,
        out_specs=[vmem] * 3,
        scratch_shapes=[pltpu.SMEM(facies_scale.shape, f32)]
        + [pltpu.VMEM(value.shape, value.dtype) for value in fields] + [pltpu.SemaphoreType.DMA((6,))],
        name="pack",
    )(in_hbm(facies_scale), *[in_hbm(value) for value in fields])

    steps = (0, 1) if gx_count == 2 else (0, 1, -1) if gx_count > 2 else (0,)
    blocks = len(steps)
    owns = [own] + [moved(own, "gx", step) for step in steps[1:]]
    beside = pl.pallas_call(
        merge_kernel,
        out_shape=pltpu.VMEM((4, layer_count, row_count, col_count), f32),
        in_specs=[vmem] * 2,
        out_specs=vmem,
        name="merge",
    )(in_vmem(swapped(message_a, "gy", 0)), in_vmem(swapped(message_b, "gy", 1)))
    besides = [beside] + [moved(beside, "gx", step) for step in steps[1:]]
    operands = [in_vmem(value) for pair in zip(owns, besides) for value in pair]

    count = row_count // SUB
    scratch = [pltpu.SMEM(well_cells.shape, jnp.int32), pltpu.SMEM(well_rates.shape, f32), pltpu.SemaphoreType.DMA((3,))]
    whole = [pltpu.VMEM((LAYERS, width, blocks, count >> depth, SUB, LANES), f32) for depth, (width, _) in enumerate(LEVELS)]
    scratch += [whole[0], whole[0], whole[1], whole[2], State.scratch(count, LEVELS[0][0], blocks)]
    scratch += [pltpu.VMEM((1,) + block, f32), pltpu.VMEM(block, f32)]
    for depth, (width, _) in enumerate(LEVELS):
        scratch += Level.scratch(count >> depth, width, blocks)
    state = jax.ShapeDtypeStruct((1, layer_count, row_count, col_count), f32)
    grid_shape = (layer_count, row_count * gx_count, col_count * gy_count)
    pressure, shuffled, terms = pl.pallas_call(
        partial(cycle_kernel, grid_shape, blocks),
        out_shape=[state, pltpu.VMEM(block, f32), pltpu.VMEM(block, f32)],
        in_specs=[hbm] * 2 + [vmem] * (2 * blocks),
        out_specs=[hbm, vmem, vmem],
        scratch_shapes=scratch,
        compiler_params=pltpu.CompilerParams(vmem_limit_bytes=24 * 1024 * 1024),
        name="cycles",
    )(in_hbm(well_cells), in_hbm(well_rates), *operands)
    gradient = summed(terms, "scen")
    adjoint = pl.pallas_call(
        order_kernel,
        out_shape=state,
        in_specs=[vmem],
        out_specs=vmem,
        cost_estimate=pl.CostEstimate(flops=2 * row_count * LANES**2 * 8, bytes_accessed=2**18, transcendentals=0),
        name="order",
    )(in_vmem(shuffled))
    return pressure, adjoint, gradient


def solution(mesh):
    return jax.shard_map(
        shards,
        mesh=mesh,
        in_specs=(
            P(None, "gx", "gy"),
            P(None, "gx", "gy"),
            P(),
            P(None, "gx", "gy"),
            P("scen", None, "gx", "gy"),
            P("scen", None, "gx", "gy"),
            P("scen", None),
            P("scen", None),
        ),
        out_specs=(P("scen", None, "gx", "gy"), P("scen", None, "gx", "gy"), P(None, "gx", "gy")),
        check_vma=False,
    )
```

```python
from functools import partial

import jax
import jax.numpy as jnp
from jax import lax
from jax.experimental import pallas as pl
from jax.experimental.pallas import tpu as pltpu
from jax.sharding import PartitionSpec as P

WELLS = 5
FACIES = 4
LAYERS = 2
SMOOTH = 2
COARSE = 4

vertical = 0.3
damping = 0.8

LANES = 128
HALF = 64
SUB = 8
PERM, ACC, PREV, OBS = range(4)
NEAR = 26
ROOM = HALF // 2 - NEAR
LEVELS = ((2, 1), (1, 1), (1, 2))


def lane_index():
    return lax.broadcasted_iota(jnp.int32, (SUB, LANES), 1)


def row_index():
    return lax.broadcasted_iota(jnp.int32, (SUB, LANES), 0)


def lane_roll(value, shift):
    return pltpu.roll(value, shift % LANES, value.ndim - 1)


def row_roll(value, shift):
    return pltpu.roll(value, shift % SUB, 0)


def shuffle(value, inverse):
    rows = lax.broadcasted_iota(jnp.int32, (LANES, LANES), 0)
    cols = lax.broadcasted_iota(jnp.int32, (LANES, LANES), 1)
    natural, place = (cols, rows) if inverse else (rows, cols)
    matrix = (natural == 2 * (place % HALF) + place // HALF).astype(jnp.bfloat16)
    rest = value.reshape(-1, LANES)
    total = None
    for _ in range(3):
        part = rest.astype(jnp.bfloat16)
        rest = rest - part.astype(jnp.float32)
        moved_part = jnp.dot(part, matrix, preferred_element_type=jnp.float32)
        total = moved_part if total is None else total + moved_part
    return total.reshape(value.shape)


def place_in_half(shape):
    return lax.broadcasted_iota(jnp.int32, shape, len(shape) - 1) % HALF


def spare_lanes(number, place):
    shift = NEAR - number * ROOM
    low, high = number * ROOM, HALF - (number + 1) * ROOM
    return (((place >= NEAR) & (place < HALF // 2), (place >= low) & (place < low + ROOM), shift),
            ((place >= HALF // 2) & (place < HALF - NEAR), (place >= high) & (place < high + ROOM), -shift))


def interleaved(rows):
    count = rows.shape[0] // SUB
    return jnp.concatenate([rows[pl.ds(t, SUB, stride=count), :] for t in range(count)], axis=0)


def put_in_order(shuffled, ordered):
    count = ordered.shape[-2] // SUB
    natural = shuffle(shuffled, True)
    for layer in range(LAYERS):
        for t in range(count):
            ordered[layer, pl.ds(t, SUB, stride=count), :] = natural[layer, t * SUB:(t + 1) * SUB]


def pack_kernel(scale_hbm, perm_log_hbm, facies_hbm, acc_hbm, prev_hbm, obs_hbm, own, message_a, message_b,
                scale, perm_log, facies, acc, prev, obs, sems):
    pairs = ((scale_hbm, scale), (perm_log_hbm, perm_log), (facies_hbm, facies), (acc_hbm, acc), (prev_hbm, prev),
             (obs_hbm, obs))
    copies = [pltpu.make_async_copy(source, target, sems.at[i]) for i, (source, target) in enumerate(pairs)]
    for copy in copies:
        copy.start()
    for copy in copies:
        copy.wait()

    def layers(ref):
        return jnp.stack([interleaved(ref.at[layer]) for layer in range(LAYERS)])

    label = layers(facies)
    factor = jnp.zeros(label.shape, jnp.float32)
    for number in range(FACIES):
        factor = factor + jnp.where(label == number, scale[number], jnp.float32(0.0))
    fields = [shuffle(value, False) for value in (jnp.exp(layers(perm_log)) * factor, layers(acc), layers(prev.at[0]), layers(obs.at[0]))]
    for number in range(4):
        own[number] = fields[number]
    place = place_in_half(label.shape)
    full = []
    for number in range(3):
        value = fields[number]
        for lanes, _, shift in spare_lanes(number, place):
            value = jnp.where(lanes, lane_roll(fields[OBS], shift), value)
        full.append(value)
    low = place_in_half(label.shape[1:]) < HALF // 2
    left_first = low == (lax.axis_index("gy") % 2 == 1)
    couples = [(full[0][layer], full[1][layer]) for layer in range(LAYERS)] + [(full[2][0], full[2][1])]
    for plane, (one, two) in enumerate(couples):
        first, second = lane_roll(one, HALF), lane_roll(two, HALF + HALF // 2)
        message_a[plane] = jnp.where(left_first, first, second)
        message_b[plane] = jnp.where(left_first, second, first)


def merge_kernel(message_a, message_b, beside):
    place = place_in_half(beside.shape[2:])
    from_a = (place < HALF // 2) != (lax.axis_index("gy") % 2 == 1)
    full = [[], [], []]
    for plane in range(3):
        a, b = message_a[plane], message_b[plane]
        one = jnp.where(from_a, a, b)
        two = lane_roll(jnp.where(from_a, b, a), -(HALF // 2))
        for number, value in zip((0, 1) if plane < 2 else (2, 2), (one, two)):
            full[number].append(value)
    near = (place < NEAR) | (place >= HALF - NEAR)
    for layer in range(LAYERS):
        observed = jnp.zeros(place.shape, jnp.float32)
        for number in range(3):
            value = full[number][layer]
            beside[number, layer] = jnp.where(near, value, 0.0)
            for _, lanes, shift in spare_lanes(number, place):
                observed = jnp.where(lanes, lane_roll(value, -shift), observed)
        beside[OBS, layer] = observed


class Level:
    def __init__(self, count, width, span, blocks, refs):
        self.count = count
        self.width = width
        self.span = span
        self.blocks = blocks
        (self.c_south, self.c_first, self.c_inner, self.c_east, self.c_west, self.c_layer, self.weight, self.diag,
         self.target, self.now, self.later) = refs

    @staticmethod
    def scratch(count, width, blocks):
        def vectors(*lead):
            return pltpu.VMEM(lead + (SUB, LANES), jnp.float32)

        whole = vectors(LAYERS, width, blocks, count)
        edge = vectors(LAYERS, blocks, count)
        return [whole, vectors(LAYERS, width, blocks), edge, edge, edge, vectors(width, blocks, count)] + [whole] * 5

    def steps(self):
        for b in range(self.blocks):
            for t in range(self.count):
                yield b, t

    def members(self):
        for layer in range(LAYERS):
            for u in range(self.width):
                yield layer, u


def row_before(values):
    edge = row_index() < 1
    rolled = [row_roll(value, 1) for value in values]
    return [jnp.where(edge, rolled[b - 1], rolled[b]) for b in range(len(values))]


def row_after(values):
    edge = row_index() >= SUB - 1
    rolled = [row_roll(value, -1) for value in values]
    return [jnp.where(edge, rolled[(b + 1) % len(values)], rolled[b]) for b in range(len(values))]


class Field:
    def __init__(self, level, source, coarse=None):
        self.source = source
        self.coarse = coarse
        self.count = level.count
        self.read = {}
        self.before, self.after = {}, {}
        for layer, u in level.members():
            lows = row_before([self.value(layer, u, b, level.count - 1) for b in range(level.blocks)])
            highs = row_after([self.value(layer, u, b, 0) for b in range(level.blocks)])
            for b in range(level.blocks):
                self.before[layer, u, b] = lows[b]
                self.after[layer, u, b] = highs[b]

    def value(self, layer, u, b, t):
        value = self.source[layer, u, b, t]
        return value if self.coarse is None else value + self.coarse[layer, 0, b, t // 2]

    def at(self, layer, u, b, t):
        if t < 0:
            return self.before[layer, u, b]
        if t >= self.count:
            return self.after[layer, u, b]
        key = layer, u, b, t
        if key not in self.read:
            self.read[key] = self.value(*key)
        return self.read[key]


def row_coeff(level, layer, u, b, t):
    return level.c_south[layer, u, b, t] if t >= 0 else level.c_first[layer, u, b]


def neighbour_sums(level, source, coarse=None):
    field = Field(level, source, coarse)
    coeffs = {}
    for b, t in level.steps():
        for member in level.members():
            for at in (t - 1, t):
                if (member, b, at) not in coeffs:
                    coeffs[member, b, at] = row_coeff(level, *member, b, at)
        layer_coeffs = [level.c_layer[u, b, t] for u in range(level.width)]
        for layer in range(LAYERS):
            here = [field.at(layer, u, b, t) for u in range(level.width)]
            east_coeff, west_coeff = level.c_east[layer, b, t], level.c_west[layer, b, t]
            if level.width == 2:
                inner = level.c_inner[layer, b, t]
                beside = [inner * here[1] + west_coeff * lane_roll(here[1], 1),
                          inner * here[0] + east_coeff * lane_roll(here[0], -1)]
            else:
                beside = [east_coeff * lane_roll(here[0], -level.span) + west_coeff * lane_roll(here[0], level.span)]
            for u in range(level.width):
                total = (coeffs[(layer, u), b, t - 1] * field.at(layer, u, b, t - 1)
                         + coeffs[(layer, u), b, t] * field.at(layer, u, b, t + 1)
                         + (beside[u] + layer_coeffs[u] * field.at(1 - layer, u, b, t)))
                yield (layer, u, b, t), here[u], total


def sweep(level, source, result, coarse=None):
    for key, value, total in neighbour_sums(level, source, coarse):
        result[key] = (1.0 - damping) * value + level.weight[key] * (level.target[key] + total)


def sweeps(level, count, coarse=None):
    for number in range(count):
        sweep(level, level.now, level.later, coarse if number == 0 else None)
        level.now, level.later = level.later, level.now


def first_sweep(level):
    for b, t in level.steps():
        for layer, u in level.members():
            key = layer, u, b, t
            level.now[key] = level.weight[key] * level.target[key]


def pair_sum(value, span):
    lower = lane_index() % (2 * span) < span
    return value + jnp.where(lower, lane_roll(value, -span), lane_roll(value, span))


def low_group(value, span):
    return jnp.where(lane_index() % (2 * span) < span, value, lane_roll(value, span))


def high_group(value, span):
    return jnp.where(lane_index() % (2 * span) < span, lane_roll(value, -span), value)


def column_sum(values, level):
    return values[0] + values[1] if level.width == 2 else pair_sum(values[0], level.span)


def restrict_residual(fine, coarse):
    residuals = {}
    for key, value, total in neighbour_sums(fine, fine.now):
        layer, u, b, t = key
        residuals[key] = fine.target[key] + total - fine.diag[key] * value
        if t % 2 == 1 and u == fine.width - 1:
            rows = [residuals[layer, v, b, t - 1] + residuals[layer, v, b, t] for v in range(fine.width)]
            coarse.target[layer, 0, b, t // 2] = column_sum(rows, fine)


def vcycle(levels):
    finest, middle, bottom = levels
    sweeps(finest, SMOOTH - 1)
    restrict_residual(finest, middle)
    first_sweep(middle)
    sweeps(middle, SMOOTH - 1)
    restrict_residual(middle, bottom)
    first_sweep(bottom)
    sweeps(bottom, COARSE - 1)
    sweeps(middle, SMOOTH, bottom.now)
    sweeps(finest, SMOOTH, middle.now)


def harmonic(left, right):
    return 2.0 * left * right / jnp.maximum(left + right, 1e-20)


def finest_coeffs(level, perm, joined):
    last = level.count - 1
    for layer, u in level.members():
        heads = [perm[layer, u, b, 0] for b in range(level.blocks)]
        rolled = [row_roll(value, -1) for value in heads]
        edge = row_index() >= SUB - 1
        for b in range(level.blocks):
            after = jnp.where(edge, joined[b] * rolled[(b + 1) % level.blocks], rolled[b])
            for t in range(level.count):
                beyond = perm[layer, u, b, t + 1] if t < last else after
                level.c_south[layer, u, b, t] = harmonic(perm[layer, u, b, t], beyond)
        firsts = row_before([level.c_south[layer, u, b, last] for b in range(level.blocks)])
        for b in range(level.blocks):
            level.c_first[layer, u, b] = firsts[b]
    for b, t in level.steps():
        for u in range(level.width):
            level.c_layer[u, b, t] = vertical * harmonic(perm[0, u, b, t], perm[1, u, b, t])
        for layer in range(LAYERS):
            even, odd = perm[layer, 0, b, t], perm[layer, 1, b, t]
            level.c_inner[layer, b, t] = harmonic(even, odd)
            east = harmonic(odd, lane_roll(even, -1))
            level.c_east[layer, b, t] = east
            level.c_west[layer, b, t] = lane_roll(east, 1)


def with_weight(level, acc):
    for b, t in level.steps():
        for layer, u in level.members():
            key = layer, u, b, t
            if level.width == 2:
                beside = level.c_inner[layer, b, t] + (level.c_west, level.c_east)[u][layer, b, t]
            else:
                beside = level.c_west[layer, b, t] + level.c_east[layer, b, t]
            diag = (row_coeff(level, layer, u, b, t - 1) + row_coeff(level, layer, u, b, t)
                    + (beside + level.c_layer[u, b, t]) + acc[key])
            level.diag[key] = diag
            level.weight[key] = damping / jnp.maximum(diag, 1e-20)


def coarse_coeffs(fine, coarse, fine_acc, coarse_acc):
    width = range(fine.width)
    for b in range(coarse.blocks):
        for layer in range(LAYERS):
            coarse.c_first[layer, 0, b] = column_sum([fine.c_first[layer, u, b] for u in width], fine)
    for b, t in coarse.steps():
        one, two = 2 * t, 2 * t + 1
        coarse.c_layer[0, b, t] = column_sum([fine.c_layer[u, b, one] + fine.c_layer[u, b, two] for u in width], fine)
        for layer in range(LAYERS):
            coarse.c_south[layer, 0, b, t] = column_sum([fine.c_south[layer, u, b, two] for u in width], fine)
            coarse_acc[layer, 0, b, t] = column_sum(
                [fine_acc[layer, u, b, one] + fine_acc[layer, u, b, two] for u in width], fine)
            west = fine.c_west[layer, b, one] + fine.c_west[layer, b, two]
            east = fine.c_east[layer, b, one] + fine.c_east[layer, b, two]
            if fine.width == 1:
                west, east = low_group(west, fine.span), high_group(east, fine.span)
            coarse.c_west[layer, b, t] = west
            coarse.c_east[layer, b, t] = east
    with_weight(coarse, coarse_acc)


def own_columns(even, odd):
    return jnp.where(lane_index() < HALF, even, lane_roll(odd, HALF))


def face_terms(level, pressure, adjoint, perm):
    def face(coeff, one, two):
        changes = [field.at(*one) - (field.at(*two) if isinstance(two, tuple) else two[number])
                   for number, field in enumerate((pressure, adjoint))]
        return (coeff * coeff) * (changes[0] * changes[1])

    rows = {(layer, u): face(level.c_first[layer, u, 0], (layer, u, 0, -1), (layer, u, 0, 0))
            for layer, u in level.members()}
    for t in range(level.count):
        between = [(1.0 / vertical) * face(level.c_layer[u, 0, t], (0, u, 0, t), (1, u, 0, t)) for u in range(2)]
        for layer in range(LAYERS):
            inner = face(level.c_inner[layer, 0, t], (layer, 0, 0, t), (layer, 1, 0, t))
            easts = [lane_roll(field.at(layer, 0, 0, t), -1) for field in (pressure, adjoint)]
            east = face(level.c_east[layer, 0, t], (layer, 1, 0, t), easts)
            terms = []
            for u in range(2):
                south = face(level.c_south[layer, u, 0, t], (layer, u, 0, t), (layer, u, 0, t + 1))
                beside = lane_roll(east, 1) if u == 0 else east
                total = rows[layer, u] + south + (inner + beside) + between[u]
                rows[layer, u] = south
                terms.append(-0.5 * total / perm[layer, u, 0, t])
            yield layer, t, own_columns(*terms)


def order_kernel(*refs):
    for shuffled, ordered in zip(refs[:2], refs[2:]):
        put_in_order(shuffled[...], ordered.at[0])


def cycle_kernel(grid_shape, blocks, *refs):
    cells_hbm, rates_hbm = refs[:2]
    inputs = [refs[2 + 2 * b:4 + 2 * b] for b in range(blocks)]
    refs = refs[2 + 2 * blocks:]
    pressure_out, adjoint_out, terms_out = refs[:3]
    cells, rates, sems, perm, acc, middle_acc, bottom_acc, states, terms_rows = refs[3:12]
    refs = refs[12:]
    copies = [pltpu.make_async_copy(cells_hbm, cells, sems.at[0]), pltpu.make_async_copy(rates_hbm, rates, sems.at[1])]
    for copy in copies:
        copy.start()
    count = inputs[0][0].shape[2] // SUB
    levels = [Level(count >> depth, width, span, blocks, refs[11 * depth:11 * depth + 11])
              for depth, (width, span) in enumerate(LEVELS)]
    finest, middle, bottom = levels

    def rows(t):
        return pl.ds(t * SUB, SUB)

    def fields(number, layer, b, t):
        low = lane_index() < HALF
        own, beside = [value[number, layer, rows(t), :] for value in inputs[b]]
        return jnp.where(low, own, beside), lane_roll(jnp.where(low, beside, own), HALF)

    gx = lax.axis_index("gx")
    if blocks == 3:
        joined = [1.0, 0.0, 1.0]
    elif blocks == 2:
        joined = [1.0 - gx.astype(jnp.float32), gx.astype(jnp.float32)]
    else:
        joined = [0.0]

    for b, t in finest.steps():
        for layer in range(LAYERS):
            perms, accs, starts = [fields(number, layer, b, t) for number in (PERM, ACC, PREV)]
            for u in range(2):
                key = layer, u, b, t
                perm[key] = perms[u]
                acc[key] = accs[u]
                finest.now[key] = starts[u]
                finest.target[key] = accs[u] * starts[u]

    for copy in copies:
        copy.wait()
    layer_count, total_rows, total_cols = grid_shape
    block_rows, block_cols = SUB * count, LANES
    for well in range(WELLS):
        cell = cells[0, well]
        layer = cell // (total_rows * total_cols)
        row = cell // total_cols % total_rows - gx * block_rows
        col = cell % total_cols - lax.axis_index("gy") * block_cols
        if blocks == 3:
            row_inside = (row >= -block_rows) & (row < 2 * block_rows)
        elif blocks == 2:
            row_inside = row >= -block_rows
        else:
            row_inside = row >= 0
        inside = row_inside & (col >= -HALF) & (col < block_cols + HALF)
        row = jnp.where(row < 0, row + blocks * block_rows, row)
        col = jnp.where(col < 0, col + 2 * block_cols, col)
        row = jnp.where(inside, row, 0)
        col = jnp.where(inside, col, 0)
        rate = jnp.where(inside, rates[0, well], 0.0)
        in_block = row % block_rows
        place = layer, col % 2, row // block_rows, in_block % count
        hit = (row_index() == in_block // count) & (lane_index() == col // 2)
        finest.target[place] = finest.target[place] + jnp.where(hit, rate, 0.0)

    finest_coeffs(finest, perm, joined)
    with_weight(finest, acc)
    coarse_coeffs(finest, middle, acc, middle_acc)
    coarse_coeffs(middle, bottom, middle_acc, bottom_acc)

    sweeps(finest, 1)
    start, other = finest.now, finest.later

    def turn(number, carry):
        finest.now, finest.later = start, other
        vcycle(levels)
        for b, t in finest.steps():
            for layer in range(LAYERS):
                observed = fields(OBS, layer, b, t)
                for u in range(2):
                    key = layer, u, b, t
                    value = finest.now[key]
                    states[(number,) + key] = value
                    target = value - observed[u]
                    finest.target[key] = target
                    start[key] = finest.weight[key] * target
        return carry

    lax.fori_loop(0, 2, turn, 0)
    pressure, adjoint = states.at[0], states.at[1]
    for t in range(count):
        for layer in range(LAYERS):
            for state, result in ((pressure, pressure_out), (adjoint, adjoint_out)):
                result[layer, rows(t), :] = own_columns(*[state[layer, u, 0, t] for u in range(2)])

    for layer, t, terms in face_terms(finest, Field(finest, pressure), Field(finest, adjoint), perm):
        terms_rows[layer, rows(t), :] = terms
    put_in_order(terms_rows[...], terms_out)


def moved(value, axis, step):
    count = lax.axis_size(axis)
    ring = axis == "gx" and count == 2
    pairs = [((i + step) % count, i) for i in range(count) if ring or 0 <= i + step < count]
    return lax.ppermute(value, axis, pairs)


def swapped(value, axis, first):
    pairs = []
    for i in range(first, lax.axis_size(axis) - 1, 2):
        pairs += [(i, i + 1), (i + 1, i)]
    return lax.ppermute(value, axis, pairs)


def summed(value, axis):
    count = lax.axis_size(axis)
    others = [lax.ppermute(value, axis, [(i, i ^ step) for i in range(count)]) for step in range(count - 1, 0, -1)]
    terms = [value] + others[::-1]
    while len(terms) > 1:
        terms = [terms[i] + terms[i + 1] for i in range(0, len(terms), 2)]
    return terms[0]


def in_hbm(value):
    return pltpu.with_memory_space_constraint(value, pltpu.HBM)


def in_vmem(value):
    return pltpu.with_memory_space_constraint(value, pltpu.VMEM)


def shards(
    perm_log,
    facies,
    facies_scale,
    accumulation,
    previous_pressure,
    observed,
    well_cells,
    well_rates,
):
    layer_count, row_count, col_count = perm_log.shape
    gx_count, gy_count = lax.axis_size("gx"), lax.axis_size("gy")
    vmem = pl.BlockSpec(memory_space=pltpu.VMEM)
    hbm = pl.BlockSpec(memory_space=pltpu.HBM)
    f32 = jnp.float32
    fields = (perm_log, facies, accumulation, previous_pressure, observed)
    block = (layer_count, row_count, col_count)
    own, message_a, message_b = pl.pallas_call(
        pack_kernel,
        out_shape=[
            pltpu.VMEM((4,) + block, f32),
            pltpu.VMEM((3,) + block[1:], f32),
            pltpu.VMEM((3,) + block[1:], f32),
        ],
        in_specs=[hbm] * 6,
        out_specs=[vmem] * 3,
        scratch_shapes=[pltpu.SMEM(facies_scale.shape, f32)]
        + [pltpu.VMEM(value.shape, value.dtype) for value in fields] + [pltpu.SemaphoreType.DMA((6,))],
        name="pack",
    )(in_hbm(facies_scale), *[in_hbm(value) for value in fields])

    steps = (0, 1) if gx_count == 2 else (0, 1, -1) if gx_count > 2 else (0,)
    blocks = len(steps)
    owns = [own] + [moved(own, "gx", step) for step in steps[1:]]
    beside = pl.pallas_call(
        merge_kernel,
        out_shape=pltpu.VMEM((4, layer_count, row_count, col_count), f32),
        in_specs=[vmem] * 2,
        out_specs=vmem,
        name="merge",
    )(in_vmem(swapped(message_a, "gy", 0)), in_vmem(swapped(message_b, "gy", 1)))
    besides = [beside] + [moved(beside, "gx", step) for step in steps[1:]]
    operands = [in_vmem(value) for pair in zip(owns, besides) for value in pair]

    count = row_count // SUB
    scratch = [pltpu.SMEM(well_cells.shape, jnp.int32), pltpu.SMEM(well_rates.shape, f32), pltpu.SemaphoreType.DMA((2,))]
    whole = [pltpu.VMEM((LAYERS, width, blocks, count >> depth, SUB, LANES), f32) for depth, (width, _) in enumerate(LEVELS)]
    scratch += [whole[0], whole[0], whole[1], whole[2]]
    scratch += [pltpu.VMEM((2, LAYERS, 2, blocks, count, SUB, LANES), f32), pltpu.VMEM(block, f32)]
    for depth, (width, _) in enumerate(LEVELS):
        scratch += Level.scratch(count >> depth, width, blocks)
    state = jax.ShapeDtypeStruct((1, layer_count, row_count, col_count), f32)
    grid_shape = (layer_count, row_count * gx_count, col_count * gy_count)
    *shuffled, terms = pl.pallas_call(
        partial(cycle_kernel, grid_shape, blocks),
        out_shape=[pltpu.VMEM(block, f32)] * 3,
        in_specs=[hbm] * 2 + [vmem] * (2 * blocks),
        out_specs=[vmem] * 3,
        scratch_shapes=scratch,
        compiler_params=pltpu.CompilerParams(vmem_limit_bytes=24 * 1024 * 1024),
        name="cycles",
    )(in_hbm(well_cells), in_hbm(well_rates), *operands)
    gradient = summed(terms, "scen")
    pressure, adjoint = pl.pallas_call(
        order_kernel,
        out_shape=[state] * 2,
        in_specs=[vmem] * 2,
        out_specs=[vmem] * 2,
        cost_estimate=pl.CostEstimate(flops=2 * row_count * LANES**2 * 16, bytes_accessed=2**19, transcendentals=0),
        name="order",
    )(*[in_vmem(value) for value in shuffled])
    return pressure, adjoint, gradient


def solution(mesh):
    return jax.shard_map(
        shards,
        mesh=mesh,
        in_specs=(
            P(None, "gx", "gy"),
            P(None, "gx", "gy"),
            P(),
            P(None, "gx", "gy"),
            P("scen", None, "gx", "gy"),
            P("scen", None, "gx", "gy"),
            P("scen", None),
            P("scen", None),
        ),
        out_specs=(P("scen", None, "gx", "gy"), P("scen", None, "gx", "gy"), P(None, "gx", "gy")),
        check_vma=False,
    )
```

```python
from functools import partial

import jax
import jax.numpy as jnp
from jax import lax
from jax.experimental import pallas as pl
from jax.experimental.pallas import tpu as pltpu
from jax.sharding import PartitionSpec as P

WELLS = 5
FACIES = 4
LAYERS = 2
SMOOTH = 2
COARSE = 4

vertical = 0.3
damping = 0.8

LANES = 128
HALF = 64
SUB = 8
PERM, ACC, PREV, OBS = range(4)
NEAR = 26
ROOM = HALF // 2 - NEAR
LEVELS = ((2, 1), (1, 1), (1, 2))


def lane_index():
    return lax.broadcasted_iota(jnp.int32, (SUB, LANES), 1)


def row_index():
    return lax.broadcasted_iota(jnp.int32, (SUB, LANES), 0)


def lane_roll(value, shift):
    return pltpu.roll(value, shift % LANES, value.ndim - 1)


def row_roll(value, shift):
    return pltpu.roll(value, shift % SUB, 0)


def shuffle(value, inverse):
    rows = lax.broadcasted_iota(jnp.int32, (LANES, LANES), 0)
    cols = lax.broadcasted_iota(jnp.int32, (LANES, LANES), 1)
    natural, place = (cols, rows) if inverse else (rows, cols)
    matrix = (natural == 2 * (place % HALF) + place // HALF).astype(jnp.bfloat16)
    rest = value.reshape(-1, LANES)
    total = None
    for _ in range(3):
        part = rest.astype(jnp.bfloat16)
        rest = rest - part.astype(jnp.float32)
        moved_part = jnp.dot(part, matrix, preferred_element_type=jnp.float32)
        total = moved_part if total is None else total + moved_part
    return total.reshape(value.shape)


def place_in_half(shape):
    return lax.broadcasted_iota(jnp.int32, shape, len(shape) - 1) % HALF


def spare_lanes(number, place):
    shift = NEAR - number * ROOM
    low, high = number * ROOM, HALF - (number + 1) * ROOM
    return (((place >= NEAR) & (place < HALF // 2), (place >= low) & (place < low + ROOM), shift),
            ((place >= HALF // 2) & (place < HALF - NEAR), (place >= high) & (place < high + ROOM), -shift))


def interleaved(rows):
    count = rows.shape[0] // SUB
    return jnp.concatenate([rows[pl.ds(t, SUB, stride=count), :] for t in range(count)], axis=0)


def put_in_order(shuffled, ordered):
    count = ordered.shape[-2] // SUB
    natural = shuffle(shuffled, True)
    for layer in range(LAYERS):
        for t in range(count):
            ordered[layer, pl.ds(t, SUB, stride=count), :] = natural[layer, t * SUB:(t + 1) * SUB]


def pack_kernel(scale_hbm, perm_log_hbm, facies_hbm, acc_hbm, prev_hbm, obs_hbm, own, message_a, message_b,
                scale, perm_log, facies, acc, prev, obs, sems):
    pairs = ((scale_hbm, scale), (perm_log_hbm, perm_log), (facies_hbm, facies), (acc_hbm, acc), (prev_hbm, prev),
             (obs_hbm, obs))
    copies = [pltpu.make_async_copy(source, target, sems.at[i]) for i, (source, target) in enumerate(pairs)]
    for copy in copies:
        copy.start()
    for copy in copies:
        copy.wait()

    def layers(ref):
        return jnp.stack([interleaved(ref.at[layer]) for layer in range(LAYERS)])

    label = layers(facies)
    factor = jnp.zeros(label.shape, jnp.float32)
    for number in range(FACIES):
        factor = factor + jnp.where(label == number, scale[number], jnp.float32(0.0))
    fields = [shuffle(value, False) for value in (jnp.exp(layers(perm_log)) * factor, layers(acc), layers(prev.at[0]), layers(obs.at[0]))]
    for number in range(4):
        own[number] = fields[number]
    place = place_in_half(label.shape)
    full = []
    for number in range(3):
        value = fields[number]
        for lanes, _, shift in spare_lanes(number, place):
            value = jnp.where(lanes, lane_roll(fields[OBS], shift), value)
        full.append(value)
    low = place_in_half(label.shape[1:]) < HALF // 2
    left_first = low == (lax.axis_index("gy") % 2 == 1)
    couples = [(full[0][layer], full[1][layer]) for layer in range(LAYERS)] + [(full[2][0], full[2][1])]
    for plane, (one, two) in enumerate(couples):
        first, second = lane_roll(one, HALF), lane_roll(two, HALF + HALF // 2)
        message_a[plane] = jnp.where(left_first, first, second)
        message_b[plane] = jnp.where(left_first, second, first)


def merge_kernel(message_a, message_b, beside):
    place = place_in_half(beside.shape[2:])
    from_a = (place < HALF // 2) != (lax.axis_index("gy") % 2 == 1)
    full = [[], [], []]
    for plane in range(3):
        a, b = message_a[plane], message_b[plane]
        one = jnp.where(from_a, a, b)
        two = lane_roll(jnp.where(from_a, b, a), -(HALF // 2))
        for number, value in zip((0, 1) if plane < 2 else (2, 2), (one, two)):
            full[number].append(value)
    near = (place < NEAR) | (place >= HALF - NEAR)
    for layer in range(LAYERS):
        observed = jnp.zeros(place.shape, jnp.float32)
        for number in range(3):
            value = full[number][layer]
            beside[number, layer] = jnp.where(near, value, 0.0)
            for _, lanes, shift in spare_lanes(number, place):
                observed = jnp.where(lanes, lane_roll(value, -shift), observed)
        beside[OBS, layer] = observed


class Level:
    def __init__(self, count, width, span, blocks, refs):
        self.count = count
        self.width = width
        self.span = span
        self.blocks = blocks
        (self.c_south, self.c_first, self.c_inner, self.c_east, self.c_west, self.c_layer, self.weight, self.diag,
         self.target, self.now, self.later) = refs

    @staticmethod
    def scratch(count, width, blocks):
        def vectors(*lead):
            return pltpu.VMEM(lead + (SUB, LANES), jnp.float32)

        whole = vectors(LAYERS, width, blocks, count)
        edge = vectors(LAYERS, blocks, count)
        return [whole, vectors(LAYERS, width, blocks), edge, edge, edge, vectors(width, blocks, count)] + [whole] * 5

    def steps(self):
        for b in range(self.blocks):
            for t in range(self.count):
                yield b, t

    def members(self):
        for layer in range(LAYERS):
            for u in range(self.width):
                yield layer, u


def row_before(values):
    edge = row_index() < 1
    rolled = [row_roll(value, 1) for value in values]
    return [jnp.where(edge, rolled[b - 1], rolled[b]) for b in range(len(values))]


def row_after(values):
    edge = row_index() >= SUB - 1
    rolled = [row_roll(value, -1) for value in values]
    return [jnp.where(edge, rolled[(b + 1) % len(values)], rolled[b]) for b in range(len(values))]


class Field:
    def __init__(self, level, source, coarse=None):
        self.source = source
        self.coarse = coarse
        self.count = level.count
        self.read = {}
        self.before, self.after = {}, {}
        for layer, u in level.members():
            lows = row_before([self.value(layer, u, b, level.count - 1) for b in range(level.blocks)])
            highs = row_after([self.value(layer, u, b, 0) for b in range(level.blocks)])
            for b in range(level.blocks):
                self.before[layer, u, b] = lows[b]
                self.after[layer, u, b] = highs[b]

    def value(self, layer, u, b, t):
        value = self.source[layer, u, b, t]
        return value if self.coarse is None else value + self.coarse[layer, 0, b, t // 2]

    def at(self, layer, u, b, t):
        if t < 0:
            return self.before[layer, u, b]
        if t >= self.count:
            return self.after[layer, u, b]
        key = layer, u, b, t
        if key not in self.read:
            self.read[key] = self.value(*key)
        return self.read[key]


def row_coeff(level, layer, u, b, t):
    return level.c_south[layer, u, b, t] if t >= 0 else level.c_first[layer, u, b]


def neighbour_sums(level, source, coarse=None):
    field = Field(level, source, coarse)
    coeffs = {}
    for b, t in level.steps():
        for member in level.members():
            for at in (t - 1, t):
                if (member, b, at) not in coeffs:
                    coeffs[member, b, at] = row_coeff(level, *member, b, at)
        layer_coeffs = [level.c_layer[u, b, t] for u in range(level.width)]
        for layer in range(LAYERS):
            here = [field.at(layer, u, b, t) for u in range(level.width)]
            east_coeff, west_coeff = level.c_east[layer, b, t], level.c_west[layer, b, t]
            if level.width == 2:
                inner = level.c_inner[layer, b, t]
                beside = [inner * here[1] + west_coeff * lane_roll(here[1], 1),
                          inner * here[0] + east_coeff * lane_roll(here[0], -1)]
            else:
                beside = [east_coeff * lane_roll(here[0], -level.span) + west_coeff * lane_roll(here[0], level.span)]
            for u in range(level.width):
                total = (coeffs[(layer, u), b, t - 1] * field.at(layer, u, b, t - 1)
                         + coeffs[(layer, u), b, t] * field.at(layer, u, b, t + 1)
                         + (beside[u] + layer_coeffs[u] * field.at(1 - layer, u, b, t)))
                yield (layer, u, b, t), here[u], total


def sweep(level, source, result, coarse=None):
    for key, value, total in neighbour_sums(level, source, coarse):
        result[key] = (1.0 - damping) * value + level.weight[key] * (level.target[key] + total)


def sweeps(level, count, coarse=None):
    for number in range(count):
        sweep(level, level.now, level.later, coarse if number == 0 else None)
        level.now, level.later = level.later, level.now


def first_sweep(level):
    for b, t in level.steps():
        for layer, u in level.members():
            key = layer, u, b, t
            level.now[key] = level.weight[key] * level.target[key]


def pair_sum(value, span):
    lower = lane_index() % (2 * span) < span
    return value + jnp.where(lower, lane_roll(value, -span), lane_roll(value, span))


def low_group(value, span):
    return jnp.where(lane_index() % (2 * span) < span, value, lane_roll(value, span))


def high_group(value, span):
    return jnp.where(lane_index() % (2 * span) < span, lane_roll(value, -span), value)


def column_sum(values, level):
    return values[0] + values[1] if level.width == 2 else pair_sum(values[0], level.span)


def restrict_residual(fine, coarse):
    residuals = {}
    for key, value, total in neighbour_sums(fine, fine.now):
        layer, u, b, t = key
        residuals[key] = fine.target[key] + total - fine.diag[key] * value
        if t % 2 == 1 and u == fine.width - 1:
            rows = [residuals[layer, v, b, t - 1] + residuals[layer, v, b, t] for v in range(fine.width)]
            coarse.target[layer, 0, b, t // 2] = column_sum(rows, fine)


def vcycle(levels):
    finest, middle, bottom = levels
    sweeps(finest, SMOOTH - 1)
    restrict_residual(finest, middle)
    first_sweep(middle)
    sweeps(middle, SMOOTH - 1)
    restrict_residual(middle, bottom)
    first_sweep(bottom)
    sweeps(bottom, COARSE - 1)
    sweeps(middle, SMOOTH, bottom.now)
    sweeps(finest, SMOOTH, middle.now)


def harmonic(left, right):
    return 2.0 * left * right / jnp.maximum(left + right, 1e-20)


def finest_coeffs(level, perm, joined):
    last = level.count - 1
    for layer, u in level.members():
        heads = [perm[layer, u, b, 0] for b in range(level.blocks)]
        rolled = [row_roll(value, -1) for value in heads]
        edge = row_index() >= SUB - 1
        for b in range(level.blocks):
            after = jnp.where(edge, joined[b] * rolled[(b + 1) % level.blocks], rolled[b])
            for t in range(level.count):
                beyond = perm[layer, u, b, t + 1] if t < last else after
                level.c_south[layer, u, b, t] = harmonic(perm[layer, u, b, t], beyond)
        firsts = row_before([level.c_south[layer, u, b, last] for b in range(level.blocks)])
        for b in range(level.blocks):
            level.c_first[layer, u, b] = firsts[b]
    for b, t in level.steps():
        for u in range(level.width):
            level.c_layer[u, b, t] = vertical * harmonic(perm[0, u, b, t], perm[1, u, b, t])
        for layer in range(LAYERS):
            even, odd = perm[layer, 0, b, t], perm[layer, 1, b, t]
            level.c_inner[layer, b, t] = harmonic(even, odd)
            east = harmonic(odd, lane_roll(even, -1))
            level.c_east[layer, b, t] = east
            level.c_west[layer, b, t] = lane_roll(east, 1)


def with_weight(level, acc):
    for b, t in level.steps():
        for layer, u in level.members():
            key = layer, u, b, t
            if level.width == 2:
                beside = level.c_inner[layer, b, t] + (level.c_west, level.c_east)[u][layer, b, t]
            else:
                beside = level.c_west[layer, b, t] + level.c_east[layer, b, t]
            diag = (row_coeff(level, layer, u, b, t - 1) + row_coeff(level, layer, u, b, t)
                    + (beside + level.c_layer[u, b, t]) + acc[key])
            level.diag[key] = diag
            level.weight[key] = damping / jnp.maximum(diag, 1e-20)


def coarse_coeffs(fine, coarse, fine_acc, coarse_acc):
    width = range(fine.width)
    for b in range(coarse.blocks):
        for layer in range(LAYERS):
            coarse.c_first[layer, 0, b] = column_sum([fine.c_first[layer, u, b] for u in width], fine)
    for b, t in coarse.steps():
        one, two = 2 * t, 2 * t + 1
        coarse.c_layer[0, b, t] = column_sum([fine.c_layer[u, b, one] + fine.c_layer[u, b, two] for u in width], fine)
        for layer in range(LAYERS):
            coarse.c_south[layer, 0, b, t] = column_sum([fine.c_south[layer, u, b, two] for u in width], fine)
            coarse_acc[layer, 0, b, t] = column_sum(
                [fine_acc[layer, u, b, one] + fine_acc[layer, u, b, two] for u in width], fine)
            west = fine.c_west[layer, b, one] + fine.c_west[layer, b, two]
            east = fine.c_east[layer, b, one] + fine.c_east[layer, b, two]
            if fine.width == 1:
                west, east = low_group(west, fine.span), high_group(east, fine.span)
            coarse.c_west[layer, b, t] = west
            coarse.c_east[layer, b, t] = east
    with_weight(coarse, coarse_acc)


def own_columns(even, odd):
    return jnp.where(lane_index() < HALF, even, lane_roll(odd, HALF))


def face_terms(level, pressure, adjoint, perm):
    def face(coeff, one, two):
        changes = [field.at(*one) - (field.at(*two) if isinstance(two, tuple) else two[number])
                   for number, field in enumerate((pressure, adjoint))]
        return (coeff * coeff) * (changes[0] * changes[1])

    rows = {(layer, u): face(level.c_first[layer, u, 0], (layer, u, 0, -1), (layer, u, 0, 0))
            for layer, u in level.members()}
    for t in range(level.count):
        between = [(1.0 / vertical) * face(level.c_layer[u, 0, t], (0, u, 0, t), (1, u, 0, t)) for u in range(2)]
        for layer in range(LAYERS):
            inner = face(level.c_inner[layer, 0, t], (layer, 0, 0, t), (layer, 1, 0, t))
            easts = [lane_roll(field.at(layer, 0, 0, t), -1) for field in (pressure, adjoint)]
            east = face(level.c_east[layer, 0, t], (layer, 1, 0, t), easts)
            terms = []
            for u in range(2):
                south = face(level.c_south[layer, u, 0, t], (layer, u, 0, t), (layer, u, 0, t + 1))
                beside = lane_roll(east, 1) if u == 0 else east
                total = rows[layer, u] + south + (inner + beside) + between[u]
                rows[layer, u] = south
                terms.append(-0.5 * total / perm[layer, u, 0, t])
            yield layer, t, own_columns(*terms)


def order_kernel(*refs):
    for shuffled, ordered in zip(refs[:2], refs[2:]):
        put_in_order(shuffled[...], ordered.at[0])


def cycle_kernel(grid_shape, blocks, *refs):
    cells_hbm, rates_hbm = refs[:2]
    inputs = [refs[2 + 2 * b:4 + 2 * b] for b in range(blocks)]
    refs = refs[2 + 2 * blocks:]
    pressure_out, adjoint_out, terms_out = refs[:3]
    cells, rates, sems, perm, acc, middle_acc, bottom_acc, states, terms_rows = refs[3:12]
    refs = refs[12:]
    copies = [pltpu.make_async_copy(cells_hbm, cells, sems.at[0]), pltpu.make_async_copy(rates_hbm, rates, sems.at[1])]
    for copy in copies:
        copy.start()
    count = inputs[0][0].shape[2] // SUB
    levels = [Level(count >> depth, width, span, blocks, refs[11 * depth:11 * depth + 11])
              for depth, (width, span) in enumerate(LEVELS)]
    finest, middle, bottom = levels

    def rows(t):
        return pl.ds(t * SUB, SUB)

    def fields(number, layer, b, t):
        low = lane_index() < HALF
        own, beside = [value[number, layer, rows(t), :] for value in inputs[b]]
        return jnp.where(low, own, beside), lane_roll(jnp.where(low, beside, own), HALF)

    gx = lax.axis_index("gx")
    if blocks == 3:
        joined = [1.0, 0.0, 1.0]
    elif blocks == 2:
        joined = [1.0 - gx.astype(jnp.float32), gx.astype(jnp.float32)]
    else:
        joined = [0.0]

    for b, t in finest.steps():
        for layer in range(LAYERS):
            perms, accs, starts = [fields(number, layer, b, t) for number in (PERM, ACC, PREV)]
            for u in range(2):
                key = layer, u, b, t
                perm[key] = perms[u]
                acc[key] = accs[u]
                finest.now[key] = starts[u]
                finest.target[key] = accs[u] * starts[u]

    for copy in copies:
        copy.wait()
    layer_count, total_rows, total_cols = grid_shape
    block_rows, block_cols = SUB * count, LANES
    for well in range(WELLS):
        cell = cells[0, well]
        layer = cell // (total_rows * total_cols)
        row = cell // total_cols % total_rows - gx * block_rows
        col = cell % total_cols - lax.axis_index("gy") * block_cols
        if blocks == 3:
            row_inside = (row >= -block_rows) & (row < 2 * block_rows)
        elif blocks == 2:
            row_inside = row >= -block_rows
        else:
            row_inside = row >= 0
        inside = row_inside & (col >= -HALF) & (col < block_cols + HALF)
        row = jnp.where(row < 0, row + blocks * block_rows, row)
        col = jnp.where(col < 0, col + 2 * block_cols, col)
        row = jnp.where(inside, row, 0)
        col = jnp.where(inside, col, 0)
        rate = jnp.where(inside, rates[0, well], 0.0)
        in_block = row % block_rows
        place = layer, col % 2, row // block_rows, in_block % count
        hit = (row_index() == in_block // count) & (lane_index() == col // 2)
        finest.target[place] = finest.target[place] + jnp.where(hit, rate, 0.0)

    finest_coeffs(finest, perm, joined)
    with_weight(finest, acc)
    coarse_coeffs(finest, middle, acc, middle_acc)
    coarse_coeffs(middle, bottom, middle_acc, bottom_acc)

    sweeps(finest, 1)
    start, other = finest.now, finest.later

    def turn(number, carry):
        finest.now, finest.later = start, other
        vcycle(levels)
        for b, t in finest.steps():
            for layer in range(LAYERS):
                observed = fields(OBS, layer, b, t)
                for u in range(2):
                    key = layer, u, b, t
                    value = finest.now[key]
                    states[(number,) + key] = value
                    target = value - observed[u]
                    finest.target[key] = target
                    start[key] = finest.weight[key] * target
        return carry

    lax.fori_loop(0, 2, turn, 0)
    pressure, adjoint = states.at[0], states.at[1]
    for t in range(count):
        for layer in range(LAYERS):
            for state, result in ((pressure, pressure_out), (adjoint, adjoint_out)):
                result[layer, rows(t), :] = own_columns(*[state[layer, u, 0, t] for u in range(2)])

    for layer, t, terms in face_terms(finest, Field(finest, pressure), Field(finest, adjoint), perm):
        terms_rows[layer, rows(t), :] = terms
    put_in_order(terms_rows[...], terms_out)


def moved(value, axis, step):
    count = lax.axis_size(axis)
    ring = axis == "gx" and count == 2
    pairs = [((i + step) % count, i) for i in range(count) if ring or 0 <= i + step < count]
    return lax.ppermute(value, axis, pairs)


def swapped(value, axis, first):
    pairs = []
    for i in range(first, lax.axis_size(axis) - 1, 2):
        pairs += [(i, i + 1), (i + 1, i)]
    return lax.ppermute(value, axis, pairs)


def summed(value, axis):
    count = lax.axis_size(axis)
    others = [lax.ppermute(value, axis, [(i, i ^ step) for i in range(count)]) for step in range(count - 1, 0, -1)]
    terms = [value] + others[::-1]
    while len(terms) > 1:
        terms = [terms[i] + terms[i + 1] for i in range(0, len(terms), 2)]
    return terms[0]


def in_hbm(value):
    return pltpu.with_memory_space_constraint(value, pltpu.HBM)


def in_vmem(value):
    return pltpu.with_memory_space_constraint(value, pltpu.VMEM)


def shards(
    perm_log,
    facies,
    facies_scale,
    accumulation,
    previous_pressure,
    observed,
    well_cells,
    well_rates,
):
    layer_count, row_count, col_count = perm_log.shape
    gx_count, gy_count = lax.axis_size("gx"), lax.axis_size("gy")
    vmem = pl.BlockSpec(memory_space=pltpu.VMEM)
    hbm = pl.BlockSpec(memory_space=pltpu.HBM)
    f32 = jnp.float32
    fields = (perm_log, facies, accumulation, previous_pressure, observed)
    block = (layer_count, row_count, col_count)
    own, message_a, message_b = pl.pallas_call(
        pack_kernel,
        out_shape=[
            pltpu.VMEM((4,) + block, f32),
            pltpu.VMEM((3,) + block[1:], f32),
            pltpu.VMEM((3,) + block[1:], f32),
        ],
        in_specs=[hbm] * 6,
        out_specs=[vmem] * 3,
        scratch_shapes=[pltpu.SMEM(facies_scale.shape, f32)]
        + [pltpu.VMEM(value.shape, value.dtype) for value in fields] + [pltpu.SemaphoreType.DMA((6,))],
        name="pack",
    )(in_hbm(facies_scale), *[in_hbm(value) for value in fields])

    steps = (0, 1) if gx_count == 2 else (0, 1, -1) if gx_count > 2 else (0,)
    blocks = len(steps)
    owns = [own] + [moved(own, "gx", step) for step in steps[1:]]
    merge = pl.pallas_call(
        merge_kernel,
        out_shape=pltpu.VMEM((4,) + block, f32),
        in_specs=[vmem] * 2,
        out_specs=vmem,
        cost_estimate=pl.CostEstimate(flops=2**20, bytes_accessed=2**19, transcendentals=0),
        name="merge",
    )
    messages = swapped(message_a, "gy", 0), swapped(message_b, "gy", 1)
    besides = [merge(*[in_vmem(value) for value in messages])]
    for step in steps[1:]:
        besides.append(merge(*[in_vmem(moved(value, "gx", step)) for value in messages]))
    operands = [in_vmem(value) for pair in zip(owns, besides) for value in pair]

    count = row_count // SUB
    scratch = [pltpu.SMEM(well_cells.shape, jnp.int32), pltpu.SMEM(well_rates.shape, f32), pltpu.SemaphoreType.DMA((2,))]
    whole = [pltpu.VMEM((LAYERS, width, blocks, count >> depth, SUB, LANES), f32) for depth, (width, _) in enumerate(LEVELS)]
    scratch += [whole[0], whole[0], whole[1], whole[2]]
    scratch += [pltpu.VMEM((2, LAYERS, 2, blocks, count, SUB, LANES), f32), pltpu.VMEM(block, f32)]
    for depth, (width, _) in enumerate(LEVELS):
        scratch += Level.scratch(count >> depth, width, blocks)
    state = jax.ShapeDtypeStruct((1, layer_count, row_count, col_count), f32)
    grid_shape = (layer_count, row_count * gx_count, col_count * gy_count)
    *shuffled, terms = pl.pallas_call(
        partial(cycle_kernel, grid_shape, blocks),
        out_shape=[pltpu.VMEM(block, f32)] * 3,
        in_specs=[hbm] * 2 + [vmem] * (2 * blocks),
        out_specs=[vmem] * 3,
        scratch_shapes=scratch,
        compiler_params=pltpu.CompilerParams(vmem_limit_bytes=24 * 1024 * 1024),
        name="cycles",
    )(in_hbm(well_cells), in_hbm(well_rates), *operands)
    gradient = summed(terms, "scen")
    pressure, adjoint = pl.pallas_call(
        order_kernel,
        out_shape=[state] * 2,
        in_specs=[vmem] * 2,
        out_specs=[vmem] * 2,
        cost_estimate=pl.CostEstimate(flops=2 * row_count * LANES**2 * 16, bytes_accessed=2**19, transcendentals=0),
        name="order",
    )(*[in_vmem(value) for value in shuffled])
    return pressure, adjoint, gradient


def solution(mesh):
    return jax.shard_map(
        shards,
        mesh=mesh,
        in_specs=(
            P(None, "gx", "gy"),
            P(None, "gx", "gy"),
            P(),
            P(None, "gx", "gy"),
            P("scen", None, "gx", "gy"),
            P("scen", None, "gx", "gy"),
            P("scen", None),
            P("scen", None),
        ),
        out_specs=(P("scen", None, "gx", "gy"), P("scen", None, "gx", "gy"), P(None, "gx", "gy")),
        check_vma=False,
    )
```

```python
from functools import partial

import jax
import jax.numpy as jnp
from jax import lax
from jax.experimental import pallas as pl
from jax.experimental.pallas import tpu as pltpu
from jax.sharding import PartitionSpec as P

WELLS = 5
FACIES = 4
LAYERS = 2
SMOOTH = 2
COARSE = 4

vertical = 0.3
damping = 0.8

LANES = 128
HALF = 64
SUB = 8
PERM, ACC, PREV, OBS = range(4)
NEAR = 26
ROOM = HALF // 2 - NEAR
LEVELS = ((2, 1), (1, 1), (1, 2))


def lane_index():
    return lax.broadcasted_iota(jnp.int32, (SUB, LANES), 1)


def row_index():
    return lax.broadcasted_iota(jnp.int32, (SUB, LANES), 0)


def lane_roll(value, shift):
    return pltpu.roll(value, shift % LANES, value.ndim - 1)


def row_roll(value, shift):
    return pltpu.roll(value, shift % SUB, 0)


def shuffle(value, inverse):
    rows = lax.broadcasted_iota(jnp.int32, (LANES, LANES), 0)
    cols = lax.broadcasted_iota(jnp.int32, (LANES, LANES), 1)
    natural, place = (cols, rows) if inverse else (rows, cols)
    matrix = (natural == 2 * (place % HALF) + place // HALF).astype(jnp.bfloat16)
    rest = value.reshape(-1, LANES)
    total = None
    for _ in range(3):
        part = rest.astype(jnp.bfloat16)
        rest = rest - part.astype(jnp.float32)
        moved_part = jnp.dot(part, matrix, preferred_element_type=jnp.float32)
        total = moved_part if total is None else total + moved_part
    return total.reshape(value.shape)


def place_in_half(shape):
    return lax.broadcasted_iota(jnp.int32, shape, len(shape) - 1) % HALF


def spare_lanes(number, place):
    shift = NEAR - number * ROOM
    low, high = number * ROOM, HALF - (number + 1) * ROOM
    return (((place >= NEAR) & (place < HALF // 2), (place >= low) & (place < low + ROOM), shift),
            ((place >= HALF // 2) & (place < HALF - NEAR), (place >= high) & (place < high + ROOM), -shift))


def interleaved(rows):
    count = rows.shape[0] // SUB
    return jnp.concatenate([rows[pl.ds(t, SUB, stride=count), :] for t in range(count)], axis=0)


def put_in_order(shuffled, ordered):
    count = ordered.shape[-2] // SUB
    natural = shuffle(shuffled, True)
    for layer in range(LAYERS):
        for t in range(count):
            ordered[layer, pl.ds(t, SUB, stride=count), :] = natural[layer, t * SUB:(t + 1) * SUB]


def pack_kernel(scale_hbm, perm_log_hbm, facies_hbm, acc_hbm, prev_hbm, obs_hbm, own_a, own_b, message_a, message_b,
                scale, perm_log, facies, acc, prev, obs, sems):
    pairs = ((scale_hbm, scale), (perm_log_hbm, perm_log), (facies_hbm, facies), (acc_hbm, acc), (prev_hbm, prev),
             (obs_hbm, obs))
    copies = [pltpu.make_async_copy(source, target, sems.at[i]) for i, (source, target) in enumerate(pairs)]
    for copy in copies:
        copy.start()
    for copy in copies:
        copy.wait()

    def layers(ref):
        return jnp.stack([interleaved(ref.at[layer]) for layer in range(LAYERS)])

    label = layers(facies)
    factor = jnp.zeros(label.shape, jnp.float32)
    for number in range(FACIES):
        factor = factor + jnp.where(label == number, scale[number], jnp.float32(0.0))
    fields = [shuffle(value, False) for value in (jnp.exp(layers(perm_log)) * factor, layers(acc), layers(prev.at[0]), layers(obs.at[0]))]
    for number in range(4):
        (own_a, own_b)[number // 2][number % 2] = fields[number]
    place = place_in_half(label.shape)
    full = []
    for number in range(3):
        value = fields[number]
        for lanes, _, shift in spare_lanes(number, place):
            value = jnp.where(lanes, lane_roll(fields[OBS], shift), value)
        full.append(value)
    low = place_in_half(label.shape[1:]) < HALF // 2
    left_first = low == (lax.axis_index("gy") % 2 == 1)
    couples = [(full[0][layer], full[1][layer]) for layer in range(LAYERS)] + [(full[2][0], full[2][1])]
    for plane, (one, two) in enumerate(couples):
        first, second = lane_roll(one, HALF), lane_roll(two, HALF + HALF // 2)
        message_a[plane] = jnp.where(left_first, first, second)
        message_b[plane] = jnp.where(left_first, second, first)


def merge_kernel(message_a, message_b, beside):
    place = place_in_half(beside.shape[2:])
    from_a = (place < HALF // 2) != (lax.axis_index("gy") % 2 == 1)
    full = [[], [], []]
    for plane in range(3):
        a, b = message_a[plane], message_b[plane]
        one = jnp.where(from_a, a, b)
        two = lane_roll(jnp.where(from_a, b, a), -(HALF // 2))
        for number, value in zip((0, 1) if plane < 2 else (2, 2), (one, two)):
            full[number].append(value)
    near = (place < NEAR) | (place >= HALF - NEAR)
    for layer in range(LAYERS):
        observed = jnp.zeros(place.shape, jnp.float32)
        for number in range(3):
            value = full[number][layer]
            beside[number, layer] = jnp.where(near, value, 0.0)
            for _, lanes, shift in spare_lanes(number, place):
                observed = jnp.where(lanes, lane_roll(value, -shift), observed)
        beside[OBS, layer] = observed


class Level:
    def __init__(self, count, width, span, blocks, refs):
        self.count = count
        self.width = width
        self.span = span
        self.blocks = blocks
        (self.c_south, self.c_first, self.c_inner, self.c_east, self.c_west, self.c_layer, self.weight, self.diag,
         self.target, self.now, self.later) = refs

    @staticmethod
    def scratch(count, width, blocks):
        def vectors(*lead):
            return pltpu.VMEM(lead + (SUB, LANES), jnp.float32)

        whole = vectors(LAYERS, width, blocks, count)
        edge = vectors(LAYERS, blocks, count)
        return [whole, vectors(LAYERS, width, blocks), edge, edge, edge, vectors(width, blocks, count)] + [whole] * 5

    def steps(self):
        for b in range(self.blocks):
            for t in range(self.count):
                yield b, t

    def members(self):
        for layer in range(LAYERS):
            for u in range(self.width):
                yield layer, u


def row_before(values):
    edge = row_index() < 1
    rolled = [row_roll(value, 1) for value in values]
    return [jnp.where(edge, rolled[b - 1], rolled[b]) for b in range(len(values))]


def row_after(values):
    edge = row_index() >= SUB - 1
    rolled = [row_roll(value, -1) for value in values]
    return [jnp.where(edge, rolled[(b + 1) % len(values)], rolled[b]) for b in range(len(values))]


class Field:
    def __init__(self, level, source, coarse=None):
        self.source = source
        self.coarse = coarse
        self.count = level.count
        self.read = {}
        self.before, self.after = {}, {}
        for layer, u in level.members():
            lows = row_before([self.value(layer, u, b, level.count - 1) for b in range(level.blocks)])
            highs = row_after([self.value(layer, u, b, 0) for b in range(level.blocks)])
            for b in range(level.blocks):
                self.before[layer, u, b] = lows[b]
                self.after[layer, u, b] = highs[b]

    def value(self, layer, u, b, t):
        value = self.source[layer, u, b, t]
        return value if self.coarse is None else value + self.coarse[layer, 0, b, t // 2]

    def at(self, layer, u, b, t):
        if t < 0:
            return self.before[layer, u, b]
        if t >= self.count:
            return self.after[layer, u, b]
        key = layer, u, b, t
        if key not in self.read:
            self.read[key] = self.value(*key)
        return self.read[key]


def row_coeff(level, layer, u, b, t):
    return level.c_south[layer, u, b, t] if t >= 0 else level.c_first[layer, u, b]


def neighbour_sums(level, source, coarse=None):
    field = Field(level, source, coarse)
    coeffs = {}
    for b, t in level.steps():
        for member in level.members():
            for at in (t - 1, t):
                if (member, b, at) not in coeffs:
                    coeffs[member, b, at] = row_coeff(level, *member, b, at)
        layer_coeffs = [level.c_layer[u, b, t] for u in range(level.width)]
        for layer in range(LAYERS):
            here = [field.at(layer, u, b, t) for u in range(level.width)]
            east_coeff, west_coeff = level.c_east[layer, b, t], level.c_west[layer, b, t]
            if level.width == 2:
                inner = level.c_inner[layer, b, t]
                beside = [inner * here[1] + west_coeff * lane_roll(here[1], 1),
                          inner * here[0] + east_coeff * lane_roll(here[0], -1)]
            else:
                beside = [east_coeff * lane_roll(here[0], -level.span) + west_coeff * lane_roll(here[0], level.span)]
            for u in range(level.width):
                total = (coeffs[(layer, u), b, t - 1] * field.at(layer, u, b, t - 1)
                         + coeffs[(layer, u), b, t] * field.at(layer, u, b, t + 1)
                         + (beside[u] + layer_coeffs[u] * field.at(1 - layer, u, b, t)))
                yield (layer, u, b, t), here[u], total


def sweep(level, source, result, coarse=None):
    for key, value, total in neighbour_sums(level, source, coarse):
        result[key] = (1.0 - damping) * value + level.weight[key] * (level.target[key] + total)


def sweeps(level, count, coarse=None):
    for number in range(count):
        sweep(level, level.now, level.later, coarse if number == 0 else None)
        level.now, level.later = level.later, level.now


def first_sweep(level):
    for b, t in level.steps():
        for layer, u in level.members():
            key = layer, u, b, t
            level.now[key] = level.weight[key] * level.target[key]


def pair_sum(value, span):
    lower = lane_index() % (2 * span) < span
    return value + jnp.where(lower, lane_roll(value, -span), lane_roll(value, span))


def low_group(value, span):
    return jnp.where(lane_index() % (2 * span) < span, value, lane_roll(value, span))


def high_group(value, span):
    return jnp.where(lane_index() % (2 * span) < span, lane_roll(value, -span), value)


def column_sum(values, level):
    return values[0] + values[1] if level.width == 2 else pair_sum(values[0], level.span)


def restrict_residual(fine, coarse):
    residuals = {}
    for key, value, total in neighbour_sums(fine, fine.now):
        layer, u, b, t = key
        residuals[key] = fine.target[key] + total - fine.diag[key] * value
        if t % 2 == 1 and u == fine.width - 1:
            rows = [residuals[layer, v, b, t - 1] + residuals[layer, v, b, t] for v in range(fine.width)]
            coarse.target[layer, 0, b, t // 2] = column_sum(rows, fine)


def vcycle(levels):
    finest, middle, bottom = levels
    sweeps(finest, SMOOTH - 1)
    restrict_residual(finest, middle)
    first_sweep(middle)
    sweeps(middle, SMOOTH - 1)
    restrict_residual(middle, bottom)
    first_sweep(bottom)
    sweeps(bottom, COARSE - 1)
    sweeps(middle, SMOOTH, bottom.now)
    sweeps(finest, SMOOTH, middle.now)


def harmonic(left, right):
    return 2.0 * left * right / jnp.maximum(left + right, 1e-20)


def finest_coeffs(level, perm, joined):
    last = level.count - 1
    for layer, u in level.members():
        heads = [perm[layer, u, b, 0] for b in range(level.blocks)]
        rolled = [row_roll(value, -1) for value in heads]
        edge = row_index() >= SUB - 1
        for b in range(level.blocks):
            after = jnp.where(edge, joined[b] * rolled[(b + 1) % level.blocks], rolled[b])
            for t in range(level.count):
                beyond = perm[layer, u, b, t + 1] if t < last else after
                level.c_south[layer, u, b, t] = harmonic(perm[layer, u, b, t], beyond)
        firsts = row_before([level.c_south[layer, u, b, last] for b in range(level.blocks)])
        for b in range(level.blocks):
            level.c_first[layer, u, b] = firsts[b]
    for b, t in level.steps():
        for u in range(level.width):
            level.c_layer[u, b, t] = vertical * harmonic(perm[0, u, b, t], perm[1, u, b, t])
        for layer in range(LAYERS):
            even, odd = perm[layer, 0, b, t], perm[layer, 1, b, t]
            level.c_inner[layer, b, t] = harmonic(even, odd)
            east = harmonic(odd, lane_roll(even, -1))
            level.c_east[layer, b, t] = east
            level.c_west[layer, b, t] = lane_roll(east, 1)


def with_weight(level, acc):
    for b, t in level.steps():
        for layer, u in level.members():
            key = layer, u, b, t
            if level.width == 2:
                beside = level.c_inner[layer, b, t] + (level.c_west, level.c_east)[u][layer, b, t]
            else:
                beside = level.c_west[layer, b, t] + level.c_east[layer, b, t]
            diag = (row_coeff(level, layer, u, b, t - 1) + row_coeff(level, layer, u, b, t)
                    + (beside + level.c_layer[u, b, t]) + acc[key])
            level.diag[key] = diag
            level.weight[key] = damping / jnp.maximum(diag, 1e-20)


def coarse_coeffs(fine, coarse, fine_acc, coarse_acc):
    width = range(fine.width)
    for b in range(coarse.blocks):
        for layer in range(LAYERS):
            coarse.c_first[layer, 0, b] = column_sum([fine.c_first[layer, u, b] for u in width], fine)
    for b, t in coarse.steps():
        one, two = 2 * t, 2 * t + 1
        coarse.c_layer[0, b, t] = column_sum([fine.c_layer[u, b, one] + fine.c_layer[u, b, two] for u in width], fine)
        for layer in range(LAYERS):
            coarse.c_south[layer, 0, b, t] = column_sum([fine.c_south[layer, u, b, two] for u in width], fine)
            coarse_acc[layer, 0, b, t] = column_sum(
                [fine_acc[layer, u, b, one] + fine_acc[layer, u, b, two] for u in width], fine)
            west = fine.c_west[layer, b, one] + fine.c_west[layer, b, two]
            east = fine.c_east[layer, b, one] + fine.c_east[layer, b, two]
            if fine.width == 1:
                west, east = low_group(west, fine.span), high_group(east, fine.span)
            coarse.c_west[layer, b, t] = west
            coarse.c_east[layer, b, t] = east
    with_weight(coarse, coarse_acc)


def own_columns(even, odd):
    return jnp.where(lane_index() < HALF, even, lane_roll(odd, HALF))


def face_terms(level, pressure, adjoint, perm):
    def face(coeff, one, two):
        changes = [field.at(*one) - (field.at(*two) if isinstance(two, tuple) else two[number])
                   for number, field in enumerate((pressure, adjoint))]
        return (coeff * coeff) * (changes[0] * changes[1])

    rows = {(layer, u): face(level.c_first[layer, u, 0], (layer, u, 0, -1), (layer, u, 0, 0))
            for layer, u in level.members()}
    for t in range(level.count):
        between = [(1.0 / vertical) * face(level.c_layer[u, 0, t], (0, u, 0, t), (1, u, 0, t)) for u in range(2)]
        for layer in range(LAYERS):
            inner = face(level.c_inner[layer, 0, t], (layer, 0, 0, t), (layer, 1, 0, t))
            easts = [lane_roll(field.at(layer, 0, 0, t), -1) for field in (pressure, adjoint)]
            east = face(level.c_east[layer, 0, t], (layer, 1, 0, t), easts)
            terms = []
            for u in range(2):
                south = face(level.c_south[layer, u, 0, t], (layer, u, 0, t), (layer, u, 0, t + 1))
                beside = lane_roll(east, 1) if u == 0 else east
                total = rows[layer, u] + south + (inner + beside) + between[u]
                rows[layer, u] = south
                terms.append(-0.5 * total / perm[layer, u, 0, t])
            yield layer, t, own_columns(*terms)


def order_kernel(*refs):
    for shuffled, ordered in zip(refs[:2], refs[2:]):
        put_in_order(shuffled[...], ordered.at[0])


def cycle_kernel(grid_shape, blocks, *refs):
    cells_hbm, rates_hbm = refs[:2]
    inputs = [refs[2 + 3 * b:5 + 3 * b] for b in range(blocks)]
    refs = refs[2 + 3 * blocks:]
    pressure_out, adjoint_out, terms_out = refs[:3]
    cells, rates, sems, perm, acc, middle_acc, bottom_acc, states, terms_rows = refs[3:12]
    refs = refs[12:]
    copies = [pltpu.make_async_copy(cells_hbm, cells, sems.at[0]), pltpu.make_async_copy(rates_hbm, rates, sems.at[1])]
    for copy in copies:
        copy.start()
    count = inputs[0][0].shape[2] // SUB
    levels = [Level(count >> depth, width, span, blocks, refs[11 * depth:11 * depth + 11])
              for depth, (width, span) in enumerate(LEVELS)]
    finest, middle, bottom = levels

    def rows(t):
        return pl.ds(t * SUB, SUB)

    def fields(number, layer, b, t):
        low = lane_index() < HALF
        own = inputs[b][number // 2][number % 2, layer, rows(t), :]
        beside = inputs[b][2][number, layer, rows(t), :]
        return jnp.where(low, own, beside), lane_roll(jnp.where(low, beside, own), HALF)

    gx = lax.axis_index("gx")
    if blocks == 3:
        joined = [1.0, 0.0, 1.0]
    elif blocks == 2:
        joined = [1.0 - gx.astype(jnp.float32), gx.astype(jnp.float32)]
    else:
        joined = [0.0]

    for b, t in finest.steps():
        for layer in range(LAYERS):
            perms, accs, starts = [fields(number, layer, b, t) for number in (PERM, ACC, PREV)]
            for u in range(2):
                key = layer, u, b, t
                perm[key] = perms[u]
                acc[key] = accs[u]
                finest.now[key] = starts[u]
                finest.target[key] = accs[u] * starts[u]

    for copy in copies:
        copy.wait()
    layer_count, total_rows, total_cols = grid_shape
    block_rows, block_cols = SUB * count, LANES
    for well in range(WELLS):
        cell = cells[0, well]
        layer = cell // (total_rows * total_cols)
        row = cell // total_cols % total_rows - gx * block_rows
        col = cell % total_cols - lax.axis_index("gy") * block_cols
        if blocks == 3:
            row_inside = (row >= -block_rows) & (row < 2 * block_rows)
        elif blocks == 2:
            row_inside = row >= -block_rows
        else:
            row_inside = row >= 0
        inside = row_inside & (col >= -HALF) & (col < block_cols + HALF)
        row = jnp.where(row < 0, row + blocks * block_rows, row)
        col = jnp.where(col < 0, col + 2 * block_cols, col)
        row = jnp.where(inside, row, 0)
        col = jnp.where(inside, col, 0)
        rate = jnp.where(inside, rates[0, well], 0.0)
        in_block = row % block_rows
        place = layer, col % 2, row // block_rows, in_block % count
        hit = (row_index() == in_block // count) & (lane_index() == col // 2)
        finest.target[place] = finest.target[place] + jnp.where(hit, rate, 0.0)

    finest_coeffs(finest, perm, joined)
    with_weight(finest, acc)
    coarse_coeffs(finest, middle, acc, middle_acc)
    coarse_coeffs(middle, bottom, middle_acc, bottom_acc)

    sweeps(finest, 1)
    start, other = finest.now, finest.later

    def turn(number, carry):
        finest.now, finest.later = start, other
        vcycle(levels)
        for b, t in finest.steps():
            for layer in range(LAYERS):
                observed = fields(OBS, layer, b, t)
                for u in range(2):
                    key = layer, u, b, t
                    value = finest.now[key]
                    states[(number,) + key] = value
                    target = value - observed[u]
                    finest.target[key] = target
                    start[key] = finest.weight[key] * target
        return carry

    lax.fori_loop(0, 2, turn, 0)
    pressure, adjoint = states.at[0], states.at[1]
    for t in range(count):
        for layer in range(LAYERS):
            for state, result in ((pressure, pressure_out), (adjoint, adjoint_out)):
                result[layer, rows(t), :] = own_columns(*[state[layer, u, 0, t] for u in range(2)])

    for layer, t, terms in face_terms(finest, Field(finest, pressure), Field(finest, adjoint), perm):
        terms_rows[layer, rows(t), :] = terms
    put_in_order(terms_rows[...], terms_out)


def moved(value, axis, step):
    count = lax.axis_size(axis)
    ring = axis == "gx" and count == 2
    pairs = [((i + step) % count, i) for i in range(count) if ring or 0 <= i + step < count]
    return lax.ppermute(value, axis, pairs)


def swapped(value, axis, first):
    pairs = []
    for i in range(first, lax.axis_size(axis) - 1, 2):
        pairs += [(i, i + 1), (i + 1, i)]
    return lax.ppermute(value, axis, pairs)


def summed(value, axis):
    count = lax.axis_size(axis)
    others = [lax.ppermute(value, axis, [(i, i ^ step) for i in range(count)]) for step in range(count - 1, 0, -1)]
    terms = [value] + others[::-1]
    while len(terms) > 1:
        terms = [terms[i] + terms[i + 1] for i in range(0, len(terms), 2)]
    return terms[0]


def in_hbm(value):
    return pltpu.with_memory_space_constraint(value, pltpu.HBM)


def in_vmem(value):
    return pltpu.with_memory_space_constraint(value, pltpu.VMEM)


def shards(
    perm_log,
    facies,
    facies_scale,
    accumulation,
    previous_pressure,
    observed,
    well_cells,
    well_rates,
):
    layer_count, row_count, col_count = perm_log.shape
    gx_count, gy_count = lax.axis_size("gx"), lax.axis_size("gy")
    vmem = pl.BlockSpec(memory_space=pltpu.VMEM)
    hbm = pl.BlockSpec(memory_space=pltpu.HBM)
    f32 = jnp.float32
    fields = (perm_log, facies, accumulation, previous_pressure, observed)
    block = (layer_count, row_count, col_count)
    own_a, own_b, message_a, message_b = pl.pallas_call(
        pack_kernel,
        out_shape=[
            pltpu.VMEM((2,) + block, f32),
            pltpu.VMEM((2,) + block, f32),
            pltpu.VMEM((3,) + block[1:], f32),
            pltpu.VMEM((3,) + block[1:], f32),
        ],
        in_specs=[hbm] * 6,
        out_specs=[vmem] * 4,
        scratch_shapes=[pltpu.SMEM(facies_scale.shape, f32)]
        + [pltpu.VMEM(value.shape, value.dtype) for value in fields] + [pltpu.SemaphoreType.DMA((6,))],
        name="pack",
    )(in_hbm(facies_scale), *[in_hbm(value) for value in fields])

    steps = (0, 1) if gx_count == 2 else (0, 1, -1) if gx_count > 2 else (0,)
    blocks = len(steps)
    owns = [(own_a, own_b)] + [(moved(own_a, "gx", step), moved(own_b, "gx", step)) for step in steps[1:]]
    merge = pl.pallas_call(
        merge_kernel,
        out_shape=pltpu.VMEM((4,) + block, f32),
        in_specs=[vmem] * 2,
        out_specs=vmem,
        cost_estimate=pl.CostEstimate(flops=2**20, bytes_accessed=2**19, transcendentals=0),
        name="merge",
    )
    messages = swapped(message_a, "gy", 0), swapped(message_b, "gy", 1)
    besides = [merge(*[in_vmem(value) for value in messages])]
    for step in steps[1:]:
        besides.append(merge(*[in_vmem(moved(value, "gx", step)) for value in messages]))
    operands = [in_vmem(value) for own, beside in zip(owns, besides) for value in (*own, beside)]

    count = row_count // SUB
    scratch = [pltpu.SMEM(well_cells.shape, jnp.int32), pltpu.SMEM(well_rates.shape, f32), pltpu.SemaphoreType.DMA((2,))]
    whole = [pltpu.VMEM((LAYERS, width, blocks, count >> depth, SUB, LANES), f32) for depth, (width, _) in enumerate(LEVELS)]
    scratch += [whole[0], whole[0], whole[1], whole[2]]
    scratch += [pltpu.VMEM((2, LAYERS, 2, blocks, count, SUB, LANES), f32), pltpu.VMEM(block, f32)]
    for depth, (width, _) in enumerate(LEVELS):
        scratch += Level.scratch(count >> depth, width, blocks)
    state = jax.ShapeDtypeStruct((1, layer_count, row_count, col_count), f32)
    grid_shape = (layer_count, row_count * gx_count, col_count * gy_count)
    *shuffled, terms = pl.pallas_call(
        partial(cycle_kernel, grid_shape, blocks),
        out_shape=[pltpu.VMEM(block, f32)] * 3,
        in_specs=[hbm] * 2 + [vmem] * (3 * blocks),
        out_specs=[vmem] * 3,
        scratch_shapes=scratch,
        compiler_params=pltpu.CompilerParams(vmem_limit_bytes=24 * 1024 * 1024),
        name="cycles",
    )(in_hbm(well_cells), in_hbm(well_rates), *operands)
    gradient = summed(terms, "scen")
    pressure, adjoint = pl.pallas_call(
        order_kernel,
        out_shape=[state] * 2,
        in_specs=[vmem] * 2,
        out_specs=[vmem] * 2,
        cost_estimate=pl.CostEstimate(flops=2 * row_count * LANES**2 * 16, bytes_accessed=2**19, transcendentals=0),
        name="order",
    )(*[in_vmem(value) for value in shuffled])
    return pressure, adjoint, gradient


def solution(mesh):
    return jax.shard_map(
        shards,
        mesh=mesh,
        in_specs=(
            P(None, "gx", "gy"),
            P(None, "gx", "gy"),
            P(),
            P(None, "gx", "gy"),
            P("scen", None, "gx", "gy"),
            P("scen", None, "gx", "gy"),
            P("scen", None),
            P("scen", None),
        ),
        out_specs=(P("scen", None, "gx", "gy"), P("scen", None, "gx", "gy"), P(None, "gx", "gy")),
        check_vma=False,
    )
```

```python
from functools import partial

import jax
import jax.numpy as jnp
from jax import lax
from jax.experimental import pallas as pl
from jax.experimental.pallas import tpu as pltpu
from jax.sharding import PartitionSpec as P

WELLS = 5
FACIES = 4
LAYERS = 2
SMOOTH = 2
COARSE = 4

vertical = 0.3
damping = 0.8

LANES = 128
HALF = 64
SUB = 8
PERM, ACC, PREV, OBS = range(4)
NEAR = 26
ROOM = HALF // 2 - NEAR
LEVELS = ((2, 1), (1, 1), (1, 2))


def lane_index():
    return lax.broadcasted_iota(jnp.int32, (SUB, LANES), 1)


def row_index():
    return lax.broadcasted_iota(jnp.int32, (SUB, LANES), 0)


def lane_roll(value, shift):
    return pltpu.roll(value, shift % LANES, value.ndim - 1)


def row_roll(value, shift):
    return pltpu.roll(value, shift % SUB, 0)


def shuffle(value, inverse):
    rows = lax.broadcasted_iota(jnp.int32, (LANES, LANES), 0)
    cols = lax.broadcasted_iota(jnp.int32, (LANES, LANES), 1)
    natural, place = (cols, rows) if inverse else (rows, cols)
    matrix = (natural == 2 * (place % HALF) + place // HALF).astype(jnp.bfloat16)
    rest = value.reshape(-1, LANES)
    total = None
    for _ in range(3):
        part = rest.astype(jnp.bfloat16)
        rest = rest - part.astype(jnp.float32)
        moved_part = jnp.dot(part, matrix, preferred_element_type=jnp.float32)
        total = moved_part if total is None else total + moved_part
    return total.reshape(value.shape)


def place_in_half(shape):
    return lax.broadcasted_iota(jnp.int32, shape, len(shape) - 1) % HALF


def spare_lanes(number, place):
    shift = NEAR - number * ROOM
    low, high = number * ROOM, HALF - (number + 1) * ROOM
    return (((place >= NEAR) & (place < HALF // 2), (place >= low) & (place < low + ROOM), shift),
            ((place >= HALF // 2) & (place < HALF - NEAR), (place >= high) & (place < high + ROOM), -shift))


def interleaved(rows):
    count = rows.shape[0] // SUB
    return jnp.concatenate([rows[pl.ds(t, SUB, stride=count), :] for t in range(count)], axis=0)


def put_in_order(shuffled, ordered):
    count = ordered.shape[-2] // SUB
    natural = shuffle(shuffled, True)
    for layer in range(LAYERS):
        for t in range(count):
            ordered[layer, pl.ds(t, SUB, stride=count), :] = natural[layer, t * SUB:(t + 1) * SUB]


def pack_kernel(scale_hbm, perm_log_hbm, facies_hbm, acc_hbm, prev_hbm, obs_hbm, own_a, own_b, message_a, message_b,
                scale, perm_log, facies, acc, prev, obs, sems):
    pairs = ((scale_hbm, scale), (perm_log_hbm, perm_log), (facies_hbm, facies), (acc_hbm, acc), (prev_hbm, prev),
             (obs_hbm, obs))
    copies = [pltpu.make_async_copy(source, target, sems.at[i]) for i, (source, target) in enumerate(pairs)]
    for copy in copies:
        copy.start()
    for copy in copies:
        copy.wait()

    def layers(ref):
        return jnp.stack([interleaved(ref.at[layer]) for layer in range(LAYERS)])

    label = layers(facies)
    factor = jnp.zeros(label.shape, jnp.float32)
    for number in range(FACIES):
        factor = factor + jnp.where(label == number, scale[number], jnp.float32(0.0))
    fields = [shuffle(value, False) for value in (jnp.exp(layers(perm_log)) * factor, layers(acc), layers(prev.at[0]), layers(obs.at[0]))]
    for number in range(4):
        (own_a, own_b)[number // 2][number % 2] = fields[number]
    place = place_in_half(label.shape)
    full = []
    for number in range(3):
        value = fields[number]
        for lanes, _, shift in spare_lanes(number, place):
            value = jnp.where(lanes, lane_roll(fields[OBS], shift), value)
        full.append(value)
    low = place_in_half(label.shape[1:]) < HALF // 2
    left_first = low == (lax.axis_index("gy") % 2 == 0)
    couples = [(full[0][layer], full[1][layer]) for layer in range(LAYERS)] + [(full[2][0], full[2][1])]
    for plane, (one, two) in enumerate(couples):
        first, second = lane_roll(one, HALF), lane_roll(two, HALF + HALF // 2)
        message_a[plane] = jnp.where(left_first, first, second)
        message_b[plane] = jnp.where(left_first, second, first)


def merge_kernel(message_a, message_b, beside):
    place = place_in_half(beside.shape[2:])
    from_a = (place < HALF // 2) != (lax.axis_index("gy") % 2 == 0)
    full = [[], [], []]
    for plane in range(3):
        a, b = message_a[plane], message_b[plane]
        one = jnp.where(from_a, a, b)
        two = lane_roll(jnp.where(from_a, b, a), -(HALF // 2))
        for number, value in zip((0, 1) if plane < 2 else (2, 2), (one, two)):
            full[number].append(value)
    near = (place < NEAR) | (place >= HALF - NEAR)
    for layer in range(LAYERS):
        observed = jnp.zeros(place.shape, jnp.float32)
        for number in range(3):
            value = full[number][layer]
            beside[number, layer] = jnp.where(near, value, 0.0)
            for _, lanes, shift in spare_lanes(number, place):
                observed = jnp.where(lanes, lane_roll(value, -shift), observed)
        beside[OBS, layer] = observed


class Level:
    def __init__(self, count, width, span, blocks, refs):
        self.count = count
        self.width = width
        self.span = span
        self.blocks = blocks
        (self.c_south, self.c_first, self.c_inner, self.c_east, self.c_west, self.c_layer, self.weight, self.diag,
         self.target, self.now, self.later) = refs

    @staticmethod
    def scratch(count, width, blocks):
        def vectors(*lead):
            return pltpu.VMEM(lead + (SUB, LANES), jnp.float32)

        whole = vectors(LAYERS, width, blocks, count)
        edge = vectors(LAYERS, blocks, count)
        return [whole, vectors(LAYERS, width, blocks), edge, edge, edge, vectors(width, blocks, count)] + [whole] * 5

    def steps(self):
        for b in range(self.blocks):
            for t in range(self.count):
                yield b, t

    def members(self):
        for layer in range(LAYERS):
            for u in range(self.width):
                yield layer, u


def row_before(values):
    edge = row_index() < 1
    rolled = [row_roll(value, 1) for value in values]
    return [jnp.where(edge, rolled[b - 1], rolled[b]) for b in range(len(values))]


def row_after(values):
    edge = row_index() >= SUB - 1
    rolled = [row_roll(value, -1) for value in values]
    return [jnp.where(edge, rolled[(b + 1) % len(values)], rolled[b]) for b in range(len(values))]


class Field:
    def __init__(self, level, source, coarse=None):
        self.source = source
        self.coarse = coarse
        self.count = level.count
        self.read = {}
        self.before, self.after = {}, {}
        for layer, u in level.members():
            lows = row_before([self.value(layer, u, b, level.count - 1) for b in range(level.blocks)])
            highs = row_after([self.value(layer, u, b, 0) for b in range(level.blocks)])
            for b in range(level.blocks):
                self.before[layer, u, b] = lows[b]
                self.after[layer, u, b] = highs[b]

    def value(self, layer, u, b, t):
        value = self.source[layer, u, b, t]
        return value if self.coarse is None else value + self.coarse[layer, 0, b, t // 2]

    def at(self, layer, u, b, t):
        if t < 0:
            return self.before[layer, u, b]
        if t >= self.count:
            return self.after[layer, u, b]
        key = layer, u, b, t
        if key not in self.read:
            self.read[key] = self.value(*key)
        return self.read[key]


def row_coeff(level, layer, u, b, t):
    return level.c_south[layer, u, b, t] if t >= 0 else level.c_first[layer, u, b]


def neighbour_sums(level, source, coarse=None):
    field = Field(level, source, coarse)
    coeffs = {}
    for b, t in level.steps():
        for member in level.members():
            for at in (t - 1, t):
                if (member, b, at) not in coeffs:
                    coeffs[member, b, at] = row_coeff(level, *member, b, at)
        layer_coeffs = [level.c_layer[u, b, t] for u in range(level.width)]
        for layer in range(LAYERS):
            here = [field.at(layer, u, b, t) for u in range(level.width)]
            east_coeff, west_coeff = level.c_east[layer, b, t], level.c_west[layer, b, t]
            if level.width == 2:
                inner = level.c_inner[layer, b, t]
                beside = [inner * here[1] + west_coeff * lane_roll(here[1], 1),
                          inner * here[0] + east_coeff * lane_roll(here[0], -1)]
            else:
                beside = [east_coeff * lane_roll(here[0], -level.span) + west_coeff * lane_roll(here[0], level.span)]
            for u in range(level.width):
                total = (coeffs[(layer, u), b, t - 1] * field.at(layer, u, b, t - 1)
                         + coeffs[(layer, u), b, t] * field.at(layer, u, b, t + 1)
                         + (beside[u] + layer_coeffs[u] * field.at(1 - layer, u, b, t)))
                yield (layer, u, b, t), here[u], total


def sweep(level, source, result, coarse=None):
    for key, value, total in neighbour_sums(level, source, coarse):
        result[key] = (1.0 - damping) * value + level.weight[key] * (level.target[key] + total)


def sweeps(level, count, coarse=None):
    for number in range(count):
        sweep(level, level.now, level.later, coarse if number == 0 else None)
        level.now, level.later = level.later, level.now


def first_sweep(level):
    for b, t in level.steps():
        for layer, u in level.members():
            key = layer, u, b, t
            level.now[key] = level.weight[key] * level.target[key]


def pair_sum(value, span):
    lower = lane_index() % (2 * span) < span
    return value + jnp.where(lower, lane_roll(value, -span), lane_roll(value, span))


def low_group(value, span):
    return jnp.where(lane_index() % (2 * span) < span, value, lane_roll(value, span))


def high_group(value, span):
    return jnp.where(lane_index() % (2 * span) < span, lane_roll(value, -span), value)


def column_sum(values, level):
    return values[0] + values[1] if level.width == 2 else pair_sum(values[0], level.span)


def restrict_residual(fine, coarse):
    residuals = {}
    for key, value, total in neighbour_sums(fine, fine.now):
        layer, u, b, t = key
        residuals[key] = fine.target[key] + total - fine.diag[key] * value
        if t % 2 == 1 and u == fine.width - 1:
            rows = [residuals[layer, v, b, t - 1] + residuals[layer, v, b, t] for v in range(fine.width)]
            coarse.target[layer, 0, b, t // 2] = column_sum(rows, fine)


def vcycle(levels):
    finest, middle, bottom = levels
    sweeps(finest, SMOOTH - 1)
    restrict_residual(finest, middle)
    first_sweep(middle)
    sweeps(middle, SMOOTH - 1)
    restrict_residual(middle, bottom)
    first_sweep(bottom)
    sweeps(bottom, COARSE - 1)
    sweeps(middle, SMOOTH, bottom.now)
    sweeps(finest, SMOOTH, middle.now)


def harmonic(left, right):
    return 2.0 * left * right / jnp.maximum(left + right, 1e-20)


def finest_coeffs(level, perm, joined):
    last = level.count - 1
    for layer, u in level.members():
        heads = [perm[layer, u, b, 0] for b in range(level.blocks)]
        rolled = [row_roll(value, -1) for value in heads]
        edge = row_index() >= SUB - 1
        for b in range(level.blocks):
            after = jnp.where(edge, joined[b] * rolled[(b + 1) % level.blocks], rolled[b])
            for t in range(level.count):
                beyond = perm[layer, u, b, t + 1] if t < last else after
                level.c_south[layer, u, b, t] = harmonic(perm[layer, u, b, t], beyond)
        firsts = row_before([level.c_south[layer, u, b, last] for b in range(level.blocks)])
        for b in range(level.blocks):
            level.c_first[layer, u, b] = firsts[b]
    for b, t in level.steps():
        for u in range(level.width):
            level.c_layer[u, b, t] = vertical * harmonic(perm[0, u, b, t], perm[1, u, b, t])
        for layer in range(LAYERS):
            even, odd = perm[layer, 0, b, t], perm[layer, 1, b, t]
            level.c_inner[layer, b, t] = harmonic(even, odd)
            east = harmonic(odd, lane_roll(even, -1))
            level.c_east[layer, b, t] = east
            level.c_west[layer, b, t] = lane_roll(east, 1)


def with_weight(level, acc):
    for b, t in level.steps():
        for layer, u in level.members():
            key = layer, u, b, t
            if level.width == 2:
                beside = level.c_inner[layer, b, t] + (level.c_west, level.c_east)[u][layer, b, t]
            else:
                beside = level.c_west[layer, b, t] + level.c_east[layer, b, t]
            diag = (row_coeff(level, layer, u, b, t - 1) + row_coeff(level, layer, u, b, t)
                    + (beside + level.c_layer[u, b, t]) + acc[key])
            level.diag[key] = diag
            level.weight[key] = damping / jnp.maximum(diag, 1e-20)


def coarse_coeffs(fine, coarse, fine_acc, coarse_acc):
    width = range(fine.width)
    for b in range(coarse.blocks):
        for layer in range(LAYERS):
            coarse.c_first[layer, 0, b] = column_sum([fine.c_first[layer, u, b] for u in width], fine)
    for b, t in coarse.steps():
        one, two = 2 * t, 2 * t + 1
        coarse.c_layer[0, b, t] = column_sum([fine.c_layer[u, b, one] + fine.c_layer[u, b, two] for u in width], fine)
        for layer in range(LAYERS):
            coarse.c_south[layer, 0, b, t] = column_sum([fine.c_south[layer, u, b, two] for u in width], fine)
            coarse_acc[layer, 0, b, t] = column_sum(
                [fine_acc[layer, u, b, one] + fine_acc[layer, u, b, two] for u in width], fine)
            west = fine.c_west[layer, b, one] + fine.c_west[layer, b, two]
            east = fine.c_east[layer, b, one] + fine.c_east[layer, b, two]
            if fine.width == 1:
                west, east = low_group(west, fine.span), high_group(east, fine.span)
            coarse.c_west[layer, b, t] = west
            coarse.c_east[layer, b, t] = east
    with_weight(coarse, coarse_acc)


def own_columns(even, odd):
    return jnp.where(lane_index() < HALF, even, lane_roll(odd, HALF))


def face_terms(level, pressure, adjoint, perm):
    def face(coeff, one, two):
        changes = [field.at(*one) - (field.at(*two) if isinstance(two, tuple) else two[number])
                   for number, field in enumerate((pressure, adjoint))]
        return (coeff * coeff) * (changes[0] * changes[1])

    rows = {(layer, u): face(level.c_first[layer, u, 0], (layer, u, 0, -1), (layer, u, 0, 0))
            for layer, u in level.members()}
    for t in range(level.count):
        between = [(1.0 / vertical) * face(level.c_layer[u, 0, t], (0, u, 0, t), (1, u, 0, t)) for u in range(2)]
        for layer in range(LAYERS):
            inner = face(level.c_inner[layer, 0, t], (layer, 0, 0, t), (layer, 1, 0, t))
            easts = [lane_roll(field.at(layer, 0, 0, t), -1) for field in (pressure, adjoint)]
            east = face(level.c_east[layer, 0, t], (layer, 1, 0, t), easts)
            terms = []
            for u in range(2):
                south = face(level.c_south[layer, u, 0, t], (layer, u, 0, t), (layer, u, 0, t + 1))
                beside = lane_roll(east, 1) if u == 0 else east
                total = rows[layer, u] + south + (inner + beside) + between[u]
                rows[layer, u] = south
                terms.append(-0.5 * total / perm[layer, u, 0, t])
            yield layer, t, own_columns(*terms)


def order_kernel(*refs):
    for shuffled, ordered in zip(refs[:2], refs[2:]):
        put_in_order(shuffled[...], ordered.at[0])


def cycle_kernel(grid_shape, blocks, *refs):
    cells_hbm, rates_hbm = refs[:2]
    inputs = [refs[2 + 3 * b:5 + 3 * b] for b in range(blocks)]
    refs = refs[2 + 3 * blocks:]
    pressure_out, adjoint_out, terms_out = refs[:3]
    cells, rates, sems, perm, acc, middle_acc, bottom_acc, states, terms_rows = refs[3:12]
    refs = refs[12:]
    copies = [pltpu.make_async_copy(cells_hbm, cells, sems.at[0]), pltpu.make_async_copy(rates_hbm, rates, sems.at[1])]
    for copy in copies:
        copy.start()
    count = inputs[0][0].shape[2] // SUB
    levels = [Level(count >> depth, width, span, blocks, refs[11 * depth:11 * depth + 11])
              for depth, (width, span) in enumerate(LEVELS)]
    finest, middle, bottom = levels

    def rows(t):
        return pl.ds(t * SUB, SUB)

    def fields(number, layer, b, t):
        low = lane_index() < HALF
        own = inputs[b][number // 2][number % 2, layer, rows(t), :]
        beside = inputs[b][2][number, layer, rows(t), :]
        return jnp.where(low, own, beside), lane_roll(jnp.where(low, beside, own), HALF)

    gx = lax.axis_index("gx")
    if blocks == 3:
        joined = [1.0, 0.0, 1.0]
    elif blocks == 2:
        joined = [1.0 - gx.astype(jnp.float32), gx.astype(jnp.float32)]
    else:
        joined = [0.0]

    for b, t in finest.steps():
        for layer in range(LAYERS):
            perms, accs, starts = [fields(number, layer, b, t) for number in (PERM, ACC, PREV)]
            for u in range(2):
                key = layer, u, b, t
                perm[key] = perms[u]
                acc[key] = accs[u]
                finest.now[key] = starts[u]
                finest.target[key] = accs[u] * starts[u]

    for copy in copies:
        copy.wait()
    layer_count, total_rows, total_cols = grid_shape
    block_rows, block_cols = SUB * count, LANES
    for well in range(WELLS):
        cell = cells[0, well]
        layer = cell // (total_rows * total_cols)
        row = cell // total_cols % total_rows - gx * block_rows
        col = cell % total_cols - lax.axis_index("gy") * block_cols
        if blocks == 3:
            row_inside = (row >= -block_rows) & (row < 2 * block_rows)
        elif blocks == 2:
            row_inside = row >= -block_rows
        else:
            row_inside = row >= 0
        inside = row_inside & (col >= -HALF) & (col < block_cols + HALF)
        row = jnp.where(row < 0, row + blocks * block_rows, row)
        col = jnp.where(col < 0, col + 2 * block_cols, col)
        row = jnp.where(inside, row, 0)
        col = jnp.where(inside, col, 0)
        rate = jnp.where(inside, rates[0, well], 0.0)
        in_block = row % block_rows
        place = layer, col % 2, row // block_rows, in_block % count
        hit = (row_index() == in_block // count) & (lane_index() == col // 2)
        finest.target[place] = finest.target[place] + jnp.where(hit, rate, 0.0)

    finest_coeffs(finest, perm, joined)
    with_weight(finest, acc)
    coarse_coeffs(finest, middle, acc, middle_acc)
    coarse_coeffs(middle, bottom, middle_acc, bottom_acc)

    sweeps(finest, 1)
    start, other = finest.now, finest.later

    def turn(number, carry):
        finest.now, finest.later = start, other
        vcycle(levels)
        for b, t in finest.steps():
            for layer in range(LAYERS):
                observed = fields(OBS, layer, b, t)
                for u in range(2):
                    key = layer, u, b, t
                    value = finest.now[key]
                    states[(number,) + key] = value
                    target = value - observed[u]
                    finest.target[key] = target
                    start[key] = finest.weight[key] * target
        return carry

    lax.fori_loop(0, 2, turn, 0)
    pressure, adjoint = states.at[0], states.at[1]
    for t in range(count):
        for layer in range(LAYERS):
            for state, result in ((pressure, pressure_out), (adjoint, adjoint_out)):
                result[layer, rows(t), :] = own_columns(*[state[layer, u, 0, t] for u in range(2)])

    for layer, t, terms in face_terms(finest, Field(finest, pressure), Field(finest, adjoint), perm):
        terms_rows[layer, rows(t), :] = terms
    put_in_order(terms_rows[...], terms_out)


def moved(value, axis, step):
    count = lax.axis_size(axis)
    ring = axis == "gx" and count == 2
    pairs = [((i + step) % count, i) for i in range(count) if ring or 0 <= i + step < count]
    return lax.ppermute(value, axis, pairs)


def swapped(value, axis, first):
    pairs = []
    for i in range(first, lax.axis_size(axis) - 1, 2):
        pairs += [(i, i + 1), (i + 1, i)]
    return lax.ppermute(value, axis, pairs)


def summed(value, axis):
    count = lax.axis_size(axis)
    others = [lax.ppermute(value, axis, [(i, i ^ step) for i in range(count)]) for step in range(count - 1, 0, -1)]
    terms = [value] + others[::-1]
    while len(terms) > 1:
        terms = [terms[i] + terms[i + 1] for i in range(0, len(terms), 2)]
    return terms[0]


def in_hbm(value):
    return pltpu.with_memory_space_constraint(value, pltpu.HBM)


def in_vmem(value):
    return pltpu.with_memory_space_constraint(value, pltpu.VMEM)


def shards(
    perm_log,
    facies,
    facies_scale,
    accumulation,
    previous_pressure,
    observed,
    well_cells,
    well_rates,
):
    layer_count, row_count, col_count = perm_log.shape
    gx_count, gy_count = lax.axis_size("gx"), lax.axis_size("gy")
    vmem = pl.BlockSpec(memory_space=pltpu.VMEM)
    hbm = pl.BlockSpec(memory_space=pltpu.HBM)
    f32 = jnp.float32
    fields = (perm_log, facies, accumulation, previous_pressure, observed)
    block = (layer_count, row_count, col_count)
    own_a, own_b, message_a, message_b = pl.pallas_call(
        pack_kernel,
        out_shape=[
            pltpu.VMEM((2,) + block, f32),
            pltpu.VMEM((2,) + block, f32),
            pltpu.VMEM((3,) + block[1:], f32),
            pltpu.VMEM((3,) + block[1:], f32),
        ],
        in_specs=[hbm] * 6,
        out_specs=[vmem] * 4,
        scratch_shapes=[pltpu.SMEM(facies_scale.shape, f32)]
        + [pltpu.VMEM(value.shape, value.dtype) for value in fields] + [pltpu.SemaphoreType.DMA((6,))],
        name="pack",
    )(in_hbm(facies_scale), *[in_hbm(value) for value in fields])

    steps = (0, 1) if gx_count == 2 else (0, 1, -1) if gx_count > 2 else (0,)
    blocks = len(steps)
    owns = [(own_a, own_b)] + [(moved(own_a, "gx", step), moved(own_b, "gx", step)) for step in steps[1:]]
    merge = pl.pallas_call(
        merge_kernel,
        out_shape=pltpu.VMEM((4,) + block, f32),
        in_specs=[vmem] * 2,
        out_specs=vmem,
        cost_estimate=pl.CostEstimate(flops=2**20, bytes_accessed=2**19, transcendentals=0),
        name="merge",
    )
    messages = swapped(message_a, "gy", 1), swapped(message_b, "gy", 0)
    besides = [merge(*[in_vmem(value) for value in messages])]
    for step in steps[1:]:
        besides.append(merge(*[in_vmem(moved(value, "gx", step)) for value in messages]))
    operands = [in_vmem(value) for own, beside in zip(owns, besides) for value in (*own, beside)]

    count = row_count // SUB
    scratch = [pltpu.SMEM(well_cells.shape, jnp.int32), pltpu.SMEM(well_rates.shape, f32), pltpu.SemaphoreType.DMA((2,))]
    whole = [pltpu.VMEM((LAYERS, width, blocks, count >> depth, SUB, LANES), f32) for depth, (width, _) in enumerate(LEVELS)]
    scratch += [whole[0], whole[0], whole[1], whole[2]]
    scratch += [pltpu.VMEM((2, LAYERS, 2, blocks, count, SUB, LANES), f32), pltpu.VMEM(block, f32)]
    for depth, (width, _) in enumerate(LEVELS):
        scratch += Level.scratch(count >> depth, width, blocks)
    state = jax.ShapeDtypeStruct((1, layer_count, row_count, col_count), f32)
    grid_shape = (layer_count, row_count * gx_count, col_count * gy_count)
    *shuffled, terms = pl.pallas_call(
        partial(cycle_kernel, grid_shape, blocks),
        out_shape=[pltpu.VMEM(block, f32)] * 3,
        in_specs=[hbm] * 2 + [vmem] * (3 * blocks),
        out_specs=[vmem] * 3,
        scratch_shapes=scratch,
        compiler_params=pltpu.CompilerParams(vmem_limit_bytes=24 * 1024 * 1024),
        name="cycles",
    )(in_hbm(well_cells), in_hbm(well_rates), *operands)
    gradient = summed(terms, "scen")
    pressure, adjoint = pl.pallas_call(
        order_kernel,
        out_shape=[state] * 2,
        in_specs=[vmem] * 2,
        out_specs=[vmem] * 2,
        cost_estimate=pl.CostEstimate(flops=2 * row_count * LANES**2 * 16, bytes_accessed=2**19, transcendentals=0),
        name="order",
    )(*[in_vmem(value) for value in shuffled])
    return pressure, adjoint, gradient


def solution(mesh):
    return jax.shard_map(
        shards,
        mesh=mesh,
        in_specs=(
            P(None, "gx", "gy"),
            P(None, "gx", "gy"),
            P(),
            P(None, "gx", "gy"),
            P("scen", None, "gx", "gy"),
            P("scen", None, "gx", "gy"),
            P("scen", None),
            P("scen", None),
        ),
        out_specs=(P("scen", None, "gx", "gy"), P("scen", None, "gx", "gy"), P(None, "gx", "gy")),
        check_vma=False,
    )
```

```python
from functools import partial

import jax
import jax.numpy as jnp
from jax import lax
from jax.experimental import pallas as pl
from jax.experimental.pallas import tpu as pltpu
from jax.sharding import PartitionSpec as P

WELLS = 5
FACIES = 4
LAYERS = 2
SMOOTH = 2
COARSE = 4

vertical = 0.3
damping = 0.8

LANES = 128
HALF = 64
SUB = 8
PERM, ACC, PREV, OBS = range(4)
NEAR = 26
ROOM = HALF // 2 - NEAR
LEVELS = ((2, 1), (1, 1), (1, 2))


def lane_index():
    return lax.broadcasted_iota(jnp.int32, (SUB, LANES), 1)


def row_index():
    return lax.broadcasted_iota(jnp.int32, (SUB, LANES), 0)


def lane_roll(value, shift):
    return pltpu.roll(value, shift % LANES, value.ndim - 1)


def row_roll(value, shift):
    return pltpu.roll(value, shift % SUB, 0)


def shuffle(value, inverse):
    rows = lax.broadcasted_iota(jnp.int32, (LANES, LANES), 0)
    cols = lax.broadcasted_iota(jnp.int32, (LANES, LANES), 1)
    natural, place = (cols, rows) if inverse else (rows, cols)
    matrix = (natural == 2 * (place % HALF) + place // HALF).astype(jnp.bfloat16)
    rest = value.reshape(-1, LANES)
    total = None
    for _ in range(3):
        part = rest.astype(jnp.bfloat16)
        rest = rest - part.astype(jnp.float32)
        moved_part = jnp.dot(part, matrix, preferred_element_type=jnp.float32)
        total = moved_part if total is None else total + moved_part
    return total.reshape(value.shape)


def place_in_half(shape):
    return lax.broadcasted_iota(jnp.int32, shape, len(shape) - 1) % HALF


def spare_lanes(number, place):
    shift = NEAR - number * ROOM
    low, high = number * ROOM, HALF - (number + 1) * ROOM
    return (((place >= NEAR) & (place < HALF // 2), (place >= low) & (place < low + ROOM), shift),
            ((place >= HALF // 2) & (place < HALF - NEAR), (place >= high) & (place < high + ROOM), -shift))


def interleaved(rows):
    count = rows.shape[0] // SUB
    return jnp.concatenate([rows[pl.ds(t, SUB, stride=count), :] for t in range(count)], axis=0)


def put_in_order(shuffled, ordered):
    count = ordered.shape[-2] // SUB
    natural = shuffle(shuffled, True)
    for layer in range(LAYERS):
        for t in range(count):
            ordered[layer, pl.ds(t, SUB, stride=count), :] = natural[layer, t * SUB:(t + 1) * SUB]


def pack_kernel(scale_hbm, perm_log_hbm, facies_hbm, acc_hbm, prev_hbm, obs_hbm, own_a, own_b, message_a, message_b,
                scale, perm_log, facies, acc, prev, obs, sems):
    pairs = ((scale_hbm, scale), (perm_log_hbm, perm_log), (facies_hbm, facies), (acc_hbm, acc), (prev_hbm, prev),
             (obs_hbm, obs))
    copies = [pltpu.make_async_copy(source, target, sems.at[i]) for i, (source, target) in enumerate(pairs)]
    for copy in copies:
        copy.start()
    for copy in copies:
        copy.wait()

    def layers(ref):
        return jnp.stack([interleaved(ref.at[layer]) for layer in range(LAYERS)])

    label = layers(facies)
    factor = jnp.zeros(label.shape, jnp.float32)
    for number in range(FACIES):
        factor = factor + jnp.where(label == number, scale[number], jnp.float32(0.0))
    fields = [shuffle(value, False) for value in (jnp.exp(layers(perm_log)) * factor, layers(acc), layers(prev.at[0]), layers(obs.at[0]))]
    for number in range(4):
        (own_a, own_b)[number // 2][number % 2] = fields[number]
    place = place_in_half(label.shape)
    full = []
    for number in range(3):
        value = fields[number]
        for lanes, _, shift in spare_lanes(number, place):
            value = jnp.where(lanes, lane_roll(fields[OBS], shift), value)
        full.append(value)
    low = place_in_half(label.shape[1:]) < HALF // 2
    left_first = low == (lax.axis_index("gy") % 2 == 1)
    couples = [(full[0][layer], full[1][layer]) for layer in range(LAYERS)] + [(full[2][0], full[2][1])]
    for plane, (one, two) in enumerate(couples):
        first, second = lane_roll(one, HALF), lane_roll(two, HALF + HALF // 2)
        message_a[plane] = jnp.where(left_first, first, second)
        message_b[plane] = jnp.where(left_first, second, first)


def merge(message_a, message_b, beside):
    place = place_in_half(beside.shape[2:])
    from_a = (place < HALF // 2) != (lax.axis_index("gy") % 2 == 1)
    full = [[], [], []]
    for plane in range(3):
        a, b = message_a[plane], message_b[plane]
        one = jnp.where(from_a, a, b)
        two = lane_roll(jnp.where(from_a, b, a), -(HALF // 2))
        for number, value in zip((0, 1) if plane < 2 else (2, 2), (one, two)):
            full[number].append(value)
    near = (place < NEAR) | (place >= HALF - NEAR)
    for layer in range(LAYERS):
        observed = jnp.zeros(place.shape, jnp.float32)
        for number in range(3):
            value = full[number][layer]
            beside[number, layer] = jnp.where(near, value, 0.0)
            for _, lanes, shift in spare_lanes(number, place):
                observed = jnp.where(lanes, lane_roll(value, -shift), observed)
        beside[OBS, layer] = observed


def block_kernel(own_a, own_b, message_a, message_b, vectors, c_south, c_inner, c_east, c_west, c_layer, beside):
    merge(message_a, message_b, beside)
    count = own_a.shape[2] // SUB
    low = lane_index() < HALF
    perm = {}
    for t in range(count):
        rows = pl.ds(t * SUB, SUB)
        for layer in range(LAYERS):
            for number in range(4):
                own, outer = (own_a, own_b)[number // 2][number % 2, layer, rows, :], beside[number, layer, rows, :]
                pair = jnp.where(low, own, outer), lane_roll(jnp.where(low, outer, own), HALF)
                for u in range(2):
                    vectors[number, layer, u, t] = pair[u]
                    if number == PERM:
                        perm[layer, u, t] = pair[u]
            even, odd = perm[layer, 0, t], perm[layer, 1, t]
            c_inner[layer, t] = harmonic(even, odd)
            east = harmonic(odd, lane_roll(even, -1))
            c_east[layer, t] = east
            c_west[layer, t] = lane_roll(east, 1)
            for u in range(2):
                if t > 0:
                    c_south[layer, u, t - 1] = harmonic(perm[layer, u, t - 1], perm[layer, u, t])
        for u in range(2):
            c_layer[u, t] = vertical * harmonic(perm[0, u, t], perm[1, u, t])


class Blocks:
    def __init__(self, refs, field=None, last=None):
        self.refs = refs
        self.field = () if field is None else (field,)
        self.last = last

    def __getitem__(self, key):
        *lead, b, t = key
        ref = self.refs[b]
        if self.last is not None and t == ref.shape[-3] - 1:
            return self.last[(*lead, b)]
        return ref[(*self.field, *lead, t)]


class Level:
    def __init__(self, count, width, span, blocks, refs):
        self.count = count
        self.width = width
        self.span = span
        self.blocks = blocks
        (self.c_south, self.c_first, self.c_inner, self.c_east, self.c_west, self.c_layer, self.weight, self.diag,
         self.target, self.now, self.later) = refs

    @staticmethod
    def scratch(count, width, blocks):
        def vectors(*lead):
            return pltpu.VMEM(lead + (SUB, LANES), jnp.float32)

        if width == 2:
            return [vectors(LAYERS, width, blocks)] * 2 + [vectors(LAYERS, width, blocks, count)] * 5

        whole = vectors(LAYERS, width, blocks, count)
        edge = vectors(LAYERS, blocks, count)
        return [whole, vectors(LAYERS, width, blocks), edge, edge, edge, vectors(width, blocks, count)] + [whole] * 5

    def steps(self):
        for b in range(self.blocks):
            for t in range(self.count):
                yield b, t

    def members(self):
        for layer in range(LAYERS):
            for u in range(self.width):
                yield layer, u


def row_before(values):
    edge = row_index() < 1
    rolled = [row_roll(value, 1) for value in values]
    return [jnp.where(edge, rolled[b - 1], rolled[b]) for b in range(len(values))]


def row_after(values):
    edge = row_index() >= SUB - 1
    rolled = [row_roll(value, -1) for value in values]
    return [jnp.where(edge, rolled[(b + 1) % len(values)], rolled[b]) for b in range(len(values))]


class Field:
    def __init__(self, level, source, coarse=None):
        self.source = source
        self.coarse = coarse
        self.count = level.count
        self.read = {}
        self.before, self.after = {}, {}
        for layer, u in level.members():
            lows = row_before([self.value(layer, u, b, level.count - 1) for b in range(level.blocks)])
            highs = row_after([self.value(layer, u, b, 0) for b in range(level.blocks)])
            for b in range(level.blocks):
                self.before[layer, u, b] = lows[b]
                self.after[layer, u, b] = highs[b]

    def value(self, layer, u, b, t):
        value = self.source[layer, u, b, t]
        return value if self.coarse is None else value + self.coarse[layer, 0, b, t // 2]

    def at(self, layer, u, b, t):
        if t < 0:
            return self.before[layer, u, b]
        if t >= self.count:
            return self.after[layer, u, b]
        key = layer, u, b, t
        if key not in self.read:
            self.read[key] = self.value(*key)
        return self.read[key]


def row_coeff(level, layer, u, b, t):
    return level.c_south[layer, u, b, t] if t >= 0 else level.c_first[layer, u, b]


def neighbour_sums(level, source, coarse=None):
    field = Field(level, source, coarse)
    coeffs = {}
    for b, t in level.steps():
        for member in level.members():
            for at in (t - 1, t):
                if (member, b, at) not in coeffs:
                    coeffs[member, b, at] = row_coeff(level, *member, b, at)
        layer_coeffs = [level.c_layer[u, b, t] for u in range(level.width)]
        for layer in range(LAYERS):
            here = [field.at(layer, u, b, t) for u in range(level.width)]
            east_coeff, west_coeff = level.c_east[layer, b, t], level.c_west[layer, b, t]
            if level.width == 2:
                inner = level.c_inner[layer, b, t]
                beside = [inner * here[1] + west_coeff * lane_roll(here[1], 1),
                          inner * here[0] + east_coeff * lane_roll(here[0], -1)]
            else:
                beside = [east_coeff * lane_roll(here[0], -level.span) + west_coeff * lane_roll(here[0], level.span)]
            for u in range(level.width):
                total = (coeffs[(layer, u), b, t - 1] * field.at(layer, u, b, t - 1)
                         + coeffs[(layer, u), b, t] * field.at(layer, u, b, t + 1)
                         + (beside[u] + layer_coeffs[u] * field.at(1 - layer, u, b, t)))
                yield (layer, u, b, t), here[u], total


def sweep(level, source, result, coarse=None):
    for key, value, total in neighbour_sums(level, source, coarse):
        result[key] = (1.0 - damping) * value + level.weight[key] * (level.target[key] + total)


def sweeps(level, count, coarse=None):
    for number in range(count):
        sweep(level, level.now, level.later, coarse if number == 0 else None)
        level.now, level.later = level.later, level.now


def first_sweep(level):
    for b, t in level.steps():
        for layer, u in level.members():
            key = layer, u, b, t
            level.now[key] = level.weight[key] * level.target[key]


def pair_sum(value, span):
    lower = lane_index() % (2 * span) < span
    return value + jnp.where(lower, lane_roll(value, -span), lane_roll(value, span))


def low_group(value, span):
    return jnp.where(lane_index() % (2 * span) < span, value, lane_roll(value, span))


def high_group(value, span):
    return jnp.where(lane_index() % (2 * span) < span, lane_roll(value, -span), value)


def column_sum(values, level):
    return values[0] + values[1] if level.width == 2 else pair_sum(values[0], level.span)


def restrict_residual(fine, coarse):
    residuals = {}
    for key, value, total in neighbour_sums(fine, fine.now):
        layer, u, b, t = key
        residuals[key] = fine.target[key] + total - fine.diag[key] * value
        if t % 2 == 1 and u == fine.width - 1:
            rows = [residuals[layer, v, b, t - 1] + residuals[layer, v, b, t] for v in range(fine.width)]
            coarse.target[layer, 0, b, t // 2] = column_sum(rows, fine)


def vcycle(levels):
    finest, middle, bottom = levels
    sweeps(finest, SMOOTH - 1)
    restrict_residual(finest, middle)
    first_sweep(middle)
    sweeps(middle, SMOOTH - 1)
    restrict_residual(middle, bottom)
    first_sweep(bottom)
    sweeps(bottom, COARSE - 1)
    sweeps(middle, SMOOTH, bottom.now)
    sweeps(finest, SMOOTH, middle.now)


def harmonic(left, right):
    return 2.0 * left * right / jnp.maximum(left + right, 1e-20)


def joining_coeffs(level, perm, c_last, joined):
    last = level.count - 1
    edge = row_index() >= SUB - 1
    for layer, u in level.members():
        rolled = [row_roll(perm[layer, u, b, 0], -1) for b in range(level.blocks)]
        souths = []
        for b in range(level.blocks):
            after = jnp.where(edge, joined[b] * rolled[(b + 1) % level.blocks], rolled[b])
            souths.append(harmonic(perm[layer, u, b, last], after))
        firsts = row_before(souths)
        for b in range(level.blocks):
            c_last[layer, u, b] = souths[b]
            level.c_first[layer, u, b] = firsts[b]


def with_weight(level, acc):
    for b, t in level.steps():
        for layer, u in level.members():
            key = layer, u, b, t
            if level.width == 2:
                beside = level.c_inner[layer, b, t] + (level.c_west, level.c_east)[u][layer, b, t]
            else:
                beside = level.c_west[layer, b, t] + level.c_east[layer, b, t]
            diag = (row_coeff(level, layer, u, b, t - 1) + row_coeff(level, layer, u, b, t)
                    + (beside + level.c_layer[u, b, t]) + acc[key])
            level.diag[key] = diag
            level.weight[key] = damping / jnp.maximum(diag, 1e-20)


def coarse_coeffs(fine, coarse, fine_acc, coarse_acc):
    width = range(fine.width)
    for b in range(coarse.blocks):
        for layer in range(LAYERS):
            coarse.c_first[layer, 0, b] = column_sum([fine.c_first[layer, u, b] for u in width], fine)
    for b, t in coarse.steps():
        one, two = 2 * t, 2 * t + 1
        coarse.c_layer[0, b, t] = column_sum([fine.c_layer[u, b, one] + fine.c_layer[u, b, two] for u in width], fine)
        for layer in range(LAYERS):
            coarse.c_south[layer, 0, b, t] = column_sum([fine.c_south[layer, u, b, two] for u in width], fine)
            coarse_acc[layer, 0, b, t] = column_sum(
                [fine_acc[layer, u, b, one] + fine_acc[layer, u, b, two] for u in width], fine)
            west = fine.c_west[layer, b, one] + fine.c_west[layer, b, two]
            east = fine.c_east[layer, b, one] + fine.c_east[layer, b, two]
            if fine.width == 1:
                west, east = low_group(west, fine.span), high_group(east, fine.span)
            coarse.c_west[layer, b, t] = west
            coarse.c_east[layer, b, t] = east
    with_weight(coarse, coarse_acc)


def own_columns(even, odd):
    return jnp.where(lane_index() < HALF, even, lane_roll(odd, HALF))


def face_terms(level, pressure, adjoint, perm):
    def face(coeff, one, two):
        changes = [field.at(*one) - (field.at(*two) if isinstance(two, tuple) else two[number])
                   for number, field in enumerate((pressure, adjoint))]
        return (coeff * coeff) * (changes[0] * changes[1])

    rows = {(layer, u): face(level.c_first[layer, u, 0], (layer, u, 0, -1), (layer, u, 0, 0))
            for layer, u in level.members()}
    for t in range(level.count):
        between = [(1.0 / vertical) * face(level.c_layer[u, 0, t], (0, u, 0, t), (1, u, 0, t)) for u in range(2)]
        for layer in range(LAYERS):
            inner = face(level.c_inner[layer, 0, t], (layer, 0, 0, t), (layer, 1, 0, t))
            easts = [lane_roll(field.at(layer, 0, 0, t), -1) for field in (pressure, adjoint)]
            east = face(level.c_east[layer, 0, t], (layer, 1, 0, t), easts)
            terms = []
            for u in range(2):
                south = face(level.c_south[layer, u, 0, t], (layer, u, 0, t), (layer, u, 0, t + 1))
                beside = lane_roll(east, 1) if u == 0 else east
                total = rows[layer, u] + south + (inner + beside) + between[u]
                rows[layer, u] = south
                terms.append(-0.5 * total / perm[layer, u, 0, t])
            yield layer, t, own_columns(*terms)


def order_kernel(*refs):
    for shuffled, ordered in zip(refs[:2], refs[2:]):
        put_in_order(shuffled[...], ordered.at[0])


def cycle_kernel(grid_shape, blocks, *refs):
    cells_hbm, rates_hbm = refs[:2]
    inputs = list(zip(*[refs[2 + 6 * b:8 + 6 * b] for b in range(blocks)]))
    refs = refs[2 + 6 * blocks:]
    pressure_out, adjoint_out, terms_out = refs[:3]
    cells, rates, sems, middle_acc, bottom_acc, states, terms_rows = refs[3:10]
    refs = refs[10:]
    copies = [pltpu.make_async_copy(cells_hbm, cells, sems.at[0]), pltpu.make_async_copy(rates_hbm, rates, sems.at[1])]
    for copy in copies:
        copy.start()
    perm, acc, previous, observed = [Blocks(inputs[0], number) for number in range(4)]
    count = inputs[0][0].shape[3]
    c_last = refs[0]
    coeffs = [Blocks(inputs[1], last=c_last), refs[1]] + [Blocks(value) for value in inputs[2:]]
    level_refs = [coeffs + list(refs[2:7]), refs[7:18], refs[18:29]]
    levels = [Level(count >> depth, width, span, blocks, level_refs[depth])
              for depth, (width, span) in enumerate(LEVELS)]
    finest, middle, bottom = levels

    def rows(t):
        return pl.ds(t * SUB, SUB)

    gx = lax.axis_index("gx")
    if blocks == 3:
        joined = [1.0, 0.0, 1.0]
    elif blocks == 2:
        joined = [1.0 - gx.astype(jnp.float32), gx.astype(jnp.float32)]
    else:
        joined = [0.0]

    for b, t in finest.steps():
        for layer, u in finest.members():
            key = layer, u, b, t
            start = previous[key]
            finest.now[key] = start
            finest.target[key] = acc[key] * start

    for copy in copies:
        copy.wait()
    layer_count, total_rows, total_cols = grid_shape
    block_rows, block_cols = SUB * count, LANES
    for well in range(WELLS):
        cell = cells[0, well]
        layer = cell // (total_rows * total_cols)
        row = cell // total_cols % total_rows - gx * block_rows
        col = cell % total_cols - lax.axis_index("gy") * block_cols
        if blocks == 3:
            row_inside = (row >= -block_rows) & (row < 2 * block_rows)
        elif blocks == 2:
            row_inside = row >= -block_rows
        else:
            row_inside = row >= 0
        inside = row_inside & (col >= -HALF) & (col < block_cols + HALF)
        row = jnp.where(row < 0, row + blocks * block_rows, row)
        col = jnp.where(col < 0, col + 2 * block_cols, col)
        row = jnp.where(inside, row, 0)
        col = jnp.where(inside, col, 0)
        rate = jnp.where(inside, rates[0, well], 0.0)
        in_block = row % block_rows
        place = layer, col % 2, row // block_rows, in_block % count
        hit = (row_index() == in_block // count) & (lane_index() == col // 2)
        finest.target[place] = finest.target[place] + jnp.where(hit, rate, 0.0)

    joining_coeffs(finest, perm, c_last, joined)
    with_weight(finest, acc)
    coarse_coeffs(finest, middle, acc, middle_acc)
    coarse_coeffs(middle, bottom, middle_acc, bottom_acc)

    sweeps(finest, 1)
    start, other = finest.now, finest.later

    def turn(number, carry):
        finest.now, finest.later = start, other
        vcycle(levels)
        for b, t in finest.steps():
            for layer, u in finest.members():
                key = layer, u, b, t
                value = finest.now[key]
                states[(number,) + key] = value
                target = value - observed[key]
                finest.target[key] = target
                start[key] = finest.weight[key] * target
        return carry

    lax.fori_loop(0, 2, turn, 0)
    pressure, adjoint = states.at[0], states.at[1]
    for t in range(count):
        for layer in range(LAYERS):
            for state, result in ((pressure, pressure_out), (adjoint, adjoint_out)):
                result[layer, rows(t), :] = own_columns(*[state[layer, u, 0, t] for u in range(2)])

    for layer, t, terms in face_terms(finest, Field(finest, pressure), Field(finest, adjoint), perm):
        terms_rows[layer, rows(t), :] = terms
    put_in_order(terms_rows[...], terms_out)


def moved(value, axis, step):
    count = lax.axis_size(axis)
    ring = axis == "gx" and count == 2
    pairs = [((i + step) % count, i) for i in range(count) if ring or 0 <= i + step < count]
    return lax.ppermute(value, axis, pairs)


def swapped(value, axis, first):
    pairs = []
    for i in range(first, lax.axis_size(axis) - 1, 2):
        pairs += [(i, i + 1), (i + 1, i)]
    return lax.ppermute(value, axis, pairs)


def summed(value, axis):
    count = lax.axis_size(axis)
    others = [lax.ppermute(value, axis, [(i, i ^ step) for i in range(count)]) for step in range(count - 1, 0, -1)]
    terms = [value] + others[::-1]
    while len(terms) > 1:
        terms = [terms[i] + terms[i + 1] for i in range(0, len(terms), 2)]
    return terms[0]


def in_hbm(value):
    return pltpu.with_memory_space_constraint(value, pltpu.HBM)


def in_vmem(value):
    return pltpu.with_memory_space_constraint(value, pltpu.VMEM)


def shards(
    perm_log,
    facies,
    facies_scale,
    accumulation,
    previous_pressure,
    observed,
    well_cells,
    well_rates,
):
    layer_count, row_count, col_count = perm_log.shape
    gx_count, gy_count = lax.axis_size("gx"), lax.axis_size("gy")
    vmem = pl.BlockSpec(memory_space=pltpu.VMEM)
    hbm = pl.BlockSpec(memory_space=pltpu.HBM)
    f32 = jnp.float32
    fields = (perm_log, facies, accumulation, previous_pressure, observed)
    block = (layer_count, row_count, col_count)
    own_a, own_b, message_a, message_b = pl.pallas_call(
        pack_kernel,
        out_shape=[
            pltpu.VMEM((2,) + block, f32),
            pltpu.VMEM((2,) + block, f32),
            pltpu.VMEM((3,) + block[1:], f32),
            pltpu.VMEM((3,) + block[1:], f32),
        ],
        in_specs=[hbm] * 6,
        out_specs=[vmem] * 4,
        scratch_shapes=[pltpu.SMEM(facies_scale.shape, f32)]
        + [pltpu.VMEM(value.shape, value.dtype) for value in fields] + [pltpu.SemaphoreType.DMA((6,))],
        name="pack",
    )(in_hbm(facies_scale), *[in_hbm(value) for value in fields])

    steps = (0, 1) if gx_count == 2 else (0, 1, -1) if gx_count > 2 else (0,)
    blocks = len(steps)
    owns = [(own_a, own_b)] + [(moved(own_a, "gx", step), moved(own_b, "gx", step)) for step in steps[1:]]
    count = row_count // SUB

    def vectors(*lead):
        return pltpu.VMEM(lead + (count, SUB, LANES), f32)

    level_zero = pl.pallas_call(
        block_kernel,
        out_shape=[vectors(4, LAYERS, 2), vectors(LAYERS, 2)] + [vectors(LAYERS)] * 3 + [vectors(2)],
        in_specs=[vmem] * 4,
        out_specs=[vmem] * 6,
        scratch_shapes=[pltpu.VMEM((4,) + block, f32)],
        cost_estimate=pl.CostEstimate(flops=2**21, bytes_accessed=2**21, transcendentals=0),
        name="level_zero",
    )
    messages = swapped(message_a, "gy", 0), swapped(message_b, "gy", 1)
    operands = []
    for (one, two), step in zip(owns, steps):
        sides = messages if step == 0 else [moved(value, "gx", step) for value in messages]
        operands += level_zero(*[in_vmem(value) for value in (one, two, *sides)])
    operands = [in_vmem(value) for value in operands]

    scratch = [pltpu.SMEM(well_cells.shape, jnp.int32), pltpu.SMEM(well_rates.shape, f32), pltpu.SemaphoreType.DMA((2,))]
    whole = [pltpu.VMEM((LAYERS, width, blocks, count >> depth, SUB, LANES), f32) for depth, (width, _) in enumerate(LEVELS)]
    scratch += [whole[1], whole[2]]
    scratch += [pltpu.VMEM((2, LAYERS, 2, blocks, count, SUB, LANES), f32), pltpu.VMEM(block, f32)]
    for depth, (width, _) in enumerate(LEVELS):
        scratch += Level.scratch(count >> depth, width, blocks)
    state = jax.ShapeDtypeStruct((1, layer_count, row_count, col_count), f32)
    grid_shape = (layer_count, row_count * gx_count, col_count * gy_count)
    *shuffled, terms = pl.pallas_call(
        partial(cycle_kernel, grid_shape, blocks),
        out_shape=[pltpu.VMEM(block, f32)] * 3,
        in_specs=[hbm] * 2 + [vmem] * (6 * blocks),
        out_specs=[vmem] * 3,
        scratch_shapes=scratch,
        compiler_params=pltpu.CompilerParams(vmem_limit_bytes=24 * 1024 * 1024),
        name="cycles",
    )(in_hbm(well_cells), in_hbm(well_rates), *operands)
    gradient = summed(terms, "scen")
    pressure, adjoint = pl.pallas_call(
        order_kernel,
        out_shape=[state] * 2,
        in_specs=[vmem] * 2,
        out_specs=[vmem] * 2,
        cost_estimate=pl.CostEstimate(flops=2 * row_count * LANES**2 * 16, bytes_accessed=2**19, transcendentals=0),
        name="order",
    )(*[in_vmem(value) for value in shuffled])
    return pressure, adjoint, gradient


def solution(mesh):
    return jax.shard_map(
        shards,
        mesh=mesh,
        in_specs=(
            P(None, "gx", "gy"),
            P(None, "gx", "gy"),
            P(),
            P(None, "gx", "gy"),
            P("scen", None, "gx", "gy"),
            P("scen", None, "gx", "gy"),
            P("scen", None),
            P("scen", None),
        ),
        out_specs=(P("scen", None, "gx", "gy"), P("scen", None, "gx", "gy"), P(None, "gx", "gy")),
        check_vma=False,
    )
```

```python
from functools import partial

import jax
import jax.numpy as jnp
from jax import lax
from jax.experimental import pallas as pl
from jax.experimental.pallas import tpu as pltpu
from jax.sharding import PartitionSpec as P

WELLS = 5
FACIES = 4
LAYERS = 2
SMOOTH = 2
COARSE = 4

vertical = 0.3
damping = 0.8

LANES = 128
HALF = 64
SUB = 8
PERM, ACC, PREV, OBS = range(4)
NEAR = 26
ROOM = HALF // 2 - NEAR
LEVELS = ((2, 1), (1, 1), (1, 2))


def lane_index():
    return lax.broadcasted_iota(jnp.int32, (SUB, LANES), 1)


def row_index():
    return lax.broadcasted_iota(jnp.int32, (SUB, LANES), 0)


def lane_roll(value, shift):
    return pltpu.roll(value, shift % LANES, value.ndim - 1)


def row_roll(value, shift):
    return pltpu.roll(value, shift % SUB, 0)


def shuffle(value, inverse):
    rows = lax.broadcasted_iota(jnp.int32, (LANES, LANES), 0)
    cols = lax.broadcasted_iota(jnp.int32, (LANES, LANES), 1)
    natural, place = (cols, rows) if inverse else (rows, cols)
    matrix = (natural == 2 * (place % HALF) + place // HALF).astype(jnp.bfloat16)
    rest = value.reshape(-1, LANES)
    total = None
    for _ in range(3):
        part = rest.astype(jnp.bfloat16)
        rest = rest - part.astype(jnp.float32)
        moved_part = jnp.dot(part, matrix, preferred_element_type=jnp.float32)
        total = moved_part if total is None else total + moved_part
    return total.reshape(value.shape)


def place_in_half(shape):
    return lax.broadcasted_iota(jnp.int32, shape, len(shape) - 1) % HALF


def spare_lanes(number, place):
    shift = NEAR - number * ROOM
    low, high = number * ROOM, HALF - (number + 1) * ROOM
    return (((place >= NEAR) & (place < HALF // 2), (place >= low) & (place < low + ROOM), shift),
            ((place >= HALF // 2) & (place < HALF - NEAR), (place >= high) & (place < high + ROOM), -shift))


def interleaved(rows):
    count = rows.shape[0] // SUB
    return jnp.concatenate([rows[pl.ds(t, SUB, stride=count), :] for t in range(count)], axis=0)


def put_in_order(shuffled, ordered):
    count = ordered.shape[-2] // SUB
    natural = shuffle(shuffled, True)
    for layer in range(LAYERS):
        for t in range(count):
            ordered[layer, pl.ds(t, SUB, stride=count), :] = natural[layer, t * SUB:(t + 1) * SUB]


def pack_kernel(scale_hbm, perm_log_hbm, facies_hbm, acc_hbm, prev_hbm, obs_hbm, own_a, own_b, message_a, message_b,
                scale, perm_log, facies, acc, prev, obs, sems):
    pairs = ((acc_hbm, acc), (prev_hbm, prev), (obs_hbm, obs), (scale_hbm, scale), (perm_log_hbm, perm_log),
             (facies_hbm, facies))
    copies = [pltpu.make_async_copy(source, target, sems.at[i]) for i, (source, target) in enumerate(pairs)]
    for copy in copies:
        copy.start()

    def layers(ref):
        return jnp.stack([interleaved(ref.at[layer]) for layer in range(LAYERS)])

    fields = [None]
    for copy, ref in zip(copies[:3], (acc, prev.at[0], obs.at[0])):
        copy.wait()
        fields.append(shuffle(layers(ref), False))
    for copy in copies[3:]:
        copy.wait()
    label = layers(facies)
    factor = jnp.zeros(label.shape, jnp.float32)
    for number in range(FACIES):
        factor = factor + jnp.where(label == number, scale[number], jnp.float32(0.0))
    fields[PERM] = shuffle(jnp.exp(layers(perm_log)) * factor, False)
    for number in range(4):
        (own_a, own_b)[number // 2][number % 2] = fields[number]
    place = place_in_half(label.shape)
    full = []
    for number in range(3):
        value = fields[number]
        for lanes, _, shift in spare_lanes(number, place):
            value = jnp.where(lanes, lane_roll(fields[OBS], shift), value)
        full.append(value)
    low = place_in_half(label.shape[1:]) < HALF // 2
    left_first = low == (lax.axis_index("gy") % 2 == 1)
    couples = [(full[0][layer], full[1][layer]) for layer in range(LAYERS)] + [(full[2][0], full[2][1])]
    for plane, (one, two) in enumerate(couples):
        first, second = lane_roll(one, HALF), lane_roll(two, HALF + HALF // 2)
        message_a[plane] = jnp.where(left_first, first, second)
        message_b[plane] = jnp.where(left_first, second, first)


def merge_kernel(message_a, message_b, beside):
    place = place_in_half(beside.shape[2:])
    from_a = (place < HALF // 2) != (lax.axis_index("gy") % 2 == 1)
    full = [[], [], []]
    for plane in range(3):
        a, b = message_a[plane], message_b[plane]
        one = jnp.where(from_a, a, b)
        two = lane_roll(jnp.where(from_a, b, a), -(HALF // 2))
        for number, value in zip((0, 1) if plane < 2 else (2, 2), (one, two)):
            full[number].append(value)
    near = (place < NEAR) | (place >= HALF - NEAR)
    for layer in range(LAYERS):
        observed = jnp.zeros(place.shape, jnp.float32)
        for number in range(3):
            value = full[number][layer]
            beside[number, layer] = jnp.where(near, value, 0.0)
            for _, lanes, shift in spare_lanes(number, place):
                observed = jnp.where(lanes, lane_roll(value, -shift), observed)
        beside[OBS, layer] = observed


class Level:
    def __init__(self, count, width, span, blocks, refs):
        self.count = count
        self.width = width
        self.span = span
        self.blocks = blocks
        (self.c_south, self.c_first, self.c_inner, self.c_east, self.c_west, self.c_layer, self.weight, self.diag,
         self.target, self.now, self.later) = refs

    @staticmethod
    def scratch(count, width, blocks):
        def vectors(*lead):
            return pltpu.VMEM(lead + (SUB, LANES), jnp.float32)

        whole = vectors(LAYERS, width, blocks, count)
        edge = vectors(LAYERS, blocks, count)
        return [whole, vectors(LAYERS, width, blocks), edge, edge, edge, vectors(width, blocks, count)] + [whole] * 5

    def steps(self):
        for b in range(self.blocks):
            for t in range(self.count):
                yield b, t

    def members(self):
        for layer in range(LAYERS):
            for u in range(self.width):
                yield layer, u


def row_before(values):
    edge = row_index() < 1
    rolled = [row_roll(value, 1) for value in values]
    return [jnp.where(edge, rolled[b - 1], rolled[b]) for b in range(len(values))]


def row_after(values):
    edge = row_index() >= SUB - 1
    rolled = [row_roll(value, -1) for value in values]
    return [jnp.where(edge, rolled[(b + 1) % len(values)], rolled[b]) for b in range(len(values))]


class Field:
    def __init__(self, level, source, coarse=None):
        self.source = source
        self.coarse = coarse
        self.count = level.count
        self.read = {}
        self.before, self.after = {}, {}
        for layer, u in level.members():
            lows = row_before([self.value(layer, u, b, level.count - 1) for b in range(level.blocks)])
            highs = row_after([self.value(layer, u, b, 0) for b in range(level.blocks)])
            for b in range(level.blocks):
                self.before[layer, u, b] = lows[b]
                self.after[layer, u, b] = highs[b]

    def value(self, layer, u, b, t):
        value = self.source[layer, u, b, t]
        return value if self.coarse is None else value + self.coarse[layer, 0, b, t // 2]

    def at(self, layer, u, b, t):
        if t < 0:
            return self.before[layer, u, b]
        if t >= self.count:
            return self.after[layer, u, b]
        key = layer, u, b, t
        if key not in self.read:
            self.read[key] = self.value(*key)
        return self.read[key]


def row_coeff(level, layer, u, b, t):
    return level.c_south[layer, u, b, t] if t >= 0 else level.c_first[layer, u, b]


def neighbour_sums(level, source, coarse=None):
    field = Field(level, source, coarse)
    coeffs = {}
    for b, t in level.steps():
        for member in level.members():
            for at in (t - 1, t):
                if (member, b, at) not in coeffs:
                    coeffs[member, b, at] = row_coeff(level, *member, b, at)
        layer_coeffs = [level.c_layer[u, b, t] for u in range(level.width)]
        for layer in range(LAYERS):
            here = [field.at(layer, u, b, t) for u in range(level.width)]
            east_coeff, west_coeff = level.c_east[layer, b, t], level.c_west[layer, b, t]
            if level.width == 2:
                inner = level.c_inner[layer, b, t]
                beside = [inner * here[1] + west_coeff * lane_roll(here[1], 1),
                          inner * here[0] + east_coeff * lane_roll(here[0], -1)]
            else:
                beside = [east_coeff * lane_roll(here[0], -level.span) + west_coeff * lane_roll(here[0], level.span)]
            for u in range(level.width):
                total = (coeffs[(layer, u), b, t - 1] * field.at(layer, u, b, t - 1)
                         + coeffs[(layer, u), b, t] * field.at(layer, u, b, t + 1)
                         + (beside[u] + layer_coeffs[u] * field.at(1 - layer, u, b, t)))
                yield (layer, u, b, t), here[u], total


def sweep(level, source, result, coarse=None):
    for key, value, total in neighbour_sums(level, source, coarse):
        result[key] = (1.0 - damping) * value + level.weight[key] * (level.target[key] + total)


def sweeps(level, count, coarse=None):
    for number in range(count):
        sweep(level, level.now, level.later, coarse if number == 0 else None)
        level.now, level.later = level.later, level.now


def first_sweep(level):
    for b, t in level.steps():
        for layer, u in level.members():
            key = layer, u, b, t
            level.now[key] = level.weight[key] * level.target[key]


def pair_sum(value, span):
    lower = lane_index() % (2 * span) < span
    return value + jnp.where(lower, lane_roll(value, -span), lane_roll(value, span))


def low_group(value, span):
    return jnp.where(lane_index() % (2 * span) < span, value, lane_roll(value, span))


def high_group(value, span):
    return jnp.where(lane_index() % (2 * span) < span, lane_roll(value, -span), value)


def column_sum(values, level):
    return values[0] + values[1] if level.width == 2 else pair_sum(values[0], level.span)


def restrict_residual(fine, coarse):
    residuals = {}
    for key, value, total in neighbour_sums(fine, fine.now):
        layer, u, b, t = key
        residuals[key] = fine.target[key] + total - fine.diag[key] * value
        if t % 2 == 1 and u == fine.width - 1:
            rows = [residuals[layer, v, b, t - 1] + residuals[layer, v, b, t] for v in range(fine.width)]
            coarse.target[layer, 0, b, t // 2] = column_sum(rows, fine)


def vcycle(levels):
    finest, middle, bottom = levels
    sweeps(finest, SMOOTH - 1)
    restrict_residual(finest, middle)
    first_sweep(middle)
    sweeps(middle, SMOOTH - 1)
    restrict_residual(middle, bottom)
    first_sweep(bottom)
    sweeps(bottom, COARSE - 1)
    sweeps(middle, SMOOTH, bottom.now)
    sweeps(finest, SMOOTH, middle.now)


def harmonic(left, right):
    return 2.0 * left * right / jnp.maximum(left + right, 1e-20)


def finest_coeffs(level, perm, joined):
    last = level.count - 1
    for layer, u in level.members():
        heads = [perm[layer, u, b, 0] for b in range(level.blocks)]
        rolled = [row_roll(value, -1) for value in heads]
        edge = row_index() >= SUB - 1
        for b in range(level.blocks):
            after = jnp.where(edge, joined[b] * rolled[(b + 1) % level.blocks], rolled[b])
            for t in range(level.count):
                beyond = perm[layer, u, b, t + 1] if t < last else after
                level.c_south[layer, u, b, t] = harmonic(perm[layer, u, b, t], beyond)
        firsts = row_before([level.c_south[layer, u, b, last] for b in range(level.blocks)])
        for b in range(level.blocks):
            level.c_first[layer, u, b] = firsts[b]
    for b, t in level.steps():
        for u in range(level.width):
            level.c_layer[u, b, t] = vertical * harmonic(perm[0, u, b, t], perm[1, u, b, t])
        for layer in range(LAYERS):
            even, odd = perm[layer, 0, b, t], perm[layer, 1, b, t]
            level.c_inner[layer, b, t] = harmonic(even, odd)
            east = harmonic(odd, lane_roll(even, -1))
            level.c_east[layer, b, t] = east
            level.c_west[layer, b, t] = lane_roll(east, 1)


def with_weight(level, acc):
    for b, t in level.steps():
        for layer, u in level.members():
            key = layer, u, b, t
            if level.width == 2:
                beside = level.c_inner[layer, b, t] + (level.c_west, level.c_east)[u][layer, b, t]
            else:
                beside = level.c_west[layer, b, t] + level.c_east[layer, b, t]
            diag = (row_coeff(level, layer, u, b, t - 1) + row_coeff(level, layer, u, b, t)
                    + (beside + level.c_layer[u, b, t]) + acc[key])
            level.diag[key] = diag
            level.weight[key] = damping / jnp.maximum(diag, 1e-20)


def coarse_coeffs(fine, coarse, fine_acc, coarse_acc):
    width = range(fine.width)
    for b in range(coarse.blocks):
        for layer in range(LAYERS):
            coarse.c_first[layer, 0, b] = column_sum([fine.c_first[layer, u, b] for u in width], fine)
    for b, t in coarse.steps():
        one, two = 2 * t, 2 * t + 1
        coarse.c_layer[0, b, t] = column_sum([fine.c_layer[u, b, one] + fine.c_layer[u, b, two] for u in width], fine)
        for layer in range(LAYERS):
            coarse.c_south[layer, 0, b, t] = column_sum([fine.c_south[layer, u, b, two] for u in width], fine)
            coarse_acc[layer, 0, b, t] = column_sum(
                [fine_acc[layer, u, b, one] + fine_acc[layer, u, b, two] for u in width], fine)
            west = fine.c_west[layer, b, one] + fine.c_west[layer, b, two]
            east = fine.c_east[layer, b, one] + fine.c_east[layer, b, two]
            if fine.width == 1:
                west, east = low_group(west, fine.span), high_group(east, fine.span)
            coarse.c_west[layer, b, t] = west
            coarse.c_east[layer, b, t] = east
    with_weight(coarse, coarse_acc)


def own_columns(even, odd):
    return jnp.where(lane_index() < HALF, even, lane_roll(odd, HALF))


def face_terms(level, pressure, adjoint, perm):
    def face(coeff, one, two):
        changes = [field.at(*one) - (field.at(*two) if isinstance(two, tuple) else two[number])
                   for number, field in enumerate((pressure, adjoint))]
        return (coeff * coeff) * (changes[0] * changes[1])

    rows = {(layer, u): face(level.c_first[layer, u, 0], (layer, u, 0, -1), (layer, u, 0, 0))
            for layer, u in level.members()}
    for t in range(level.count):
        between = [(1.0 / vertical) * face(level.c_layer[u, 0, t], (0, u, 0, t), (1, u, 0, t)) for u in range(2)]
        for layer in range(LAYERS):
            inner = face(level.c_inner[layer, 0, t], (layer, 0, 0, t), (layer, 1, 0, t))
            easts = [lane_roll(field.at(layer, 0, 0, t), -1) for field in (pressure, adjoint)]
            east = face(level.c_east[layer, 0, t], (layer, 1, 0, t), easts)
            terms = []
            for u in range(2):
                south = face(level.c_south[layer, u, 0, t], (layer, u, 0, t), (layer, u, 0, t + 1))
                beside = lane_roll(east, 1) if u == 0 else east
                total = rows[layer, u] + south + (inner + beside) + between[u]
                rows[layer, u] = south
                terms.append(-0.5 * total / perm[layer, u, 0, t])
            yield layer, t, own_columns(*terms)


def order_kernel(*refs):
    for shuffled, ordered in zip(refs[:2], refs[2:]):
        put_in_order(shuffled[...], ordered.at[0])


def split(value, size):
    if size & (size - 1) == 0:
        return value >> (size.bit_length() - 1), value & (size - 1)
    return value // size, value % size


def cycle_kernel(grid_shape, blocks, *refs):
    cells_hbm, rates_hbm = refs[:2]
    inputs = [refs[2 + 3 * b:5 + 3 * b] for b in range(blocks)]
    refs = refs[2 + 3 * blocks:]
    pressure_out, adjoint_out, terms_out = refs[:3]
    cells, rates, sems, perm, acc, middle_acc, bottom_acc, states, terms_rows = refs[3:12]
    refs = refs[12:]
    copies = [pltpu.make_async_copy(cells_hbm, cells, sems.at[0]), pltpu.make_async_copy(rates_hbm, rates, sems.at[1])]
    for copy in copies:
        copy.start()
    count = inputs[0][0].shape[2] // SUB
    levels = [Level(count >> depth, width, span, blocks, refs[11 * depth:11 * depth + 11])
              for depth, (width, span) in enumerate(LEVELS)]
    finest, middle, bottom = levels

    def rows(t):
        return pl.ds(t * SUB, SUB)

    def fields(number, layer, b, t):
        low = lane_index() < HALF
        own = inputs[b][number // 2][number % 2, layer, rows(t), :]
        beside = inputs[b][2][number, layer, rows(t), :]
        return jnp.where(low, own, beside), lane_roll(jnp.where(low, beside, own), HALF)

    gx = lax.axis_index("gx")
    if blocks == 3:
        joined = [1.0, 0.0, 1.0]
    elif blocks == 2:
        joined = [1.0 - gx.astype(jnp.float32), gx.astype(jnp.float32)]
    else:
        joined = [0.0]

    for b, t in finest.steps():
        for layer in range(LAYERS):
            perms, accs, starts = [fields(number, layer, b, t) for number in (PERM, ACC, PREV)]
            for u in range(2):
                key = layer, u, b, t
                perm[key] = perms[u]
                acc[key] = accs[u]
                finest.now[key] = starts[u]
                finest.target[key] = accs[u] * starts[u]

    finest_coeffs(finest, perm, joined)
    with_weight(finest, acc)
    coarse_coeffs(finest, middle, acc, middle_acc)
    coarse_coeffs(middle, bottom, middle_acc, bottom_acc)

    for copy in copies:
        copy.wait()
    layer_count, total_rows, total_cols = grid_shape
    block_rows, block_cols = SUB * count, LANES
    for well in range(WELLS):
        cell = cells[0, well]
        layer, cell = split(cell, total_rows * total_cols)
        row, col = split(cell, total_cols)
        row = row - gx * block_rows
        col = col - lax.axis_index("gy") * block_cols
        if blocks == 3:
            row_inside = (row >= -block_rows) & (row < 2 * block_rows)
        elif blocks == 2:
            row_inside = row >= -block_rows
        else:
            row_inside = row >= 0
        inside = row_inside & (col >= -HALF) & (col < block_cols + HALF)
        row = jnp.where(row < 0, row + blocks * block_rows, row)
        col = jnp.where(col < 0, col + 2 * block_cols, col)
        row = jnp.where(inside, row, 0)
        col = jnp.where(inside, col, 0)
        rate = jnp.where(inside, rates[0, well], 0.0)
        b, in_block = split(row, block_rows)
        s, t = split(in_block, count)
        lane, u = split(col, 2)
        place = layer, u, b, t
        hit = (row_index() == s) & (lane_index() == lane)
        finest.target[place] = finest.target[place] + jnp.where(hit, rate, 0.0)

    sweeps(finest, 1)
    start, other = finest.now, finest.later

    def turn(number, carry):
        finest.now, finest.later = start, other
        vcycle(levels)
        for b, t in finest.steps():
            for layer in range(LAYERS):
                observed = fields(OBS, layer, b, t)
                for u in range(2):
                    key = layer, u, b, t
                    value = finest.now[key]
                    states[(number,) + key] = value
                    target = value - observed[u]
                    finest.target[key] = target
                    start[key] = finest.weight[key] * target
        return carry

    lax.fori_loop(0, 2, turn, 0)
    pressure, adjoint = states.at[0], states.at[1]
    for t in range(count):
        for layer in range(LAYERS):
            for state, result in ((pressure, pressure_out), (adjoint, adjoint_out)):
                result[layer, rows(t), :] = own_columns(*[state[layer, u, 0, t] for u in range(2)])

    for layer, t, terms in face_terms(finest, Field(finest, pressure), Field(finest, adjoint), perm):
        terms_rows[layer, rows(t), :] = terms
    put_in_order(terms_rows[...], terms_out)


def moved(value, axis, step):
    count = lax.axis_size(axis)
    ring = axis == "gx" and count == 2
    pairs = [((i + step) % count, i) for i in range(count) if ring or 0 <= i + step < count]
    return lax.ppermute(value, axis, pairs)


def swapped(value, axis, first):
    pairs = []
    for i in range(first, lax.axis_size(axis) - 1, 2):
        pairs += [(i, i + 1), (i + 1, i)]
    return lax.ppermute(value, axis, pairs)


def summed(value, axis):
    count = lax.axis_size(axis)
    others = [lax.ppermute(value, axis, [(i, i ^ step) for i in range(count)]) for step in range(count - 1, 0, -1)]
    terms = [value] + others[::-1]
    while len(terms) > 1:
        terms = [terms[i] + terms[i + 1] for i in range(0, len(terms), 2)]
    return terms[0]


def in_hbm(value):
    return pltpu.with_memory_space_constraint(value, pltpu.HBM)


def in_vmem(value):
    return pltpu.with_memory_space_constraint(value, pltpu.VMEM)


def shards(
    perm_log,
    facies,
    facies_scale,
    accumulation,
    previous_pressure,
    observed,
    well_cells,
    well_rates,
):
    layer_count, row_count, col_count = perm_log.shape
    gx_count, gy_count = lax.axis_size("gx"), lax.axis_size("gy")
    vmem = pl.BlockSpec(memory_space=pltpu.VMEM)
    hbm = pl.BlockSpec(memory_space=pltpu.HBM)
    f32 = jnp.float32
    fields = (perm_log, facies, accumulation, previous_pressure, observed)
    block = (layer_count, row_count, col_count)
    own_a, own_b, message_a, message_b = pl.pallas_call(
        pack_kernel,
        out_shape=[
            pltpu.VMEM((2,) + block, f32),
            pltpu.VMEM((2,) + block, f32),
            pltpu.VMEM((3,) + block[1:], f32),
            pltpu.VMEM((3,) + block[1:], f32),
        ],
        in_specs=[hbm] * 6,
        out_specs=[vmem] * 4,
        scratch_shapes=[pltpu.SMEM(facies_scale.shape, f32)]
        + [pltpu.VMEM(value.shape, value.dtype) for value in fields] + [pltpu.SemaphoreType.DMA((6,))],
        name="pack",
    )(in_hbm(facies_scale), *[in_hbm(value) for value in fields])

    steps = (0, 1) if gx_count == 2 else (0, 1, -1) if gx_count > 2 else (0,)
    blocks = len(steps)
    owns = [(own_a, own_b)] + [(moved(own_a, "gx", step), moved(own_b, "gx", step)) for step in steps[1:]]
    merge = pl.pallas_call(
        merge_kernel,
        out_shape=pltpu.VMEM((4,) + block, f32),
        in_specs=[vmem] * 2,
        out_specs=vmem,
        cost_estimate=pl.CostEstimate(flops=2**20, bytes_accessed=2**19, transcendentals=0),
        name="merge",
    )
    messages = swapped(message_a, "gy", 0), swapped(message_b, "gy", 1)
    besides = [merge(*[in_vmem(value) for value in messages])]
    for step in steps[1:]:
        besides.append(merge(*[in_vmem(moved(value, "gx", step)) for value in messages]))
    operands = [in_vmem(value) for own, beside in zip(owns, besides) for value in (*own, beside)]

    count = row_count // SUB
    scratch = [pltpu.SMEM(well_cells.shape, jnp.int32), pltpu.SMEM(well_rates.shape, f32), pltpu.SemaphoreType.DMA((2,))]
    whole = [pltpu.VMEM((LAYERS, width, blocks, count >> depth, SUB, LANES), f32) for depth, (width, _) in enumerate(LEVELS)]
    scratch += [whole[0], whole[0], whole[1], whole[2]]
    scratch += [pltpu.VMEM((2, LAYERS, 2, blocks, count, SUB, LANES), f32), pltpu.VMEM(block, f32)]
    for depth, (width, _) in enumerate(LEVELS):
        scratch += Level.scratch(count >> depth, width, blocks)
    state = jax.ShapeDtypeStruct((1, layer_count, row_count, col_count), f32)
    grid_shape = (layer_count, row_count * gx_count, col_count * gy_count)
    *shuffled, terms = pl.pallas_call(
        partial(cycle_kernel, grid_shape, blocks),
        out_shape=[pltpu.VMEM(block, f32)] * 3,
        in_specs=[hbm] * 2 + [vmem] * (3 * blocks),
        out_specs=[vmem] * 3,
        scratch_shapes=scratch,
        compiler_params=pltpu.CompilerParams(vmem_limit_bytes=24 * 1024 * 1024),
        name="cycles",
    )(in_hbm(well_cells), in_hbm(well_rates), *operands)
    gradient = summed(terms, "scen")
    pressure, adjoint = pl.pallas_call(
        order_kernel,
        out_shape=[state] * 2,
        in_specs=[vmem] * 2,
        out_specs=[vmem] * 2,
        cost_estimate=pl.CostEstimate(flops=2 * row_count * LANES**2 * 16, bytes_accessed=2**19, transcendentals=0),
        name="order",
    )(*[in_vmem(value) for value in shuffled])
    return pressure, adjoint, gradient


def solution(mesh):
    return jax.shard_map(
        shards,
        mesh=mesh,
        in_specs=(
            P(None, "gx", "gy"),
            P(None, "gx", "gy"),
            P(),
            P(None, "gx", "gy"),
            P("scen", None, "gx", "gy"),
            P("scen", None, "gx", "gy"),
            P("scen", None),
            P("scen", None),
        ),
        out_specs=(P("scen", None, "gx", "gy"), P("scen", None, "gx", "gy"), P(None, "gx", "gy")),
        check_vma=False,
    )
```

```python
from functools import partial

import jax
import jax.numpy as jnp
from jax import lax
from jax.experimental import pallas as pl
from jax.experimental.pallas import tpu as pltpu
from jax.sharding import PartitionSpec as P

WELLS = 5
FACIES = 4
LAYERS = 2
SMOOTH = 2
COARSE = 4

vertical = 0.3
damping = 0.8

LANES = 128
HALF = 64
SUB = 8
PERM, ACC, PREV, OBS = range(4)
NEAR = 26
ROOM = HALF // 2 - NEAR
LEVELS = ((2, 1), (1, 1), (1, 2))


def lane_index():
    return lax.broadcasted_iota(jnp.int32, (SUB, LANES), 1)


def row_index():
    return lax.broadcasted_iota(jnp.int32, (SUB, LANES), 0)


def lane_roll(value, shift):
    return pltpu.roll(value, shift % LANES, value.ndim - 1)


def row_roll(value, shift):
    return pltpu.roll(value, shift % SUB, 0)


def shuffle(value, inverse):
    rows = lax.broadcasted_iota(jnp.int32, (LANES, LANES), 0)
    cols = lax.broadcasted_iota(jnp.int32, (LANES, LANES), 1)
    natural, place = (cols, rows) if inverse else (rows, cols)
    matrix = (natural == 2 * (place % HALF) + place // HALF).astype(jnp.bfloat16)
    rest = value.reshape(-1, LANES)
    count = rest.shape[0]
    parts = []
    for _ in range(3):
        parts.append(rest.astype(jnp.bfloat16))
        rest = rest - parts[-1].astype(jnp.float32)
    moved_parts = jnp.dot(jnp.concatenate(parts, 0), matrix, preferred_element_type=jnp.float32)
    total = moved_parts[:count] + moved_parts[count:2 * count] + moved_parts[2 * count:]
    return total.reshape(value.shape)


def place_in_half(shape):
    return lax.broadcasted_iota(jnp.int32, shape, len(shape) - 1) % HALF


def spare_lanes(number, place):
    shift = NEAR - number * ROOM
    low, high = number * ROOM, HALF - (number + 1) * ROOM
    return (((place >= NEAR) & (place < HALF // 2), (place >= low) & (place < low + ROOM), shift),
            ((place >= HALF // 2) & (place < HALF - NEAR), (place >= high) & (place < high + ROOM), -shift))


def interleaved(rows):
    count = rows.shape[0] // SUB
    return jnp.concatenate([rows[pl.ds(t, SUB, stride=count), :] for t in range(count)], axis=0)


def put_in_order(shuffled, ordered):
    count = ordered.shape[-2] // SUB
    natural = shuffle(shuffled, True)
    for layer in range(LAYERS):
        for t in range(count):
            ordered[layer, pl.ds(t, SUB, stride=count), :] = natural[layer, t * SUB:(t + 1) * SUB]


def pack_kernel(scale_hbm, perm_log_hbm, facies_hbm, acc_hbm, prev_hbm, obs_hbm, own_a, own_b, message_a, message_b,
                scale, perm_log, facies, acc, prev, obs, sems):
    pairs = ((scale_hbm, scale), (perm_log_hbm, perm_log), (facies_hbm, facies), (acc_hbm, acc), (prev_hbm, prev),
             (obs_hbm, obs))
    copies = [pltpu.make_async_copy(source, target, sems.at[i]) for i, (source, target) in enumerate(pairs)]
    for copy in copies:
        copy.start()

    def layers(ref):
        return jnp.stack([interleaved(ref.at[layer]) for layer in range(LAYERS)])

    for copy in copies:
        copy.wait()
    label = layers(facies)
    factor = jnp.zeros(label.shape, jnp.float32)
    for number in range(FACIES):
        factor = factor + jnp.where(label == number, scale[number], jnp.float32(0.0))
    fields = shuffle(
        jnp.stack([jnp.exp(layers(perm_log)) * factor, layers(acc), layers(prev.at[0]), layers(obs.at[0])]), False)
    for number in range(4):
        (own_a, own_b)[number // 2][number % 2] = fields[number]
    place = place_in_half(label.shape)
    full = []
    for number in range(3):
        value = fields[number]
        for lanes, _, shift in spare_lanes(number, place):
            value = jnp.where(lanes, lane_roll(fields[OBS], shift), value)
        full.append(value)
    low = place_in_half(label.shape[1:]) < HALF // 2
    left_first = low == (lax.axis_index("gy") % 2 == 1)
    couples = [(full[0][layer], full[1][layer]) for layer in range(LAYERS)] + [(full[2][0], full[2][1])]
    for plane, (one, two) in enumerate(couples):
        first, second = lane_roll(one, HALF), lane_roll(two, HALF + HALF // 2)
        message_a[plane] = jnp.where(left_first, first, second)
        message_b[plane] = jnp.where(left_first, second, first)


def merge_kernel(message_a, message_b, beside):
    place = place_in_half(beside.shape[2:])
    from_a = (place < HALF // 2) != (lax.axis_index("gy") % 2 == 1)
    full = [[], [], []]
    for plane in range(3):
        a, b = message_a[plane], message_b[plane]
        one = jnp.where(from_a, a, b)
        two = lane_roll(jnp.where(from_a, b, a), -(HALF // 2))
        for number, value in zip((0, 1) if plane < 2 else (2, 2), (one, two)):
            full[number].append(value)
    near = (place < NEAR) | (place >= HALF - NEAR)
    for layer in range(LAYERS):
        observed = jnp.zeros(place.shape, jnp.float32)
        for number in range(3):
            value = full[number][layer]
            beside[number, layer] = jnp.where(near, value, 0.0)
            for _, lanes, shift in spare_lanes(number, place):
                observed = jnp.where(lanes, lane_roll(value, -shift), observed)
        beside[OBS, layer] = observed


class Level:
    def __init__(self, count, width, span, blocks, refs):
        self.count = count
        self.width = width
        self.span = span
        self.blocks = blocks
        (self.c_south, self.c_first, self.c_inner, self.c_east, self.c_west, self.c_layer, self.weight, self.diag,
         self.target, self.now, self.later) = refs

    @staticmethod
    def scratch(count, width, blocks):
        def vectors(*lead):
            return pltpu.VMEM(lead + (SUB, LANES), jnp.float32)

        whole = vectors(LAYERS, width, blocks, count)
        edge = vectors(LAYERS, blocks, count)
        return [whole, vectors(LAYERS, width, blocks), edge, edge, edge, vectors(width, blocks, count)] + [whole] * 5

    def steps(self):
        for b in range(self.blocks):
            for t in range(self.count):
                yield b, t

    def members(self):
        for layer in range(LAYERS):
            for u in range(self.width):
                yield layer, u


def row_before(values):
    edge = row_index() < 1
    rolled = [row_roll(value, 1) for value in values]
    return [jnp.where(edge, rolled[b - 1], rolled[b]) for b in range(len(values))]


def row_after(values):
    edge = row_index() >= SUB - 1
    rolled = [row_roll(value, -1) for value in values]
    return [jnp.where(edge, rolled[(b + 1) % len(values)], rolled[b]) for b in range(len(values))]


class Field:
    def __init__(self, level, source, coarse=None):
        self.source = source
        self.coarse = coarse
        self.count = level.count
        self.read = {}
        self.before, self.after = {}, {}
        for layer, u in level.members():
            lows = row_before([self.value(layer, u, b, level.count - 1) for b in range(level.blocks)])
            highs = row_after([self.value(layer, u, b, 0) for b in range(level.blocks)])
            for b in range(level.blocks):
                self.before[layer, u, b] = lows[b]
                self.after[layer, u, b] = highs[b]

    def value(self, layer, u, b, t):
        value = self.source[layer, u, b, t]
        return value if self.coarse is None else value + self.coarse[layer, 0, b, t // 2]

    def at(self, layer, u, b, t):
        if t < 0:
            return self.before[layer, u, b]
        if t >= self.count:
            return self.after[layer, u, b]
        key = layer, u, b, t
        if key not in self.read:
            self.read[key] = self.value(*key)
        return self.read[key]


def row_coeff(level, layer, u, b, t):
    return level.c_south[layer, u, b, t] if t >= 0 else level.c_first[layer, u, b]


def neighbour_sums(level, source, coarse=None):
    field = Field(level, source, coarse)
    coeffs = {}
    for b, t in level.steps():
        for member in level.members():
            for at in (t - 1, t):
                if (member, b, at) not in coeffs:
                    coeffs[member, b, at] = row_coeff(level, *member, b, at)
        layer_coeffs = [level.c_layer[u, b, t] for u in range(level.width)]
        for layer in range(LAYERS):
            here = [field.at(layer, u, b, t) for u in range(level.width)]
            east_coeff, west_coeff = level.c_east[layer, b, t], level.c_west[layer, b, t]
            if level.width == 2:
                inner = level.c_inner[layer, b, t]
                beside = [inner * here[1] + west_coeff * lane_roll(here[1], 1),
                          inner * here[0] + east_coeff * lane_roll(here[0], -1)]
            else:
                beside = [east_coeff * lane_roll(here[0], -level.span) + west_coeff * lane_roll(here[0], level.span)]
            for u in range(level.width):
                total = (coeffs[(layer, u), b, t - 1] * field.at(layer, u, b, t - 1)
                         + coeffs[(layer, u), b, t] * field.at(layer, u, b, t + 1)
                         + (beside[u] + layer_coeffs[u] * field.at(1 - layer, u, b, t)))
                yield (layer, u, b, t), here[u], total


def sweep(level, source, result, coarse=None):
    for key, value, total in neighbour_sums(level, source, coarse):
        result[key] = (1.0 - damping) * value + level.weight[key] * (level.target[key] + total)


def sweeps(level, count, coarse=None):
    for number in range(count):
        sweep(level, level.now, level.later, coarse if number == 0 else None)
        level.now, level.later = level.later, level.now


def first_sweep(level):
    for b, t in level.steps():
        for layer, u in level.members():
            key = layer, u, b, t
            level.now[key] = level.weight[key] * level.target[key]


def pair_sum(value, span):
    lower = lane_index() % (2 * span) < span
    return value + jnp.where(lower, lane_roll(value, -span), lane_roll(value, span))


def low_group(value, span):
    return jnp.where(lane_index() % (2 * span) < span, value, lane_roll(value, span))


def high_group(value, span):
    return jnp.where(lane_index() % (2 * span) < span, lane_roll(value, -span), value)


def column_sum(values, level):
    return values[0] + values[1] if level.width == 2 else pair_sum(values[0], level.span)


def restrict_residual(fine, coarse):
    residuals = {}
    for key, value, total in neighbour_sums(fine, fine.now):
        layer, u, b, t = key
        residuals[key] = fine.target[key] + total - fine.diag[key] * value
        if t % 2 == 1 and u == fine.width - 1:
            rows = [residuals[layer, v, b, t - 1] + residuals[layer, v, b, t] for v in range(fine.width)]
            coarse.target[layer, 0, b, t // 2] = column_sum(rows, fine)


def vcycle(levels):
    finest, middle, bottom = levels
    sweeps(finest, SMOOTH - 1)
    restrict_residual(finest, middle)
    first_sweep(middle)
    sweeps(middle, SMOOTH - 1)
    restrict_residual(middle, bottom)
    first_sweep(bottom)
    sweeps(bottom, COARSE - 1)
    sweeps(middle, SMOOTH, bottom.now)
    sweeps(finest, SMOOTH, middle.now)


def harmonic(left, right):
    return 2.0 * left * right / jnp.maximum(left + right, 1e-20)


def finest_coeffs(level, perm, joined):
    last = level.count - 1
    for layer, u in level.members():
        heads = [perm[layer, u, b, 0] for b in range(level.blocks)]
        rolled = [row_roll(value, -1) for value in heads]
        edge = row_index() >= SUB - 1
        for b in range(level.blocks):
            after = jnp.where(edge, joined[b] * rolled[(b + 1) % level.blocks], rolled[b])
            for t in range(level.count):
                beyond = perm[layer, u, b, t + 1] if t < last else after
                level.c_south[layer, u, b, t] = harmonic(perm[layer, u, b, t], beyond)
        firsts = row_before([level.c_south[layer, u, b, last] for b in range(level.blocks)])
        for b in range(level.blocks):
            level.c_first[layer, u, b] = firsts[b]
    for b, t in level.steps():
        for u in range(level.width):
            level.c_layer[u, b, t] = vertical * harmonic(perm[0, u, b, t], perm[1, u, b, t])
        for layer in range(LAYERS):
            even, odd = perm[layer, 0, b, t], perm[layer, 1, b, t]
            level.c_inner[layer, b, t] = harmonic(even, odd)
            east = harmonic(odd, lane_roll(even, -1))
            level.c_east[layer, b, t] = east
            level.c_west[layer, b, t] = lane_roll(east, 1)


def with_weight(level, acc):
    for b, t in level.steps():
        for layer, u in level.members():
            key = layer, u, b, t
            if level.width == 2:
                beside = level.c_inner[layer, b, t] + (level.c_west, level.c_east)[u][layer, b, t]
            else:
                beside = level.c_west[layer, b, t] + level.c_east[layer, b, t]
            diag = (row_coeff(level, layer, u, b, t - 1) + row_coeff(level, layer, u, b, t)
                    + (beside + level.c_layer[u, b, t]) + acc[key])
            level.diag[key] = diag
            level.weight[key] = damping / jnp.maximum(diag, 1e-20)


def coarse_coeffs(fine, coarse, fine_acc, coarse_acc):
    width = range(fine.width)
    for b in range(coarse.blocks):
        for layer in range(LAYERS):
            coarse.c_first[layer, 0, b] = column_sum([fine.c_first[layer, u, b] for u in width], fine)
    for b, t in coarse.steps():
        one, two = 2 * t, 2 * t + 1
        coarse.c_layer[0, b, t] = column_sum([fine.c_layer[u, b, one] + fine.c_layer[u, b, two] for u in width], fine)
        for layer in range(LAYERS):
            coarse.c_south[layer, 0, b, t] = column_sum([fine.c_south[layer, u, b, two] for u in width], fine)
            coarse_acc[layer, 0, b, t] = column_sum(
                [fine_acc[layer, u, b, one] + fine_acc[layer, u, b, two] for u in width], fine)
            west = fine.c_west[layer, b, one] + fine.c_west[layer, b, two]
            east = fine.c_east[layer, b, one] + fine.c_east[layer, b, two]
            if fine.width == 1:
                west, east = low_group(west, fine.span), high_group(east, fine.span)
            coarse.c_west[layer, b, t] = west
            coarse.c_east[layer, b, t] = east
    with_weight(coarse, coarse_acc)


def own_columns(even, odd):
    return jnp.where(lane_index() < HALF, even, lane_roll(odd, HALF))


def face_terms(level, pressure, adjoint, perm):
    def face(coeff, one, two):
        changes = [field.at(*one) - (field.at(*two) if isinstance(two, tuple) else two[number])
                   for number, field in enumerate((pressure, adjoint))]
        return (coeff * coeff) * (changes[0] * changes[1])

    rows = {(layer, u): face(level.c_first[layer, u, 0], (layer, u, 0, -1), (layer, u, 0, 0))
            for layer, u in level.members()}
    for t in range(level.count):
        between = [(1.0 / vertical) * face(level.c_layer[u, 0, t], (0, u, 0, t), (1, u, 0, t)) for u in range(2)]
        for layer in range(LAYERS):
            inner = face(level.c_inner[layer, 0, t], (layer, 0, 0, t), (layer, 1, 0, t))
            easts = [lane_roll(field.at(layer, 0, 0, t), -1) for field in (pressure, adjoint)]
            east = face(level.c_east[layer, 0, t], (layer, 1, 0, t), easts)
            terms = []
            for u in range(2):
                south = face(level.c_south[layer, u, 0, t], (layer, u, 0, t), (layer, u, 0, t + 1))
                beside = lane_roll(east, 1) if u == 0 else east
                total = rows[layer, u] + south + (inner + beside) + between[u]
                rows[layer, u] = south
                terms.append(-0.5 * total / perm[layer, u, 0, t])
            yield layer, t, own_columns(*terms)


def order_kernel(*refs):
    for shuffled, ordered in zip(refs[:2], refs[2:]):
        put_in_order(shuffled[...], ordered.at[0])


def split(value, size):
    if size & (size - 1) == 0:
        return value >> (size.bit_length() - 1), value & (size - 1)
    return value // size, value % size


def cycle_kernel(grid_shape, blocks, *refs):
    cells_hbm, rates_hbm = refs[:2]
    inputs = [refs[2 + 3 * b:5 + 3 * b] for b in range(blocks)]
    refs = refs[2 + 3 * blocks:]
    pressure_out, adjoint_out, terms_out = refs[:3]
    cells, rates, sems, perm, acc, middle_acc, bottom_acc, states, terms_rows = refs[3:12]
    refs = refs[12:]
    copies = [pltpu.make_async_copy(cells_hbm, cells, sems.at[0]), pltpu.make_async_copy(rates_hbm, rates, sems.at[1])]
    for copy in copies:
        copy.start()
    count = inputs[0][0].shape[2] // SUB
    levels = [Level(count >> depth, width, span, blocks, refs[11 * depth:11 * depth + 11])
              for depth, (width, span) in enumerate(LEVELS)]
    finest, middle, bottom = levels

    def rows(t):
        return pl.ds(t * SUB, SUB)

    def fields(number, layer, b, t):
        low = lane_index() < HALF
        own = inputs[b][number // 2][number % 2, layer, rows(t), :]
        beside = inputs[b][2][number, layer, rows(t), :]
        return jnp.where(low, own, beside), lane_roll(jnp.where(low, beside, own), HALF)

    gx = lax.axis_index("gx")
    if blocks == 3:
        joined = [1.0, 0.0, 1.0]
    elif blocks == 2:
        joined = [1.0 - gx.astype(jnp.float32), gx.astype(jnp.float32)]
    else:
        joined = [0.0]

    for b, t in finest.steps():
        for layer in range(LAYERS):
            perms, accs, starts = [fields(number, layer, b, t) for number in (PERM, ACC, PREV)]
            for u in range(2):
                key = layer, u, b, t
                perm[key] = perms[u]
                acc[key] = accs[u]
                finest.now[key] = starts[u]
                finest.target[key] = accs[u] * starts[u]

    finest_coeffs(finest, perm, joined)
    with_weight(finest, acc)
    coarse_coeffs(finest, middle, acc, middle_acc)
    coarse_coeffs(middle, bottom, middle_acc, bottom_acc)

    for copy in copies:
        copy.wait()
    layer_count, total_rows, total_cols = grid_shape
    block_rows, block_cols = SUB * count, LANES
    for well in range(WELLS):
        cell = cells[0, well]
        layer, cell = split(cell, total_rows * total_cols)
        row, col = split(cell, total_cols)
        row = row - gx * block_rows
        col = col - lax.axis_index("gy") * block_cols
        if blocks == 3:
            row_inside = (row >= -block_rows) & (row < 2 * block_rows)
        elif blocks == 2:
            row_inside = row >= -block_rows
        else:
            row_inside = row >= 0
        inside = row_inside & (col >= -HALF) & (col < block_cols + HALF)
        row = jnp.where(row < 0, row + blocks * block_rows, row)
        col = jnp.where(col < 0, col + 2 * block_cols, col)
        row = jnp.where(inside, row, 0)
        col = jnp.where(inside, col, 0)
        rate = jnp.where(inside, rates[0, well], 0.0)
        b, in_block = split(row, block_rows)
        s, t = split(in_block, count)
        lane, u = split(col, 2)
        place = layer, u, b, t
        hit = (row_index() == s) & (lane_index() == lane)
        finest.target[place] = finest.target[place] + jnp.where(hit, rate, 0.0)

    sweeps(finest, 1)
    start, other = finest.now, finest.later

    def turn(number, carry):
        finest.now, finest.later = start, other
        vcycle(levels)
        for b, t in finest.steps():
            for layer in range(LAYERS):
                observed = fields(OBS, layer, b, t)
                for u in range(2):
                    key = layer, u, b, t
                    value = finest.now[key]
                    states[(number,) + key] = value
                    target = value - observed[u]
                    finest.target[key] = target
                    start[key] = finest.weight[key] * target
        return carry

    lax.fori_loop(0, 2, turn, 0)
    pressure, adjoint = states.at[0], states.at[1]
    for t in range(count):
        for layer in range(LAYERS):
            for state, result in ((pressure, pressure_out), (adjoint, adjoint_out)):
                result[layer, rows(t), :] = own_columns(*[state[layer, u, 0, t] for u in range(2)])

    for layer, t, terms in face_terms(finest, Field(finest, pressure), Field(finest, adjoint), perm):
        terms_rows[layer, rows(t), :] = terms
    put_in_order(terms_rows[...], terms_out)


def moved(value, axis, step):
    count = lax.axis_size(axis)
    ring = axis == "gx" and count == 2
    pairs = [((i + step) % count, i) for i in range(count) if ring or 0 <= i + step < count]
    return lax.ppermute(value, axis, pairs)


def swapped(value, axis, first):
    pairs = []
    for i in range(first, lax.axis_size(axis) - 1, 2):
        pairs += [(i, i + 1), (i + 1, i)]
    return lax.ppermute(value, axis, pairs)


def summed(value, axis):
    count = lax.axis_size(axis)
    others = [lax.ppermute(value, axis, [(i, i ^ step) for i in range(count)]) for step in range(count - 1, 0, -1)]
    terms = [value] + others[::-1]
    while len(terms) > 1:
        terms = [terms[i] + terms[i + 1] for i in range(0, len(terms), 2)]
    return terms[0]


def in_hbm(value):
    return pltpu.with_memory_space_constraint(value, pltpu.HBM)


def in_vmem(value):
    return pltpu.with_memory_space_constraint(value, pltpu.VMEM)


def shards(
    perm_log,
    facies,
    facies_scale,
    accumulation,
    previous_pressure,
    observed,
    well_cells,
    well_rates,
):
    layer_count, row_count, col_count = perm_log.shape
    gx_count, gy_count = lax.axis_size("gx"), lax.axis_size("gy")
    vmem = pl.BlockSpec(memory_space=pltpu.VMEM)
    hbm = pl.BlockSpec(memory_space=pltpu.HBM)
    f32 = jnp.float32
    fields = (perm_log, facies, accumulation, previous_pressure, observed)
    block = (layer_count, row_count, col_count)
    own_a, own_b, message_a, message_b = pl.pallas_call(
        pack_kernel,
        out_shape=[
            pltpu.VMEM((2,) + block, f32),
            pltpu.VMEM((2,) + block, f32),
            pltpu.VMEM((3,) + block[1:], f32),
            pltpu.VMEM((3,) + block[1:], f32),
        ],
        in_specs=[hbm] * 6,
        out_specs=[vmem] * 4,
        scratch_shapes=[pltpu.SMEM(facies_scale.shape, f32)]
        + [pltpu.VMEM(value.shape, value.dtype) for value in fields] + [pltpu.SemaphoreType.DMA((6,))],
        name="pack",
    )(in_hbm(facies_scale), *[in_hbm(value) for value in fields])

    steps = (0, 1) if gx_count == 2 else (0, 1, -1) if gx_count > 2 else (0,)
    blocks = len(steps)
    owns = [(own_a, own_b)] + [(moved(own_a, "gx", step), moved(own_b, "gx", step)) for step in steps[1:]]
    merge = pl.pallas_call(
        merge_kernel,
        out_shape=pltpu.VMEM((4,) + block, f32),
        in_specs=[vmem] * 2,
        out_specs=vmem,
        cost_estimate=pl.CostEstimate(flops=2**20, bytes_accessed=2**19, transcendentals=0),
        name="merge",
    )
    messages = swapped(message_a, "gy", 0), swapped(message_b, "gy", 1)
    besides = [merge(*[in_vmem(value) for value in messages])]
    for step in steps[1:]:
        besides.append(merge(*[in_vmem(moved(value, "gx", step)) for value in messages]))
    operands = [in_vmem(value) for own, beside in zip(owns, besides) for value in (*own, beside)]

    count = row_count // SUB
    scratch = [pltpu.SMEM(well_cells.shape, jnp.int32), pltpu.SMEM(well_rates.shape, f32), pltpu.SemaphoreType.DMA((2,))]
    whole = [pltpu.VMEM((LAYERS, width, blocks, count >> depth, SUB, LANES), f32) for depth, (width, _) in enumerate(LEVELS)]
    scratch += [whole[0], whole[0], whole[1], whole[2]]
    scratch += [pltpu.VMEM((2, LAYERS, 2, blocks, count, SUB, LANES), f32), pltpu.VMEM(block, f32)]
    for depth, (width, _) in enumerate(LEVELS):
        scratch += Level.scratch(count >> depth, width, blocks)
    state = jax.ShapeDtypeStruct((1, layer_count, row_count, col_count), f32)
    grid_shape = (layer_count, row_count * gx_count, col_count * gy_count)
    *shuffled, terms = pl.pallas_call(
        partial(cycle_kernel, grid_shape, blocks),
        out_shape=[pltpu.VMEM(block, f32)] * 3,
        in_specs=[hbm] * 2 + [vmem] * (3 * blocks),
        out_specs=[vmem] * 3,
        scratch_shapes=scratch,
        compiler_params=pltpu.CompilerParams(vmem_limit_bytes=24 * 1024 * 1024),
        name="cycles",
    )(in_hbm(well_cells), in_hbm(well_rates), *operands)
    gradient = summed(terms, "scen")
    pressure, adjoint = pl.pallas_call(
        order_kernel,
        out_shape=[state] * 2,
        in_specs=[vmem] * 2,
        out_specs=[vmem] * 2,
        cost_estimate=pl.CostEstimate(flops=2 * row_count * LANES**2 * 16, bytes_accessed=2**19, transcendentals=0),
        name="order",
    )(*[in_vmem(value) for value in shuffled])
    return pressure, adjoint, gradient


def solution(mesh):
    return jax.shard_map(
        shards,
        mesh=mesh,
        in_specs=(
            P(None, "gx", "gy"),
            P(None, "gx", "gy"),
            P(),
            P(None, "gx", "gy"),
            P("scen", None, "gx", "gy"),
            P("scen", None, "gx", "gy"),
            P("scen", None),
            P("scen", None),
        ),
        out_specs=(P("scen", None, "gx", "gy"), P("scen", None, "gx", "gy"), P(None, "gx", "gy")),
        check_vma=False,
    )
```
